32 devices in a mesh: groups: 2 (over y), ctx: 16 (over z, x, core).
Axes of the slice: x: 2, y: 2, z: 4, core: 2. Of those that a mesh axis runs over, the one named last changes fastest.
Arguments:
- normed_input: bfloat16 [2048, 8192], P(('groups', 'ctx')), parts along dimension 0, may hold values from -5 to 5
- query_base: bfloat16 [2048, 4096], P(('groups', 'ctx')), parts along dimension 0, may hold values from -6 to 6
- key_base: bfloat16 [2048, 512], P(('groups', 'ctx')), parts along dimension 0, may hold values from -6 to 6
- value_base: bfloat16 [2048, 512], P(('groups', 'ctx')), parts along dimension 0, may hold values from -4 to 4
- adapter_pool: bfloat16 [16, 2686976], P('ctx'), may hold values from -1 to 1
- stretch_adapter: int32 [4], P('groups'), parts along dimension 0, may hold values from 0 to 15
- adapter_owner: int32 [16], replicated, may hold values from 0 to 15, each once
Outputs:
- attended: bfloat16 [2048, 4096], P(('groups', 'ctx')), parts along dimension 0
- out_delta: bfloat16 [2048, 8192], P(('groups', 'ctx')), parts along dimension 0
The draws below stay inside these ranges and needn't reach their ends.
There are 2 independent parts, one for each index of `groups`. The reference program is written for one: setup_inputs(seed, part) draws one part's arguments, and reference() takes and returns one part's arrays. A program takes and returns all parts, laid end to end along the dimension named above; an argument that names none is the same for every part. Nothing has to cross between parts.
All inputs are finite; a program needn't handle non-finite values.
Results may differ from the reference program's by a relative error of at most 0.018.
Values may be sent and summed in bfloat16 or wider, within the bound.
No kernel may reach another device: no remote copies, remote signals or barrier semaphores. Data moves between devices by JAX's collectives and lax.ppermute only.
A program may use at most 192 MiB of HBM per device.

```python
import math
import jax
import jax.numpy as jnp
import numpy as np
from jax import lax

D = 8192
QH = 32
KEYVALUE_HEADS = 4
HEAD_SIZE = 128
ADAPTER_RANK = 64
BLOCK_TOKENS = 512
SEQ = 1024
NCHUNK = 2
ADAPTERS = 16
QKV_POOL = 1900544
POOL = 2686976


def draw_query_base(key, part):
    return jnp.clip(jax.random.normal(jax.random.fold_in(key, 11), (SEQ, QH * HEAD_SIZE), jnp.float32), -4.0, 4.0).astype(jnp.bfloat16)


def draw_key_base(key, part):
    return jnp.clip(jax.random.normal(jax.random.fold_in(key, 13), (SEQ, KEYVALUE_HEADS * HEAD_SIZE), jnp.float32), -4.0, 4.0).astype(jnp.bfloat16)


def draw_adapter_pool(key, part):
    raw_values = jnp.clip(jax.random.normal(jax.random.fold_in(key, 17), (ADAPTERS, POOL), jnp.float32), -4.0, 4.0)
    column = jnp.arange(POOL)
    bound_one = 3 * ADAPTER_RANK * D
    bound_two = bound_one + ADAPTER_RANK * QH * HEAD_SIZE
    bound_three = bound_two + 2 * ADAPTER_RANK * KEYVALUE_HEADS * HEAD_SIZE
    bound_four = bound_three + ADAPTER_RANK * QH * HEAD_SIZE
    in_keyval = (column - bound_two) % (2 * KEYVALUE_HEADS * HEAD_SIZE)
    column_scale = jnp.where(column < bound_one, D ** (-0.5), jnp.where(column < bound_two, 0.01, jnp.where(column < bound_three, jnp.where(in_keyval < KEYVALUE_HEADS * HEAD_SIZE, 0.01, 0.06), jnp.where(column < bound_four, (QH * HEAD_SIZE) ** (-0.5), 0.25))))
    return (raw_values * column_scale.astype(jnp.float32)[None, :]).astype(jnp.bfloat16)


def block_levels(stream_key, extent, split, low, top_value):
    gain = 1.0
    for dim, parts in split:
        draws = jax.random.uniform(jax.random.fold_in(jax.random.fold_in(stream_key, 6), dim), (parts,), jnp.float32, low / len(split), top_value / len(split))
        gain = gain * jnp.repeat(jnp.exp(draws), extent[dim] // parts).reshape((-1,) + (1,) * (len(extent) - 1 - dim))
    return gain


def rank_bounds(amount, lean):
    portions = [(1 << 20) // math.isqrt(standing ** lean) + 1 for standing in range(1, amount + 1)]
    spread = 1 + sum(portions) // (1 << 30)
    return np.cumsum(np.array([max(1, weight // spread) for weight in portions]))


def ranked(stream_key, shape, amount, slope):
    table = rank_bounds(amount, slope)
    ticket = jax.random.randint(jax.random.fold_in(stream_key, 1), shape, 0, int(table[amount - 1]))
    rank = jnp.searchsorted(jnp.asarray(table, jnp.int32), ticket, side="right")
    return jax.random.permutation(jax.random.fold_in(stream_key, 2), amount)[rank].astype(jnp.int32)


def scatter_about(rng, shape, spread, reach, shards=(), kind=jnp.bfloat16):
    values = jax.random.normal(rng, shape, jnp.float32) * spread
    if len(shards) > 0:
        values = block_levels(rng, shape, shards, -0.22, 0.18) * values
    return jnp.clip(values, min=-reach, max=reach).astype(kind)


def setup_inputs(seed: int = 0, part: int = 0) -> dict:
    arg_keys = jax.random.split(jax.random.key(seed), 8)
    own_keys = jax.random.split(jax.random.fold_in(arg_keys[7], part), 8)
    return {
        "normed_input": scatter_about(own_keys[0], (SEQ, D), 1.0, 5.0, ((0, 16),)),
        "query_base": draw_query_base(jax.random.fold_in(jax.random.fold_in(arg_keys[7], part), 71), part),
        "key_base": draw_key_base(jax.random.fold_in(jax.random.fold_in(arg_keys[7], part), 71), part),
        "value_base": scatter_about(own_keys[3], (SEQ, KEYVALUE_HEADS * HEAD_SIZE), 1.0, 4.0, ((0, 16),)),
        "adapter_pool": draw_adapter_pool(jax.random.fold_in(arg_keys[7], 71), part),
        "stretch_adapter": ranked(own_keys[5], (NCHUNK,), ADAPTERS, 2),
        "adapter_owner": jax.random.permutation(arg_keys[6], ADAPTERS).astype(jnp.int32),
    }


adapter_scale = 2.0
rope_base = 500000.0
mask_floor = -1.0e30


def rotate(delta, token_positions, heads):
    half_dim = HEAD_SIZE // 2
    frequency = rope_base ** (-(jnp.arange(half_dim, dtype=jnp.float32) * 2.0) / HEAD_SIZE)
    angle = token_positions.astype(jnp.float32)[:, None] * frequency[None, :]
    cosine = jnp.cos(angle)[:, None, :]
    sine_part = jnp.sin(angle)[:, None, :]
    shaped = delta.reshape(delta.shape[0], heads, HEAD_SIZE)
    first_half = shaped[..., :half_dim]
    second_half = shaped[..., half_dim:]
    joined = jnp.concatenate([first_half * cosine - second_half * sine_part, second_half * cosine + first_half * sine_part], -1)
    return joined.reshape(delta.shape[0], heads * HEAD_SIZE)


def adapter_inputs(hidden_state_rows, query_row_block, key_row_block, value_row_block, projection_piece, token_positions):
    split_one = D * 3 * ADAPTER_RANK
    split_two = split_one + ADAPTER_RANK * QH * HEAD_SIZE
    down_qkv = projection_piece[:split_one].reshape(D, 3 * ADAPTER_RANK)
    query_up_weight = projection_piece[split_one:split_two].reshape(ADAPTER_RANK, QH * HEAD_SIZE)
    keyvalue_up_weight = projection_piece[split_two:].reshape(ADAPTER_RANK, 2 * KEYVALUE_HEADS * HEAD_SIZE)
    narrow_product = jnp.dot(hidden_state_rows, down_qkv, preferred_element_type=jnp.float32).astype(jnp.bfloat16)
    query_correction = adapter_scale * jnp.dot(narrow_product[:, :ADAPTER_RANK], query_up_weight, preferred_element_type=jnp.float32)
    key_correction = adapter_scale * jnp.dot(narrow_product[:, ADAPTER_RANK:2 * ADAPTER_RANK], keyvalue_up_weight[:, :KEYVALUE_HEADS * HEAD_SIZE], preferred_element_type=jnp.float32)
    value_correction = adapter_scale * jnp.dot(narrow_product[:, 2 * ADAPTER_RANK:], keyvalue_up_weight[:, KEYVALUE_HEADS * HEAD_SIZE:], preferred_element_type=jnp.float32)
    queries = (query_row_block.astype(jnp.float32) + rotate(query_correction, token_positions, QH)).astype(jnp.bfloat16)
    new_keys = (key_row_block.astype(jnp.float32) + rotate(key_correction, token_positions, KEYVALUE_HEADS)).astype(jnp.bfloat16)
    new_values = (value_row_block.astype(jnp.float32) + value_correction).astype(jnp.bfloat16)
    return queries, new_keys, new_values


def output_delta(attended_rows, out_part):
    down_out = out_part[:QH * HEAD_SIZE * ADAPTER_RANK].reshape(QH * HEAD_SIZE, ADAPTER_RANK)
    raised_output = out_part[QH * HEAD_SIZE * ADAPTER_RANK:].reshape(ADAPTER_RANK, D)
    narrow_product = jnp.dot(attended_rows, down_out, preferred_element_type=jnp.float32).astype(jnp.bfloat16)
    return (adapter_scale * jnp.dot(narrow_product, raised_output, preferred_element_type=jnp.float32)).astype(jnp.bfloat16)


def reference(normed_input, query_base, key_base, value_base, adapter_pool, stretch_adapter, adapter_owner):
    adapter_ids = jnp.arange(ADAPTERS, dtype=jnp.int32)
    slots = jnp.sum(jnp.where(stretch_adapter[:, None] == adapter_ids[None, :], adapter_owner[None, :], 0), axis=1).astype(jnp.int32)

    def one_stretch(stretch_index):
        starting_row = stretch_index * BLOCK_TOKENS
        token_positions = starting_row + jnp.arange(BLOCK_TOKENS, dtype=jnp.int32)
        pool_row = lax.dynamic_index_in_dim(adapter_pool, slots[stretch_index], 0, keepdims=False)
        return adapter_inputs(lax.dynamic_slice_in_dim(normed_input, starting_row, BLOCK_TOKENS, 0),
                           lax.dynamic_slice_in_dim(query_base, starting_row, BLOCK_TOKENS, 0),
                           lax.dynamic_slice_in_dim(key_base, starting_row, BLOCK_TOKENS, 0),
                           lax.dynamic_slice_in_dim(value_base, starting_row, BLOCK_TOKENS, 0),
                           pool_row[:QKV_POOL], token_positions)

    stretch_list = jnp.arange(NCHUNK, dtype=jnp.int32)
    queries, all_keys, all_values = lax.map(one_stretch, stretch_list)
    queries = queries.reshape(SEQ, QH * HEAD_SIZE)
    key_heads = all_keys.reshape(SEQ, KEYVALUE_HEADS, HEAD_SIZE).astype(jnp.float32)
    value_heads = all_values.reshape(SEQ, KEYVALUE_HEADS, HEAD_SIZE).astype(jnp.float32)
    group_size = QH // KEYVALUE_HEADS
    block_rows = min(512, SEQ)
    key_pos = jnp.arange(SEQ, dtype=jnp.int32)

    def attend(block_index):
        starting_row = block_index * block_rows
        block_q = lax.dynamic_slice_in_dim(queries, starting_row, block_rows, 0)
        head_q = block_q.reshape(block_rows, KEYVALUE_HEADS, group_size, HEAD_SIZE).transpose(1, 2, 0, 3).reshape(KEYVALUE_HEADS, group_size * block_rows, HEAD_SIZE)
        query_pos = jnp.tile(starting_row + jnp.arange(block_rows, dtype=jnp.int32), group_size)
        scores = jnp.einsum("hqd,khd->hqk", head_q.astype(jnp.float32), key_heads) * (HEAD_SIZE ** -0.5)
        allowed = (query_pos[:, None] >= key_pos[None, :])[None]
        row_max = jnp.max(jnp.where(allowed, scores, mask_floor), axis=-1)
        weights = jnp.where(allowed, jnp.exp(scores - row_max[..., None]), 0.0)
        total = jnp.sum(weights, axis=-1)
        rounded = lax.optimization_barrier(weights.astype(jnp.bfloat16))
        summed = jnp.einsum("hqk,khd->hqd", rounded.astype(jnp.float32), value_heads)
        result = summed / total[..., None]
        return result.reshape(KEYVALUE_HEADS, group_size, block_rows, HEAD_SIZE).transpose(2, 0, 1, 3).reshape(block_rows, QH * HEAD_SIZE).astype(jnp.bfloat16)

    attended = lax.map(attend, jnp.arange(SEQ // block_rows, dtype=jnp.int32)).reshape(SEQ, QH * HEAD_SIZE)

    def out_stretch(stretch_index):
        starting_row = stretch_index * BLOCK_TOKENS
        pool_row = lax.dynamic_index_in_dim(adapter_pool, slots[stretch_index], 0, keepdims=False)
        return output_delta(lax.dynamic_slice_in_dim(attended, starting_row, BLOCK_TOKENS, 0), pool_row[QKV_POOL:])

    out_delta = lax.map(out_stretch, stretch_list).reshape(SEQ, D)
    return attended, out_delta
```

```python
from functools import partial
import math

import jax
import jax.numpy as jnp
from jax import lax
from jax.experimental import pallas as pl
from jax.experimental.pallas import tpu as pltpu
from jax.sharding import PartitionSpec as P

D = 8192
QH = 32
KEYVALUE_HEADS = 4
HEAD_SIZE = 128
ADAPTER_RANK = 64
BLOCK_TOKENS = 512
QKV_POOL = 1900544


adapter_scale = 2.0
rope_base = 500000.0
mask_floor = -1e30


def from_partner(block, axis, apart):
    count = lax.axis_size(axis)
    route = []
    for low in range(count):
        high = low | 1 << apart
        if high != low and high < count:
            route += [(low, high), (high, low)]
    return lax.ppermute(block, axis, route)


def rotate(delta, token_positions, heads):
    half_dim = HEAD_SIZE // 2
    frequency = rope_base ** (-(jnp.arange(half_dim, dtype=jnp.float32) * 2.0) / HEAD_SIZE)
    angle = token_positions.astype(jnp.float32)[:, None] * frequency[None, :]
    cosine = jnp.cos(angle)[:, None, :]
    sine_part = jnp.sin(angle)[:, None, :]
    shaped = delta.reshape(delta.shape[0], heads, HEAD_SIZE)
    first_half = shaped[..., :half_dim]
    second_half = shaped[..., half_dim:]
    joined = jnp.concatenate(
        [
            first_half * cosine - second_half * sine_part,
            second_half * cosine + first_half * sine_part,
        ],
        -1,
    )
    return joined.reshape(delta.shape[0], heads * HEAD_SIZE)


def project_heads(
    narrow_product, query_row_block, key_row_block, value_row_block, upper_part, token_positions
):
    query_up_weight = upper_part[: ADAPTER_RANK * QH * HEAD_SIZE].reshape(
        ADAPTER_RANK, QH * HEAD_SIZE
    )
    keyvalue_up_weight = upper_part[ADAPTER_RANK * QH * HEAD_SIZE :].reshape(
        ADAPTER_RANK, 2 * KEYVALUE_HEADS * HEAD_SIZE
    )
    query_correction = adapter_scale * jnp.dot(
        narrow_product[:, :ADAPTER_RANK], query_up_weight, preferred_element_type=jnp.float32
    )
    key_correction = adapter_scale * jnp.dot(
        narrow_product[:, ADAPTER_RANK : 2 * ADAPTER_RANK],
        keyvalue_up_weight[:, : KEYVALUE_HEADS * HEAD_SIZE],
        preferred_element_type=jnp.float32,
    )
    value_correction = adapter_scale * jnp.dot(
        narrow_product[:, 2 * ADAPTER_RANK :],
        keyvalue_up_weight[:, KEYVALUE_HEADS * HEAD_SIZE :],
        preferred_element_type=jnp.float32,
    )
    queries = (
        query_row_block.astype(jnp.float32) + rotate(query_correction, token_positions, QH)
    ).astype(jnp.bfloat16)
    new_keys = (
        key_row_block.astype(jnp.float32) + rotate(key_correction, token_positions, KEYVALUE_HEADS)
    ).astype(jnp.bfloat16)
    new_values = (value_row_block.astype(jnp.float32) + value_correction).astype(jnp.bfloat16)
    return (queries, new_keys, new_values)


def output_delta(attended_rows, out_part):
    down_out = out_part[: QH * HEAD_SIZE * ADAPTER_RANK].reshape(QH * HEAD_SIZE, ADAPTER_RANK)
    raised_output = out_part[QH * HEAD_SIZE * ADAPTER_RANK :].reshape(ADAPTER_RANK, D)
    narrow_product = jnp.dot(attended_rows, down_out, preferred_element_type=jnp.float32).astype(
        jnp.bfloat16
    )
    return (
        adapter_scale * jnp.dot(narrow_product, raised_output, preferred_element_type=jnp.float32)
    ).astype(jnp.bfloat16)


def head_major(query_row_block):
    count_rows = query_row_block.shape[0]
    group_size = QH // KEYVALUE_HEADS
    return (
        query_row_block.reshape(count_rows, KEYVALUE_HEADS, group_size, HEAD_SIZE)
        .transpose(1, 2, 0, 3)
        .reshape(KEYVALUE_HEADS, group_size * count_rows, HEAD_SIZE)
    )


def row_major(head_rows, count_rows):
    group_size = QH // KEYVALUE_HEADS
    return (
        head_rows.reshape(KEYVALUE_HEADS, group_size, count_rows, HEAD_SIZE)
        .transpose(2, 0, 1, 3)
        .reshape(count_rows, QH * HEAD_SIZE)
    )


def online_update(current, queries, query_pos, key_slice, value_slice, key_start):
    run_max, run_sum, run_acc = current
    scores = jnp.einsum(
        "hqd,khd->hqk", queries, key_slice, preferred_element_type=jnp.float32
    ) * HEAD_SIZE ** (-0.5)
    key_pos = key_start + jnp.arange(key_slice.shape[0], dtype=jnp.int32)
    allowed = (query_pos[:, None] >= key_pos[None, :])[None]
    new_max = jnp.maximum(run_max, jnp.max(jnp.where(allowed, scores, mask_floor), axis=-1))
    weights = jnp.where(allowed, jnp.exp(scores - new_max[..., None]), 0.0)
    rescale = jnp.exp(run_max - new_max)
    new_sum = run_sum * rescale + jnp.sum(weights, axis=-1)
    new_acc = run_acc * rescale[..., None] + jnp.einsum(
        "hqk,khd->hqd",
        weights.astype(jnp.bfloat16),
        value_slice,
        preferred_element_type=jnp.float32,
    )
    return (new_max, new_sum, new_acc)


def unchanged(current):
    return current


def fold_keys(carry_state, shard_part, prepared):
    key_row_block, value_row_block = shard_part
    key_count = key_row_block.shape[0]
    sub_width = math.gcd(key_count, 1024)
    key_heads = key_row_block.reshape(key_count // sub_width, sub_width, KEYVALUE_HEADS, HEAD_SIZE)
    value_heads = value_row_block.reshape(
        key_count // sub_width, sub_width, KEYVALUE_HEADS, HEAD_SIZE
    )

    def one_step(sub_index, carried):
        key_start = sub_index * sub_width
        key_slice = lax.dynamic_index_in_dim(key_heads, sub_index, 0, keepdims=False)
        value_slice = lax.dynamic_index_in_dim(value_heads, sub_index, 0, keepdims=False)
        updated = []
        for (queries, query_pos), running in zip(prepared, carried):
            advance = partial(
                online_update,
                queries=queries,
                query_pos=query_pos,
                key_slice=key_slice,
                value_slice=value_slice,
                key_start=key_start,
            )
            updated.append(lax.cond(key_start <= jnp.max(query_pos), advance, unchanged, running))
        return tuple(updated)

    return lax.fori_loop(0, key_count // sub_width, one_step, carry_state)


def finish_block(result, count_rows):
    run_max, run_sum, run_acc = result
    divisor = jnp.where(run_sum > 0.0, run_sum, 1.0)
    return row_major(run_acc / divisor[..., None], count_rows).astype(jnp.bfloat16)


def spread_shards(
    normed_input, query_base, key_base, value_base, adapter_pool, stretch_adapter, adapter_owner
):
    cycle_size = lax.axis_size("ctx")
    my_index = lax.axis_index("ctx")
    tok_rows = normed_input.shape[0]
    token_positions = my_index * tok_rows + jnp.arange(tok_rows, dtype=jnp.int32)
    device_ids = jnp.arange(cycle_size, dtype=jnp.int32)
    stretch_of = device_ids * tok_rows // BLOCK_TOKENS
    stretch_ids = jnp.arange(stretch_adapter.shape[0], dtype=jnp.int32)
    adapter_of = jnp.sum(
        jnp.where(stretch_of[:, None] == stretch_ids[None, :], stretch_adapter[None, :], 0), axis=1
    )
    adapter_ids = jnp.arange(adapter_owner.shape[0], dtype=jnp.int32)
    slot_of = jnp.sum(
        jnp.where(adapter_of[:, None] == adapter_ids[None, :], adapter_owner[None, :], 0), axis=1
    )
    down_size = 3 * ADAPTER_RANK * D
    group_count = BLOCK_TOKENS // tok_rows
    levels = group_count.bit_length() - 1
    local_index = my_index % group_count
    col_width = D // group_count
    piece_len = down_size // (group_count * cycle_size)
    pool_rows = adapter_pool.shape[0]
    down_shaped = adapter_pool[:, :down_size].reshape(pool_rows, group_count, cycle_size, piece_len)
    spread_down = lax.all_to_all(down_shaped, "ctx", split_axis=2, concat_axis=0, tiled=True)
    flat_down = spread_down.reshape(-1, piece_len)
    wanted = jnp.take(flat_down, slot_of * group_count + device_ids % group_count, axis=0)[
        :, None, :
    ]
    down_slice = lax.all_to_all(wanted, "ctx", split_axis=0, concat_axis=1, tiled=True).reshape(
        col_width, 3 * ADAPTER_RANK
    )
    spread_rest = lax.all_to_all(
        adapter_pool[:, down_size:], "ctx", split_axis=1, concat_axis=0, tiled=True
    )
    rest_row = lax.all_to_all(
        jnp.take(spread_rest, slot_of, axis=0), "ctx", split_axis=0, concat_axis=1, tiled=True
    )[0]
    upper_part = rest_row[: QKV_POOL - down_size]
    out_part = rest_row[QKV_POOL - down_size :]
    pieces = normed_input.reshape(tok_rows, group_count, col_width)
    slice_order = jnp.bitwise_xor(local_index, jnp.arange(group_count, dtype=jnp.int32))
    moving = jnp.take(pieces, slice_order, axis=1).transpose(1, 0, 2)
    for level in range(levels):
        shaped = moving.reshape(group_count >> level + 1, 2, 1 << level, tok_rows, col_width)
        arrived = from_partner(shaped[:, 1], "ctx", level)
        moving = jnp.stack([shaped[:, 0], arrived], 1).reshape(group_count, tok_rows, col_width)
    partial_rows = jnp.dot(
        moving.reshape(group_count * tok_rows, col_width),
        down_slice,
        preferred_element_type=jnp.float32,
    ).reshape(group_count, tok_rows, 3 * ADAPTER_RANK)
    for level in reversed(range(levels)):
        halves = partial_rows.reshape(2, partial_rows.shape[0] // 2, tok_rows, 3 * ADAPTER_RANK)
        partial_rows = halves[0] + from_partner(
            halves[1].astype(jnp.bfloat16), "ctx", level
        ).astype(jnp.float32)
    narrow_product = partial_rows[0].astype(jnp.bfloat16)
    queries, new_keys, new_values = project_heads(
        narrow_product, query_base, key_base, value_base, upper_part, token_positions
    )
    group_size = QH // KEYVALUE_HEADS
    blocks = [(queries, token_positions)]
    prepared = [
        (head_major(block_q), jnp.tile(block_pos, group_size)) for block_q, block_pos in blocks
    ]
    initial = tuple(
        (
            (
                jnp.full((KEYVALUE_HEADS, head_q.shape[1]), mask_floor, jnp.float32),
                jnp.zeros((KEYVALUE_HEADS, head_q.shape[1]), jnp.float32),
                jnp.zeros((KEYVALUE_HEADS, head_q.shape[1], HEAD_SIZE), jnp.float32),
            )
            for head_q, block_pos in prepared
        )
    )
    finals = fold_keys(
        initial,
        (
            lax.all_gather(new_keys, "ctx", axis=0, tiled=True),
            lax.all_gather(new_values, "ctx", axis=0, tiled=True),
        ),
        prepared,
    )
    attended = finish_block(finals[0], tok_rows)
    out_delta = output_delta(attended, out_part)
    return (attended, out_delta)


SECTIONS = (
    (0, D * 3 * ADAPTER_RANK // 128),
    (D * 3 * ADAPTER_RANK // 128, ADAPTER_RANK * QH * HEAD_SIZE // 128),
    (14336, 2 * ADAPTER_RANK * KEYVALUE_HEADS * HEAD_SIZE // 128),
    (14848, QH * HEAD_SIZE * ADAPTER_RANK // 128),
    (16896, ADAPTER_RANK * D // 128),
)
PIECES = 8
PIECE_ROWS = 20992 // (2 * PIECES)
DOWN_ROWS = 768
GROUP = QH // KEYVALUE_HEADS


def pack_kernel(place_ref, pool, own, other, buffers, sems):
    plane = place_ref[0]
    core = place_ref[1]

    def copies(piece, slot):
        listed = []
        offset = 0
        for number, (first, rows) in enumerate(SECTIONS):
            share = rows // (2 * PIECES)
            begin = pl.multiple_of((first + (piece * 2 + plane) * share) * 128, 4096)
            listed.append(
                pltpu.make_async_copy(
                    pool.at[:, pl.ds(begin, share * 128)],
                    buffers.at[slot, :, pl.ds(offset, share * 128)],
                    sems.at[slot, number],
                )
            )
            offset += share * 128
        return listed

    for copy in copies(0, 0):
        copy.start()

    def step(piece, carried):
        slot = lax.rem(piece, 2)

        @pl.when(piece < PIECES - 1)
        def _():
            for copy in copies(piece + 1, 1 - slot):
                copy.start()

        for copy in copies(piece, slot):
            copy.wait()

        def convert(target):
            def chunk(index, inner):
                line = buffers[slot, :, pl.ds(pl.multiple_of(index * 4096, 4096), 4096)]
                block = line.astype(jnp.float32).reshape(32, 128).astype(jnp.bfloat16)
                target[piece // 2, pl.ds(pl.multiple_of(index * 32, 32), 32), :] = block
                return inner

            lax.fori_loop(0, PIECE_ROWS // 32, chunk, 0)

        mine = lax.rem(piece, 2) == core

        @pl.when(mine)
        def _():
            convert(own)

        @pl.when(jnp.logical_not(mine))
        def _():
            convert(other)

        return carried

    lax.fori_loop(0, PIECES, step, 0)


def pack_row(place, pool):
    slab = jax.ShapeDtypeStruct((PIECES // 2, PIECE_ROWS, 128), jnp.bfloat16)
    return pl.pallas_call(
        pack_kernel,
        out_shape=(slab, slab),
        in_specs=[
            pl.BlockSpec(memory_space=pltpu.SMEM),
            pl.BlockSpec(memory_space=pl.ANY),
        ],
        out_specs=(
            pl.BlockSpec(memory_space=pltpu.VMEM),
            pl.BlockSpec(memory_space=pltpu.VMEM),
        ),
        scratch_shapes=[
            pltpu.VMEM((2, 1, PIECE_ROWS * 128), jnp.bfloat16),
            pltpu.SemaphoreType.DMA((2, len(SECTIONS))),
        ],
        compiler_params=pltpu.CompilerParams(vmem_limit_bytes=16 << 20),
        cost_estimate=pl.CostEstimate(flops=0, bytes_accessed=8 << 20, transcendentals=0),
    )(place, pool)


def attend_kernel(
    place_ref,
    query_block,
    key_block,
    value_block,
    own_rank,
    all_rank,
    query_up,
    key_up,
    value_up,
    cosines,
    sines,
    down_out,
    up_out,
    attended,
    out_delta,
    total,
):
    step = pl.program_id(0)
    rows = query_block.shape[0]
    base = place_ref[0] * rows
    dot = partial(jnp.dot, preferred_element_type=jnp.float32)

    def turned(delta, cosine, sine):
        return delta * cosine + pltpu.roll(delta, HEAD_SIZE // 2, 1) * sine

    keys = []
    values = []
    for block in range(key_up.shape[0]):
        span = slice(block * BLOCK_TOKENS, (block + 1) * BLOCK_TOKENS)
        delta = adapter_scale * dot(all_rank[span, :ADAPTER_RANK], key_up[block])
        delta = turned(delta, cosines[span, :], sines[span, :])
        keys.append((key_block[span, :].astype(jnp.float32) + delta).astype(jnp.bfloat16))
        delta = adapter_scale * dot(all_rank[span, ADAPTER_RANK:], value_up[block])
        values.append((value_block[span, :].astype(jnp.float32) + delta).astype(jnp.bfloat16))
    keys = jnp.concatenate(keys, 0)
    values = jnp.concatenate(values, 0)
    here = pl.ds(pl.multiple_of(base, rows), rows)
    cosine = cosines[here, :]
    sine = sines[here, :]
    delta = adapter_scale * dot(own_rank[:, :ADAPTER_RANK], query_up[...])
    added = jnp.zeros((rows, ADAPTER_RANK), jnp.float32)
    half = GROUP // 2
    for first in range(0, GROUP, half):
        queries = []
        for head in range(first, first + half):
            span = slice(head * HEAD_SIZE, (head + 1) * HEAD_SIZE)
            moved = turned(delta[:, span], cosine, sine)
            queries.append(
                (query_block[:, span].astype(jnp.float32) + moved).astype(jnp.bfloat16)
            )
        queries = jnp.concatenate(queries, 0)
        scores = lax.dot_general(
            queries, keys, (((1,), (1,)), ((), ())), preferred_element_type=jnp.float32
        ) * HEAD_SIZE ** (-0.5)
        row = lax.broadcasted_iota(jnp.int32, scores.shape, 0)
        column = lax.broadcasted_iota(jnp.int32, scores.shape, 1)
        scores = jnp.where(column <= base + lax.rem(row, rows), scores, mask_floor)
        weights = jnp.exp(scores - jnp.max(scores, axis=-1, keepdims=True))
        divisor = jnp.sum(weights, axis=-1, keepdims=True)
        result = (dot(weights.astype(jnp.bfloat16), values) / divisor).astype(jnp.bfloat16)
        for place, head in enumerate(range(first, first + half)):
            span = slice(head * HEAD_SIZE, (head + 1) * HEAD_SIZE)
            part = result[place * rows : (place + 1) * rows]
            attended[:, span] = part
            added += dot(part, down_out[span, :])

    @pl.when(step == 0)
    def _():
        total[...] = jnp.zeros_like(total)

    total[...] += added

    @pl.when(step == pl.num_programs(0) - 1)
    def _():
        narrow = total[...].astype(jnp.bfloat16)
        out_delta[...] = (adapter_scale * dot(narrow, up_out[...])).astype(jnp.bfloat16)


def attend(
    place,
    query_base,
    base_rows,
    own_rank,
    all_rank,
    query_up,
    keyval_up,
    cosines,
    sines,
    down_out,
    up_out,
):
    rows = query_base.shape[0]
    seq = base_rows.shape[0]
    blocks = keyval_up.shape[0]
    width = GROUP * HEAD_SIZE

    def whole(shape):
        return pl.BlockSpec(shape, lambda h: (0,) * len(shape))

    return pl.pallas_call(
        attend_kernel,
        grid=(KEYVALUE_HEADS,),
        out_shape=(
            jax.ShapeDtypeStruct((rows, QH * HEAD_SIZE), jnp.bfloat16),
            jax.ShapeDtypeStruct((rows, D), jnp.bfloat16),
        ),
        in_specs=[
            pl.BlockSpec(memory_space=pltpu.SMEM),
            pl.BlockSpec((rows, width), lambda h: (0, h)),
            pl.BlockSpec((seq, HEAD_SIZE), lambda h: (0, h)),
            pl.BlockSpec((seq, HEAD_SIZE), lambda h: (0, h + KEYVALUE_HEADS)),
            whole(own_rank.shape),
            whole(all_rank.shape),
            pl.BlockSpec((ADAPTER_RANK, width), lambda h: (0, h)),
            pl.BlockSpec((blocks, ADAPTER_RANK, HEAD_SIZE), lambda h: (0, 0, h)),
            pl.BlockSpec((blocks, ADAPTER_RANK, HEAD_SIZE), lambda h: (0, 0, h + KEYVALUE_HEADS)),
            whole(cosines.shape),
            whole(sines.shape),
            pl.BlockSpec((width, ADAPTER_RANK), lambda h: (h, 0)),
            whole(up_out.shape),
        ],
        out_specs=(
            pl.BlockSpec((rows, width), lambda h: (0, h)),
            whole((rows, D)),
        ),
        scratch_shapes=[pltpu.VMEM((rows, ADAPTER_RANK), jnp.float32)],
        compiler_params=pltpu.CompilerParams(vmem_limit_bytes=40 << 20),
        cost_estimate=pl.CostEstimate(
            flops=4 * rows * QH * seq * HEAD_SIZE,
            bytes_accessed=10 << 20,
            transcendentals=rows * QH * seq,
        ),
    )(
        place,
        query_base,
        base_rows,
        base_rows,
        own_rank,
        all_rank,
        query_up,
        keyval_up,
        keyval_up,
        cosines,
        sines,
        down_out,
        up_out,
    )


def fetch_pieces(group, chips, odd, own, sibling):
    plane = lax.axis_index("groups")
    index = lax.axis_index("ctx")
    core = index % 2
    chip = index // 2
    home = plane == group
    block = index // PIECES
    seat = chip % 4

    def source(piece, parity):
        slot = jnp.where(home, piece, 3 - piece)
        mine = lax.dynamic_index_in_dim(own, slot, 0, keepdims=False)
        theirs = lax.dynamic_index_in_dim(sibling, slot, 0, keepdims=False)
        return jnp.where(parity == core, mine, theirs)

    def route(piece, wanted):
        pairs = []
        for owner, number in wanted:
            for side in range(2):
                near = group * 16 + 2 * owner + side
                far = (1 - group) * 16 + 2 * owner + side
                target = group * 16 + number * PIECES + side
                pairs.append((near, target + 2 * piece))
                pairs.append((far, target + 2 * (3 - piece)))
        return pairs

    def send(wanted, parity):
        return [
            lax.ppermute(source(piece, parity), ("groups", "ctx"), route(piece, wanted))
            for piece in range(4)
        ]

    def pick(arrived):
        near = lax.select_n(seat, *arrived)
        far = lax.select_n(seat, *arrived[::-1])
        return jnp.stack([near, far])

    def leaf(first, second):
        def run():
            if first == second:
                one = send([(first, 0)], odd[0])
                two = send([(second, 1)], odd[1])
                arrived = [jnp.where(block == 0, a, b) for a, b in zip(one, two)]
            else:
                parity = jnp.where(chip == first, odd[0], odd[1])
                arrived = send([(first, 0), (second, 1)], parity)
            return pick(arrived)

        return run

    leaves = [leaf(first, second) for first in range(8) for second in range(8)]
    return lax.switch(chips[0] * 8 + chips[1], leaves)


def direct_shards(
    normed_input, query_base, key_base, value_base, adapter_pool, stretch_adapter, adapter_owner
):
    plane = lax.axis_index("groups")
    index = lax.axis_index("ctx")
    core = index % 2
    tok_rows = normed_input.shape[0]
    ctx = lax.axis_size("ctx")
    seq = ctx * tok_rows
    blocks = [list(range(PIECES)), list(range(PIECES, 2 * PIECES))]
    place = jnp.stack([plane, core]).astype(jnp.int32)

    elsewhere = lax.ppermute(stretch_adapter, "groups", [(0, 1), (1, 0)])
    ids = jnp.arange(adapter_owner.shape[0], dtype=jnp.int32)
    slots = []
    for group in range(2):
        wanted = jnp.where(plane == group, stretch_adapter, elsewhere)
        slots.append(
            jnp.sum(jnp.where(wanted[:, None] == ids[None, :], adapter_owner[None, :], 0), axis=1)
        )

    own, other = pack_row(place, adapter_pool)
    sibling = lax.ppermute(other, "ctx", [(i, i ^ 1) for i in range(ctx)])

    moving = normed_input.reshape(tok_rows, PIECES, D // PIECES).transpose(1, 0, 2)
    moving = lax.all_to_all(moving, "ctx", 0, 0, axis_index_groups=blocks)

    base_rows = lax.all_gather(
        jnp.concatenate([key_base, value_base], 1), "ctx", axis=0, tiled=True
    )

    halves = [
        fetch_pieces(group, slots[group] // 2, slots[group] % 2, own, sibling)
        for group in range(2)
    ]
    pair = jnp.where(plane == 0, halves[0], halves[1])
    piece = jnp.where(plane == 0, pair, pair[::-1])

    down_slice = piece[:, :DOWN_ROWS].reshape(D // PIECES, 3 * ADAPTER_RANK)
    partial_rows = jnp.dot(
        moving.reshape(BLOCK_TOKENS, D // PIECES), down_slice, preferred_element_type=jnp.float32
    ).astype(jnp.bfloat16)
    partial_rows = lax.all_to_all(
        partial_rows.reshape(PIECES, tok_rows, 3 * ADAPTER_RANK),
        "ctx",
        0,
        0,
        axis_index_groups=blocks,
    )
    own_rank = jnp.sum(partial_rows.astype(jnp.float32), axis=0).astype(jnp.bfloat16)
    all_rank = lax.all_gather(own_rank[:, ADAPTER_RANK:], "ctx", axis=0, tiled=True)

    rest = piece[:, DOWN_ROWS:]
    keyval_up = lax.all_gather(rest[:, 128:160], "ctx").reshape(
        2, ADAPTER_RANK, 2 * KEYVALUE_HEADS * HEAD_SIZE
    )
    rest = lax.all_gather(rest, "ctx", axis_index_groups=blocks)
    query_up = rest[:, :, :128].reshape(ADAPTER_RANK, QH * HEAD_SIZE)
    down_out = rest[:, :, 160:288].reshape(QH * HEAD_SIZE, ADAPTER_RANK)
    up_out = rest[:, :, 288:].reshape(ADAPTER_RANK, D)

    half_dim = HEAD_SIZE // 2
    frequency = rope_base ** (-(jnp.arange(half_dim, dtype=jnp.float32) * 2.0) / HEAD_SIZE)
    angle = jnp.arange(seq, dtype=jnp.int32).astype(jnp.float32)[:, None] * frequency[None, :]
    cosine = jnp.cos(angle)
    sine = jnp.sin(angle)
    cosines = jnp.concatenate([cosine, cosine], 1)
    sines = jnp.concatenate([-sine, sine], 1)
    return attend(
        index.reshape(1).astype(jnp.int32),
        query_base,
        base_rows,
        own_rank,
        all_rank,
        query_up,
        keyval_up,
        cosines,
        sines,
        down_out,
        up_out,
    )


def shards(normed_input, query_base, key_base, value_base, adapter_pool, stretch_adapter, owner):
    fits = (
        lax.axis_size("groups") == 2
        and lax.axis_size("ctx") == 2 * PIECES
        and normed_input.shape[0] * PIECES == BLOCK_TOKENS
        and adapter_pool.shape[0] == 1
    )
    plan = direct_shards if fits else spread_shards
    return plan(
        normed_input, query_base, key_base, value_base, adapter_pool, stretch_adapter, owner
    )


def solution(mesh):
    placed = (
        P(("groups", "ctx"), None),
        P(("groups", "ctx"), None),
        P(("groups", "ctx"), None),
        P(("groups", "ctx"), None),
        P("ctx", None),
        P("groups"),
        P(),
    )
    return jax.shard_map(
        shards,
        mesh=mesh,
        in_specs=placed,
        out_specs=(P(("groups", "ctx"), None), P(("groups", "ctx"), None)),
        check_vma=False,
    )
```

```python
from functools import partial
import math

import jax
import jax.numpy as jnp
from jax import lax
from jax.experimental import pallas as pl
from jax.experimental.pallas import tpu as pltpu
from jax.sharding import PartitionSpec as P

D = 8192
QH = 32
KEYVALUE_HEADS = 4
HEAD_SIZE = 128
ADAPTER_RANK = 64
BLOCK_TOKENS = 512
QKV_POOL = 1900544


adapter_scale = 2.0
rope_base = 500000.0
mask_floor = -1e30


def from_partner(block, axis, apart):
    count = lax.axis_size(axis)
    route = []
    for low in range(count):
        high = low | 1 << apart
        if high != low and high < count:
            route += [(low, high), (high, low)]
    return lax.ppermute(block, axis, route)


def rotate(delta, token_positions, heads):
    half_dim = HEAD_SIZE // 2
    frequency = rope_base ** (-(jnp.arange(half_dim, dtype=jnp.float32) * 2.0) / HEAD_SIZE)
    angle = token_positions.astype(jnp.float32)[:, None] * frequency[None, :]
    cosine = jnp.cos(angle)[:, None, :]
    sine_part = jnp.sin(angle)[:, None, :]
    shaped = delta.reshape(delta.shape[0], heads, HEAD_SIZE)
    first_half = shaped[..., :half_dim]
    second_half = shaped[..., half_dim:]
    joined = jnp.concatenate(
        [
            first_half * cosine - second_half * sine_part,
            second_half * cosine + first_half * sine_part,
        ],
        -1,
    )
    return joined.reshape(delta.shape[0], heads * HEAD_SIZE)


def project_heads(
    narrow_product, query_row_block, key_row_block, value_row_block, upper_part, token_positions
):
    query_up_weight = upper_part[: ADAPTER_RANK * QH * HEAD_SIZE].reshape(
        ADAPTER_RANK, QH * HEAD_SIZE
    )
    keyvalue_up_weight = upper_part[ADAPTER_RANK * QH * HEAD_SIZE :].reshape(
        ADAPTER_RANK, 2 * KEYVALUE_HEADS * HEAD_SIZE
    )
    query_correction = adapter_scale * jnp.dot(
        narrow_product[:, :ADAPTER_RANK], query_up_weight, preferred_element_type=jnp.float32
    )
    key_correction = adapter_scale * jnp.dot(
        narrow_product[:, ADAPTER_RANK : 2 * ADAPTER_RANK],
        keyvalue_up_weight[:, : KEYVALUE_HEADS * HEAD_SIZE],
        preferred_element_type=jnp.float32,
    )
    value_correction = adapter_scale * jnp.dot(
        narrow_product[:, 2 * ADAPTER_RANK :],
        keyvalue_up_weight[:, KEYVALUE_HEADS * HEAD_SIZE :],
        preferred_element_type=jnp.float32,
    )
    queries = (
        query_row_block.astype(jnp.float32) + rotate(query_correction, token_positions, QH)
    ).astype(jnp.bfloat16)
    new_keys = (
        key_row_block.astype(jnp.float32) + rotate(key_correction, token_positions, KEYVALUE_HEADS)
    ).astype(jnp.bfloat16)
    new_values = (value_row_block.astype(jnp.float32) + value_correction).astype(jnp.bfloat16)
    return (queries, new_keys, new_values)


def output_delta(attended_rows, out_part):
    down_out = out_part[: QH * HEAD_SIZE * ADAPTER_RANK].reshape(QH * HEAD_SIZE, ADAPTER_RANK)
    raised_output = out_part[QH * HEAD_SIZE * ADAPTER_RANK :].reshape(ADAPTER_RANK, D)
    narrow_product = jnp.dot(attended_rows, down_out, preferred_element_type=jnp.float32).astype(
        jnp.bfloat16
    )
    return (
        adapter_scale * jnp.dot(narrow_product, raised_output, preferred_element_type=jnp.float32)
    ).astype(jnp.bfloat16)


def head_major(query_row_block):
    count_rows = query_row_block.shape[0]
    group_size = QH // KEYVALUE_HEADS
    return (
        query_row_block.reshape(count_rows, KEYVALUE_HEADS, group_size, HEAD_SIZE)
        .transpose(1, 2, 0, 3)
        .reshape(KEYVALUE_HEADS, group_size * count_rows, HEAD_SIZE)
    )


def row_major(head_rows, count_rows):
    group_size = QH // KEYVALUE_HEADS
    return (
        head_rows.reshape(KEYVALUE_HEADS, group_size, count_rows, HEAD_SIZE)
        .transpose(2, 0, 1, 3)
        .reshape(count_rows, QH * HEAD_SIZE)
    )


def online_update(current, queries, query_pos, key_slice, value_slice, key_start):
    run_max, run_sum, run_acc = current
    scores = jnp.einsum(
        "hqd,khd->hqk", queries, key_slice, preferred_element_type=jnp.float32
    ) * HEAD_SIZE ** (-0.5)
    key_pos = key_start + jnp.arange(key_slice.shape[0], dtype=jnp.int32)
    allowed = (query_pos[:, None] >= key_pos[None, :])[None]
    new_max = jnp.maximum(run_max, jnp.max(jnp.where(allowed, scores, mask_floor), axis=-1))
    weights = jnp.where(allowed, jnp.exp(scores - new_max[..., None]), 0.0)
    rescale = jnp.exp(run_max - new_max)
    new_sum = run_sum * rescale + jnp.sum(weights, axis=-1)
    new_acc = run_acc * rescale[..., None] + jnp.einsum(
        "hqk,khd->hqd",
        weights.astype(jnp.bfloat16),
        value_slice,
        preferred_element_type=jnp.float32,
    )
    return (new_max, new_sum, new_acc)


def unchanged(current):
    return current


def fold_keys(carry_state, shard_part, prepared):
    key_row_block, value_row_block = shard_part
    key_count = key_row_block.shape[0]
    sub_width = math.gcd(key_count, 1024)
    key_heads = key_row_block.reshape(key_count // sub_width, sub_width, KEYVALUE_HEADS, HEAD_SIZE)
    value_heads = value_row_block.reshape(
        key_count // sub_width, sub_width, KEYVALUE_HEADS, HEAD_SIZE
    )

    def one_step(sub_index, carried):
        key_start = sub_index * sub_width
        key_slice = lax.dynamic_index_in_dim(key_heads, sub_index, 0, keepdims=False)
        value_slice = lax.dynamic_index_in_dim(value_heads, sub_index, 0, keepdims=False)
        updated = []
        for (queries, query_pos), running in zip(prepared, carried):
            advance = partial(
                online_update,
                queries=queries,
                query_pos=query_pos,
                key_slice=key_slice,
                value_slice=value_slice,
                key_start=key_start,
            )
            updated.append(lax.cond(key_start <= jnp.max(query_pos), advance, unchanged, running))
        return tuple(updated)

    return lax.fori_loop(0, key_count // sub_width, one_step, carry_state)


def finish_block(result, count_rows):
    run_max, run_sum, run_acc = result
    divisor = jnp.where(run_sum > 0.0, run_sum, 1.0)
    return row_major(run_acc / divisor[..., None], count_rows).astype(jnp.bfloat16)


def spread_shards(
    normed_input, query_base, key_base, value_base, adapter_pool, stretch_adapter, adapter_owner
):
    cycle_size = lax.axis_size("ctx")
    my_index = lax.axis_index("ctx")
    tok_rows = normed_input.shape[0]
    token_positions = my_index * tok_rows + jnp.arange(tok_rows, dtype=jnp.int32)
    device_ids = jnp.arange(cycle_size, dtype=jnp.int32)
    stretch_of = device_ids * tok_rows // BLOCK_TOKENS
    stretch_ids = jnp.arange(stretch_adapter.shape[0], dtype=jnp.int32)
    adapter_of = jnp.sum(
        jnp.where(stretch_of[:, None] == stretch_ids[None, :], stretch_adapter[None, :], 0), axis=1
    )
    adapter_ids = jnp.arange(adapter_owner.shape[0], dtype=jnp.int32)
    slot_of = jnp.sum(
        jnp.where(adapter_of[:, None] == adapter_ids[None, :], adapter_owner[None, :], 0), axis=1
    )
    down_size = 3 * ADAPTER_RANK * D
    group_count = BLOCK_TOKENS // tok_rows
    levels = group_count.bit_length() - 1
    local_index = my_index % group_count
    col_width = D // group_count
    piece_len = down_size // (group_count * cycle_size)
    pool_rows = adapter_pool.shape[0]
    down_shaped = adapter_pool[:, :down_size].reshape(pool_rows, group_count, cycle_size, piece_len)
    spread_down = lax.all_to_all(down_shaped, "ctx", split_axis=2, concat_axis=0, tiled=True)
    flat_down = spread_down.reshape(-1, piece_len)
    wanted = jnp.take(flat_down, slot_of * group_count + device_ids % group_count, axis=0)[
        :, None, :
    ]
    down_slice = lax.all_to_all(wanted, "ctx", split_axis=0, concat_axis=1, tiled=True).reshape(
        col_width, 3 * ADAPTER_RANK
    )
    spread_rest = lax.all_to_all(
        adapter_pool[:, down_size:], "ctx", split_axis=1, concat_axis=0, tiled=True
    )
    rest_row = lax.all_to_all(
        jnp.take(spread_rest, slot_of, axis=0), "ctx", split_axis=0, concat_axis=1, tiled=True
    )[0]
    upper_part = rest_row[: QKV_POOL - down_size]
    out_part = rest_row[QKV_POOL - down_size :]
    pieces = normed_input.reshape(tok_rows, group_count, col_width)
    slice_order = jnp.bitwise_xor(local_index, jnp.arange(group_count, dtype=jnp.int32))
    moving = jnp.take(pieces, slice_order, axis=1).transpose(1, 0, 2)
    for level in range(levels):
        shaped = moving.reshape(group_count >> level + 1, 2, 1 << level, tok_rows, col_width)
        arrived = from_partner(shaped[:, 1], "ctx", level)
        moving = jnp.stack([shaped[:, 0], arrived], 1).reshape(group_count, tok_rows, col_width)
    partial_rows = jnp.dot(
        moving.reshape(group_count * tok_rows, col_width),
        down_slice,
        preferred_element_type=jnp.float32,
    ).reshape(group_count, tok_rows, 3 * ADAPTER_RANK)
    for level in reversed(range(levels)):
        halves = partial_rows.reshape(2, partial_rows.shape[0] // 2, tok_rows, 3 * ADAPTER_RANK)
        partial_rows = halves[0] + from_partner(
            halves[1].astype(jnp.bfloat16), "ctx", level
        ).astype(jnp.float32)
    narrow_product = partial_rows[0].astype(jnp.bfloat16)
    queries, new_keys, new_values = project_heads(
        narrow_product, query_base, key_base, value_base, upper_part, token_positions
    )
    group_size = QH // KEYVALUE_HEADS
    blocks = [(queries, token_positions)]
    prepared = [
        (head_major(block_q), jnp.tile(block_pos, group_size)) for block_q, block_pos in blocks
    ]
    initial = tuple(
        (
            (
                jnp.full((KEYVALUE_HEADS, head_q.shape[1]), mask_floor, jnp.float32),
                jnp.zeros((KEYVALUE_HEADS, head_q.shape[1]), jnp.float32),
                jnp.zeros((KEYVALUE_HEADS, head_q.shape[1], HEAD_SIZE), jnp.float32),
            )
            for head_q, block_pos in prepared
        )
    )
    finals = fold_keys(
        initial,
        (
            lax.all_gather(new_keys, "ctx", axis=0, tiled=True),
            lax.all_gather(new_values, "ctx", axis=0, tiled=True),
        ),
        prepared,
    )
    attended = finish_block(finals[0], tok_rows)
    out_delta = output_delta(attended, out_part)
    return (attended, out_delta)


PIECES = 8
GROUP = QH // KEYVALUE_HEADS
DOWN = ((0, 12288),)
REST = ((12288, 2048), (14336, 512), (14848, 2048), (16896, 4096))


def pack_kernel(sections, pool, *refs):
    out, buffers, sems = refs[-3:]
    plane = lax.axis_index("groups")
    slabs, slab_rows = out.shape[:2]

    def copies(slab, slot):
        listed = []
        offset = 0
        for number, (first, rows) in enumerate(sections):
            share = rows // (4 * PIECES)
            quarter = 2 * plane + slab // PIECES
            begin = first + (lax.rem(slab, PIECES) * 4 + quarter) * share
            listed.append(
                pltpu.make_async_copy(
                    pool.at[:, pl.ds(pl.multiple_of(begin * 128, 2048), share * 128)],
                    buffers.at[slot, :, pl.ds(offset, share * 128)],
                    sems.at[slot, number],
                )
            )
            offset += share * 128
        return listed

    for copy in copies(0, 0):
        copy.start()

    def step(slab, carried):
        slot = lax.rem(slab, 2)

        @pl.when(slab < slabs - 1)
        def _():
            for copy in copies(slab + 1, 1 - slot):
                copy.start()

        for copy in copies(slab, slot):
            copy.wait()

        def chunk(index, inner):
            line = buffers[slot, :, pl.ds(pl.multiple_of(index * 2048, 2048), 2048)]
            block = line.astype(jnp.float32).reshape(16, 128).astype(jnp.bfloat16)
            out[slab, pl.ds(pl.multiple_of(index * 16, 16), 16), :] = block
            return inner

        lax.fori_loop(0, slab_rows // 16, chunk, 0, unroll=8)
        return carried

    lax.fori_loop(0, slabs, step, 0)


def pack_row(pool, sections, *after):
    slab_rows = sum(rows for _, rows in sections) // (4 * PIECES)
    return pl.pallas_call(
        partial(pack_kernel, sections),
        out_shape=jax.ShapeDtypeStruct((2 * PIECES, slab_rows, 128), jnp.bfloat16),
        in_specs=[pl.BlockSpec(memory_space=pl.ANY)] * (1 + len(after)),
        out_specs=pl.BlockSpec(memory_space=pltpu.VMEM),
        scratch_shapes=[
            pltpu.VMEM((2, 1, slab_rows * 128), jnp.bfloat16),
            pltpu.SemaphoreType.DMA((2, len(sections))),
        ],
        compiler_params=pltpu.CompilerParams(vmem_limit_bytes=60 << 20),
        cost_estimate=pl.CostEstimate(flops=0, bytes_accessed=8 << 20, transcendentals=0),
    )(pool, *after)


def attend_kernel(
    query_block,
    key_block,
    value_block,
    own_rank,
    all_rank,
    query_up,
    key_up,
    value_up,
    cosines,
    sines,
    down_out,
    up_out,
    attended,
    out_delta,
    total,
):
    step = pl.program_id(0)
    rows = query_block.shape[0]
    base = lax.axis_index("ctx") * rows
    dot = partial(jnp.dot, preferred_element_type=jnp.float32)

    def turned(delta, cosine, sine):
        return delta * cosine + pltpu.roll(delta, HEAD_SIZE // 2, 1) * sine

    keys = []
    values = []
    half = lax.axis_index("ctx") * rows // BLOCK_TOKENS
    for block in range(key_up.shape[0]):
        span = slice(block * BLOCK_TOKENS, (block + 1) * BLOCK_TOKENS)
        delta = adapter_scale * dot(all_rank[span, :ADAPTER_RANK], key_up[block ^ half])
        delta = turned(delta, cosines[span, :], sines[span, :])
        keys.append((key_block[span, :].astype(jnp.float32) + delta).astype(jnp.bfloat16))
        delta = adapter_scale * dot(all_rank[span, ADAPTER_RANK:], value_up[block ^ half])
        values.append((value_block[span, :].astype(jnp.float32) + delta).astype(jnp.bfloat16))
    keys = jnp.concatenate(keys, 0)
    values = jnp.concatenate(values, 0)
    here = pl.ds(pl.multiple_of(base, rows), rows)
    cosine = cosines[here, :]
    sine = sines[here, :]
    delta = adapter_scale * dot(own_rank[:, :ADAPTER_RANK], query_up[...])
    added = jnp.zeros((rows, ADAPTER_RANK), jnp.float32)
    taken = GROUP // 2
    for first in range(0, GROUP, taken):
        queries = []
        for head in range(first, first + taken):
            span = slice(head * HEAD_SIZE, (head + 1) * HEAD_SIZE)
            moved = turned(delta[:, span], cosine, sine)
            queries.append(
                (query_block[:, span].astype(jnp.float32) + moved).astype(jnp.bfloat16)
            )
        queries = jnp.concatenate(queries, 0)
        scores = lax.dot_general(
            queries, keys, (((1,), (1,)), ((), ())), preferred_element_type=jnp.float32
        ) * HEAD_SIZE ** (-0.5)
        row = lax.broadcasted_iota(jnp.int32, scores.shape, 0)
        column = lax.broadcasted_iota(jnp.int32, scores.shape, 1)
        scores = jnp.where(column <= base + lax.rem(row, rows), scores, mask_floor)
        weights = jnp.exp(scores - jnp.max(scores, axis=-1, keepdims=True))
        divisor = jnp.sum(weights, axis=-1, keepdims=True)
        result = (dot(weights.astype(jnp.bfloat16), values) / divisor).astype(jnp.bfloat16)
        for place, head in enumerate(range(first, first + taken)):
            span = slice(head * HEAD_SIZE, (head + 1) * HEAD_SIZE)
            part = result[place * rows : (place + 1) * rows]
            attended[:, span] = part
            added += dot(part, down_out[span, :])

    @pl.when(step == 0)
    def _():
        total[...] = jnp.zeros_like(total)

    total[...] += added

    @pl.when(step == pl.num_programs(0) - 1)
    def _():
        narrow = total[...].astype(jnp.bfloat16)
        out_delta[...] = (adapter_scale * dot(narrow, up_out[...])).astype(jnp.bfloat16)


def attend(
    query_base,
    base_rows,
    own_rank,
    all_rank,
    query_up,
    keyval_up,
    cosines,
    sines,
    down_out,
    up_out,
):
    rows = query_base.shape[0]
    seq = base_rows.shape[0]
    blocks = keyval_up.shape[0]
    width = GROUP * HEAD_SIZE

    def whole(shape):
        return pl.BlockSpec(shape, lambda h: (0,) * len(shape))

    return pl.pallas_call(
        attend_kernel,
        grid=(KEYVALUE_HEADS,),
        out_shape=(
            jax.ShapeDtypeStruct((rows, QH * HEAD_SIZE), jnp.bfloat16),
            jax.ShapeDtypeStruct((rows, D), jnp.bfloat16),
        ),
        in_specs=[
            pl.BlockSpec((rows, width), lambda h: (0, h)),
            pl.BlockSpec((seq, HEAD_SIZE), lambda h: (0, h)),
            pl.BlockSpec((seq, HEAD_SIZE), lambda h: (0, h + KEYVALUE_HEADS)),
            whole(own_rank.shape),
            whole(all_rank.shape),
            pl.BlockSpec((ADAPTER_RANK, width), lambda h: (0, h)),
            pl.BlockSpec((blocks, ADAPTER_RANK, HEAD_SIZE), lambda h: (0, 0, h)),
            pl.BlockSpec((blocks, ADAPTER_RANK, HEAD_SIZE), lambda h: (0, 0, h + KEYVALUE_HEADS)),
            whole(cosines.shape),
            whole(sines.shape),
            pl.BlockSpec((width, ADAPTER_RANK), lambda h: (h, 0)),
            whole(up_out.shape),
        ],
        out_specs=(
            pl.BlockSpec((rows, width), lambda h: (0, h)),
            whole((rows, D)),
        ),
        scratch_shapes=[pltpu.VMEM((rows, ADAPTER_RANK), jnp.float32)],
        compiler_params=pltpu.CompilerParams(vmem_limit_bytes=60 << 20),
        cost_estimate=pl.CostEstimate(
            flops=4 * rows * QH * seq * HEAD_SIZE,
            bytes_accessed=10 << 20,
            transcendentals=rows * QH * seq,
        ),
    )(
        query_base,
        base_rows,
        base_rows,
        own_rank,
        all_rank,
        query_up,
        keyval_up,
        keyval_up,
        cosines,
        sines,
        down_out,
        up_out,
    )


def swap(block, mask):
    return lax.ppermute(block, ("groups", "ctx"), [(i, i ^ mask) for i in range(4 * PIECES)])


def fetch_piece(packed, slots, corner, mirrored=None):
    spread = lax.all_to_all(packed, "ctx", 0, 0)
    arrived = []
    for flip, mask in enumerate((0, PIECES, 2 * PIECES, 3 * PIECES)):
        row = lax.dynamic_index_in_dim(slots, corner ^ flip, 0, keepdims=False)
        block = lax.dynamic_index_in_dim(spread, row, 0, keepdims=False)
        if mirrored is not None:
            row = lax.dynamic_index_in_dim(slots, corner ^ flip ^ 1, 0, keepdims=False)
            other = lax.dynamic_index_in_dim(spread, row, 0, keepdims=False)
            block = jnp.concatenate([block, other[mirrored]])
        arrived.append(swap(block, mask) if mask else block)
    low = corner % 2 == 0
    arrived = [jnp.where(low, arrived[q], arrived[q ^ 1]) for q in range(4)]
    high = corner < 2
    return jnp.stack([jnp.where(high, arrived[q], arrived[q ^ 2]) for q in range(4)])


def direct_shards(
    normed_input, query_base, key_base, value_base, adapter_pool, stretch_adapter, adapter_owner
):
    plane = lax.axis_index("groups")
    index = lax.axis_index("ctx")
    tok_rows = normed_input.shape[0]
    ctx = lax.axis_size("ctx")
    seq = ctx * tok_rows
    blocks = [list(range(PIECES)), list(range(PIECES, 2 * PIECES))]
    corner = 2 * plane + index // PIECES

    elsewhere = swap(stretch_adapter, 2 * PIECES)
    wanted = jnp.where(
        plane == 0,
        jnp.concatenate([stretch_adapter, elsewhere]),
        jnp.concatenate([elsewhere, stretch_adapter]),
    )
    ids = jnp.arange(adapter_owner.shape[0], dtype=jnp.int32)
    slots = jnp.sum(jnp.where(wanted[:, None] == ids[None, :], adapter_owner[None, :], 0), axis=1)

    moving = normed_input.reshape(tok_rows, PIECES, D // PIECES).transpose(1, 0, 2)
    moving = lax.all_to_all(moving, "ctx", 0, 0, axis_index_groups=blocks)
    base_rows = lax.all_gather(
        jnp.concatenate([key_base, value_base], 1), "ctx", axis=0, tiled=True
    )

    packed_rest = pack_row(adapter_pool, REST)
    packed_down = pack_row(adapter_pool, DOWN, packed_rest)
    rest = fetch_piece(packed_rest, slots, corner, slice(64, 80))
    rest, base_rows = lax.optimization_barrier((rest, base_rows))
    rest = lax.all_gather(rest, "ctx", axis_index_groups=blocks)
    query_up = rest[:, :, :64].reshape(ADAPTER_RANK, QH * HEAD_SIZE)
    keyval_up = jnp.stack([rest[:, :, 64:80], rest[:, :, 272:]])
    keyval_up = keyval_up.reshape(2, ADAPTER_RANK, 2 * KEYVALUE_HEADS * HEAD_SIZE)
    down_out = rest[:, :, 80:144].reshape(QH * HEAD_SIZE, ADAPTER_RANK)
    up_out = rest[:, :, 144:272].reshape(ADAPTER_RANK, D)

    down_slice = fetch_piece(packed_down, slots, corner)
    down_slice = down_slice.reshape(D // PIECES, 3 * ADAPTER_RANK)
    partial_rows = jnp.dot(
        moving.reshape(BLOCK_TOKENS, D // PIECES), down_slice, preferred_element_type=jnp.float32
    ).astype(jnp.bfloat16)
    partial_rows = lax.all_to_all(
        partial_rows.reshape(PIECES, tok_rows, 3 * ADAPTER_RANK),
        "ctx",
        0,
        0,
        axis_index_groups=blocks,
    )
    own_rank = jnp.sum(partial_rows.astype(jnp.float32), axis=0).astype(jnp.bfloat16)
    all_rank = jnp.broadcast_to(own_rank[None, :, ADAPTER_RANK:], (ctx, tok_rows, 2 * ADAPTER_RANK))
    all_rank = lax.all_to_all(all_rank, "ctx", 0, 0).reshape(seq, 2 * ADAPTER_RANK)

    half_dim = HEAD_SIZE // 2
    frequency = rope_base ** (-(jnp.arange(half_dim, dtype=jnp.float32) * 2.0) / HEAD_SIZE)
    angle = jnp.arange(seq, dtype=jnp.int32).astype(jnp.float32)[:, None] * frequency[None, :]
    cosine = jnp.cos(angle)
    sine = jnp.sin(angle)
    cosines = jnp.concatenate([cosine, cosine], 1)
    sines = jnp.concatenate([-sine, sine], 1)
    return attend(
        query_base,
        base_rows,
        own_rank,
        all_rank,
        query_up,
        keyval_up,
        cosines,
        sines,
        down_out,
        up_out,
    )


def shards(normed_input, query_base, key_base, value_base, adapter_pool, stretch_adapter, owner):
    fits = (
        lax.axis_size("groups") == 2
        and lax.axis_size("ctx") == 2 * PIECES
        and normed_input.shape[0] * PIECES == BLOCK_TOKENS
        and adapter_pool.shape[0] == 1
    )
    plan = direct_shards if fits else spread_shards
    return plan(
        normed_input, query_base, key_base, value_base, adapter_pool, stretch_adapter, owner
    )


def solution(mesh):
    placed = (
        P(("groups", "ctx"), None),
        P(("groups", "ctx"), None),
        P(("groups", "ctx"), None),
        P(("groups", "ctx"), None),
        P("ctx", None),
        P("groups"),
        P(),
    )
    return jax.shard_map(
        shards,
        mesh=mesh,
        in_specs=placed,
        out_specs=(P(("groups", "ctx"), None), P(("groups", "ctx"), None)),
        check_vma=False,
    )
```

```python
from functools import partial
import math

import jax
import jax.numpy as jnp
from jax import lax
from jax.experimental import pallas as pl
from jax.experimental.pallas import tpu as pltpu
from jax.sharding import PartitionSpec as P

D = 8192
QH = 32
KEYVALUE_HEADS = 4
HEAD_SIZE = 128
ADAPTER_RANK = 64
BLOCK_TOKENS = 512
QKV_POOL = 1900544


adapter_scale = 2.0
rope_base = 500000.0
mask_floor = -1e30


def from_partner(block, axis, apart):
    count = lax.axis_size(axis)
    route = []
    for low in range(count):
        high = low | 1 << apart
        if high != low and high < count:
            route += [(low, high), (high, low)]
    return lax.ppermute(block, axis, route)


def rotate(delta, token_positions, heads):
    half_dim = HEAD_SIZE // 2
    frequency = rope_base ** (-(jnp.arange(half_dim, dtype=jnp.float32) * 2.0) / HEAD_SIZE)
    angle = token_positions.astype(jnp.float32)[:, None] * frequency[None, :]
    cosine = jnp.cos(angle)[:, None, :]
    sine_part = jnp.sin(angle)[:, None, :]
    shaped = delta.reshape(delta.shape[0], heads, HEAD_SIZE)
    first_half = shaped[..., :half_dim]
    second_half = shaped[..., half_dim:]
    joined = jnp.concatenate(
        [
            first_half * cosine - second_half * sine_part,
            second_half * cosine + first_half * sine_part,
        ],
        -1,
    )
    return joined.reshape(delta.shape[0], heads * HEAD_SIZE)


def project_heads(
    narrow_product, query_row_block, key_row_block, value_row_block, upper_part, token_positions
):
    query_up_weight = upper_part[: ADAPTER_RANK * QH * HEAD_SIZE].reshape(
        ADAPTER_RANK, QH * HEAD_SIZE
    )
    keyvalue_up_weight = upper_part[ADAPTER_RANK * QH * HEAD_SIZE :].reshape(
        ADAPTER_RANK, 2 * KEYVALUE_HEADS * HEAD_SIZE
    )
    query_correction = adapter_scale * jnp.dot(
        narrow_product[:, :ADAPTER_RANK], query_up_weight, preferred_element_type=jnp.float32
    )
    key_correction = adapter_scale * jnp.dot(
        narrow_product[:, ADAPTER_RANK : 2 * ADAPTER_RANK],
        keyvalue_up_weight[:, : KEYVALUE_HEADS * HEAD_SIZE],
        preferred_element_type=jnp.float32,
    )
    value_correction = adapter_scale * jnp.dot(
        narrow_product[:, 2 * ADAPTER_RANK :],
        keyvalue_up_weight[:, KEYVALUE_HEADS * HEAD_SIZE :],
        preferred_element_type=jnp.float32,
    )
    queries = (
        query_row_block.astype(jnp.float32) + rotate(query_correction, token_positions, QH)
    ).astype(jnp.bfloat16)
    new_keys = (
        key_row_block.astype(jnp.float32) + rotate(key_correction, token_positions, KEYVALUE_HEADS)
    ).astype(jnp.bfloat16)
    new_values = (value_row_block.astype(jnp.float32) + value_correction).astype(jnp.bfloat16)
    return (queries, new_keys, new_values)


def output_delta(attended_rows, out_part):
    down_out = out_part[: QH * HEAD_SIZE * ADAPTER_RANK].reshape(QH * HEAD_SIZE, ADAPTER_RANK)
    raised_output = out_part[QH * HEAD_SIZE * ADAPTER_RANK :].reshape(ADAPTER_RANK, D)
    narrow_product = jnp.dot(attended_rows, down_out, preferred_element_type=jnp.float32).astype(
        jnp.bfloat16
    )
    return (
        adapter_scale * jnp.dot(narrow_product, raised_output, preferred_element_type=jnp.float32)
    ).astype(jnp.bfloat16)


def head_major(query_row_block):
    count_rows = query_row_block.shape[0]
    group_size = QH // KEYVALUE_HEADS
    return (
        query_row_block.reshape(count_rows, KEYVALUE_HEADS, group_size, HEAD_SIZE)
        .transpose(1, 2, 0, 3)
        .reshape(KEYVALUE_HEADS, group_size * count_rows, HEAD_SIZE)
    )


def row_major(head_rows, count_rows):
    group_size = QH // KEYVALUE_HEADS
    return (
        head_rows.reshape(KEYVALUE_HEADS, group_size, count_rows, HEAD_SIZE)
        .transpose(2, 0, 1, 3)
        .reshape(count_rows, QH * HEAD_SIZE)
    )


def online_update(current, queries, query_pos, key_slice, value_slice, key_start):
    run_max, run_sum, run_acc = current
    scores = jnp.einsum(
        "hqd,khd->hqk", queries, key_slice, preferred_element_type=jnp.float32
    ) * HEAD_SIZE ** (-0.5)
    key_pos = key_start + jnp.arange(key_slice.shape[0], dtype=jnp.int32)
    allowed = (query_pos[:, None] >= key_pos[None, :])[None]
    new_max = jnp.maximum(run_max, jnp.max(jnp.where(allowed, scores, mask_floor), axis=-1))
    weights = jnp.where(allowed, jnp.exp(scores - new_max[..., None]), 0.0)
    rescale = jnp.exp(run_max - new_max)
    new_sum = run_sum * rescale + jnp.sum(weights, axis=-1)
    new_acc = run_acc * rescale[..., None] + jnp.einsum(
        "hqk,khd->hqd",
        weights.astype(jnp.bfloat16),
        value_slice,
        preferred_element_type=jnp.float32,
    )
    return (new_max, new_sum, new_acc)


def unchanged(current):
    return current


def fold_keys(carry_state, shard_part, prepared):
    key_row_block, value_row_block = shard_part
    key_count = key_row_block.shape[0]
    sub_width = math.gcd(key_count, 1024)
    key_heads = key_row_block.reshape(key_count // sub_width, sub_width, KEYVALUE_HEADS, HEAD_SIZE)
    value_heads = value_row_block.reshape(
        key_count // sub_width, sub_width, KEYVALUE_HEADS, HEAD_SIZE
    )

    def one_step(sub_index, carried):
        key_start = sub_index * sub_width
        key_slice = lax.dynamic_index_in_dim(key_heads, sub_index, 0, keepdims=False)
        value_slice = lax.dynamic_index_in_dim(value_heads, sub_index, 0, keepdims=False)
        updated = []
        for (queries, query_pos), running in zip(prepared, carried):
            advance = partial(
                online_update,
                queries=queries,
                query_pos=query_pos,
                key_slice=key_slice,
                value_slice=value_slice,
                key_start=key_start,
            )
            updated.append(lax.cond(key_start <= jnp.max(query_pos), advance, unchanged, running))
        return tuple(updated)

    return lax.fori_loop(0, key_count // sub_width, one_step, carry_state)


def finish_block(result, count_rows):
    run_max, run_sum, run_acc = result
    divisor = jnp.where(run_sum > 0.0, run_sum, 1.0)
    return row_major(run_acc / divisor[..., None], count_rows).astype(jnp.bfloat16)


def spread_shards(
    normed_input, query_base, key_base, value_base, adapter_pool, stretch_adapter, adapter_owner
):
    cycle_size = lax.axis_size("ctx")
    my_index = lax.axis_index("ctx")
    tok_rows = normed_input.shape[0]
    token_positions = my_index * tok_rows + jnp.arange(tok_rows, dtype=jnp.int32)
    device_ids = jnp.arange(cycle_size, dtype=jnp.int32)
    stretch_of = device_ids * tok_rows // BLOCK_TOKENS
    stretch_ids = jnp.arange(stretch_adapter.shape[0], dtype=jnp.int32)
    adapter_of = jnp.sum(
        jnp.where(stretch_of[:, None] == stretch_ids[None, :], stretch_adapter[None, :], 0), axis=1
    )
    adapter_ids = jnp.arange(adapter_owner.shape[0], dtype=jnp.int32)
    slot_of = jnp.sum(
        jnp.where(adapter_of[:, None] == adapter_ids[None, :], adapter_owner[None, :], 0), axis=1
    )
    down_size = 3 * ADAPTER_RANK * D
    group_count = BLOCK_TOKENS // tok_rows
    levels = group_count.bit_length() - 1
    local_index = my_index % group_count
    col_width = D // group_count
    piece_len = down_size // (group_count * cycle_size)
    pool_rows = adapter_pool.shape[0]
    down_shaped = adapter_pool[:, :down_size].reshape(pool_rows, group_count, cycle_size, piece_len)
    spread_down = lax.all_to_all(down_shaped, "ctx", split_axis=2, concat_axis=0, tiled=True)
    flat_down = spread_down.reshape(-1, piece_len)
    wanted = jnp.take(flat_down, slot_of * group_count + device_ids % group_count, axis=0)[
        :, None, :
    ]
    down_slice = lax.all_to_all(wanted, "ctx", split_axis=0, concat_axis=1, tiled=True).reshape(
        col_width, 3 * ADAPTER_RANK
    )
    spread_rest = lax.all_to_all(
        adapter_pool[:, down_size:], "ctx", split_axis=1, concat_axis=0, tiled=True
    )
    rest_row = lax.all_to_all(
        jnp.take(spread_rest, slot_of, axis=0), "ctx", split_axis=0, concat_axis=1, tiled=True
    )[0]
    upper_part = rest_row[: QKV_POOL - down_size]
    out_part = rest_row[QKV_POOL - down_size :]
    pieces = normed_input.reshape(tok_rows, group_count, col_width)
    slice_order = jnp.bitwise_xor(local_index, jnp.arange(group_count, dtype=jnp.int32))
    moving = jnp.take(pieces, slice_order, axis=1).transpose(1, 0, 2)
    for level in range(levels):
        shaped = moving.reshape(group_count >> level + 1, 2, 1 << level, tok_rows, col_width)
        arrived = from_partner(shaped[:, 1], "ctx", level)
        moving = jnp.stack([shaped[:, 0], arrived], 1).reshape(group_count, tok_rows, col_width)
    partial_rows = jnp.dot(
        moving.reshape(group_count * tok_rows, col_width),
        down_slice,
        preferred_element_type=jnp.float32,
    ).reshape(group_count, tok_rows, 3 * ADAPTER_RANK)
    for level in reversed(range(levels)):
        halves = partial_rows.reshape(2, partial_rows.shape[0] // 2, tok_rows, 3 * ADAPTER_RANK)
        partial_rows = halves[0] + from_partner(
            halves[1].astype(jnp.bfloat16), "ctx", level
        ).astype(jnp.float32)
    narrow_product = partial_rows[0].astype(jnp.bfloat16)
    queries, new_keys, new_values = project_heads(
        narrow_product, query_base, key_base, value_base, upper_part, token_positions
    )
    group_size = QH // KEYVALUE_HEADS
    blocks = [(queries, token_positions)]
    prepared = [
        (head_major(block_q), jnp.tile(block_pos, group_size)) for block_q, block_pos in blocks
    ]
    initial = tuple(
        (
            (
                jnp.full((KEYVALUE_HEADS, head_q.shape[1]), mask_floor, jnp.float32),
                jnp.zeros((KEYVALUE_HEADS, head_q.shape[1]), jnp.float32),
                jnp.zeros((KEYVALUE_HEADS, head_q.shape[1], HEAD_SIZE), jnp.float32),
            )
            for head_q, block_pos in prepared
        )
    )
    finals = fold_keys(
        initial,
        (
            lax.all_gather(new_keys, "ctx", axis=0, tiled=True),
            lax.all_gather(new_values, "ctx", axis=0, tiled=True),
        ),
        prepared,
    )
    attended = finish_block(finals[0], tok_rows)
    out_delta = output_delta(attended, out_part)
    return (attended, out_delta)


PIECES = 8
GROUP = QH // KEYVALUE_HEADS
DOWN = ((0, 12288),)
REST = ((12288, 2048), (14336, 512), (14848, 2048), (16896, 4096))


def pack_kernel(sections, pool, *refs):
    out, buffers, sems = refs[-3:]
    plane = lax.axis_index("groups")
    slabs, slab_rows = out.shape[:2]

    def copies(slab):
        listed = []
        offset = 0
        for first, rows in sections:
            share = rows // (2 * PIECES)
            begin = first + (slab * 2 + plane) * share
            listed.append(
                pltpu.make_async_copy(
                    pool.at[:, pl.ds(pl.multiple_of(begin * 128, 2048), share * 128)],
                    buffers.at[slab, :, pl.ds(offset, share * 128)],
                    sems.at[slab, len(listed)],
                )
            )
            offset += share * 128
        return listed

    for slab in range(slabs):
        for copy in copies(slab):
            copy.start()

    def step(slab, carried):
        for copy in copies(slab):
            copy.wait()

        def chunk(index, inner):
            line = buffers[slab, :, pl.ds(pl.multiple_of(index * 2048, 2048), 2048)]
            block = line.astype(jnp.float32).reshape(16, 128).astype(jnp.bfloat16)
            out[slab, pl.ds(pl.multiple_of(index * 16, 16), 16), :] = block
            return inner

        lax.fori_loop(0, slab_rows // 16, chunk, 0, unroll=8)
        return carried

    lax.fori_loop(0, slabs, step, 0)


def pack_row(pool, sections, *after):
    slab_rows = sum(rows for _, rows in sections) // (2 * PIECES)
    return pl.pallas_call(
        partial(pack_kernel, sections),
        out_shape=jax.ShapeDtypeStruct((PIECES, slab_rows, 128), jnp.bfloat16),
        in_specs=[pl.BlockSpec(memory_space=pl.ANY)] * (1 + len(after)),
        out_specs=pl.BlockSpec(memory_space=pltpu.VMEM),
        scratch_shapes=[
            pltpu.VMEM((PIECES, 1, slab_rows * 128), jnp.bfloat16),
            pltpu.SemaphoreType.DMA((PIECES, len(sections))),
        ],
        compiler_params=pltpu.CompilerParams(vmem_limit_bytes=60 << 20),
        cost_estimate=pl.CostEstimate(flops=0, bytes_accessed=8 << 20, transcendentals=0),
    )(pool, *after)


def pick_kernel(mirrored, here, there, owner, spread, *refs):
    outs, sems = refs[:4], refs[4]
    half = lax.axis_index("ctx") // PIECES
    rows = spread.shape[1]
    copies = []
    for flip, out in enumerate(outs):
        wishes = there if flip >= 2 else here
        block = half ^ (flip & 1)
        row = lax.rem(owner[wishes[block]], PIECES)
        copies.append(
            pltpu.make_async_copy(spread.at[row], out.at[pl.ds(0, rows)], sems.at[flip, 0])
        )
        if mirrored is not None:
            first, count = mirrored
            row = lax.rem(owner[wishes[1 - block]], PIECES)
            copies.append(
                pltpu.make_async_copy(
                    spread.at[row, pl.ds(first, count)],
                    out.at[pl.ds(rows, count)],
                    sems.at[flip, 1],
                )
            )
    for copy in copies:
        copy.start()
    for copy in copies:
        copy.wait()


def pick(spread, here, there, owner, mirrored):
    rows = spread.shape[1] + (mirrored[1] if mirrored else 0)
    slab = jax.ShapeDtypeStruct((rows, 128), jnp.bfloat16)
    return pl.pallas_call(
        partial(pick_kernel, mirrored),
        out_shape=(slab,) * 4,
        in_specs=[pl.BlockSpec(memory_space=pltpu.SMEM)] * 3 + [pl.BlockSpec(memory_space=pl.ANY)],
        out_specs=(pl.BlockSpec(memory_space=pl.ANY),) * 4,
        scratch_shapes=[pltpu.SemaphoreType.DMA((4, 2))],
        cost_estimate=pl.CostEstimate(flops=0, bytes_accessed=2 << 20, transcendentals=0),
    )(here, there, owner, spread)


def attend_kernel(
    query_block,
    key_same,
    key_other,
    value_same,
    value_other,
    own_rank,
    all_rank,
    query_up,
    key_up,
    value_up,
    cosines,
    sines,
    down_out,
    up_out,
    attended,
    out_delta,
    total,
    keys,
    values,
):
    step = pl.program_id(0)
    rows = query_block.shape[0]
    base = lax.axis_index("ctx") * rows
    dot = partial(jnp.dot, preferred_element_type=jnp.float32)

    def turned(delta, cosine, sine):
        return delta * cosine + pltpu.roll(delta, HEAD_SIZE // 2, 1) * sine

    half = lax.axis_index("ctx") * rows // BLOCK_TOKENS
    core = lax.rem(lax.axis_index("ctx"), 2)
    for block in range(key_up.shape[0]):
        for chip in range(block * PIECES // 2, (block + 1) * PIECES // 2):
            for apart in range(2):
                first = (2 * chip + (core ^ apart)) * rows
                span = pl.ds(pl.multiple_of(first, rows), rows)
                key_base = (key_other if apart else key_same)[chip]
                value_base = (value_other if apart else value_same)[chip]
                delta = adapter_scale * dot(all_rank[span, :ADAPTER_RANK], key_up[block ^ half])
                delta = turned(delta, cosines[span, :], sines[span, :])
                keys[span, :] = (key_base.astype(jnp.float32) + delta).astype(jnp.bfloat16)
                delta = adapter_scale * dot(all_rank[span, ADAPTER_RANK:], value_up[block ^ half])
                values[span, :] = (value_base.astype(jnp.float32) + delta).astype(jnp.bfloat16)
    here = pl.ds(pl.multiple_of(base, rows), rows)
    cosine = cosines[here, :]
    sine = sines[here, :]
    delta = adapter_scale * dot(own_rank[:, :ADAPTER_RANK], query_up[...])
    added = jnp.zeros((rows, ADAPTER_RANK), jnp.float32)
    taken = GROUP // 2
    for first in range(0, GROUP, taken):
        queries = []
        for head in range(first, first + taken):
            span = slice(head * HEAD_SIZE, (head + 1) * HEAD_SIZE)
            moved = turned(delta[:, span], cosine, sine)
            queries.append(
                (query_block[:, span].astype(jnp.float32) + moved).astype(jnp.bfloat16)
            )
        queries = jnp.concatenate(queries, 0)
        scores = lax.dot_general(
            queries, keys[...], (((1,), (1,)), ((), ())), preferred_element_type=jnp.float32
        ) * HEAD_SIZE ** (-0.5)
        row = lax.broadcasted_iota(jnp.int32, scores.shape, 0)
        column = lax.broadcasted_iota(jnp.int32, scores.shape, 1)
        scores = jnp.where(column <= base + lax.rem(row, rows), scores, mask_floor)
        weights = jnp.exp(scores - jnp.max(scores, axis=-1, keepdims=True))
        divisor = jnp.sum(weights, axis=-1, keepdims=True)
        result = (dot(weights.astype(jnp.bfloat16), values[...]) / divisor).astype(jnp.bfloat16)
        for place, head in enumerate(range(first, first + taken)):
            span = slice(head * HEAD_SIZE, (head + 1) * HEAD_SIZE)
            part = result[place * rows : (place + 1) * rows]
            attended[:, span] = part
            added += dot(part, down_out[span, :])

    @pl.when(step == 0)
    def _():
        total[...] = jnp.zeros_like(total)

    total[...] += added

    @pl.when(step == pl.num_programs(0) - 1)
    def _():
        narrow = total[...].astype(jnp.bfloat16)
        out_delta[...] = (adapter_scale * dot(narrow, up_out[...])).astype(jnp.bfloat16)


def attend(
    query_base,
    base_rows,
    base_other,
    own_rank,
    all_rank,
    query_up,
    keyval_up,
    cosines,
    sines,
    down_out,
    up_out,
):
    rows = query_base.shape[0]
    chips = base_rows.shape[0]
    seq = 2 * chips * rows
    blocks = keyval_up.shape[0]
    width = GROUP * HEAD_SIZE

    def whole(shape):
        return pl.BlockSpec(shape, lambda h: (0,) * len(shape))

    return pl.pallas_call(
        attend_kernel,
        grid=(KEYVALUE_HEADS,),
        out_shape=(
            jax.ShapeDtypeStruct((rows, QH * HEAD_SIZE), jnp.bfloat16),
            jax.ShapeDtypeStruct((rows, D), jnp.bfloat16),
        ),
        in_specs=[
            pl.BlockSpec((rows, width), lambda h: (0, h)),
            pl.BlockSpec((chips, rows, HEAD_SIZE), lambda h: (0, 0, h)),
            pl.BlockSpec((chips, rows, HEAD_SIZE), lambda h: (0, 0, h)),
            pl.BlockSpec((chips, rows, HEAD_SIZE), lambda h: (0, 0, h + KEYVALUE_HEADS)),
            pl.BlockSpec((chips, rows, HEAD_SIZE), lambda h: (0, 0, h + KEYVALUE_HEADS)),
            whole(own_rank.shape),
            whole(all_rank.shape),
            pl.BlockSpec((ADAPTER_RANK, width), lambda h: (0, h)),
            pl.BlockSpec((blocks, ADAPTER_RANK, HEAD_SIZE), lambda h: (0, 0, h)),
            pl.BlockSpec((blocks, ADAPTER_RANK, HEAD_SIZE), lambda h: (0, 0, h + KEYVALUE_HEADS)),
            whole(cosines.shape),
            whole(sines.shape),
            pl.BlockSpec((width, ADAPTER_RANK), lambda h: (h, 0)),
            whole(up_out.shape),
        ],
        out_specs=(
            pl.BlockSpec((rows, width), lambda h: (0, h)),
            whole((rows, D)),
        ),
        scratch_shapes=[
            pltpu.VMEM((rows, ADAPTER_RANK), jnp.float32),
            pltpu.VMEM((seq, HEAD_SIZE), jnp.bfloat16),
            pltpu.VMEM((seq, HEAD_SIZE), jnp.bfloat16),
        ],
        compiler_params=pltpu.CompilerParams(vmem_limit_bytes=60 << 20),
        cost_estimate=pl.CostEstimate(
            flops=4 * rows * QH * seq * HEAD_SIZE,
            bytes_accessed=10 << 20,
            transcendentals=rows * QH * seq,
        ),
    )(
        query_base,
        base_rows,
        base_other,
        base_rows,
        base_other,
        own_rank,
        all_rank,
        query_up,
        keyval_up,
        keyval_up,
        cosines,
        sines,
        down_out,
        up_out,
    )


def swap(block, mask):
    return lax.ppermute(block, ("groups", "ctx"), [(i, i ^ mask) for i in range(4 * PIECES)])


def direct_shards(
    normed_input, query_base, key_base, value_base, adapter_pool, stretch_adapter, adapter_owner
):
    plane = lax.axis_index("groups")
    index = lax.axis_index("ctx")
    core = index % 2
    half = index // PIECES
    tok_rows = normed_input.shape[0]
    ctx = lax.axis_size("ctx")
    seq = ctx * tok_rows
    blocks = [list(range(PIECES)), list(range(PIECES, 2 * PIECES))]
    same_core = [list(range(c, ctx, 2)) for c in range(2)]
    block_core = [list(range(s + c, s + PIECES, 2)) for s in (0, PIECES) for c in range(2)]

    moving = normed_input.reshape(tok_rows, PIECES, D // PIECES).transpose(1, 0, 2)
    moving = lax.all_to_all(moving, "ctx", 0, 0, axis_index_groups=blocks)
    elsewhere = swap(stretch_adapter, 2 * PIECES)
    base_rows = lax.all_gather(
        jnp.concatenate([key_base, value_base], 1), "ctx", axis_index_groups=same_core
    )

    packed_rest = pack_row(adapter_pool, REST, elsewhere)
    packed_down = pack_row(adapter_pool, DOWN, packed_rest, moving)
    ids = jnp.arange(adapter_owner.shape[0], dtype=jnp.int32)
    slots = jnp.sum(
        jnp.where(stretch_adapter[:, None] == ids[None, :], adapter_owner[None, :], 0), axis=1
    )
    near = (slots // PIECES) == half

    def fetch(packed, mirrored=None):
        spread = lax.all_to_all(packed, "ctx", 0, 0, axis_index_groups=blocks)
        sent = pick(spread, stretch_adapter, elsewhere, adapter_owner, mirrored)
        return [swap(block, flip * PIECES) if flip else block for flip, block in enumerate(sent)]

    def settle(arrived, close):
        own = jnp.where(close, arrived[0], arrived[1])
        other = jnp.where(close, arrived[2], arrived[3])
        low = plane == 0
        return jnp.stack([jnp.where(low, own, other), jnp.where(low, other, own)])

    close = jnp.where(half == 0, near[0], near[1])
    far_close = jnp.where(half == 0, near[1], near[0])
    rest = fetch(packed_rest, (128, 32))
    mine = jnp.arange(rest[0].shape[0], dtype=jnp.int32)[:, None] < 544
    rest = settle(rest, jnp.where(mine, close, far_close))
    rest, base_rows = lax.optimization_barrier((rest, base_rows))
    base_other = swap(base_rows, 1)
    rest = lax.all_gather(rest, "ctx", axis_index_groups=block_core)
    rest_other = swap(rest, 1)

    def section(first, last):
        same = rest[:, :, first:last]
        other = rest_other[:, :, first:last]
        return jnp.stack(
            [jnp.where(core == 0, same, other), jnp.where(core == 0, other, same)], 1
        )

    query_up = section(0, 128).reshape(ADAPTER_RANK, QH * HEAD_SIZE)
    keyval_up = jnp.stack([section(128, 160), section(544, 576)])
    keyval_up = keyval_up.reshape(2, ADAPTER_RANK, 2 * KEYVALUE_HEADS * HEAD_SIZE)
    down_out = section(160, 288).reshape(QH * HEAD_SIZE, ADAPTER_RANK)
    up_out = section(288, 544).reshape(ADAPTER_RANK, D)

    down_slice = settle(fetch(packed_down), close).reshape(D // PIECES, 3 * ADAPTER_RANK)
    partial_rows = jnp.dot(
        moving.reshape(BLOCK_TOKENS, D // PIECES), down_slice, preferred_element_type=jnp.float32
    ).astype(jnp.bfloat16)
    partial_rows = lax.all_to_all(
        partial_rows.reshape(PIECES, tok_rows, 3 * ADAPTER_RANK),
        "ctx",
        0,
        0,
        axis_index_groups=blocks,
    )
    own_rank = jnp.sum(partial_rows.astype(jnp.float32), axis=0).astype(jnp.bfloat16)
    all_rank = jnp.broadcast_to(own_rank[None, :, ADAPTER_RANK:], (ctx, tok_rows, 2 * ADAPTER_RANK))
    all_rank = lax.all_to_all(all_rank, "ctx", 0, 0).reshape(seq, 2 * ADAPTER_RANK)

    half_dim = HEAD_SIZE // 2
    frequency = rope_base ** (-(jnp.arange(half_dim, dtype=jnp.float32) * 2.0) / HEAD_SIZE)
    angle = jnp.arange(seq, dtype=jnp.int32).astype(jnp.float32)[:, None] * frequency[None, :]
    cosine = jnp.cos(angle)
    sine = jnp.sin(angle)
    cosines = jnp.concatenate([cosine, cosine], 1)
    sines = jnp.concatenate([-sine, sine], 1)
    return attend(
        query_base,
        base_rows,
        base_other,
        own_rank,
        all_rank,
        query_up,
        keyval_up,
        cosines,
        sines,
        down_out,
        up_out,
    )


def shards(normed_input, query_base, key_base, value_base, adapter_pool, stretch_adapter, owner):
    fits = (
        lax.axis_size("groups") == 2
        and lax.axis_size("ctx") == 2 * PIECES
        and normed_input.shape[0] * PIECES == BLOCK_TOKENS
        and adapter_pool.shape[0] == 1
    )
    plan = direct_shards if fits else spread_shards
    return plan(
        normed_input, query_base, key_base, value_base, adapter_pool, stretch_adapter, owner
    )


def solution(mesh):
    placed = (
        P(("groups", "ctx"), None),
        P(("groups", "ctx"), None),
        P(("groups", "ctx"), None),
        P(("groups", "ctx"), None),
        P("ctx", None),
        P("groups"),
        P(),
    )
    return jax.shard_map(
        shards,
        mesh=mesh,
        in_specs=placed,
        out_specs=(P(("groups", "ctx"), None), P(("groups", "ctx"), None)),
        check_vma=False,
    )
```

```python
from functools import partial
import math

import jax
import jax.numpy as jnp
from jax import lax
from jax.experimental import pallas as pl
from jax.experimental.pallas import tpu as pltpu
from jax.sharding import PartitionSpec as P

D = 8192
QH = 32
KEYVALUE_HEADS = 4
HEAD_SIZE = 128
ADAPTER_RANK = 64
BLOCK_TOKENS = 512
QKV_POOL = 1900544


adapter_scale = 2.0
rope_base = 500000.0
mask_floor = -1e30


def from_partner(block, axis, apart):
    count = lax.axis_size(axis)
    route = []
    for low in range(count):
        high = low | 1 << apart
        if high != low and high < count:
            route += [(low, high), (high, low)]
    return lax.ppermute(block, axis, route)


def rotate(delta, token_positions, heads):
    half_dim = HEAD_SIZE // 2
    frequency = rope_base ** (-(jnp.arange(half_dim, dtype=jnp.float32) * 2.0) / HEAD_SIZE)
    angle = token_positions.astype(jnp.float32)[:, None] * frequency[None, :]
    cosine = jnp.cos(angle)[:, None, :]
    sine_part = jnp.sin(angle)[:, None, :]
    shaped = delta.reshape(delta.shape[0], heads, HEAD_SIZE)
    first_half = shaped[..., :half_dim]
    second_half = shaped[..., half_dim:]
    joined = jnp.concatenate(
        [
            first_half * cosine - second_half * sine_part,
            second_half * cosine + first_half * sine_part,
        ],
        -1,
    )
    return joined.reshape(delta.shape[0], heads * HEAD_SIZE)


def project_heads(
    narrow_product, query_row_block, key_row_block, value_row_block, upper_part, token_positions
):
    query_up_weight = upper_part[: ADAPTER_RANK * QH * HEAD_SIZE].reshape(
        ADAPTER_RANK, QH * HEAD_SIZE
    )
    keyvalue_up_weight = upper_part[ADAPTER_RANK * QH * HEAD_SIZE :].reshape(
        ADAPTER_RANK, 2 * KEYVALUE_HEADS * HEAD_SIZE
    )
    query_correction = adapter_scale * jnp.dot(
        narrow_product[:, :ADAPTER_RANK], query_up_weight, preferred_element_type=jnp.float32
    )
    key_correction = adapter_scale * jnp.dot(
        narrow_product[:, ADAPTER_RANK : 2 * ADAPTER_RANK],
        keyvalue_up_weight[:, : KEYVALUE_HEADS * HEAD_SIZE],
        preferred_element_type=jnp.float32,
    )
    value_correction = adapter_scale * jnp.dot(
        narrow_product[:, 2 * ADAPTER_RANK :],
        keyvalue_up_weight[:, KEYVALUE_HEADS * HEAD_SIZE :],
        preferred_element_type=jnp.float32,
    )
    queries = (
        query_row_block.astype(jnp.float32) + rotate(query_correction, token_positions, QH)
    ).astype(jnp.bfloat16)
    new_keys = (
        key_row_block.astype(jnp.float32) + rotate(key_correction, token_positions, KEYVALUE_HEADS)
    ).astype(jnp.bfloat16)
    new_values = (value_row_block.astype(jnp.float32) + value_correction).astype(jnp.bfloat16)
    return (queries, new_keys, new_values)


def output_delta(attended_rows, out_part):
    down_out = out_part[: QH * HEAD_SIZE * ADAPTER_RANK].reshape(QH * HEAD_SIZE, ADAPTER_RANK)
    raised_output = out_part[QH * HEAD_SIZE * ADAPTER_RANK :].reshape(ADAPTER_RANK, D)
    narrow_product = jnp.dot(attended_rows, down_out, preferred_element_type=jnp.float32).astype(
        jnp.bfloat16
    )
    return (
        adapter_scale * jnp.dot(narrow_product, raised_output, preferred_element_type=jnp.float32)
    ).astype(jnp.bfloat16)


def head_major(query_row_block):
    count_rows = query_row_block.shape[0]
    group_size = QH // KEYVALUE_HEADS
    return (
        query_row_block.reshape(count_rows, KEYVALUE_HEADS, group_size, HEAD_SIZE)
        .transpose(1, 2, 0, 3)
        .reshape(KEYVALUE_HEADS, group_size * count_rows, HEAD_SIZE)
    )


def row_major(head_rows, count_rows):
    group_size = QH // KEYVALUE_HEADS
    return (
        head_rows.reshape(KEYVALUE_HEADS, group_size, count_rows, HEAD_SIZE)
        .transpose(2, 0, 1, 3)
        .reshape(count_rows, QH * HEAD_SIZE)
    )


def online_update(current, queries, query_pos, key_slice, value_slice, key_start):
    run_max, run_sum, run_acc = current
    scores = jnp.einsum(
        "hqd,khd->hqk", queries, key_slice, preferred_element_type=jnp.float32
    ) * HEAD_SIZE ** (-0.5)
    key_pos = key_start + jnp.arange(key_slice.shape[0], dtype=jnp.int32)
    allowed = (query_pos[:, None] >= key_pos[None, :])[None]
    new_max = jnp.maximum(run_max, jnp.max(jnp.where(allowed, scores, mask_floor), axis=-1))
    weights = jnp.where(allowed, jnp.exp(scores - new_max[..., None]), 0.0)
    rescale = jnp.exp(run_max - new_max)
    new_sum = run_sum * rescale + jnp.sum(weights, axis=-1)
    new_acc = run_acc * rescale[..., None] + jnp.einsum(
        "hqk,khd->hqd",
        weights.astype(jnp.bfloat16),
        value_slice,
        preferred_element_type=jnp.float32,
    )
    return (new_max, new_sum, new_acc)


def unchanged(current):
    return current


def fold_keys(carry_state, shard_part, prepared):
    key_row_block, value_row_block = shard_part
    key_count = key_row_block.shape[0]
    sub_width = math.gcd(key_count, 1024)
    key_heads = key_row_block.reshape(key_count // sub_width, sub_width, KEYVALUE_HEADS, HEAD_SIZE)
    value_heads = value_row_block.reshape(
        key_count // sub_width, sub_width, KEYVALUE_HEADS, HEAD_SIZE
    )

    def one_step(sub_index, carried):
        key_start = sub_index * sub_width
        key_slice = lax.dynamic_index_in_dim(key_heads, sub_index, 0, keepdims=False)
        value_slice = lax.dynamic_index_in_dim(value_heads, sub_index, 0, keepdims=False)
        updated = []
        for (queries, query_pos), running in zip(prepared, carried):
            advance = partial(
                online_update,
                queries=queries,
                query_pos=query_pos,
                key_slice=key_slice,
                value_slice=value_slice,
                key_start=key_start,
            )
            updated.append(lax.cond(key_start <= jnp.max(query_pos), advance, unchanged, running))
        return tuple(updated)

    return lax.fori_loop(0, key_count // sub_width, one_step, carry_state)


def finish_block(result, count_rows):
    run_max, run_sum, run_acc = result
    divisor = jnp.where(run_sum > 0.0, run_sum, 1.0)
    return row_major(run_acc / divisor[..., None], count_rows).astype(jnp.bfloat16)


def spread_shards(
    normed_input, query_base, key_base, value_base, adapter_pool, stretch_adapter, adapter_owner
):
    cycle_size = lax.axis_size("ctx")
    my_index = lax.axis_index("ctx")
    tok_rows = normed_input.shape[0]
    token_positions = my_index * tok_rows + jnp.arange(tok_rows, dtype=jnp.int32)
    device_ids = jnp.arange(cycle_size, dtype=jnp.int32)
    stretch_of = device_ids * tok_rows // BLOCK_TOKENS
    stretch_ids = jnp.arange(stretch_adapter.shape[0], dtype=jnp.int32)
    adapter_of = jnp.sum(
        jnp.where(stretch_of[:, None] == stretch_ids[None, :], stretch_adapter[None, :], 0), axis=1
    )
    adapter_ids = jnp.arange(adapter_owner.shape[0], dtype=jnp.int32)
    slot_of = jnp.sum(
        jnp.where(adapter_of[:, None] == adapter_ids[None, :], adapter_owner[None, :], 0), axis=1
    )
    down_size = 3 * ADAPTER_RANK * D
    group_count = BLOCK_TOKENS // tok_rows
    levels = group_count.bit_length() - 1
    local_index = my_index % group_count
    col_width = D // group_count
    piece_len = down_size // (group_count * cycle_size)
    pool_rows = adapter_pool.shape[0]
    down_shaped = adapter_pool[:, :down_size].reshape(pool_rows, group_count, cycle_size, piece_len)
    spread_down = lax.all_to_all(down_shaped, "ctx", split_axis=2, concat_axis=0, tiled=True)
    flat_down = spread_down.reshape(-1, piece_len)
    wanted = jnp.take(flat_down, slot_of * group_count + device_ids % group_count, axis=0)[
        :, None, :
    ]
    down_slice = lax.all_to_all(wanted, "ctx", split_axis=0, concat_axis=1, tiled=True).reshape(
        col_width, 3 * ADAPTER_RANK
    )
    spread_rest = lax.all_to_all(
        adapter_pool[:, down_size:], "ctx", split_axis=1, concat_axis=0, tiled=True
    )
    rest_row = lax.all_to_all(
        jnp.take(spread_rest, slot_of, axis=0), "ctx", split_axis=0, concat_axis=1, tiled=True
    )[0]
    upper_part = rest_row[: QKV_POOL - down_size]
    out_part = rest_row[QKV_POOL - down_size :]
    pieces = normed_input.reshape(tok_rows, group_count, col_width)
    slice_order = jnp.bitwise_xor(local_index, jnp.arange(group_count, dtype=jnp.int32))
    moving = jnp.take(pieces, slice_order, axis=1).transpose(1, 0, 2)
    for level in range(levels):
        shaped = moving.reshape(group_count >> level + 1, 2, 1 << level, tok_rows, col_width)
        arrived = from_partner(shaped[:, 1], "ctx", level)
        moving = jnp.stack([shaped[:, 0], arrived], 1).reshape(group_count, tok_rows, col_width)
    partial_rows = jnp.dot(
        moving.reshape(group_count * tok_rows, col_width),
        down_slice,
        preferred_element_type=jnp.float32,
    ).reshape(group_count, tok_rows, 3 * ADAPTER_RANK)
    for level in reversed(range(levels)):
        halves = partial_rows.reshape(2, partial_rows.shape[0] // 2, tok_rows, 3 * ADAPTER_RANK)
        partial_rows = halves[0] + from_partner(
            halves[1].astype(jnp.bfloat16), "ctx", level
        ).astype(jnp.float32)
    narrow_product = partial_rows[0].astype(jnp.bfloat16)
    queries, new_keys, new_values = project_heads(
        narrow_product, query_base, key_base, value_base, upper_part, token_positions
    )
    group_size = QH // KEYVALUE_HEADS
    blocks = [(queries, token_positions)]
    prepared = [
        (head_major(block_q), jnp.tile(block_pos, group_size)) for block_q, block_pos in blocks
    ]
    initial = tuple(
        (
            (
                jnp.full((KEYVALUE_HEADS, head_q.shape[1]), mask_floor, jnp.float32),
                jnp.zeros((KEYVALUE_HEADS, head_q.shape[1]), jnp.float32),
                jnp.zeros((KEYVALUE_HEADS, head_q.shape[1], HEAD_SIZE), jnp.float32),
            )
            for head_q, block_pos in prepared
        )
    )
    finals = fold_keys(
        initial,
        (
            lax.all_gather(new_keys, "ctx", axis=0, tiled=True),
            lax.all_gather(new_values, "ctx", axis=0, tiled=True),
        ),
        prepared,
    )
    attended = finish_block(finals[0], tok_rows)
    out_delta = output_delta(attended, out_part)
    return (attended, out_delta)


PIECES = 8
GROUP = QH // KEYVALUE_HEADS
DOWN = ((0, 12288),)
REST = ((12288, 2048), (14336, 512), (14848, 2048), (16896, 4096))


def pack_kernel(sections, pool, *refs):
    out, buffers, sems = refs[-3:]
    plane = lax.axis_index("groups")
    slabs, slab_rows = out.shape[:2]

    def copies(slab):
        listed = []
        offset = 0
        for first, rows in sections:
            share = rows // (2 * PIECES)
            begin = first + (slab * 2 + plane) * share
            listed.append(
                pltpu.make_async_copy(
                    pool.at[:, pl.ds(pl.multiple_of(begin * 128, 2048), share * 128)],
                    buffers.at[slab, :, pl.ds(offset, share * 128)],
                    sems.at[slab, len(listed)],
                )
            )
            offset += share * 128
        return listed

    for slab in range(slabs):
        for copy in copies(slab):
            copy.start()

    def step(slab, carried):
        for copy in copies(slab):
            copy.wait()

        def chunk(index, inner):
            line = buffers[slab, :, pl.ds(pl.multiple_of(index * 2048, 2048), 2048)]
            block = line.astype(jnp.float32).reshape(16, 128).astype(jnp.bfloat16)
            out[slab, pl.ds(pl.multiple_of(index * 16, 16), 16), :] = block
            return inner

        lax.fori_loop(0, slab_rows // 16, chunk, 0, unroll=8)
        return carried

    lax.fori_loop(0, slabs, step, 0)


def pack_row(pool, sections, *after):
    slab_rows = sum(rows for _, rows in sections) // (2 * PIECES)
    return pl.pallas_call(
        partial(pack_kernel, sections),
        out_shape=jax.ShapeDtypeStruct((PIECES, slab_rows, 128), jnp.bfloat16),
        in_specs=[pl.BlockSpec(memory_space=pl.ANY)] * (1 + len(after)),
        out_specs=pl.BlockSpec(memory_space=pltpu.VMEM),
        scratch_shapes=[
            pltpu.VMEM((PIECES, 1, slab_rows * 128), jnp.bfloat16),
            pltpu.SemaphoreType.DMA((PIECES, len(sections))),
        ],
        compiler_params=pltpu.CompilerParams(vmem_limit_bytes=60 << 20),
        cost_estimate=pl.CostEstimate(flops=0, bytes_accessed=8 << 20, transcendentals=0),
    )(pool, *after)


def pick_kernel(mirrored, here, there, owner, spread, *refs):
    outs, sems = refs[:4], refs[4]
    half = lax.axis_index("ctx") // PIECES
    rows = spread.shape[1]
    copies = []
    for flip, out in enumerate(outs):
        wishes = there if flip >= 2 else here
        block = half ^ (flip & 1)
        row = lax.rem(owner[wishes[block]], PIECES)
        copies.append(
            pltpu.make_async_copy(spread.at[row], out.at[pl.ds(0, rows)], sems.at[flip, 0])
        )
        if mirrored is not None:
            first, count = mirrored
            row = lax.rem(owner[wishes[1 - block]], PIECES)
            copies.append(
                pltpu.make_async_copy(
                    spread.at[row, pl.ds(first, count)],
                    out.at[pl.ds(rows, count)],
                    sems.at[flip, 1],
                )
            )
    for copy in copies:
        copy.start()
    for copy in copies:
        copy.wait()


def pick(spread, here, there, owner, mirrored):
    rows = spread.shape[1] + (mirrored[1] if mirrored else 0)
    slab = jax.ShapeDtypeStruct((rows, 128), jnp.bfloat16)
    return pl.pallas_call(
        partial(pick_kernel, mirrored),
        out_shape=(slab,) * 4,
        in_specs=[pl.BlockSpec(memory_space=pltpu.SMEM)] * 3 + [pl.BlockSpec(memory_space=pl.ANY)],
        out_specs=(pl.BlockSpec(memory_space=pltpu.VMEM),) * 4,
        scratch_shapes=[pltpu.SemaphoreType.DMA((4, 2))],
        compiler_params=pltpu.CompilerParams(vmem_limit_bytes=16 << 20),
        cost_estimate=pl.CostEstimate(flops=0, bytes_accessed=2 << 20, transcendentals=0),
    )(here, there, owner, spread)


def assemble_kernel(*refs):
    pieces, out, sems = refs[:PIECES], refs[PIECES], refs[PIECES + 1]
    seat = lax.rem(lax.axis_index("ctx"), PIECES)
    copies = [
        pltpu.make_async_copy(piece, out.at[seat ^ apart], sems.at[apart])
        for apart, piece in enumerate(pieces)
    ]
    for copy in copies:
        copy.start()
    for copy in copies:
        copy.wait()


def assemble(pieces):
    return pl.pallas_call(
        assemble_kernel,
        out_shape=jax.ShapeDtypeStruct((PIECES,) + pieces[0].shape, jnp.bfloat16),
        in_specs=[pl.BlockSpec(memory_space=pl.ANY)] * PIECES,
        out_specs=pl.BlockSpec(memory_space=pltpu.VMEM),
        scratch_shapes=[pltpu.SemaphoreType.DMA((PIECES,))],
        compiler_params=pltpu.CompilerParams(vmem_limit_bytes=16 << 20),
        cost_estimate=pl.CostEstimate(flops=0, bytes_accessed=6 << 20, transcendentals=0),
    )(*pieces)


def attend_kernel(
    query_block,
    key_same,
    key_other,
    value_same,
    value_other,
    own_rank,
    all_rank,
    query_up,
    key_up,
    value_up,
    cosines,
    sines,
    down_out,
    up_out,
    attended,
    out_delta,
    total,
    keys,
    values,
):
    step = pl.program_id(0)
    rows = query_block.shape[0]
    base = lax.axis_index("ctx") * rows
    dot = partial(jnp.dot, preferred_element_type=jnp.float32)

    def turned(delta, cosine, sine):
        return delta * cosine + pltpu.roll(delta, HEAD_SIZE // 2, 1) * sine

    half = lax.axis_index("ctx") * rows // BLOCK_TOKENS
    core = lax.rem(lax.axis_index("ctx"), 2)
    for block in range(key_up.shape[0]):
        for chip in range(block * PIECES // 2, (block + 1) * PIECES // 2):
            for apart in range(2):
                first = (2 * chip + (core ^ apart)) * rows
                span = pl.ds(pl.multiple_of(first, rows), rows)
                key_base = (key_other if apart else key_same)[chip]
                value_base = (value_other if apart else value_same)[chip]
                delta = adapter_scale * dot(all_rank[span, :ADAPTER_RANK], key_up[block ^ half])
                delta = turned(delta, cosines[span, :], sines[span, :])
                keys[span, :] = (key_base.astype(jnp.float32) + delta).astype(jnp.bfloat16)
                delta = adapter_scale * dot(all_rank[span, ADAPTER_RANK:], value_up[block ^ half])
                values[span, :] = (value_base.astype(jnp.float32) + delta).astype(jnp.bfloat16)
    here = pl.ds(pl.multiple_of(base, rows), rows)
    cosine = cosines[here, :]
    sine = sines[here, :]
    delta = adapter_scale * dot(own_rank[:, :ADAPTER_RANK], query_up[...])
    added = jnp.zeros((rows, ADAPTER_RANK), jnp.float32)
    taken = GROUP // 2
    for first in range(0, GROUP, taken):
        queries = []
        for head in range(first, first + taken):
            span = slice(head * HEAD_SIZE, (head + 1) * HEAD_SIZE)
            moved = turned(delta[:, span], cosine, sine)
            queries.append(
                (query_block[:, span].astype(jnp.float32) + moved).astype(jnp.bfloat16)
            )
        queries = jnp.concatenate(queries, 0)
        scores = lax.dot_general(
            queries, keys[...], (((1,), (1,)), ((), ())), preferred_element_type=jnp.float32
        ) * HEAD_SIZE ** (-0.5)
        row = lax.broadcasted_iota(jnp.int32, scores.shape, 0)
        column = lax.broadcasted_iota(jnp.int32, scores.shape, 1)
        scores = jnp.where(column <= base + lax.rem(row, rows), scores, mask_floor)
        weights = jnp.exp(scores - jnp.max(scores, axis=-1, keepdims=True))
        divisor = jnp.sum(weights, axis=-1, keepdims=True)
        result = (dot(weights.astype(jnp.bfloat16), values[...]) / divisor).astype(jnp.bfloat16)
        for place, head in enumerate(range(first, first + taken)):
            span = slice(head * HEAD_SIZE, (head + 1) * HEAD_SIZE)
            part = result[place * rows : (place + 1) * rows]
            attended[:, span] = part
            added += dot(part, down_out[span, :])

    @pl.when(step == 0)
    def _():
        total[...] = jnp.zeros_like(total)

    total[...] += added

    @pl.when(step == pl.num_programs(0) - 1)
    def _():
        narrow = total[...].astype(jnp.bfloat16)
        out_delta[...] = (adapter_scale * dot(narrow, up_out[...])).astype(jnp.bfloat16)


def attend(
    query_base,
    base_rows,
    base_other,
    own_rank,
    all_rank,
    query_up,
    keyval_up,
    cosines,
    sines,
    down_out,
    up_out,
):
    rows = query_base.shape[0]
    chips = base_rows.shape[0]
    seq = 2 * chips * rows
    blocks = keyval_up.shape[0]
    width = GROUP * HEAD_SIZE

    def whole(shape):
        return pl.BlockSpec(shape, lambda h: (0,) * len(shape))

    return pl.pallas_call(
        attend_kernel,
        grid=(KEYVALUE_HEADS,),
        out_shape=(
            jax.ShapeDtypeStruct((rows, QH * HEAD_SIZE), jnp.bfloat16),
            jax.ShapeDtypeStruct((rows, D), jnp.bfloat16),
        ),
        in_specs=[
            pl.BlockSpec((rows, width), lambda h: (0, h)),
            pl.BlockSpec((chips, rows, HEAD_SIZE), lambda h: (0, 0, h)),
            pl.BlockSpec((chips, rows, HEAD_SIZE), lambda h: (0, 0, h)),
            pl.BlockSpec((chips, rows, HEAD_SIZE), lambda h: (0, 0, h + KEYVALUE_HEADS)),
            pl.BlockSpec((chips, rows, HEAD_SIZE), lambda h: (0, 0, h + KEYVALUE_HEADS)),
            whole(own_rank.shape),
            whole(all_rank.shape),
            pl.BlockSpec((ADAPTER_RANK, width), lambda h: (0, h)),
            pl.BlockSpec((blocks, ADAPTER_RANK, HEAD_SIZE), lambda h: (0, 0, h)),
            pl.BlockSpec((blocks, ADAPTER_RANK, HEAD_SIZE), lambda h: (0, 0, h + KEYVALUE_HEADS)),
            whole(cosines.shape),
            whole(sines.shape),
            pl.BlockSpec((width, ADAPTER_RANK), lambda h: (h, 0)),
            whole(up_out.shape),
        ],
        out_specs=(
            pl.BlockSpec((rows, width), lambda h: (0, h)),
            whole((rows, D)),
        ),
        scratch_shapes=[
            pltpu.VMEM((rows, ADAPTER_RANK), jnp.float32),
            pltpu.VMEM((seq, HEAD_SIZE), jnp.bfloat16),
            pltpu.VMEM((seq, HEAD_SIZE), jnp.bfloat16),
        ],
        compiler_params=pltpu.CompilerParams(vmem_limit_bytes=60 << 20),
        cost_estimate=pl.CostEstimate(
            flops=4 * rows * QH * seq * HEAD_SIZE,
            bytes_accessed=10 << 20,
            transcendentals=rows * QH * seq,
        ),
    )(
        query_base,
        base_rows,
        base_other,
        base_rows,
        base_other,
        own_rank,
        all_rank,
        query_up,
        keyval_up,
        keyval_up,
        cosines,
        sines,
        down_out,
        up_out,
    )


def swap(block, mask):
    return lax.ppermute(block, ("groups", "ctx"), [(i, i ^ mask) for i in range(4 * PIECES)])


def direct_shards(
    normed_input, query_base, key_base, value_base, adapter_pool, stretch_adapter, adapter_owner
):
    plane = lax.axis_index("groups")
    index = lax.axis_index("ctx")
    core = index % 2
    half = index // PIECES
    tok_rows = normed_input.shape[0]
    ctx = lax.axis_size("ctx")
    seq = ctx * tok_rows
    blocks = [list(range(PIECES)), list(range(PIECES, 2 * PIECES))]
    same_core = [list(range(c, ctx, 2)) for c in range(2)]

    base_rows = lax.all_gather(
        jnp.concatenate([key_base, value_base], 1), "ctx", axis_index_groups=same_core
    )
    elsewhere = swap(stretch_adapter, 2 * PIECES)
    packed_rest = pack_row(adapter_pool, REST)
    packed_down = pack_row(adapter_pool, DOWN, packed_rest, elsewhere)
    ids = jnp.arange(adapter_owner.shape[0], dtype=jnp.int32)
    slots = jnp.sum(
        jnp.where(stretch_adapter[:, None] == ids[None, :], adapter_owner[None, :], 0), axis=1
    )
    near = (slots // PIECES) == half

    def fetch(spread, mirrored=None):
        sent = pick(spread, stretch_adapter, elsewhere, adapter_owner, mirrored)
        return [swap(block, flip * PIECES) if flip else block for flip, block in enumerate(sent)]

    def settle(arrived, close):
        own = jnp.where(close, arrived[0], arrived[1])
        other = jnp.where(close, arrived[2], arrived[3])
        low = plane == 0
        return jnp.stack([jnp.where(low, own, other), jnp.where(low, other, own)])

    close = jnp.where(half == 0, near[0], near[1])
    far_close = jnp.where(half == 0, near[1], near[0])
    spread_rest = lax.all_to_all(packed_rest, "ctx", 0, 0, axis_index_groups=blocks)
    spread_down = lax.all_to_all(packed_down, "ctx", 0, 0, axis_index_groups=blocks)
    moving = normed_input.reshape(tok_rows, PIECES, D // PIECES).transpose(1, 0, 2)
    moving, spread_down = lax.optimization_barrier((moving, spread_down))
    moving = lax.all_to_all(moving, "ctx", 0, 0, axis_index_groups=blocks)

    rest = fetch(spread_rest, (128, 32))
    mine = jnp.arange(rest[0].shape[0], dtype=jnp.int32)[:, None] < 544
    rest = settle(rest, jnp.where(mine, close, far_close))
    rest = [swap(rest, apart) if apart else rest for apart in (0, 2, 4, 6)]
    rest = assemble([piece for block in rest for piece in (block, swap(block, 1))])
    query_up = rest[:, :, :128].reshape(ADAPTER_RANK, QH * HEAD_SIZE)
    keyval_up = jnp.stack([rest[:, :, 128:160], rest[:, :, 544:]])
    keyval_up = keyval_up.reshape(2, ADAPTER_RANK, 2 * KEYVALUE_HEADS * HEAD_SIZE)
    down_out = rest[:, :, 160:288].reshape(QH * HEAD_SIZE, ADAPTER_RANK)
    up_out = rest[:, :, 288:544].reshape(ADAPTER_RANK, D)

    arrived = fetch(spread_down)
    arrived, base_rows = lax.optimization_barrier((arrived, base_rows))
    base_other = swap(base_rows, 1)
    down_slice = settle(arrived, close).reshape(D // PIECES, 3 * ADAPTER_RANK)
    partial_rows = jnp.dot(
        moving.reshape(BLOCK_TOKENS, D // PIECES), down_slice, preferred_element_type=jnp.float32
    ).astype(jnp.bfloat16)
    partial_rows = lax.all_to_all(
        partial_rows.reshape(PIECES, tok_rows, 3 * ADAPTER_RANK),
        "ctx",
        0,
        0,
        axis_index_groups=blocks,
    )
    own_rank = jnp.sum(partial_rows.astype(jnp.float32), axis=0).astype(jnp.bfloat16)
    all_rank = jnp.broadcast_to(own_rank[None, :, ADAPTER_RANK:], (ctx, tok_rows, 2 * ADAPTER_RANK))
    all_rank = lax.all_to_all(all_rank, "ctx", 0, 0).reshape(seq, 2 * ADAPTER_RANK)

    half_dim = HEAD_SIZE // 2
    frequency = rope_base ** (-(jnp.arange(half_dim, dtype=jnp.float32) * 2.0) / HEAD_SIZE)
    angle = jnp.arange(seq, dtype=jnp.int32).astype(jnp.float32)[:, None] * frequency[None, :]
    cosine = jnp.cos(angle)
    sine = jnp.sin(angle)
    cosines = jnp.concatenate([cosine, cosine], 1)
    sines = jnp.concatenate([-sine, sine], 1)
    return attend(
        query_base,
        base_rows,
        base_other,
        own_rank,
        all_rank,
        query_up,
        keyval_up,
        cosines,
        sines,
        down_out,
        up_out,
    )


def shards(normed_input, query_base, key_base, value_base, adapter_pool, stretch_adapter, owner):
    fits = (
        lax.axis_size("groups") == 2
        and lax.axis_size("ctx") == 2 * PIECES
        and normed_input.shape[0] * PIECES == BLOCK_TOKENS
        and adapter_pool.shape[0] == 1
    )
    plan = direct_shards if fits else spread_shards
    return plan(
        normed_input, query_base, key_base, value_base, adapter_pool, stretch_adapter, owner
    )


def solution(mesh):
    placed = (
        P(("groups", "ctx"), None),
        P(("groups", "ctx"), None),
        P(("groups", "ctx"), None),
        P(("groups", "ctx"), None),
        P("ctx", None),
        P("groups"),
        P(),
    )
    return jax.shard_map(
        shards,
        mesh=mesh,
        in_specs=placed,
        out_specs=(P(("groups", "ctx"), None), P(("groups", "ctx"), None)),
        check_vma=False,
    )
```

```python
from functools import partial
import math

import jax
import jax.numpy as jnp
from jax import lax
from jax.experimental import pallas as pl
from jax.experimental.pallas import tpu as pltpu
from jax.sharding import PartitionSpec as P

D = 8192
QH = 32
KEYVALUE_HEADS = 4
HEAD_SIZE = 128
ADAPTER_RANK = 64
BLOCK_TOKENS = 512
QKV_POOL = 1900544


adapter_scale = 2.0
rope_base = 500000.0
mask_floor = -1e30


def from_partner(block, axis, apart):
    count = lax.axis_size(axis)
    route = []
    for low in range(count):
        high = low | 1 << apart
        if high != low and high < count:
            route += [(low, high), (high, low)]
    return lax.ppermute(block, axis, route)


def rotate(delta, token_positions, heads):
    half_dim = HEAD_SIZE // 2
    frequency = rope_base ** (-(jnp.arange(half_dim, dtype=jnp.float32) * 2.0) / HEAD_SIZE)
    angle = token_positions.astype(jnp.float32)[:, None] * frequency[None, :]
    cosine = jnp.cos(angle)[:, None, :]
    sine_part = jnp.sin(angle)[:, None, :]
    shaped = delta.reshape(delta.shape[0], heads, HEAD_SIZE)
    first_half = shaped[..., :half_dim]
    second_half = shaped[..., half_dim:]
    joined = jnp.concatenate(
        [
            first_half * cosine - second_half * sine_part,
            second_half * cosine + first_half * sine_part,
        ],
        -1,
    )
    return joined.reshape(delta.shape[0], heads * HEAD_SIZE)


def project_heads(
    narrow_product, query_row_block, key_row_block, value_row_block, upper_part, token_positions
):
    query_up_weight = upper_part[: ADAPTER_RANK * QH * HEAD_SIZE].reshape(
        ADAPTER_RANK, QH * HEAD_SIZE
    )
    keyvalue_up_weight = upper_part[ADAPTER_RANK * QH * HEAD_SIZE :].reshape(
        ADAPTER_RANK, 2 * KEYVALUE_HEADS * HEAD_SIZE
    )
    query_correction = adapter_scale * jnp.dot(
        narrow_product[:, :ADAPTER_RANK], query_up_weight, preferred_element_type=jnp.float32
    )
    key_correction = adapter_scale * jnp.dot(
        narrow_product[:, ADAPTER_RANK : 2 * ADAPTER_RANK],
        keyvalue_up_weight[:, : KEYVALUE_HEADS * HEAD_SIZE],
        preferred_element_type=jnp.float32,
    )
    value_correction = adapter_scale * jnp.dot(
        narrow_product[:, 2 * ADAPTER_RANK :],
        keyvalue_up_weight[:, KEYVALUE_HEADS * HEAD_SIZE :],
        preferred_element_type=jnp.float32,
    )
    queries = (
        query_row_block.astype(jnp.float32) + rotate(query_correction, token_positions, QH)
    ).astype(jnp.bfloat16)
    new_keys = (
        key_row_block.astype(jnp.float32) + rotate(key_correction, token_positions, KEYVALUE_HEADS)
    ).astype(jnp.bfloat16)
    new_values = (value_row_block.astype(jnp.float32) + value_correction).astype(jnp.bfloat16)
    return (queries, new_keys, new_values)


def output_delta(attended_rows, out_part):
    down_out = out_part[: QH * HEAD_SIZE * ADAPTER_RANK].reshape(QH * HEAD_SIZE, ADAPTER_RANK)
    raised_output = out_part[QH * HEAD_SIZE * ADAPTER_RANK :].reshape(ADAPTER_RANK, D)
    narrow_product = jnp.dot(attended_rows, down_out, preferred_element_type=jnp.float32).astype(
        jnp.bfloat16
    )
    return (
        adapter_scale * jnp.dot(narrow_product, raised_output, preferred_element_type=jnp.float32)
    ).astype(jnp.bfloat16)


def head_major(query_row_block):
    count_rows = query_row_block.shape[0]
    group_size = QH // KEYVALUE_HEADS
    return (
        query_row_block.reshape(count_rows, KEYVALUE_HEADS, group_size, HEAD_SIZE)
        .transpose(1, 2, 0, 3)
        .reshape(KEYVALUE_HEADS, group_size * count_rows, HEAD_SIZE)
    )


def row_major(head_rows, count_rows):
    group_size = QH // KEYVALUE_HEADS
    return (
        head_rows.reshape(KEYVALUE_HEADS, group_size, count_rows, HEAD_SIZE)
        .transpose(2, 0, 1, 3)
        .reshape(count_rows, QH * HEAD_SIZE)
    )


def online_update(current, queries, query_pos, key_slice, value_slice, key_start):
    run_max, run_sum, run_acc = current
    scores = jnp.einsum(
        "hqd,khd->hqk", queries, key_slice, preferred_element_type=jnp.float32
    ) * HEAD_SIZE ** (-0.5)
    key_pos = key_start + jnp.arange(key_slice.shape[0], dtype=jnp.int32)
    allowed = (query_pos[:, None] >= key_pos[None, :])[None]
    new_max = jnp.maximum(run_max, jnp.max(jnp.where(allowed, scores, mask_floor), axis=-1))
    weights = jnp.where(allowed, jnp.exp(scores - new_max[..., None]), 0.0)
    rescale = jnp.exp(run_max - new_max)
    new_sum = run_sum * rescale + jnp.sum(weights, axis=-1)
    new_acc = run_acc * rescale[..., None] + jnp.einsum(
        "hqk,khd->hqd",
        weights.astype(jnp.bfloat16),
        value_slice,
        preferred_element_type=jnp.float32,
    )
    return (new_max, new_sum, new_acc)


def unchanged(current):
    return current


def fold_keys(carry_state, shard_part, prepared):
    key_row_block, value_row_block = shard_part
    key_count = key_row_block.shape[0]
    sub_width = math.gcd(key_count, 1024)
    key_heads = key_row_block.reshape(key_count // sub_width, sub_width, KEYVALUE_HEADS, HEAD_SIZE)
    value_heads = value_row_block.reshape(
        key_count // sub_width, sub_width, KEYVALUE_HEADS, HEAD_SIZE
    )

    def one_step(sub_index, carried):
        key_start = sub_index * sub_width
        key_slice = lax.dynamic_index_in_dim(key_heads, sub_index, 0, keepdims=False)
        value_slice = lax.dynamic_index_in_dim(value_heads, sub_index, 0, keepdims=False)
        updated = []
        for (queries, query_pos), running in zip(prepared, carried):
            advance = partial(
                online_update,
                queries=queries,
                query_pos=query_pos,
                key_slice=key_slice,
                value_slice=value_slice,
                key_start=key_start,
            )
            updated.append(lax.cond(key_start <= jnp.max(query_pos), advance, unchanged, running))
        return tuple(updated)

    return lax.fori_loop(0, key_count // sub_width, one_step, carry_state)


def finish_block(result, count_rows):
    run_max, run_sum, run_acc = result
    divisor = jnp.where(run_sum > 0.0, run_sum, 1.0)
    return row_major(run_acc / divisor[..., None], count_rows).astype(jnp.bfloat16)


def spread_shards(
    normed_input, query_base, key_base, value_base, adapter_pool, stretch_adapter, adapter_owner
):
    cycle_size = lax.axis_size("ctx")
    my_index = lax.axis_index("ctx")
    tok_rows = normed_input.shape[0]
    token_positions = my_index * tok_rows + jnp.arange(tok_rows, dtype=jnp.int32)
    device_ids = jnp.arange(cycle_size, dtype=jnp.int32)
    stretch_of = device_ids * tok_rows // BLOCK_TOKENS
    stretch_ids = jnp.arange(stretch_adapter.shape[0], dtype=jnp.int32)
    adapter_of = jnp.sum(
        jnp.where(stretch_of[:, None] == stretch_ids[None, :], stretch_adapter[None, :], 0), axis=1
    )
    adapter_ids = jnp.arange(adapter_owner.shape[0], dtype=jnp.int32)
    slot_of = jnp.sum(
        jnp.where(adapter_of[:, None] == adapter_ids[None, :], adapter_owner[None, :], 0), axis=1
    )
    down_size = 3 * ADAPTER_RANK * D
    group_count = BLOCK_TOKENS // tok_rows
    levels = group_count.bit_length() - 1
    local_index = my_index % group_count
    col_width = D // group_count
    piece_len = down_size // (group_count * cycle_size)
    pool_rows = adapter_pool.shape[0]
    down_shaped = adapter_pool[:, :down_size].reshape(pool_rows, group_count, cycle_size, piece_len)
    spread_down = lax.all_to_all(down_shaped, "ctx", split_axis=2, concat_axis=0, tiled=True)
    flat_down = spread_down.reshape(-1, piece_len)
    wanted = jnp.take(flat_down, slot_of * group_count + device_ids % group_count, axis=0)[
        :, None, :
    ]
    down_slice = lax.all_to_all(wanted, "ctx", split_axis=0, concat_axis=1, tiled=True).reshape(
        col_width, 3 * ADAPTER_RANK
    )
    spread_rest = lax.all_to_all(
        adapter_pool[:, down_size:], "ctx", split_axis=1, concat_axis=0, tiled=True
    )
    rest_row = lax.all_to_all(
        jnp.take(spread_rest, slot_of, axis=0), "ctx", split_axis=0, concat_axis=1, tiled=True
    )[0]
    upper_part = rest_row[: QKV_POOL - down_size]
    out_part = rest_row[QKV_POOL - down_size :]
    pieces = normed_input.reshape(tok_rows, group_count, col_width)
    slice_order = jnp.bitwise_xor(local_index, jnp.arange(group_count, dtype=jnp.int32))
    moving = jnp.take(pieces, slice_order, axis=1).transpose(1, 0, 2)
    for level in range(levels):
        shaped = moving.reshape(group_count >> level + 1, 2, 1 << level, tok_rows, col_width)
        arrived = from_partner(shaped[:, 1], "ctx", level)
        moving = jnp.stack([shaped[:, 0], arrived], 1).reshape(group_count, tok_rows, col_width)
    partial_rows = jnp.dot(
        moving.reshape(group_count * tok_rows, col_width),
        down_slice,
        preferred_element_type=jnp.float32,
    ).reshape(group_count, tok_rows, 3 * ADAPTER_RANK)
    for level in reversed(range(levels)):
        halves = partial_rows.reshape(2, partial_rows.shape[0] // 2, tok_rows, 3 * ADAPTER_RANK)
        partial_rows = halves[0] + from_partner(
            halves[1].astype(jnp.bfloat16), "ctx", level
        ).astype(jnp.float32)
    narrow_product = partial_rows[0].astype(jnp.bfloat16)
    queries, new_keys, new_values = project_heads(
        narrow_product, query_base, key_base, value_base, upper_part, token_positions
    )
    group_size = QH // KEYVALUE_HEADS
    blocks = [(queries, token_positions)]
    prepared = [
        (head_major(block_q), jnp.tile(block_pos, group_size)) for block_q, block_pos in blocks
    ]
    initial = tuple(
        (
            (
                jnp.full((KEYVALUE_HEADS, head_q.shape[1]), mask_floor, jnp.float32),
                jnp.zeros((KEYVALUE_HEADS, head_q.shape[1]), jnp.float32),
                jnp.zeros((KEYVALUE_HEADS, head_q.shape[1], HEAD_SIZE), jnp.float32),
            )
            for head_q, block_pos in prepared
        )
    )
    finals = fold_keys(
        initial,
        (
            lax.all_gather(new_keys, "ctx", axis=0, tiled=True),
            lax.all_gather(new_values, "ctx", axis=0, tiled=True),
        ),
        prepared,
    )
    attended = finish_block(finals[0], tok_rows)
    out_delta = output_delta(attended, out_part)
    return (attended, out_delta)


PIECES = 8
GROUP = QH // KEYVALUE_HEADS
DOWN = ((0, 12288),)
REST = ((12288, 2048), (14336, 512), (14848, 2048), (16896, 4096))


def pack_kernel(sections, pool, *refs):
    out, buffers, sems = refs[-3:]
    plane = lax.axis_index("groups")
    slabs, slab_rows = out.shape[:2]

    def copies(slab):
        listed = []
        offset = 0
        for first, rows in sections:
            share = rows // (2 * PIECES)
            begin = first + (slab * 2 + plane) * share
            listed.append(
                pltpu.make_async_copy(
                    pool.at[:, pl.ds(pl.multiple_of(begin * 128, 2048), share * 128)],
                    buffers.at[slab, :, pl.ds(offset, share * 128)],
                    sems.at[slab, len(listed)],
                )
            )
            offset += share * 128
        return listed

    for slab in range(slabs):
        for copy in copies(slab):
            copy.start()

    def step(slab, carried):
        for copy in copies(slab):
            copy.wait()

        def chunk(index, inner):
            line = buffers[slab, :, pl.ds(pl.multiple_of(index * 2048, 2048), 2048)]
            block = line.astype(jnp.float32).reshape(16, 128).astype(jnp.bfloat16)
            out[slab, pl.ds(pl.multiple_of(index * 16, 16), 16), :] = block
            return inner

        lax.fori_loop(0, slab_rows // 16, chunk, 0, unroll=8)
        return carried

    lax.fori_loop(0, slabs, step, 0)


def pack_row(pool, sections, *after):
    slab_rows = sum(rows for _, rows in sections) // (2 * PIECES)
    return pl.pallas_call(
        partial(pack_kernel, sections),
        out_shape=jax.ShapeDtypeStruct((PIECES, slab_rows, 128), jnp.bfloat16),
        in_specs=[pl.BlockSpec(memory_space=pl.ANY)] * (1 + len(after)),
        out_specs=pl.BlockSpec(memory_space=pltpu.VMEM),
        scratch_shapes=[
            pltpu.VMEM((PIECES, 1, slab_rows * 128), jnp.bfloat16),
            pltpu.SemaphoreType.DMA((PIECES, len(sections))),
        ],
        compiler_params=pltpu.CompilerParams(vmem_limit_bytes=60 << 20),
        cost_estimate=pl.CostEstimate(flops=0, bytes_accessed=8 << 20, transcendentals=0),
    )(pool, *after)


def pick_kernel(mirrored, here, there, owner, spread, *refs):
    outs, sems = refs[:4], refs[4]
    half = lax.axis_index("ctx") // PIECES
    rows = spread.shape[1]
    copies = []
    for flip, out in enumerate(outs):
        wishes = there if flip >= 2 else here
        block = half ^ (flip & 1)
        row = lax.rem(owner[wishes[block]], PIECES)
        copies.append(
            pltpu.make_async_copy(spread.at[row], out.at[pl.ds(0, rows)], sems.at[flip, 0])
        )
        if mirrored is not None:
            first, count = mirrored
            row = lax.rem(owner[wishes[1 - block]], PIECES)
            copies.append(
                pltpu.make_async_copy(
                    spread.at[row, pl.ds(first, count)],
                    out.at[pl.ds(rows, count)],
                    sems.at[flip, 1],
                )
            )
    for copy in copies:
        copy.start()
    for copy in copies:
        copy.wait()


def pick(spread, here, there, owner, mirrored):
    rows = spread.shape[1] + (mirrored[1] if mirrored else 0)
    slab = jax.ShapeDtypeStruct((rows, 128), jnp.bfloat16)
    return pl.pallas_call(
        partial(pick_kernel, mirrored),
        out_shape=(slab,) * 4,
        in_specs=[pl.BlockSpec(memory_space=pltpu.SMEM)] * 3 + [pl.BlockSpec(memory_space=pl.ANY)],
        out_specs=(pl.BlockSpec(memory_space=pltpu.VMEM),) * 4,
        scratch_shapes=[pltpu.SemaphoreType.DMA((4, 2))],
        compiler_params=pltpu.CompilerParams(vmem_limit_bytes=16 << 20),
        cost_estimate=pl.CostEstimate(flops=0, bytes_accessed=2 << 20, transcendentals=0),
    )(here, there, owner, spread)


def assemble_kernel(*refs):
    pieces, out, sems = refs[:PIECES], refs[PIECES], refs[PIECES + 1]
    seat = lax.rem(lax.axis_index("ctx"), PIECES)
    copies = [
        pltpu.make_async_copy(piece, out.at[seat ^ apart], sems.at[apart])
        for apart, piece in enumerate(pieces)
    ]
    for copy in copies:
        copy.start()
    for copy in copies:
        copy.wait()


def assemble(pieces):
    return pl.pallas_call(
        assemble_kernel,
        out_shape=jax.ShapeDtypeStruct((PIECES,) + pieces[0].shape, jnp.bfloat16),
        in_specs=[pl.BlockSpec(memory_space=pltpu.VMEM)] * PIECES,
        out_specs=pl.BlockSpec(memory_space=pltpu.VMEM),
        scratch_shapes=[pltpu.SemaphoreType.DMA((PIECES,))],
        compiler_params=pltpu.CompilerParams(vmem_limit_bytes=16 << 20),
        cost_estimate=pl.CostEstimate(flops=0, bytes_accessed=6 << 20, transcendentals=0),
    )(*pieces)


def attend_kernel(
    query_block,
    key_base,
    value_base,
    own_rank,
    all_rank,
    query_up,
    key_up,
    value_up,
    cosines,
    sines,
    down_out,
    up_out,
    attended,
    out_delta,
    total,
    keys,
    values,
):
    step = pl.program_id(0)
    rows = query_block.shape[0]
    base = lax.axis_index("ctx") * rows
    dot = partial(jnp.dot, preferred_element_type=jnp.float32)

    def turned(delta, cosine, sine):
        return delta * cosine + pltpu.roll(delta, HEAD_SIZE // 2, 1) * sine

    half = lax.axis_index("ctx") * rows // BLOCK_TOKENS
    for apart in range(key_up.shape[0]):
        for seat in range(PIECES):
            first = ((half ^ apart) * PIECES + seat) * rows
            span = pl.ds(pl.multiple_of(first, rows), rows)
            delta = adapter_scale * dot(all_rank[span, :ADAPTER_RANK], key_up[apart])
            delta = turned(delta, cosines[span, :], sines[span, :])
            full = key_base[seat, apart].astype(jnp.float32) + delta
            keys[span, :] = full.astype(jnp.bfloat16)
            delta = adapter_scale * dot(all_rank[span, ADAPTER_RANK:], value_up[apart])
            full = value_base[seat, apart].astype(jnp.float32) + delta
            values[span, :] = full.astype(jnp.bfloat16)
    here = pl.ds(pl.multiple_of(base, rows), rows)
    cosine = cosines[here, :]
    sine = sines[here, :]
    delta = adapter_scale * dot(own_rank[:, :ADAPTER_RANK], query_up[...])
    added = jnp.zeros((rows, ADAPTER_RANK), jnp.float32)
    taken = GROUP // 2
    for first in range(0, GROUP, taken):
        queries = []
        for head in range(first, first + taken):
            span = slice(head * HEAD_SIZE, (head + 1) * HEAD_SIZE)
            moved = turned(delta[:, span], cosine, sine)
            queries.append(
                (query_block[:, span].astype(jnp.float32) + moved).astype(jnp.bfloat16)
            )
        queries = jnp.concatenate(queries, 0)
        scores = lax.dot_general(
            queries, keys[...], (((1,), (1,)), ((), ())), preferred_element_type=jnp.float32
        ) * HEAD_SIZE ** (-0.5)
        row = lax.broadcasted_iota(jnp.int32, scores.shape, 0)
        column = lax.broadcasted_iota(jnp.int32, scores.shape, 1)
        scores = jnp.where(column <= base + lax.rem(row, rows), scores, mask_floor)
        weights = jnp.exp(scores - jnp.max(scores, axis=-1, keepdims=True))
        divisor = jnp.sum(weights, axis=-1, keepdims=True)
        result = (dot(weights.astype(jnp.bfloat16), values[...]) / divisor).astype(jnp.bfloat16)
        for place, head in enumerate(range(first, first + taken)):
            span = slice(head * HEAD_SIZE, (head + 1) * HEAD_SIZE)
            part = result[place * rows : (place + 1) * rows]
            attended[:, span] = part
            added += dot(part, down_out[span, :])

    @pl.when(step == 0)
    def _():
        total[...] = jnp.zeros_like(total)

    total[...] += added

    @pl.when(step == pl.num_programs(0) - 1)
    def _():
        narrow = total[...].astype(jnp.bfloat16)
        out_delta[...] = (adapter_scale * dot(narrow, up_out[...])).astype(jnp.bfloat16)


def attend(
    query_base,
    base,
    own_rank,
    all_rank,
    query_up,
    keyval_up,
    cosines,
    sines,
    down_out,
    up_out,
):
    rows = query_base.shape[0]
    seq = base.shape[0] * base.shape[1] * rows
    blocks = keyval_up.shape[0]
    width = GROUP * HEAD_SIZE

    def whole(shape):
        return pl.BlockSpec(shape, lambda h: (0,) * len(shape))

    return pl.pallas_call(
        attend_kernel,
        grid=(KEYVALUE_HEADS,),
        out_shape=(
            jax.ShapeDtypeStruct((rows, QH * HEAD_SIZE), jnp.bfloat16),
            jax.ShapeDtypeStruct((rows, D), jnp.bfloat16),
        ),
        in_specs=[
            pl.BlockSpec((rows, width), lambda h: (0, h)),
            pl.BlockSpec((PIECES, 2, rows, HEAD_SIZE), lambda h: (0, 0, 0, h)),
            pl.BlockSpec((PIECES, 2, rows, HEAD_SIZE), lambda h: (0, 0, 0, h + KEYVALUE_HEADS)),
            whole(own_rank.shape),
            whole(all_rank.shape),
            pl.BlockSpec((ADAPTER_RANK, width), lambda h: (0, h)),
            pl.BlockSpec((blocks, ADAPTER_RANK, HEAD_SIZE), lambda h: (0, 0, h)),
            pl.BlockSpec((blocks, ADAPTER_RANK, HEAD_SIZE), lambda h: (0, 0, h + KEYVALUE_HEADS)),
            whole(cosines.shape),
            whole(sines.shape),
            pl.BlockSpec((width, ADAPTER_RANK), lambda h: (h, 0)),
            whole(up_out.shape),
        ],
        out_specs=(
            pl.BlockSpec((rows, width), lambda h: (0, h)),
            whole((rows, D)),
        ),
        scratch_shapes=[
            pltpu.VMEM((rows, ADAPTER_RANK), jnp.float32),
            pltpu.VMEM((seq, HEAD_SIZE), jnp.bfloat16),
            pltpu.VMEM((seq, HEAD_SIZE), jnp.bfloat16),
        ],
        compiler_params=pltpu.CompilerParams(vmem_limit_bytes=60 << 20),
        cost_estimate=pl.CostEstimate(
            flops=4 * rows * QH * seq * HEAD_SIZE,
            bytes_accessed=10 << 20,
            transcendentals=rows * QH * seq,
        ),
    )(
        query_base,
        base,
        base,
        own_rank,
        all_rank,
        query_up,
        keyval_up,
        keyval_up,
        cosines,
        sines,
        down_out,
        up_out,
    )


def swap(block, mask):
    return lax.ppermute(block, ("groups", "ctx"), [(i, i ^ mask) for i in range(4 * PIECES)])


def direct_shards(
    normed_input, query_base, key_base, value_base, adapter_pool, stretch_adapter, adapter_owner
):
    plane = lax.axis_index("groups")
    index = lax.axis_index("ctx")
    core = index % 2
    half = index // PIECES
    tok_rows = normed_input.shape[0]
    ctx = lax.axis_size("ctx")
    seq = ctx * tok_rows
    blocks = [list(range(PIECES)), list(range(PIECES, 2 * PIECES))]
    base = jnp.concatenate([key_base, value_base], 1)
    base = jnp.stack([base, swap(base, PIECES)])
    elsewhere = swap(stretch_adapter, 2 * PIECES)
    packed_rest = pack_row(adapter_pool, REST)
    packed_down = pack_row(adapter_pool, DOWN, packed_rest)
    ids = jnp.arange(adapter_owner.shape[0], dtype=jnp.int32)
    slots = jnp.sum(
        jnp.where(stretch_adapter[:, None] == ids[None, :], adapter_owner[None, :], 0), axis=1
    )
    near = (slots // PIECES) == half
    close = jnp.where(half == 0, near[0], near[1])
    far_close = jnp.where(half == 0, near[1], near[0])

    def settle(arrived, close):
        own = jnp.where(close, arrived[0], arrived[1])
        other = jnp.where(close, arrived[2], arrived[3])
        low = plane == 0
        return jnp.stack([jnp.where(low, own, other), jnp.where(low, other, own)])

    def exchange(sent):
        return [swap(block, flip * PIECES) if flip else block for flip, block in enumerate(sent)]

    def gather(block):
        parts = [swap(block, apart) if apart else block for apart in (0, 2, 4, 6)]
        return assemble([piece for part in parts for piece in (part, swap(part, 1))])

    spread_rest = lax.all_to_all(packed_rest, "ctx", 0, 0, axis_index_groups=blocks)
    sent_rest = pick(spread_rest, stretch_adapter, elsewhere, adapter_owner, (128, 32))
    sent_rest, packed_down = lax.optimization_barrier((sent_rest, packed_down))
    spread_down = lax.all_to_all(packed_down, "ctx", 0, 0, axis_index_groups=blocks)
    mine = jnp.arange(sent_rest[0].shape[0], dtype=jnp.int32)[:, None] < 544
    rest = settle(exchange(sent_rest), jnp.where(mine, close, far_close))

    rest, spread_down = lax.optimization_barrier((rest, spread_down))
    sent_down = pick(spread_down, stretch_adapter, elsewhere, adapter_owner, None)
    moving = normed_input.reshape(tok_rows, PIECES, D // PIECES).transpose(1, 0, 2)
    moving, rest, base, sent_down = lax.optimization_barrier((moving, rest, base, sent_down))
    moving = lax.all_to_all(moving, "ctx", 0, 0, axis_index_groups=blocks)
    down_slice = settle(exchange(sent_down), close).reshape(D // PIECES, 3 * ADAPTER_RANK)

    rest = gather(rest)
    query_up = rest[:, :, :128].reshape(ADAPTER_RANK, QH * HEAD_SIZE)
    keyval_up = jnp.stack([rest[:, :, 128:160], rest[:, :, 544:]])
    keyval_up = keyval_up.reshape(2, ADAPTER_RANK, 2 * KEYVALUE_HEADS * HEAD_SIZE)
    down_out = rest[:, :, 160:288].reshape(QH * HEAD_SIZE, ADAPTER_RANK)
    up_out = rest[:, :, 288:544].reshape(ADAPTER_RANK, D)
    base = gather(base)

    partial_rows = jnp.dot(
        moving.reshape(BLOCK_TOKENS, D // PIECES), down_slice, preferred_element_type=jnp.float32
    ).astype(jnp.bfloat16)
    partial_rows = lax.all_to_all(
        partial_rows.reshape(PIECES, tok_rows, 3 * ADAPTER_RANK),
        "ctx",
        0,
        0,
        axis_index_groups=blocks,
    )
    own_rank = jnp.sum(partial_rows.astype(jnp.float32), axis=0).astype(jnp.bfloat16)
    all_rank = jnp.broadcast_to(own_rank[None, :, ADAPTER_RANK:], (ctx, tok_rows, 2 * ADAPTER_RANK))
    all_rank = lax.all_to_all(all_rank, "ctx", 0, 0).reshape(seq, 2 * ADAPTER_RANK)

    half_dim = HEAD_SIZE // 2
    frequency = rope_base ** (-(jnp.arange(half_dim, dtype=jnp.float32) * 2.0) / HEAD_SIZE)
    angle = jnp.arange(seq, dtype=jnp.int32).astype(jnp.float32)[:, None] * frequency[None, :]
    cosine = jnp.cos(angle)
    sine = jnp.sin(angle)
    cosines = jnp.concatenate([cosine, cosine], 1)
    sines = jnp.concatenate([-sine, sine], 1)
    return attend(
        query_base,
        base,
        own_rank,
        all_rank,
        query_up,
        keyval_up,
        cosines,
        sines,
        down_out,
        up_out,
    )


def shards(normed_input, query_base, key_base, value_base, adapter_pool, stretch_adapter, owner):
    fits = (
        lax.axis_size("groups") == 2
        and lax.axis_size("ctx") == 2 * PIECES
        and normed_input.shape[0] * PIECES == BLOCK_TOKENS
        and adapter_pool.shape[0] == 1
    )
    plan = direct_shards if fits else spread_shards
    return plan(
        normed_input, query_base, key_base, value_base, adapter_pool, stretch_adapter, owner
    )


def solution(mesh):
    placed = (
        P(("groups", "ctx"), None),
        P(("groups", "ctx"), None),
        P(("groups", "ctx"), None),
        P(("groups", "ctx"), None),
        P("ctx", None),
        P("groups"),
        P(),
    )
    return jax.shard_map(
        shards,
        mesh=mesh,
        in_specs=placed,
        out_specs=(P(("groups", "ctx"), None), P(("groups", "ctx"), None)),
        check_vma=False,
    )
```

```python
from functools import partial
import math

import jax
import jax.numpy as jnp
from jax import lax
from jax.experimental import pallas as pl
from jax.experimental.pallas import tpu as pltpu
from jax.sharding import PartitionSpec as P

D = 8192
QH = 32
KEYVALUE_HEADS = 4
HEAD_SIZE = 128
ADAPTER_RANK = 64
BLOCK_TOKENS = 512
QKV_POOL = 1900544


adapter_scale = 2.0
rope_base = 500000.0
mask_floor = -1e30


def from_partner(block, axis, apart):
    count = lax.axis_size(axis)
    route = []
    for low in range(count):
        high = low | 1 << apart
        if high != low and high < count:
            route += [(low, high), (high, low)]
    return lax.ppermute(block, axis, route)


def rotate(delta, token_positions, heads):
    half_dim = HEAD_SIZE // 2
    frequency = rope_base ** (-(jnp.arange(half_dim, dtype=jnp.float32) * 2.0) / HEAD_SIZE)
    angle = token_positions.astype(jnp.float32)[:, None] * frequency[None, :]
    cosine = jnp.cos(angle)[:, None, :]
    sine_part = jnp.sin(angle)[:, None, :]
    shaped = delta.reshape(delta.shape[0], heads, HEAD_SIZE)
    first_half = shaped[..., :half_dim]
    second_half = shaped[..., half_dim:]
    joined = jnp.concatenate(
        [
            first_half * cosine - second_half * sine_part,
            second_half * cosine + first_half * sine_part,
        ],
        -1,
    )
    return joined.reshape(delta.shape[0], heads * HEAD_SIZE)


def project_heads(
    narrow_product, query_row_block, key_row_block, value_row_block, upper_part, token_positions
):
    query_up_weight = upper_part[: ADAPTER_RANK * QH * HEAD_SIZE].reshape(
        ADAPTER_RANK, QH * HEAD_SIZE
    )
    keyvalue_up_weight = upper_part[ADAPTER_RANK * QH * HEAD_SIZE :].reshape(
        ADAPTER_RANK, 2 * KEYVALUE_HEADS * HEAD_SIZE
    )
    query_correction = adapter_scale * jnp.dot(
        narrow_product[:, :ADAPTER_RANK], query_up_weight, preferred_element_type=jnp.float32
    )
    key_correction = adapter_scale * jnp.dot(
        narrow_product[:, ADAPTER_RANK : 2 * ADAPTER_RANK],
        keyvalue_up_weight[:, : KEYVALUE_HEADS * HEAD_SIZE],
        preferred_element_type=jnp.float32,
    )
    value_correction = adapter_scale * jnp.dot(
        narrow_product[:, 2 * ADAPTER_RANK :],
        keyvalue_up_weight[:, KEYVALUE_HEADS * HEAD_SIZE :],
        preferred_element_type=jnp.float32,
    )
    queries = (
        query_row_block.astype(jnp.float32) + rotate(query_correction, token_positions, QH)
    ).astype(jnp.bfloat16)
    new_keys = (
        key_row_block.astype(jnp.float32) + rotate(key_correction, token_positions, KEYVALUE_HEADS)
    ).astype(jnp.bfloat16)
    new_values = (value_row_block.astype(jnp.float32) + value_correction).astype(jnp.bfloat16)
    return (queries, new_keys, new_values)


def output_delta(attended_rows, out_part):
    down_out = out_part[: QH * HEAD_SIZE * ADAPTER_RANK].reshape(QH * HEAD_SIZE, ADAPTER_RANK)
    raised_output = out_part[QH * HEAD_SIZE * ADAPTER_RANK :].reshape(ADAPTER_RANK, D)
    narrow_product = jnp.dot(attended_rows, down_out, preferred_element_type=jnp.float32).astype(
        jnp.bfloat16
    )
    return (
        adapter_scale * jnp.dot(narrow_product, raised_output, preferred_element_type=jnp.float32)
    ).astype(jnp.bfloat16)


def head_major(query_row_block):
    count_rows = query_row_block.shape[0]
    group_size = QH // KEYVALUE_HEADS
    return (
        query_row_block.reshape(count_rows, KEYVALUE_HEADS, group_size, HEAD_SIZE)
        .transpose(1, 2, 0, 3)
        .reshape(KEYVALUE_HEADS, group_size * count_rows, HEAD_SIZE)
    )


def row_major(head_rows, count_rows):
    group_size = QH // KEYVALUE_HEADS
    return (
        head_rows.reshape(KEYVALUE_HEADS, group_size, count_rows, HEAD_SIZE)
        .transpose(2, 0, 1, 3)
        .reshape(count_rows, QH * HEAD_SIZE)
    )


def online_update(current, queries, query_pos, key_slice, value_slice, key_start):
    run_max, run_sum, run_acc = current
    scores = jnp.einsum(
        "hqd,khd->hqk", queries, key_slice, preferred_element_type=jnp.float32
    ) * HEAD_SIZE ** (-0.5)
    key_pos = key_start + jnp.arange(key_slice.shape[0], dtype=jnp.int32)
    allowed = (query_pos[:, None] >= key_pos[None, :])[None]
    new_max = jnp.maximum(run_max, jnp.max(jnp.where(allowed, scores, mask_floor), axis=-1))
    weights = jnp.where(allowed, jnp.exp(scores - new_max[..., None]), 0.0)
    rescale = jnp.exp(run_max - new_max)
    new_sum = run_sum * rescale + jnp.sum(weights, axis=-1)
    new_acc = run_acc * rescale[..., None] + jnp.einsum(
        "hqk,khd->hqd",
        weights.astype(jnp.bfloat16),
        value_slice,
        preferred_element_type=jnp.float32,
    )
    return (new_max, new_sum, new_acc)


def unchanged(current):
    return current


def fold_keys(carry_state, shard_part, prepared):
    key_row_block, value_row_block = shard_part
    key_count = key_row_block.shape[0]
    sub_width = math.gcd(key_count, 1024)
    key_heads = key_row_block.reshape(key_count // sub_width, sub_width, KEYVALUE_HEADS, HEAD_SIZE)
    value_heads = value_row_block.reshape(
        key_count // sub_width, sub_width, KEYVALUE_HEADS, HEAD_SIZE
    )

    def one_step(sub_index, carried):
        key_start = sub_index * sub_width
        key_slice = lax.dynamic_index_in_dim(key_heads, sub_index, 0, keepdims=False)
        value_slice = lax.dynamic_index_in_dim(value_heads, sub_index, 0, keepdims=False)
        updated = []
        for (queries, query_pos), running in zip(prepared, carried):
            advance = partial(
                online_update,
                queries=queries,
                query_pos=query_pos,
                key_slice=key_slice,
                value_slice=value_slice,
                key_start=key_start,
            )
            updated.append(lax.cond(key_start <= jnp.max(query_pos), advance, unchanged, running))
        return tuple(updated)

    return lax.fori_loop(0, key_count // sub_width, one_step, carry_state)


def finish_block(result, count_rows):
    run_max, run_sum, run_acc = result
    divisor = jnp.where(run_sum > 0.0, run_sum, 1.0)
    return row_major(run_acc / divisor[..., None], count_rows).astype(jnp.bfloat16)


def spread_shards(
    normed_input, query_base, key_base, value_base, adapter_pool, stretch_adapter, adapter_owner
):
    cycle_size = lax.axis_size("ctx")
    my_index = lax.axis_index("ctx")
    tok_rows = normed_input.shape[0]
    token_positions = my_index * tok_rows + jnp.arange(tok_rows, dtype=jnp.int32)
    device_ids = jnp.arange(cycle_size, dtype=jnp.int32)
    stretch_of = device_ids * tok_rows // BLOCK_TOKENS
    stretch_ids = jnp.arange(stretch_adapter.shape[0], dtype=jnp.int32)
    adapter_of = jnp.sum(
        jnp.where(stretch_of[:, None] == stretch_ids[None, :], stretch_adapter[None, :], 0), axis=1
    )
    adapter_ids = jnp.arange(adapter_owner.shape[0], dtype=jnp.int32)
    slot_of = jnp.sum(
        jnp.where(adapter_of[:, None] == adapter_ids[None, :], adapter_owner[None, :], 0), axis=1
    )
    down_size = 3 * ADAPTER_RANK * D
    group_count = BLOCK_TOKENS // tok_rows
    levels = group_count.bit_length() - 1
    local_index = my_index % group_count
    col_width = D // group_count
    piece_len = down_size // (group_count * cycle_size)
    pool_rows = adapter_pool.shape[0]
    down_shaped = adapter_pool[:, :down_size].reshape(pool_rows, group_count, cycle_size, piece_len)
    spread_down = lax.all_to_all(down_shaped, "ctx", split_axis=2, concat_axis=0, tiled=True)
    flat_down = spread_down.reshape(-1, piece_len)
    wanted = jnp.take(flat_down, slot_of * group_count + device_ids % group_count, axis=0)[
        :, None, :
    ]
    down_slice = lax.all_to_all(wanted, "ctx", split_axis=0, concat_axis=1, tiled=True).reshape(
        col_width, 3 * ADAPTER_RANK
    )
    spread_rest = lax.all_to_all(
        adapter_pool[:, down_size:], "ctx", split_axis=1, concat_axis=0, tiled=True
    )
    rest_row = lax.all_to_all(
        jnp.take(spread_rest, slot_of, axis=0), "ctx", split_axis=0, concat_axis=1, tiled=True
    )[0]
    upper_part = rest_row[: QKV_POOL - down_size]
    out_part = rest_row[QKV_POOL - down_size :]
    pieces = normed_input.reshape(tok_rows, group_count, col_width)
    slice_order = jnp.bitwise_xor(local_index, jnp.arange(group_count, dtype=jnp.int32))
    moving = jnp.take(pieces, slice_order, axis=1).transpose(1, 0, 2)
    for level in range(levels):
        shaped = moving.reshape(group_count >> level + 1, 2, 1 << level, tok_rows, col_width)
        arrived = from_partner(shaped[:, 1], "ctx", level)
        moving = jnp.stack([shaped[:, 0], arrived], 1).reshape(group_count, tok_rows, col_width)
    partial_rows = jnp.dot(
        moving.reshape(group_count * tok_rows, col_width),
        down_slice,
        preferred_element_type=jnp.float32,
    ).reshape(group_count, tok_rows, 3 * ADAPTER_RANK)
    for level in reversed(range(levels)):
        halves = partial_rows.reshape(2, partial_rows.shape[0] // 2, tok_rows, 3 * ADAPTER_RANK)
        partial_rows = halves[0] + from_partner(
            halves[1].astype(jnp.bfloat16), "ctx", level
        ).astype(jnp.float32)
    narrow_product = partial_rows[0].astype(jnp.bfloat16)
    queries, new_keys, new_values = project_heads(
        narrow_product, query_base, key_base, value_base, upper_part, token_positions
    )
    group_size = QH // KEYVALUE_HEADS
    blocks = [(queries, token_positions)]
    prepared = [
        (head_major(block_q), jnp.tile(block_pos, group_size)) for block_q, block_pos in blocks
    ]
    initial = tuple(
        (
            (
                jnp.full((KEYVALUE_HEADS, head_q.shape[1]), mask_floor, jnp.float32),
                jnp.zeros((KEYVALUE_HEADS, head_q.shape[1]), jnp.float32),
                jnp.zeros((KEYVALUE_HEADS, head_q.shape[1], HEAD_SIZE), jnp.float32),
            )
            for head_q, block_pos in prepared
        )
    )
    finals = fold_keys(
        initial,
        (
            lax.all_gather(new_keys, "ctx", axis=0, tiled=True),
            lax.all_gather(new_values, "ctx", axis=0, tiled=True),
        ),
        prepared,
    )
    attended = finish_block(finals[0], tok_rows)
    out_delta = output_delta(attended, out_part)
    return (attended, out_delta)


PIECES = 8
GROUP = QH // KEYVALUE_HEADS
DOWN = ((0, 12288),)
REST = ((12288, 2048), (14336, 512), (14848, 2048), (16896, 4096))


def pack_kernel(sections, pool, *refs):
    out, buffers, sems = refs[-3:]
    plane = lax.axis_index("groups")
    slabs, slab_rows = out.shape[:2]

    def copies(slab):
        listed = []
        offset = 0
        for first, rows in sections:
            share = rows // (2 * PIECES)
            begin = first + (slab * 2 + plane) * share
            listed.append(
                pltpu.make_async_copy(
                    pool.at[:, pl.ds(pl.multiple_of(begin * 128, 2048), share * 128)],
                    buffers.at[slab, :, pl.ds(offset, share * 128)],
                    sems.at[slab, len(listed)],
                )
            )
            offset += share * 128
        return listed

    for slab in range(slabs):
        for copy in copies(slab):
            copy.start()

    def step(slab, carried):
        for copy in copies(slab):
            copy.wait()

        def chunk(index, inner):
            line = buffers[slab, :, pl.ds(pl.multiple_of(index * 2048, 2048), 2048)]
            block = line.astype(jnp.float32).reshape(16, 128).astype(jnp.bfloat16)
            out[slab, pl.ds(pl.multiple_of(index * 16, 16), 16), :] = block
            return inner

        lax.fori_loop(0, slab_rows // 16, chunk, 0, unroll=8)
        return carried

    lax.fori_loop(0, slabs, step, 0)


def pack_row(pool, sections, *after):
    slab_rows = sum(rows for _, rows in sections) // (2 * PIECES)
    return pl.pallas_call(
        partial(pack_kernel, sections),
        out_shape=jax.ShapeDtypeStruct((PIECES, slab_rows, 128), jnp.bfloat16),
        in_specs=[pl.BlockSpec(memory_space=pl.ANY)] * (1 + len(after)),
        out_specs=pl.BlockSpec(memory_space=pltpu.VMEM),
        scratch_shapes=[
            pltpu.VMEM((PIECES, 1, slab_rows * 128), jnp.bfloat16),
            pltpu.SemaphoreType.DMA((PIECES, len(sections))),
        ],
        compiler_params=pltpu.CompilerParams(vmem_limit_bytes=60 << 20),
        cost_estimate=pl.CostEstimate(flops=0, bytes_accessed=8 << 20, transcendentals=0),
    )(pool, *after)


def pick_kernel(mirrored, here, there, owner, spread, *refs):
    outs, sems = refs[:4], refs[4]
    half = lax.axis_index("ctx") // PIECES
    rows = spread.shape[1]
    copies = []
    for flip, out in enumerate(outs):
        wishes = there if flip >= 2 else here
        block = half ^ (flip & 1)
        row = lax.rem(owner[wishes[block]], PIECES)
        copies.append(
            pltpu.make_async_copy(spread.at[row], out.at[pl.ds(0, rows)], sems.at[flip, 0])
        )
        if mirrored is not None:
            first, count = mirrored
            row = lax.rem(owner[wishes[1 - block]], PIECES)
            copies.append(
                pltpu.make_async_copy(
                    spread.at[row, pl.ds(first, count)],
                    out.at[pl.ds(rows, count)],
                    sems.at[flip, 1],
                )
            )
    for copy in copies:
        copy.start()
    for copy in copies:
        copy.wait()


def pick(spread, here, there, owner, mirrored):
    rows = spread.shape[1] + (mirrored[1] if mirrored else 0)
    slab = jax.ShapeDtypeStruct((rows, 128), jnp.bfloat16)
    return pl.pallas_call(
        partial(pick_kernel, mirrored),
        out_shape=(slab,) * 4,
        in_specs=[pl.BlockSpec(memory_space=pltpu.SMEM)] * 3 + [pl.BlockSpec(memory_space=pl.ANY)],
        out_specs=(pl.BlockSpec(memory_space=pltpu.VMEM),) * 4,
        scratch_shapes=[pltpu.SemaphoreType.DMA((4, 2))],
        compiler_params=pltpu.CompilerParams(vmem_limit_bytes=16 << 20),
        cost_estimate=pl.CostEstimate(flops=0, bytes_accessed=2 << 20, transcendentals=0),
    )(here, there, owner, spread)


def deal_kernel(rows, even, odd, sems):
    seat = lax.rem(lax.axis_index("ctx"), PIECES)
    width = rows.shape[1] // PIECES
    copies = []
    for apart in range(PIECES):
        first = pl.multiple_of((seat ^ apart) * width, width)
        target = (odd if apart % 2 else even).at[apart // 2]
        copies.append(
            pltpu.make_async_copy(rows.at[:, pl.ds(first, width)], target, sems.at[apart])
        )
    for copy in copies:
        copy.start()
    for copy in copies:
        copy.wait()


def deal(rows, *after):
    slab = jax.ShapeDtypeStruct((PIECES // 2, rows.shape[0], rows.shape[1] // PIECES), rows.dtype)

    def kernel(rows, *refs):
        deal_kernel(rows, *refs[-3:])

    return pl.pallas_call(
        kernel,
        out_shape=(slab, slab),
        in_specs=[pl.BlockSpec(memory_space=pl.ANY)] * (1 + len(after)),
        out_specs=(pl.BlockSpec(memory_space=pltpu.VMEM),) * 2,
        scratch_shapes=[pltpu.SemaphoreType.DMA((PIECES,))],
        compiler_params=pltpu.CompilerParams(vmem_limit_bytes=16 << 20),
        cost_estimate=pl.CostEstimate(flops=0, bytes_accessed=2 << 20, transcendentals=0),
    )(rows, *after)


def narrow_kernel(here, owner, own, mirror, across, both, *refs):
    dealt, outs, (flat, left, right) = refs[:4], refs[4:8], refs[8:]
    plane = lax.axis_index("groups")
    half = lax.axis_index("ctx") // PIECES
    close = owner[here[half]] // PIECES == half
    count = own.shape[0]

    def place(block, position):
        flat[pl.ds(pl.multiple_of(position * count, count), count), :] = block[...].astype(
            jnp.float32
        )

    @pl.when(close)
    def _():
        place(own, plane)
        place(across, 1 - plane)

    @pl.when(jnp.logical_not(close))
    def _():
        place(mirror, plane)
        place(both, 1 - plane)

    third = flat.shape[0] // 3
    one = flat[pl.ds(0, third, stride=3), :]
    two = flat[pl.ds(1, third, stride=3), :]
    three = flat[pl.ds(2, third, stride=3), :]
    lane = lax.broadcasted_iota(jnp.int32, one.shape, 1)
    two = pltpu.roll(two, 64, 1)
    three = pltpu.roll(three, 64, 1)
    left[pl.ds(0, third, stride=2), :] = one
    left[pl.ds(1, third, stride=2), :] = jnp.where(lane < 64, two, three)
    right[pl.ds(0, third, stride=2), :] = pltpu.roll(two, 64, 1)
    right[pl.ds(1, third, stride=2), :] = three
    weight = jnp.concatenate([left[...], right[...]], 1).astype(jnp.bfloat16)
    for block, out in zip(dealt, outs):
        sides, rows, depth = block.shape
        product = jnp.dot(
            block[...].reshape(sides * rows, depth), weight, preferred_element_type=jnp.float32
        )
        out[...] = product[:, : 3 * ADAPTER_RANK].reshape(out.shape).astype(jnp.bfloat16)


def narrow(here, owner, arrived, dealt):
    sides, rows, depth = dealt[0].shape
    partial_sums = jax.ShapeDtypeStruct((sides, rows, 3 * ADAPTER_RANK), jnp.bfloat16)
    return pl.pallas_call(
        narrow_kernel,
        out_shape=(partial_sums,) * 4,
        in_specs=[pl.BlockSpec(memory_space=pltpu.SMEM)] * 2
        + [pl.BlockSpec(memory_space=pltpu.VMEM)] * 8,
        out_specs=(pl.BlockSpec(memory_space=pltpu.VMEM),) * 4,
        scratch_shapes=[
            pltpu.VMEM((depth * 3 * ADAPTER_RANK // 128, 128), jnp.float32),
            pltpu.VMEM((depth, 128), jnp.float32),
            pltpu.VMEM((depth, 128), jnp.float32),
        ],
        compiler_params=pltpu.CompilerParams(vmem_limit_bytes=16 << 20),
        cost_estimate=pl.CostEstimate(
            flops=2 * 8 * rows * depth * 256, bytes_accessed=3 << 20, transcendentals=0
        ),
    )(here, owner, *arrived, *dealt)


def assemble_kernel(*refs):
    pieces, out, sems = refs[:PIECES], refs[PIECES], refs[PIECES + 1]
    seat = lax.rem(lax.axis_index("ctx"), PIECES)
    copies = [
        pltpu.make_async_copy(piece, out.at[seat ^ apart], sems.at[apart])
        for apart, piece in enumerate(pieces)
    ]
    for copy in copies:
        copy.start()
    for copy in copies:
        copy.wait()


def assemble(pieces):
    return pl.pallas_call(
        assemble_kernel,
        out_shape=jax.ShapeDtypeStruct((PIECES,) + pieces[0].shape, jnp.bfloat16),
        in_specs=[pl.BlockSpec(memory_space=pltpu.VMEM)] * PIECES,
        out_specs=pl.BlockSpec(memory_space=pltpu.VMEM),
        scratch_shapes=[pltpu.SemaphoreType.DMA((PIECES,))],
        compiler_params=pltpu.CompilerParams(vmem_limit_bytes=16 << 20),
        cost_estimate=pl.CostEstimate(flops=0, bytes_accessed=6 << 20, transcendentals=0),
    )(*pieces)


def attend_kernel(
    query_block,
    key_base,
    value_base,
    own_rank,
    all_rank,
    query_up,
    key_up,
    value_up,
    cosines,
    sines,
    down_out,
    up_out,
    attended,
    out_delta,
    total,
    keys,
    values,
):
    step = pl.program_id(0)
    rows = query_block.shape[0]
    base = lax.axis_index("ctx") * rows
    dot = partial(jnp.dot, preferred_element_type=jnp.float32)

    def turned(delta, cosine, sine):
        return delta * cosine + pltpu.roll(delta, HEAD_SIZE // 2, 1) * sine

    half = lax.axis_index("ctx") * rows // BLOCK_TOKENS
    seat = lax.rem(lax.axis_index("ctx"), PIECES)
    for side in range(key_up.shape[0]):
        for apart in range(PIECES):
            there = seat ^ apart
            first = ((half ^ side) * PIECES + there) * rows
            span = pl.ds(pl.multiple_of(first, rows), rows)
            rank = all_rank[apart % 2, apart // 2, side]
            delta = adapter_scale * dot(rank[:, :ADAPTER_RANK], key_up[side])
            delta = turned(delta, cosines[span, :], sines[span, :])
            full = key_base[there, side].astype(jnp.float32) + delta
            keys[span, :] = full.astype(jnp.bfloat16)
            delta = adapter_scale * dot(rank[:, ADAPTER_RANK:], value_up[side])
            full = value_base[there, side].astype(jnp.float32) + delta
            values[span, :] = full.astype(jnp.bfloat16)
    here = pl.ds(pl.multiple_of(base, rows), rows)
    cosine = cosines[here, :]
    sine = sines[here, :]
    delta = adapter_scale * dot(own_rank[:, :ADAPTER_RANK], query_up[...])
    added = jnp.zeros((rows, ADAPTER_RANK), jnp.float32)
    taken = GROUP // 2
    for first in range(0, GROUP, taken):
        queries = []
        for head in range(first, first + taken):
            span = slice(head * HEAD_SIZE, (head + 1) * HEAD_SIZE)
            moved = turned(delta[:, span], cosine, sine)
            queries.append(
                (query_block[:, span].astype(jnp.float32) + moved).astype(jnp.bfloat16)
            )
        queries = jnp.concatenate(queries, 0)
        scores = lax.dot_general(
            queries, keys[...], (((1,), (1,)), ((), ())), preferred_element_type=jnp.float32
        ) * HEAD_SIZE ** (-0.5)
        row = lax.broadcasted_iota(jnp.int32, scores.shape, 0)
        column = lax.broadcasted_iota(jnp.int32, scores.shape, 1)
        scores = jnp.where(column <= base + lax.rem(row, rows), scores, mask_floor)
        weights = jnp.exp(scores - jnp.max(scores, axis=-1, keepdims=True))
        divisor = jnp.sum(weights, axis=-1, keepdims=True)
        result = (dot(weights.astype(jnp.bfloat16), values[...]) / divisor).astype(jnp.bfloat16)
        for place, head in enumerate(range(first, first + taken)):
            span = slice(head * HEAD_SIZE, (head + 1) * HEAD_SIZE)
            part = result[place * rows : (place + 1) * rows]
            attended[:, span] = part
            added += dot(part, down_out[span, :])

    @pl.when(step == 0)
    def _():
        total[...] = jnp.zeros_like(total)

    total[...] += added

    @pl.when(step == pl.num_programs(0) - 1)
    def _():
        narrow = total[...].astype(jnp.bfloat16)
        out_delta[...] = (adapter_scale * dot(narrow, up_out[...])).astype(jnp.bfloat16)


def attend(
    query_base,
    base,
    own_rank,
    all_rank,
    query_up,
    keyval_up,
    cosines,
    sines,
    down_out,
    up_out,
):
    rows = query_base.shape[0]
    seq = base.shape[0] * base.shape[1] * rows
    blocks = keyval_up.shape[0]
    width = GROUP * HEAD_SIZE

    def whole(shape):
        return pl.BlockSpec(shape, lambda h: (0,) * len(shape))

    return pl.pallas_call(
        attend_kernel,
        grid=(KEYVALUE_HEADS,),
        out_shape=(
            jax.ShapeDtypeStruct((rows, QH * HEAD_SIZE), jnp.bfloat16),
            jax.ShapeDtypeStruct((rows, D), jnp.bfloat16),
        ),
        in_specs=[
            pl.BlockSpec((rows, width), lambda h: (0, h)),
            pl.BlockSpec((PIECES, 2, rows, HEAD_SIZE), lambda h: (0, 0, 0, h)),
            pl.BlockSpec((PIECES, 2, rows, HEAD_SIZE), lambda h: (0, 0, 0, h + KEYVALUE_HEADS)),
            whole(own_rank.shape),
            whole(all_rank.shape),
            pl.BlockSpec((ADAPTER_RANK, width), lambda h: (0, h)),
            pl.BlockSpec((blocks, ADAPTER_RANK, HEAD_SIZE), lambda h: (0, 0, h)),
            pl.BlockSpec((blocks, ADAPTER_RANK, HEAD_SIZE), lambda h: (0, 0, h + KEYVALUE_HEADS)),
            whole(cosines.shape),
            whole(sines.shape),
            pl.BlockSpec((width, ADAPTER_RANK), lambda h: (h, 0)),
            whole(up_out.shape),
        ],
        out_specs=(
            pl.BlockSpec((rows, width), lambda h: (0, h)),
            whole((rows, D)),
        ),
        scratch_shapes=[
            pltpu.VMEM((rows, ADAPTER_RANK), jnp.float32),
            pltpu.VMEM((seq, HEAD_SIZE), jnp.bfloat16),
            pltpu.VMEM((seq, HEAD_SIZE), jnp.bfloat16),
        ],
        compiler_params=pltpu.CompilerParams(vmem_limit_bytes=60 << 20),
        cost_estimate=pl.CostEstimate(
            flops=4 * rows * QH * seq * HEAD_SIZE,
            bytes_accessed=10 << 20,
            transcendentals=rows * QH * seq,
        ),
    )(
        query_base,
        base,
        base,
        own_rank,
        all_rank,
        query_up,
        keyval_up,
        keyval_up,
        cosines,
        sines,
        down_out,
        up_out,
    )


def swap(block, mask):
    return lax.ppermute(block, ("groups", "ctx"), [(i, i ^ mask) for i in range(4 * PIECES)])


def direct_shards(
    normed_input, query_base, key_base, value_base, adapter_pool, stretch_adapter, adapter_owner
):
    plane = lax.axis_index("groups")
    index = lax.axis_index("ctx")
    half = index // PIECES
    tok_rows = normed_input.shape[0]
    ctx = lax.axis_size("ctx")
    seq = ctx * tok_rows
    blocks = [list(range(PIECES)), list(range(PIECES, 2 * PIECES))]
    def after(block, *others):
        return lax.optimization_barrier((block, others))[0]

    elsewhere = swap(stretch_adapter, 2 * PIECES)
    packed_rest = pack_row(adapter_pool, REST)
    packed_down = pack_row(adapter_pool, DOWN, packed_rest)
    even, odd = deal(normed_input, packed_rest)
    sibling = swap(odd, 1)
    base = jnp.concatenate([key_base, value_base], 1)
    base = jnp.stack([base, swap(base, PIECES)])
    slots = jnp.sum(
        jnp.where(
            stretch_adapter[:, None] == jnp.arange(adapter_owner.shape[0], dtype=jnp.int32)[None, :],
            adapter_owner[None, :],
            0,
        ),
        axis=1,
    )
    near = (slots // PIECES) == half
    close = jnp.where(half == 0, near[0], near[1])
    far_close = jnp.where(half == 0, near[1], near[0])

    def exchange(sent):
        return [swap(block, flip * PIECES) if flip else block for flip, block in enumerate(sent)]

    def gather(block):
        four = swap(block, 4)
        return [block, swap(block, 2), four, swap(four, 2)]

    def complete(parts, *others):
        parts = [after(part, *others) for part in parts]
        return assemble([piece for part in parts for piece in (part, swap(part, 1))])

    spread_rest = lax.all_to_all(packed_rest, "ctx", 0, 0, axis_index_groups=blocks)
    sent_rest = pick(spread_rest, stretch_adapter, elsewhere, adapter_owner, (128, 32))
    packed_down = after(packed_down, sent_rest, sibling, base)
    spread_down = lax.all_to_all(packed_down, "ctx", 0, 0, axis_index_groups=blocks)
    arrived = exchange(sent_rest)
    mine = jnp.arange(arrived[0].shape[0], dtype=jnp.int32)[:, None] < 544
    wide_close = jnp.where(mine, close, far_close)
    own = jnp.where(wide_close, arrived[0], arrived[1])
    other = jnp.where(wide_close, arrived[2], arrived[3])
    rest = jnp.stack([jnp.where(plane == 0, own, other), jnp.where(plane == 0, other, own)])

    spread_down = after(spread_down, rest)
    sent_down = pick(spread_down, stretch_adapter, elsewhere, adapter_owner, None)
    arrived = exchange(sent_down)
    dealt = [jnp.stack([even[j], sibling[j]]) for j in range(PIECES // 2)]
    dealt = [swap(after(block, arrived[2]), 2 * j) if j else block for j, block in enumerate(dealt)]
    rest = gather(after(rest, arrived[2]))
    partial_sums = narrow(stretch_adapter, adapter_owner, arrived, dealt)
    base = gather(after(base, *partial_sums))

    back = [swap(block, 2 * j) if j else block for j, block in enumerate(partial_sums)]
    back = sum(block.astype(jnp.float32) for block in back)
    own_rank = back[0] + swap(back[1].astype(jnp.bfloat16), 1).astype(jnp.float32)
    own_rank = own_rank.astype(jnp.bfloat16)
    all_rank = own_rank[:, ADAPTER_RANK:]
    all_rank = jnp.stack([all_rank, swap(all_rank, PIECES)])
    all_rank = jnp.stack([swap(all_rank, apart) if apart else all_rank for apart in (0, 2, 4, 6)])
    all_rank = jnp.stack([all_rank, swap(all_rank, 1)])

    rest = complete(rest, *partial_sums)
    query_up = rest[:, :, :128].reshape(ADAPTER_RANK, QH * HEAD_SIZE)
    keyval_up = jnp.stack([rest[:, :, 128:160], rest[:, :, 544:]])
    keyval_up = keyval_up.reshape(2, ADAPTER_RANK, 2 * KEYVALUE_HEADS * HEAD_SIZE)
    down_out = rest[:, :, 160:288].reshape(QH * HEAD_SIZE, ADAPTER_RANK)
    up_out = rest[:, :, 288:544].reshape(ADAPTER_RANK, D)
    base = complete(base)

    half_dim = HEAD_SIZE // 2
    frequency = rope_base ** (-(jnp.arange(half_dim, dtype=jnp.float32) * 2.0) / HEAD_SIZE)
    angle = jnp.arange(seq, dtype=jnp.int32).astype(jnp.float32)[:, None] * frequency[None, :]
    cosine = jnp.cos(angle)
    sine = jnp.sin(angle)
    cosines = jnp.concatenate([cosine, cosine], 1)
    sines = jnp.concatenate([-sine, sine], 1)
    return attend(
        query_base,
        base,
        own_rank,
        all_rank,
        query_up,
        keyval_up,
        cosines,
        sines,
        down_out,
        up_out,
    )


def shards(normed_input, query_base, key_base, value_base, adapter_pool, stretch_adapter, owner):
    fits = (
        lax.axis_size("groups") == 2
        and lax.axis_size("ctx") == 2 * PIECES
        and normed_input.shape[0] * PIECES == BLOCK_TOKENS
        and adapter_pool.shape[0] == 1
    )
    plan = direct_shards if fits else spread_shards
    return plan(
        normed_input, query_base, key_base, value_base, adapter_pool, stretch_adapter, owner
    )


def solution(mesh):
    placed = (
        P(("groups", "ctx"), None),
        P(("groups", "ctx"), None),
        P(("groups", "ctx"), None),
        P(("groups", "ctx"), None),
        P("ctx", None),
        P("groups"),
        P(),
    )
    return jax.shard_map(
        shards,
        mesh=mesh,
        in_specs=placed,
        out_specs=(P(("groups", "ctx"), None), P(("groups", "ctx"), None)),
        check_vma=False,
    )
```

```python
from functools import partial
import math

import jax
import jax.numpy as jnp
from jax import lax
from jax.experimental import pallas as pl
from jax.experimental.pallas import tpu as pltpu
from jax.sharding import PartitionSpec as P

D = 8192
QH = 32
KEYVALUE_HEADS = 4
HEAD_SIZE = 128
ADAPTER_RANK = 64
BLOCK_TOKENS = 512
QKV_POOL = 1900544


adapter_scale = 2.0
rope_base = 500000.0
mask_floor = -1e30


def from_partner(block, axis, apart):
    count = lax.axis_size(axis)
    route = []
    for low in range(count):
        high = low | 1 << apart
        if high != low and high < count:
            route += [(low, high), (high, low)]
    return lax.ppermute(block, axis, route)


def rotate(delta, token_positions, heads):
    half_dim = HEAD_SIZE // 2
    frequency = rope_base ** (-(jnp.arange(half_dim, dtype=jnp.float32) * 2.0) / HEAD_SIZE)
    angle = token_positions.astype(jnp.float32)[:, None] * frequency[None, :]
    cosine = jnp.cos(angle)[:, None, :]
    sine_part = jnp.sin(angle)[:, None, :]
    shaped = delta.reshape(delta.shape[0], heads, HEAD_SIZE)
    first_half = shaped[..., :half_dim]
    second_half = shaped[..., half_dim:]
    joined = jnp.concatenate(
        [
            first_half * cosine - second_half * sine_part,
            second_half * cosine + first_half * sine_part,
        ],
        -1,
    )
    return joined.reshape(delta.shape[0], heads * HEAD_SIZE)


def project_heads(
    narrow_product, query_row_block, key_row_block, value_row_block, upper_part, token_positions
):
    query_up_weight = upper_part[: ADAPTER_RANK * QH * HEAD_SIZE].reshape(
        ADAPTER_RANK, QH * HEAD_SIZE
    )
    keyvalue_up_weight = upper_part[ADAPTER_RANK * QH * HEAD_SIZE :].reshape(
        ADAPTER_RANK, 2 * KEYVALUE_HEADS * HEAD_SIZE
    )
    query_correction = adapter_scale * jnp.dot(
        narrow_product[:, :ADAPTER_RANK], query_up_weight, preferred_element_type=jnp.float32
    )
    key_correction = adapter_scale * jnp.dot(
        narrow_product[:, ADAPTER_RANK : 2 * ADAPTER_RANK],
        keyvalue_up_weight[:, : KEYVALUE_HEADS * HEAD_SIZE],
        preferred_element_type=jnp.float32,
    )
    value_correction = adapter_scale * jnp.dot(
        narrow_product[:, 2 * ADAPTER_RANK :],
        keyvalue_up_weight[:, KEYVALUE_HEADS * HEAD_SIZE :],
        preferred_element_type=jnp.float32,
    )
    queries = (
        query_row_block.astype(jnp.float32) + rotate(query_correction, token_positions, QH)
    ).astype(jnp.bfloat16)
    new_keys = (
        key_row_block.astype(jnp.float32) + rotate(key_correction, token_positions, KEYVALUE_HEADS)
    ).astype(jnp.bfloat16)
    new_values = (value_row_block.astype(jnp.float32) + value_correction).astype(jnp.bfloat16)
    return (queries, new_keys, new_values)


def output_delta(attended_rows, out_part):
    down_out = out_part[: QH * HEAD_SIZE * ADAPTER_RANK].reshape(QH * HEAD_SIZE, ADAPTER_RANK)
    raised_output = out_part[QH * HEAD_SIZE * ADAPTER_RANK :].reshape(ADAPTER_RANK, D)
    narrow_product = jnp.dot(attended_rows, down_out, preferred_element_type=jnp.float32).astype(
        jnp.bfloat16
    )
    return (
        adapter_scale * jnp.dot(narrow_product, raised_output, preferred_element_type=jnp.float32)
    ).astype(jnp.bfloat16)


def head_major(query_row_block):
    count_rows = query_row_block.shape[0]
    group_size = QH // KEYVALUE_HEADS
    return (
        query_row_block.reshape(count_rows, KEYVALUE_HEADS, group_size, HEAD_SIZE)
        .transpose(1, 2, 0, 3)
        .reshape(KEYVALUE_HEADS, group_size * count_rows, HEAD_SIZE)
    )


def row_major(head_rows, count_rows):
    group_size = QH // KEYVALUE_HEADS
    return (
        head_rows.reshape(KEYVALUE_HEADS, group_size, count_rows, HEAD_SIZE)
        .transpose(2, 0, 1, 3)
        .reshape(count_rows, QH * HEAD_SIZE)
    )


def online_update(current, queries, query_pos, key_slice, value_slice, key_start):
    run_max, run_sum, run_acc = current
    scores = jnp.einsum(
        "hqd,khd->hqk", queries, key_slice, preferred_element_type=jnp.float32
    ) * HEAD_SIZE ** (-0.5)
    key_pos = key_start + jnp.arange(key_slice.shape[0], dtype=jnp.int32)
    allowed = (query_pos[:, None] >= key_pos[None, :])[None]
    new_max = jnp.maximum(run_max, jnp.max(jnp.where(allowed, scores, mask_floor), axis=-1))
    weights = jnp.where(allowed, jnp.exp(scores - new_max[..., None]), 0.0)
    rescale = jnp.exp(run_max - new_max)
    new_sum = run_sum * rescale + jnp.sum(weights, axis=-1)
    new_acc = run_acc * rescale[..., None] + jnp.einsum(
        "hqk,khd->hqd",
        weights.astype(jnp.bfloat16),
        value_slice,
        preferred_element_type=jnp.float32,
    )
    return (new_max, new_sum, new_acc)


def unchanged(current):
    return current


def fold_keys(carry_state, shard_part, prepared):
    key_row_block, value_row_block = shard_part
    key_count = key_row_block.shape[0]
    sub_width = math.gcd(key_count, 1024)
    key_heads = key_row_block.reshape(key_count // sub_width, sub_width, KEYVALUE_HEADS, HEAD_SIZE)
    value_heads = value_row_block.reshape(
        key_count // sub_width, sub_width, KEYVALUE_HEADS, HEAD_SIZE
    )

    def one_step(sub_index, carried):
        key_start = sub_index * sub_width
        key_slice = lax.dynamic_index_in_dim(key_heads, sub_index, 0, keepdims=False)
        value_slice = lax.dynamic_index_in_dim(value_heads, sub_index, 0, keepdims=False)
        updated = []
        for (queries, query_pos), running in zip(prepared, carried):
            advance = partial(
                online_update,
                queries=queries,
                query_pos=query_pos,
                key_slice=key_slice,
                value_slice=value_slice,
                key_start=key_start,
            )
            updated.append(lax.cond(key_start <= jnp.max(query_pos), advance, unchanged, running))
        return tuple(updated)

    return lax.fori_loop(0, key_count // sub_width, one_step, carry_state)


def finish_block(result, count_rows):
    run_max, run_sum, run_acc = result
    divisor = jnp.where(run_sum > 0.0, run_sum, 1.0)
    return row_major(run_acc / divisor[..., None], count_rows).astype(jnp.bfloat16)


def spread_shards(
    normed_input, query_base, key_base, value_base, adapter_pool, stretch_adapter, adapter_owner
):
    cycle_size = lax.axis_size("ctx")
    my_index = lax.axis_index("ctx")
    tok_rows = normed_input.shape[0]
    token_positions = my_index * tok_rows + jnp.arange(tok_rows, dtype=jnp.int32)
    device_ids = jnp.arange(cycle_size, dtype=jnp.int32)
    stretch_of = device_ids * tok_rows // BLOCK_TOKENS
    stretch_ids = jnp.arange(stretch_adapter.shape[0], dtype=jnp.int32)
    adapter_of = jnp.sum(
        jnp.where(stretch_of[:, None] == stretch_ids[None, :], stretch_adapter[None, :], 0), axis=1
    )
    adapter_ids = jnp.arange(adapter_owner.shape[0], dtype=jnp.int32)
    slot_of = jnp.sum(
        jnp.where(adapter_of[:, None] == adapter_ids[None, :], adapter_owner[None, :], 0), axis=1
    )
    down_size = 3 * ADAPTER_RANK * D
    group_count = BLOCK_TOKENS // tok_rows
    levels = group_count.bit_length() - 1
    local_index = my_index % group_count
    col_width = D // group_count
    piece_len = down_size // (group_count * cycle_size)
    pool_rows = adapter_pool.shape[0]
    down_shaped = adapter_pool[:, :down_size].reshape(pool_rows, group_count, cycle_size, piece_len)
    spread_down = lax.all_to_all(down_shaped, "ctx", split_axis=2, concat_axis=0, tiled=True)
    flat_down = spread_down.reshape(-1, piece_len)
    wanted = jnp.take(flat_down, slot_of * group_count + device_ids % group_count, axis=0)[
        :, None, :
    ]
    down_slice = lax.all_to_all(wanted, "ctx", split_axis=0, concat_axis=1, tiled=True).reshape(
        col_width, 3 * ADAPTER_RANK
    )
    spread_rest = lax.all_to_all(
        adapter_pool[:, down_size:], "ctx", split_axis=1, concat_axis=0, tiled=True
    )
    rest_row = lax.all_to_all(
        jnp.take(spread_rest, slot_of, axis=0), "ctx", split_axis=0, concat_axis=1, tiled=True
    )[0]
    upper_part = rest_row[: QKV_POOL - down_size]
    out_part = rest_row[QKV_POOL - down_size :]
    pieces = normed_input.reshape(tok_rows, group_count, col_width)
    slice_order = jnp.bitwise_xor(local_index, jnp.arange(group_count, dtype=jnp.int32))
    moving = jnp.take(pieces, slice_order, axis=1).transpose(1, 0, 2)
    for level in range(levels):
        shaped = moving.reshape(group_count >> level + 1, 2, 1 << level, tok_rows, col_width)
        arrived = from_partner(shaped[:, 1], "ctx", level)
        moving = jnp.stack([shaped[:, 0], arrived], 1).reshape(group_count, tok_rows, col_width)
    partial_rows = jnp.dot(
        moving.reshape(group_count * tok_rows, col_width),
        down_slice,
        preferred_element_type=jnp.float32,
    ).reshape(group_count, tok_rows, 3 * ADAPTER_RANK)
    for level in reversed(range(levels)):
        halves = partial_rows.reshape(2, partial_rows.shape[0] // 2, tok_rows, 3 * ADAPTER_RANK)
        partial_rows = halves[0] + from_partner(
            halves[1].astype(jnp.bfloat16), "ctx", level
        ).astype(jnp.float32)
    narrow_product = partial_rows[0].astype(jnp.bfloat16)
    queries, new_keys, new_values = project_heads(
        narrow_product, query_base, key_base, value_base, upper_part, token_positions
    )
    group_size = QH // KEYVALUE_HEADS
    blocks = [(queries, token_positions)]
    prepared = [
        (head_major(block_q), jnp.tile(block_pos, group_size)) for block_q, block_pos in blocks
    ]
    initial = tuple(
        (
            (
                jnp.full((KEYVALUE_HEADS, head_q.shape[1]), mask_floor, jnp.float32),
                jnp.zeros((KEYVALUE_HEADS, head_q.shape[1]), jnp.float32),
                jnp.zeros((KEYVALUE_HEADS, head_q.shape[1], HEAD_SIZE), jnp.float32),
            )
            for head_q, block_pos in prepared
        )
    )
    finals = fold_keys(
        initial,
        (
            lax.all_gather(new_keys, "ctx", axis=0, tiled=True),
            lax.all_gather(new_values, "ctx", axis=0, tiled=True),
        ),
        prepared,
    )
    attended = finish_block(finals[0], tok_rows)
    out_delta = output_delta(attended, out_part)
    return (attended, out_delta)


PIECES = 8
GROUP = QH // KEYVALUE_HEADS
FIRST = ((0, 12288), (12288, 2048), (14336, 512))
SECOND = ((14848, 2048), (16896, 4096))
DOWN_ROWS, QUERY_ROWS, KEYVAL_ROWS, DOWN_OUT_ROWS, UP_OUT_ROWS = 768, 128, 32, 128, 256
UP_ROWS = QUERY_ROWS + 2 * KEYVAL_ROWS


def pack_kernel(sections, pool, *refs):
    out, buffers, sems = refs[-3:]
    plane = lax.axis_index("groups")
    slabs, slab_rows = out.shape[:2]

    def copies(slab):
        listed = []
        offset = 0
        for first, rows in sections:
            share = rows // (2 * PIECES)
            begin = first + (slab * 2 + plane) * share
            listed.append(
                pltpu.make_async_copy(
                    pool.at[:, pl.ds(pl.multiple_of(begin * 128, 2048), share * 128)],
                    buffers.at[slab, :, pl.ds(offset, share * 128)],
                    sems.at[slab, len(listed)],
                )
            )
            offset += share * 128
        return listed

    for slab in range(slabs):
        for copy in copies(slab):
            copy.start()

    def step(slab, carried):
        for copy in copies(slab):
            copy.wait()

        def chunk(index, inner):
            line = buffers[slab, :, pl.ds(pl.multiple_of(index * 2048, 2048), 2048)]
            block = line.astype(jnp.float32).reshape(16, 128).astype(jnp.bfloat16)
            out[slab, pl.ds(pl.multiple_of(index * 16, 16), 16), :] = block
            return inner

        lax.fori_loop(0, slab_rows // 16, chunk, 0, unroll=8)
        return carried

    lax.fori_loop(0, slabs, step, 0)


def pack_row(pool, sections, *after):
    slab_rows = sum(rows for _, rows in sections) // (2 * PIECES)
    return pl.pallas_call(
        partial(pack_kernel, sections),
        out_shape=jax.ShapeDtypeStruct((PIECES, slab_rows, 128), jnp.bfloat16),
        in_specs=[pl.BlockSpec(memory_space=pl.ANY)] * (1 + len(after)),
        out_specs=pl.BlockSpec(memory_space=pltpu.VMEM),
        scratch_shapes=[
            pltpu.VMEM((PIECES, 1, slab_rows * 128), jnp.bfloat16),
            pltpu.SemaphoreType.DMA((PIECES, len(sections))),
        ],
        compiler_params=pltpu.CompilerParams(vmem_limit_bytes=60 << 20),
        cost_estimate=pl.CostEstimate(flops=0, bytes_accessed=8 << 20, transcendentals=0),
    )(pool, *after)


def pick_kernel(mirrored, here, there, owner, spread, *refs):
    sems = refs[-1]
    outs = refs[:4] if len(refs) > 3 else [refs[flip % 2].at[flip // 2] for flip in range(4)]
    half = lax.axis_index("ctx") // PIECES
    rows = spread.shape[1]
    copies = []
    for flip, out in enumerate(outs):
        wishes = there if flip >= 2 else here
        block = half ^ (flip & 1)
        row = lax.rem(owner[wishes[block]], PIECES)
        copies.append(
            pltpu.make_async_copy(spread.at[row], out.at[pl.ds(0, rows)], sems.at[flip, 0])
        )
        if mirrored is not None:
            first, count = mirrored
            row = lax.rem(owner[wishes[1 - block]], PIECES)
            copies.append(
                pltpu.make_async_copy(
                    spread.at[row, pl.ds(first, count)],
                    out.at[pl.ds(rows, count)],
                    sems.at[flip, 1],
                )
            )
    for copy in copies:
        copy.start()
    for copy in copies:
        copy.wait()


def pick(spread, here, there, owner, mirrored):
    rows = spread.shape[1] + (mirrored[1] if mirrored else 0)
    shape, count = ((rows, 128), 4) if mirrored else ((2, rows, 128), 2)
    slab = jax.ShapeDtypeStruct(shape, jnp.bfloat16)
    return pl.pallas_call(
        partial(pick_kernel, mirrored),
        out_shape=(slab,) * count,
        in_specs=[pl.BlockSpec(memory_space=pltpu.SMEM)] * 3 + [pl.BlockSpec(memory_space=pl.ANY)],
        out_specs=(pl.BlockSpec(memory_space=pltpu.VMEM),) * count,
        scratch_shapes=[pltpu.SemaphoreType.DMA((4, 2))],
        compiler_params=pltpu.CompilerParams(vmem_limit_bytes=16 << 20),
        cost_estimate=pl.CostEstimate(flops=0, bytes_accessed=2 << 20, transcendentals=0),
    )(here, there, owner, spread)


def deal_kernel(rows, even, odd, sems):
    seat = lax.rem(lax.axis_index("ctx"), PIECES)
    width = rows.shape[1] // PIECES
    copies = []
    for apart in range(PIECES):
        first = pl.multiple_of((seat ^ apart) * width, width)
        target = (odd if apart % 2 else even).at[apart // 2]
        copies.append(
            pltpu.make_async_copy(rows.at[:, pl.ds(first, width)], target, sems.at[apart])
        )
    for copy in copies:
        copy.start()
    for copy in copies:
        copy.wait()


def deal(rows, *after):
    slab = jax.ShapeDtypeStruct((PIECES // 2, rows.shape[0], rows.shape[1] // PIECES), rows.dtype)

    def kernel(rows, *refs):
        deal_kernel(rows, *refs[-3:])

    return pl.pallas_call(
        kernel,
        out_shape=(slab, slab),
        in_specs=[pl.BlockSpec(memory_space=pl.ANY)] * (1 + len(after)),
        out_specs=(pl.BlockSpec(memory_space=pltpu.VMEM),) * 2,
        scratch_shapes=[pltpu.SemaphoreType.DMA((PIECES,))],
        compiler_params=pltpu.CompilerParams(vmem_limit_bytes=16 << 20),
        cost_estimate=pl.CostEstimate(flops=0, bytes_accessed=2 << 20, transcendentals=0),
    )(rows, *after)


def nearest(here, owner, block):
    half = lax.axis_index("ctx") // PIECES
    return owner[here[block]] // PIECES == half


def choose(close, arrived, put):
    plane = lax.axis_index("groups")

    @pl.when(close)
    def _():
        put(arrived[0], plane)
        put(arrived[2], 1 - plane)

    @pl.when(jnp.logical_not(close))
    def _():
        put(arrived[1], plane)
        put(arrived[3], 1 - plane)


def join_kernel(here, owner, *refs):
    arrived, (weight, ups), (flat, left, right) = refs[:4], refs[4:6], refs[6:]
    half = lax.axis_index("ctx") // PIECES
    split = DOWN_ROWS + QUERY_ROWS + KEYVAL_ROWS

    def put_own(source, position):
        first = pl.multiple_of(position * DOWN_ROWS, DOWN_ROWS)
        flat[pl.ds(first, DOWN_ROWS), :] = source[:DOWN_ROWS, :].astype(jnp.float32)
        ups[position, : UP_ROWS - KEYVAL_ROWS, :] = source[DOWN_ROWS:split, :]

    def put_mirrored(source, position):
        ups[position, UP_ROWS - KEYVAL_ROWS :, :] = source[split:, :]

    choose(nearest(here, owner, half), arrived, put_own)
    choose(nearest(here, owner, 1 - half), arrived, put_mirrored)

    third = flat.shape[0] // 3
    one = flat[pl.ds(0, third, stride=3), :]
    two = pltpu.roll(flat[pl.ds(1, third, stride=3), :], 64, 1)
    three = pltpu.roll(flat[pl.ds(2, third, stride=3), :], 64, 1)
    lane = lax.broadcasted_iota(jnp.int32, one.shape, 1)
    left[pl.ds(0, third, stride=2), :] = one
    left[pl.ds(1, third, stride=2), :] = jnp.where(lane < 64, two, three)
    right[pl.ds(0, third, stride=2), :] = pltpu.roll(two, 64, 1)
    right[pl.ds(1, third, stride=2), :] = three
    weight[...] = jnp.concatenate([left[...], right[...]], 1).astype(jnp.bfloat16)


def join(here, owner, arrived):
    depth = D // PIECES
    return pl.pallas_call(
        join_kernel,
        out_shape=(
            jax.ShapeDtypeStruct((depth, 256), jnp.bfloat16),
            jax.ShapeDtypeStruct((2, UP_ROWS, 128), jnp.bfloat16),
        ),
        in_specs=[pl.BlockSpec(memory_space=pltpu.SMEM)] * 2
        + [pl.BlockSpec(memory_space=pltpu.VMEM)] * 4,
        out_specs=(pl.BlockSpec(memory_space=pltpu.VMEM),) * 2,
        scratch_shapes=[
            pltpu.VMEM((2 * DOWN_ROWS, 128), jnp.float32),
            pltpu.VMEM((depth, 128), jnp.float32),
            pltpu.VMEM((depth, 128), jnp.float32),
        ],
        compiler_params=pltpu.CompilerParams(vmem_limit_bytes=16 << 20),
        cost_estimate=pl.CostEstimate(flops=0, bytes_accessed=16 << 20, transcendentals=0),
    )(here, owner, *arrived)


def settle_kernel(here, there, owner, near, far, own, across):
    half = lax.axis_index("ctx") // PIECES
    for number, (wishes, out) in enumerate(((here, own), (there, across))):
        close = nearest(wishes, owner, half)

        @pl.when(close)
        def _():
            out[...] = near[number]

        @pl.when(jnp.logical_not(close))
        def _():
            out[...] = far[number]


def settle(here, there, owner, near, far):
    slab = jax.ShapeDtypeStruct(near.shape[1:], jnp.bfloat16)
    return pl.pallas_call(
        settle_kernel,
        out_shape=(slab, slab),
        in_specs=[pl.BlockSpec(memory_space=pltpu.SMEM)] * 3
        + [pl.BlockSpec(memory_space=pltpu.VMEM)] * 2,
        out_specs=(pl.BlockSpec(memory_space=pltpu.VMEM),) * 2,
        compiler_params=pltpu.CompilerParams(vmem_limit_bytes=16 << 20),
        cost_estimate=pl.CostEstimate(flops=0, bytes_accessed=1 << 20, transcendentals=0),
    )(here, there, owner, near, far)


def narrow_kernel(weight, *refs):
    for block, out in zip(refs[:4], refs[4:]):
        sides, rows, depth = block.shape
        product = jnp.dot(
            block[...].reshape(sides * rows, depth),
            weight[...],
            preferred_element_type=jnp.float32,
        )
        out[...] = product[:, : 3 * ADAPTER_RANK].reshape(out.shape).astype(jnp.bfloat16)


def narrow(weight, dealt):
    sides, rows, depth = dealt[0].shape
    partial_sums = jax.ShapeDtypeStruct((sides, rows, 3 * ADAPTER_RANK), jnp.bfloat16)
    return pl.pallas_call(
        narrow_kernel,
        out_shape=(partial_sums,) * 4,
        in_specs=[pl.BlockSpec(memory_space=pltpu.VMEM)] * 5,
        out_specs=(pl.BlockSpec(memory_space=pltpu.VMEM),) * 4,
        compiler_params=pltpu.CompilerParams(vmem_limit_bytes=16 << 20),
        cost_estimate=pl.CostEstimate(
            flops=2 * 8 * rows * depth * 256, bytes_accessed=2 << 20, transcendentals=0
        ),
    )(weight, *dealt)


def attend_kernel(
    query_block,
    key_same,
    key_other,
    value_same,
    value_other,
    own_rank,
    all_rank,
    up_same,
    up_other,
    cosines,
    sines,
    attended,
    flat_query,
    flat_keyval,
    keys,
    values,
):
    step = pl.program_id(0)
    rows = query_block.shape[0]
    base = lax.axis_index("ctx") * rows
    half = lax.axis_index("ctx") // PIECES
    seat = lax.rem(lax.axis_index("ctx"), PIECES)
    dot = partial(jnp.dot, preferred_element_type=jnp.float32)

    @pl.when(step == 0)
    def _():
        for apart in range(PIECES):
            ups = up_other if apart % 2 else up_same
            for position in range(2):
                piece = ups[apart // 2, position].astype(jnp.float32)
                place = (seat ^ apart) * 2 + position
                first = pl.multiple_of(place * QUERY_ROWS, QUERY_ROWS)
                flat_query[pl.ds(first, QUERY_ROWS), :] = piece[:QUERY_ROWS]
                first = pl.multiple_of(place * KEYVAL_ROWS, KEYVAL_ROWS)
                for side in range(2):
                    begin = QUERY_ROWS + side * KEYVAL_ROWS
                    flat_keyval[side, pl.ds(first, KEYVAL_ROWS), :] = piece[
                        begin : begin + KEYVAL_ROWS
                    ]

    def turned(delta, cosine, sine):
        return delta * cosine + pltpu.roll(delta, HEAD_SIZE // 2, 1) * sine

    def up(flat, first, stride):
        return flat[pl.ds(first, ADAPTER_RANK, stride=stride), :].astype(jnp.bfloat16)

    for side in range(2):
        heads = 2 * KEYVALUE_HEADS
        key_up = up(flat_keyval.at[side], step, heads)
        value_up = up(flat_keyval.at[side], step + KEYVALUE_HEADS, heads)
        for core in range(2):
            rank = all_rank[core, :, side].reshape(PIECES // 2 * rows, 2 * ADAPTER_RANK)
            key_delta = adapter_scale * dot(rank[:, :ADAPTER_RANK], key_up)
            value_delta = adapter_scale * dot(rank[:, ADAPTER_RANK:], value_up)
            for chip in range(PIECES // 2):
                there = seat ^ (2 * chip + core)
                first = ((half ^ side) * PIECES + there) * rows
                span = pl.ds(pl.multiple_of(first, rows), rows)
                part = slice(chip * rows, (chip + 1) * rows)
                delta = turned(key_delta[part], cosines[span, :], sines[span, :])
                full = (key_other if core else key_same)[chip, side].astype(jnp.float32) + delta
                keys[span, :] = full.astype(jnp.bfloat16)
                full = (value_other if core else value_same)[chip, side].astype(jnp.float32)
                values[span, :] = (full + value_delta[part]).astype(jnp.bfloat16)
    here = pl.ds(pl.multiple_of(base, rows), rows)
    cosine = cosines[here, :]
    sine = sines[here, :]
    taken = GROUP // 2
    for first in range(0, GROUP, taken):
        weight = [up(flat_query, step * GROUP + first + head, QH) for head in range(taken)]
        deltas = adapter_scale * dot(own_rank[:, :ADAPTER_RANK], jnp.concatenate(weight, 1))
        queries = []
        for place in range(taken):
            moved = turned(deltas[:, place * HEAD_SIZE : (place + 1) * HEAD_SIZE], cosine, sine)
            span = slice((first + place) * HEAD_SIZE, (first + place + 1) * HEAD_SIZE)
            queries.append(
                (query_block[:, span].astype(jnp.float32) + moved).astype(jnp.bfloat16)
            )
        queries = jnp.concatenate(queries, 0)
        scores = lax.dot_general(
            queries, keys[...], (((1,), (1,)), ((), ())), preferred_element_type=jnp.float32
        )
        row = lax.broadcasted_iota(jnp.int32, scores.shape, 0)
        column = lax.broadcasted_iota(jnp.int32, scores.shape, 1)
        scores = jnp.where(column <= base + lax.rem(row, rows), scores, mask_floor)
        scores = scores - jnp.max(scores, axis=-1, keepdims=True)
        weights = jnp.exp2(scores * (HEAD_SIZE ** (-0.5) * math.log2(math.e)))
        divisor = jnp.sum(weights, axis=-1, keepdims=True)
        result = (dot(weights.astype(jnp.bfloat16), values[...]) / divisor).astype(jnp.bfloat16)
        for place in range(taken):
            span = slice((first + place) * HEAD_SIZE, (first + place + 1) * HEAD_SIZE)
            attended[:, span] = result[place * rows : (place + 1) * rows]


def attend(query_base, base, own_rank, all_rank, ups, cosines, sines):
    rows = query_base.shape[0]
    seq = 4 * PIECES // 2 * rows
    width = GROUP * HEAD_SIZE

    def whole(shape):
        return pl.BlockSpec(shape, lambda h: (0,) * len(shape))

    key_spec = pl.BlockSpec((PIECES // 2, 2, rows, HEAD_SIZE), lambda h: (0, 0, 0, h))
    value_spec = pl.BlockSpec(
        (PIECES // 2, 2, rows, HEAD_SIZE), lambda h: (0, 0, 0, h + KEYVALUE_HEADS)
    )
    return pl.pallas_call(
        attend_kernel,
        grid=(KEYVALUE_HEADS,),
        out_shape=jax.ShapeDtypeStruct((rows, QH * HEAD_SIZE), jnp.bfloat16),
        in_specs=[
            pl.BlockSpec((rows, width), lambda h: (0, h)),
            key_spec,
            key_spec,
            value_spec,
            value_spec,
            whole(own_rank.shape),
            whole(all_rank.shape),
            whole(ups[0].shape),
            whole(ups[1].shape),
            whole(cosines.shape),
            whole(sines.shape),
        ],
        out_specs=pl.BlockSpec((rows, width), lambda h: (0, h)),
        scratch_shapes=[
            pltpu.VMEM((2 * PIECES * QUERY_ROWS, 128), jnp.float32),
            pltpu.VMEM((2, 2 * PIECES * KEYVAL_ROWS, 128), jnp.float32),
            pltpu.VMEM((seq, HEAD_SIZE), jnp.bfloat16),
            pltpu.VMEM((seq, HEAD_SIZE), jnp.bfloat16),
        ],
        compiler_params=pltpu.CompilerParams(vmem_limit_bytes=60 << 20),
        cost_estimate=pl.CostEstimate(
            flops=48 * rows * QH * seq * HEAD_SIZE,
            bytes_accessed=10 << 20,
            transcendentals=rows * QH * seq,
        ),
    )(query_base, base[0], base[1], base[0], base[1], own_rank, all_rank, *ups, cosines, sines)


def widen_kernel(attended, same, other, out_delta, down_out, up_out):
    plane = lax.axis_index("groups")
    seat = lax.rem(lax.axis_index("ctx"), PIECES)
    for apart in range(PIECES):
        pieces = other if apart % 2 else same
        for position in range(2):
            piece = pieces[apart // 2, position].astype(jnp.float32)
            place = (seat ^ apart) * 2 + (position ^ plane)
            first = place * 2 * DOWN_OUT_ROWS
            block = piece[:DOWN_OUT_ROWS]
            down_out[pl.ds(first, DOWN_OUT_ROWS, stride=2), :] = block
            down_out[pl.ds(first + 1, DOWN_OUT_ROWS, stride=2), :] = pltpu.roll(block, 64, 1)
            first = pl.multiple_of(place * UP_OUT_ROWS, UP_OUT_ROWS)
            up_out[pl.ds(first, UP_OUT_ROWS), :] = piece[DOWN_OUT_ROWS:]
    dot = partial(jnp.dot, preferred_element_type=jnp.float32)
    rank = dot(attended[...], down_out[...].astype(jnp.bfloat16))[:, :ADAPTER_RANK]
    rank = rank.astype(jnp.bfloat16)
    blocks = D // 128
    for first in range(0, blocks, 4):
        weight = [
            up_out[pl.ds(first + block, ADAPTER_RANK, stride=blocks), :].astype(jnp.bfloat16)
            for block in range(4)
        ]
        delta = adapter_scale * dot(rank, jnp.concatenate(weight, 1))
        out_delta[:, first * 128 : (first + 4) * 128] = delta.astype(jnp.bfloat16)


def widen(attended, pieces):
    return pl.pallas_call(
        widen_kernel,
        out_shape=jax.ShapeDtypeStruct((attended.shape[0], D), jnp.bfloat16),
        in_specs=[pl.BlockSpec(memory_space=pltpu.VMEM)] * 3,
        out_specs=pl.BlockSpec(memory_space=pltpu.VMEM),
        scratch_shapes=[
            pltpu.VMEM((QH * HEAD_SIZE, 128), jnp.float32),
            pltpu.VMEM((ADAPTER_RANK * D // 128, 128), jnp.float32),
        ],
        compiler_params=pltpu.CompilerParams(vmem_limit_bytes=32 << 20),
        cost_estimate=pl.CostEstimate(flops=1 << 27, bytes_accessed=4 << 20, transcendentals=0),
    )(attended, *pieces)


def swap(block, mask):
    return lax.ppermute(block, ("groups", "ctx"), [(i, i ^ mask) for i in range(4 * PIECES)])


def direct_shards(
    normed_input, query_base, key_base, value_base, adapter_pool, stretch_adapter, adapter_owner
):
    tok_rows = normed_input.shape[0]
    ctx = lax.axis_size("ctx")
    seq = ctx * tok_rows
    blocks = [list(range(PIECES)), list(range(PIECES, 2 * PIECES))]
    def after(block, *others):
        return lax.optimization_barrier((block, others))[0]

    def exchange(sent):
        return [swap(block, flip * PIECES) if flip else block for flip, block in enumerate(sent)]

    def along_z(block):
        return jnp.stack([block, swap(block, 4)])

    def along_x(pair):
        quad = jnp.stack([pair, swap(pair, 2)], 1)
        return quad.reshape((PIECES // 2,) + pair.shape[1:])

    elsewhere = swap(stretch_adapter, 2 * PIECES)
    packed = pack_row(adapter_pool, FIRST)
    packed_second = pack_row(adapter_pool, SECOND, packed)
    even, odd = deal(normed_input, packed)
    sibling = swap(odd, 1)
    base = jnp.concatenate([key_base, value_base], 1)
    base = jnp.stack([base, swap(base, PIECES)])

    spread = lax.all_to_all(packed, "ctx", 0, 0, axis_index_groups=blocks)
    spread = after(spread, packed_second, sibling, base)
    sent = pick(spread, stretch_adapter, elsewhere, adapter_owner, (896, KEYVAL_ROWS))
    arrived = exchange(sent)
    dealt = [after(jnp.stack([even[j], sibling[j]]), sent) for j in range(PIECES // 2)]
    dealt = [swap(block, 2 * j) if j else block for j, block in enumerate(dealt)]
    base = along_z(after(base, arrived[2]))
    packed_second = after(packed_second, arrived[2])
    spread = lax.all_to_all(packed_second, "ctx", 0, 0, axis_index_groups=blocks)

    near, far = pick(
        after(spread, arrived[1]), stretch_adapter, elsewhere, adapter_owner, None
    )
    far = swap(far, PIECES)

    weight, ups = join(stretch_adapter, adapter_owner, arrived)
    partial_sums = narrow(after(weight, near), dealt)
    back = [swap(block, 2 * j) if j else block for j, block in enumerate(partial_sums)]
    back = sum(block.astype(jnp.float32) for block in back)
    own_rank = back[0] + swap(back[1].astype(jnp.bfloat16), 1).astype(jnp.float32)
    own_rank = own_rank.astype(jnp.bfloat16)
    all_rank = own_rank[:, ADAPTER_RANK:]
    ups = along_z(after(ups, *partial_sums))
    base = along_x(after(base, own_rank))
    all_rank = jnp.stack([all_rank, swap(all_rank, PIECES)])
    far = after(far, all_rank)
    own, across = settle(stretch_adapter, elsewhere, adapter_owner, near, far)
    ends = jnp.stack([own, swap(across, 2 * PIECES)])
    ups = along_x(after(ups, all_rank))
    all_rank = jnp.stack([swap(all_rank, apart) if apart else all_rank for apart in (0, 2, 4, 6)])
    ends = along_z(after(ends, all_rank))
    base = after(base, all_rank)
    ups = after(ups, all_rank)
    all_rank = jnp.stack([all_rank, swap(all_rank, 1)])
    base = (base, swap(base, 1))
    ups = (ups, swap(ups, 1))
    ends = along_x(after(ends, all_rank))
    ends = (ends, swap(ends, 1))

    half_dim = HEAD_SIZE // 2
    frequency = rope_base ** (-(jnp.arange(half_dim, dtype=jnp.float32) * 2.0) / HEAD_SIZE)
    angle = jnp.arange(seq, dtype=jnp.int32).astype(jnp.float32)[:, None] * frequency[None, :]
    cosine = jnp.cos(angle)
    sine = jnp.sin(angle)
    cosines = jnp.concatenate([cosine, cosine], 1)
    sines = jnp.concatenate([-sine, sine], 1)
    attended = attend(query_base, base, own_rank, all_rank, ups, cosines, sines)
    return attended, widen(attended, ends)


def shards(normed_input, query_base, key_base, value_base, adapter_pool, stretch_adapter, owner):
    fits = (
        lax.axis_size("groups") == 2
        and lax.axis_size("ctx") == 2 * PIECES
        and normed_input.shape[0] * PIECES == BLOCK_TOKENS
        and adapter_pool.shape[0] == 1
    )
    plan = direct_shards if fits else spread_shards
    return plan(
        normed_input, query_base, key_base, value_base, adapter_pool, stretch_adapter, owner
    )


def solution(mesh):
    placed = (
        P(("groups", "ctx"), None),
        P(("groups", "ctx"), None),
        P(("groups", "ctx"), None),
        P(("groups", "ctx"), None),
        P("ctx", None),
        P("groups"),
        P(),
    )
    return jax.shard_map(
        shards,
        mesh=mesh,
        in_specs=placed,
        out_specs=(P(("groups", "ctx"), None), P(("groups", "ctx"), None)),
        check_vma=False,
    )
```

```python
from functools import partial
import math

import jax
import jax.numpy as jnp
from jax import lax
from jax.experimental import pallas as pl
from jax.experimental.pallas import tpu as pltpu
from jax.sharding import PartitionSpec as P

D = 8192
QH = 32
KEYVALUE_HEADS = 4
HEAD_SIZE = 128
ADAPTER_RANK = 64
BLOCK_TOKENS = 512
QKV_POOL = 1900544


adapter_scale = 2.0
rope_base = 500000.0
mask_floor = -1e30


def from_partner(block, axis, apart):
    count = lax.axis_size(axis)
    route = []
    for low in range(count):
        high = low | 1 << apart
        if high != low and high < count:
            route += [(low, high), (high, low)]
    return lax.ppermute(block, axis, route)


def rotate(delta, token_positions, heads):
    half_dim = HEAD_SIZE // 2
    frequency = rope_base ** (-(jnp.arange(half_dim, dtype=jnp.float32) * 2.0) / HEAD_SIZE)
    angle = token_positions.astype(jnp.float32)[:, None] * frequency[None, :]
    cosine = jnp.cos(angle)[:, None, :]
    sine_part = jnp.sin(angle)[:, None, :]
    shaped = delta.reshape(delta.shape[0], heads, HEAD_SIZE)
    first_half = shaped[..., :half_dim]
    second_half = shaped[..., half_dim:]
    joined = jnp.concatenate(
        [
            first_half * cosine - second_half * sine_part,
            second_half * cosine + first_half * sine_part,
        ],
        -1,
    )
    return joined.reshape(delta.shape[0], heads * HEAD_SIZE)


def project_heads(
    narrow_product, query_row_block, key_row_block, value_row_block, upper_part, token_positions
):
    query_up_weight = upper_part[: ADAPTER_RANK * QH * HEAD_SIZE].reshape(
        ADAPTER_RANK, QH * HEAD_SIZE
    )
    keyvalue_up_weight = upper_part[ADAPTER_RANK * QH * HEAD_SIZE :].reshape(
        ADAPTER_RANK, 2 * KEYVALUE_HEADS * HEAD_SIZE
    )
    query_correction = adapter_scale * jnp.dot(
        narrow_product[:, :ADAPTER_RANK], query_up_weight, preferred_element_type=jnp.float32
    )
    key_correction = adapter_scale * jnp.dot(
        narrow_product[:, ADAPTER_RANK : 2 * ADAPTER_RANK],
        keyvalue_up_weight[:, : KEYVALUE_HEADS * HEAD_SIZE],
        preferred_element_type=jnp.float32,
    )
    value_correction = adapter_scale * jnp.dot(
        narrow_product[:, 2 * ADAPTER_RANK :],
        keyvalue_up_weight[:, KEYVALUE_HEADS * HEAD_SIZE :],
        preferred_element_type=jnp.float32,
    )
    queries = (
        query_row_block.astype(jnp.float32) + rotate(query_correction, token_positions, QH)
    ).astype(jnp.bfloat16)
    new_keys = (
        key_row_block.astype(jnp.float32) + rotate(key_correction, token_positions, KEYVALUE_HEADS)
    ).astype(jnp.bfloat16)
    new_values = (value_row_block.astype(jnp.float32) + value_correction).astype(jnp.bfloat16)
    return (queries, new_keys, new_values)


def output_delta(attended_rows, out_part):
    down_out = out_part[: QH * HEAD_SIZE * ADAPTER_RANK].reshape(QH * HEAD_SIZE, ADAPTER_RANK)
    raised_output = out_part[QH * HEAD_SIZE * ADAPTER_RANK :].reshape(ADAPTER_RANK, D)
    narrow_product = jnp.dot(attended_rows, down_out, preferred_element_type=jnp.float32).astype(
        jnp.bfloat16
    )
    return (
        adapter_scale * jnp.dot(narrow_product, raised_output, preferred_element_type=jnp.float32)
    ).astype(jnp.bfloat16)


def head_major(query_row_block):
    count_rows = query_row_block.shape[0]
    group_size = QH // KEYVALUE_HEADS
    return (
        query_row_block.reshape(count_rows, KEYVALUE_HEADS, group_size, HEAD_SIZE)
        .transpose(1, 2, 0, 3)
        .reshape(KEYVALUE_HEADS, group_size * count_rows, HEAD_SIZE)
    )


def row_major(head_rows, count_rows):
    group_size = QH // KEYVALUE_HEADS
    return (
        head_rows.reshape(KEYVALUE_HEADS, group_size, count_rows, HEAD_SIZE)
        .transpose(2, 0, 1, 3)
        .reshape(count_rows, QH * HEAD_SIZE)
    )


def online_update(current, queries, query_pos, key_slice, value_slice, key_start):
    run_max, run_sum, run_acc = current
    scores = jnp.einsum(
        "hqd,khd->hqk", queries, key_slice, preferred_element_type=jnp.float32
    ) * HEAD_SIZE ** (-0.5)
    key_pos = key_start + jnp.arange(key_slice.shape[0], dtype=jnp.int32)
    allowed = (query_pos[:, None] >= key_pos[None, :])[None]
    new_max = jnp.maximum(run_max, jnp.max(jnp.where(allowed, scores, mask_floor), axis=-1))
    weights = jnp.where(allowed, jnp.exp(scores - new_max[..., None]), 0.0)
    rescale = jnp.exp(run_max - new_max)
    new_sum = run_sum * rescale + jnp.sum(weights, axis=-1)
    new_acc = run_acc * rescale[..., None] + jnp.einsum(
        "hqk,khd->hqd",
        weights.astype(jnp.bfloat16),
        value_slice,
        preferred_element_type=jnp.float32,
    )
    return (new_max, new_sum, new_acc)


def unchanged(current):
    return current


def fold_keys(carry_state, shard_part, prepared):
    key_row_block, value_row_block = shard_part
    key_count = key_row_block.shape[0]
    sub_width = math.gcd(key_count, 1024)
    key_heads = key_row_block.reshape(key_count // sub_width, sub_width, KEYVALUE_HEADS, HEAD_SIZE)
    value_heads = value_row_block.reshape(
        key_count // sub_width, sub_width, KEYVALUE_HEADS, HEAD_SIZE
    )

    def one_step(sub_index, carried):
        key_start = sub_index * sub_width
        key_slice = lax.dynamic_index_in_dim(key_heads, sub_index, 0, keepdims=False)
        value_slice = lax.dynamic_index_in_dim(value_heads, sub_index, 0, keepdims=False)
        updated = []
        for (queries, query_pos), running in zip(prepared, carried):
            advance = partial(
                online_update,
                queries=queries,
                query_pos=query_pos,
                key_slice=key_slice,
                value_slice=value_slice,
                key_start=key_start,
            )
            updated.append(lax.cond(key_start <= jnp.max(query_pos), advance, unchanged, running))
        return tuple(updated)

    return lax.fori_loop(0, key_count // sub_width, one_step, carry_state)


def finish_block(result, count_rows):
    run_max, run_sum, run_acc = result
    divisor = jnp.where(run_sum > 0.0, run_sum, 1.0)
    return row_major(run_acc / divisor[..., None], count_rows).astype(jnp.bfloat16)


def spread_shards(
    normed_input, query_base, key_base, value_base, adapter_pool, stretch_adapter, adapter_owner
):
    cycle_size = lax.axis_size("ctx")
    my_index = lax.axis_index("ctx")
    tok_rows = normed_input.shape[0]
    token_positions = my_index * tok_rows + jnp.arange(tok_rows, dtype=jnp.int32)
    device_ids = jnp.arange(cycle_size, dtype=jnp.int32)
    stretch_of = device_ids * tok_rows // BLOCK_TOKENS
    stretch_ids = jnp.arange(stretch_adapter.shape[0], dtype=jnp.int32)
    adapter_of = jnp.sum(
        jnp.where(stretch_of[:, None] == stretch_ids[None, :], stretch_adapter[None, :], 0), axis=1
    )
    adapter_ids = jnp.arange(adapter_owner.shape[0], dtype=jnp.int32)
    slot_of = jnp.sum(
        jnp.where(adapter_of[:, None] == adapter_ids[None, :], adapter_owner[None, :], 0), axis=1
    )
    down_size = 3 * ADAPTER_RANK * D
    group_count = BLOCK_TOKENS // tok_rows
    levels = group_count.bit_length() - 1
    local_index = my_index % group_count
    col_width = D // group_count
    piece_len = down_size // (group_count * cycle_size)
    pool_rows = adapter_pool.shape[0]
    down_shaped = adapter_pool[:, :down_size].reshape(pool_rows, group_count, cycle_size, piece_len)
    spread_down = lax.all_to_all(down_shaped, "ctx", split_axis=2, concat_axis=0, tiled=True)
    flat_down = spread_down.reshape(-1, piece_len)
    wanted = jnp.take(flat_down, slot_of * group_count + device_ids % group_count, axis=0)[
        :, None, :
    ]
    down_slice = lax.all_to_all(wanted, "ctx", split_axis=0, concat_axis=1, tiled=True).reshape(
        col_width, 3 * ADAPTER_RANK
    )
    spread_rest = lax.all_to_all(
        adapter_pool[:, down_size:], "ctx", split_axis=1, concat_axis=0, tiled=True
    )
    rest_row = lax.all_to_all(
        jnp.take(spread_rest, slot_of, axis=0), "ctx", split_axis=0, concat_axis=1, tiled=True
    )[0]
    upper_part = rest_row[: QKV_POOL - down_size]
    out_part = rest_row[QKV_POOL - down_size :]
    pieces = normed_input.reshape(tok_rows, group_count, col_width)
    slice_order = jnp.bitwise_xor(local_index, jnp.arange(group_count, dtype=jnp.int32))
    moving = jnp.take(pieces, slice_order, axis=1).transpose(1, 0, 2)
    for level in range(levels):
        shaped = moving.reshape(group_count >> level + 1, 2, 1 << level, tok_rows, col_width)
        arrived = from_partner(shaped[:, 1], "ctx", level)
        moving = jnp.stack([shaped[:, 0], arrived], 1).reshape(group_count, tok_rows, col_width)
    partial_rows = jnp.dot(
        moving.reshape(group_count * tok_rows, col_width),
        down_slice,
        preferred_element_type=jnp.float32,
    ).reshape(group_count, tok_rows, 3 * ADAPTER_RANK)
    for level in reversed(range(levels)):
        halves = partial_rows.reshape(2, partial_rows.shape[0] // 2, tok_rows, 3 * ADAPTER_RANK)
        partial_rows = halves[0] + from_partner(
            halves[1].astype(jnp.bfloat16), "ctx", level
        ).astype(jnp.float32)
    narrow_product = partial_rows[0].astype(jnp.bfloat16)
    queries, new_keys, new_values = project_heads(
        narrow_product, query_base, key_base, value_base, upper_part, token_positions
    )
    group_size = QH // KEYVALUE_HEADS
    blocks = [(queries, token_positions)]
    prepared = [
        (head_major(block_q), jnp.tile(block_pos, group_size)) for block_q, block_pos in blocks
    ]
    initial = tuple(
        (
            (
                jnp.full((KEYVALUE_HEADS, head_q.shape[1]), mask_floor, jnp.float32),
                jnp.zeros((KEYVALUE_HEADS, head_q.shape[1]), jnp.float32),
                jnp.zeros((KEYVALUE_HEADS, head_q.shape[1], HEAD_SIZE), jnp.float32),
            )
            for head_q, block_pos in prepared
        )
    )
    finals = fold_keys(
        initial,
        (
            lax.all_gather(new_keys, "ctx", axis=0, tiled=True),
            lax.all_gather(new_values, "ctx", axis=0, tiled=True),
        ),
        prepared,
    )
    attended = finish_block(finals[0], tok_rows)
    out_delta = output_delta(attended, out_part)
    return (attended, out_delta)


PIECES = 8
GROUP = QH // KEYVALUE_HEADS
FIRST = ((0, 12288), (12288, 2048), (14336, 512))
SECOND = ((14848, 2048), (16896, 4096))
DOWN_ROWS, QUERY_ROWS, KEYVAL_ROWS, DOWN_OUT_ROWS, UP_OUT_ROWS = 768, 128, 32, 128, 256
UP_ROWS = QUERY_ROWS + 2 * KEYVAL_ROWS


def pack_kernel(sections, pool, *refs):
    out, buffers, sems = refs[-3:]
    plane = lax.axis_index("groups")
    slabs, slab_rows = out.shape[:2]

    def copies(slab):
        listed = []
        offset = 0
        for first, rows in sections:
            share = rows // (2 * PIECES)
            begin = first + (slab * 2 + plane) * share
            listed.append(
                pltpu.make_async_copy(
                    pool.at[:, pl.ds(pl.multiple_of(begin * 128, 2048), share * 128)],
                    buffers.at[slab, :, pl.ds(offset, share * 128)],
                    sems.at[slab, len(listed)],
                )
            )
            offset += share * 128
        return listed

    for slab in range(slabs):
        for copy in copies(slab):
            copy.start()

    def step(slab, carried):
        for copy in copies(slab):
            copy.wait()

        def chunk(index, inner):
            line = buffers[slab, :, pl.ds(pl.multiple_of(index * 2048, 2048), 2048)]
            block = line.astype(jnp.float32).reshape(16, 128).astype(jnp.bfloat16)
            out[slab, pl.ds(pl.multiple_of(index * 16, 16), 16), :] = block
            return inner

        lax.fori_loop(0, slab_rows // 16, chunk, 0, unroll=8)
        return carried

    lax.fori_loop(0, slabs, step, 0)


def pack_row(pool, sections, *after):
    slab_rows = sum(rows for _, rows in sections) // (2 * PIECES)
    return pl.pallas_call(
        partial(pack_kernel, sections),
        out_shape=jax.ShapeDtypeStruct((PIECES, slab_rows, 128), jnp.bfloat16),
        in_specs=[pl.BlockSpec(memory_space=pl.ANY)] * (1 + len(after)),
        out_specs=pl.BlockSpec(memory_space=pltpu.VMEM),
        scratch_shapes=[
            pltpu.VMEM((PIECES, 1, slab_rows * 128), jnp.bfloat16),
            pltpu.SemaphoreType.DMA((PIECES, len(sections))),
        ],
        compiler_params=pltpu.CompilerParams(vmem_limit_bytes=60 << 20),
        cost_estimate=pl.CostEstimate(flops=0, bytes_accessed=8 << 20, transcendentals=0),
    )(pool, *after)


def pick_kernel(mirrored, here, there, owner, spread, *refs):
    sems = refs[-1]
    outs = refs[:4] if len(refs) > 3 else [refs[flip % 2].at[flip // 2] for flip in range(4)]
    half = lax.axis_index("ctx") // PIECES
    rows = spread.shape[1]
    copies = []
    for flip, out in enumerate(outs):
        wishes = there if flip >= 2 else here
        block = half ^ (flip & 1)
        row = lax.rem(owner[wishes[block]], PIECES)
        copies.append(
            pltpu.make_async_copy(spread.at[row], out.at[pl.ds(0, rows)], sems.at[flip, 0])
        )
        if mirrored is not None:
            first, count = mirrored
            row = lax.rem(owner[wishes[1 - block]], PIECES)
            copies.append(
                pltpu.make_async_copy(
                    spread.at[row, pl.ds(first, count)],
                    out.at[pl.ds(rows, count)],
                    sems.at[flip, 1],
                )
            )
    for copy in copies:
        copy.start()
    for copy in copies:
        copy.wait()


def pick(spread, here, there, owner, mirrored):
    rows = spread.shape[1] + (mirrored[1] if mirrored else 0)
    shape, count = ((rows, 128), 4) if mirrored else ((2, rows, 128), 2)
    slab = jax.ShapeDtypeStruct(shape, jnp.bfloat16)
    return pl.pallas_call(
        partial(pick_kernel, mirrored),
        out_shape=(slab,) * count,
        in_specs=[pl.BlockSpec(memory_space=pltpu.SMEM)] * 3 + [pl.BlockSpec(memory_space=pl.ANY)],
        out_specs=(pl.BlockSpec(memory_space=pltpu.VMEM),) * count,
        scratch_shapes=[pltpu.SemaphoreType.DMA((4, 2))],
        compiler_params=pltpu.CompilerParams(vmem_limit_bytes=16 << 20),
        cost_estimate=pl.CostEstimate(flops=0, bytes_accessed=2 << 20, transcendentals=0),
    )(here, there, owner, spread)


def deal_kernel(rows, even, odd, sems):
    seat = lax.rem(lax.axis_index("ctx"), PIECES)
    width = rows.shape[1] // PIECES
    copies = []
    for apart in range(PIECES):
        first = pl.multiple_of((seat ^ apart) * width, width)
        target = (odd if apart % 2 else even).at[apart // 2]
        copies.append(
            pltpu.make_async_copy(rows.at[:, pl.ds(first, width)], target, sems.at[apart])
        )
    for copy in copies:
        copy.start()
    for copy in copies:
        copy.wait()


def deal(rows, *after):
    slab = jax.ShapeDtypeStruct((PIECES // 2, rows.shape[0], rows.shape[1] // PIECES), rows.dtype)

    def kernel(rows, *refs):
        deal_kernel(rows, *refs[-3:])

    return pl.pallas_call(
        kernel,
        out_shape=(slab, slab),
        in_specs=[pl.BlockSpec(memory_space=pl.ANY)] * (1 + len(after)),
        out_specs=(pl.BlockSpec(memory_space=pltpu.VMEM),) * 2,
        scratch_shapes=[pltpu.SemaphoreType.DMA((PIECES,))],
        compiler_params=pltpu.CompilerParams(vmem_limit_bytes=16 << 20),
        cost_estimate=pl.CostEstimate(flops=0, bytes_accessed=2 << 20, transcendentals=0),
    )(rows, *after)


def nearest(here, owner, block):
    half = lax.axis_index("ctx") // PIECES
    return owner[here[block]] // PIECES == half


def choose(close, arrived, put):
    plane = lax.axis_index("groups")

    @pl.when(close)
    def _():
        put(arrived[0], plane)
        put(arrived[2], 1 - plane)

    @pl.when(jnp.logical_not(close))
    def _():
        put(arrived[1], plane)
        put(arrived[3], 1 - plane)


def join_kernel(here, owner, *refs):
    arrived, (weight, ups), (flat, left, right) = refs[:4], refs[4:6], refs[6:]
    half = lax.axis_index("ctx") // PIECES
    split = DOWN_ROWS + QUERY_ROWS + KEYVAL_ROWS

    def put_own(source, position):
        first = pl.multiple_of(position * DOWN_ROWS, DOWN_ROWS)
        flat[pl.ds(first, DOWN_ROWS), :] = source[:DOWN_ROWS, :].astype(jnp.float32)
        ups[position, : UP_ROWS - KEYVAL_ROWS, :] = source[DOWN_ROWS:split, :]

    def put_mirrored(source, position):
        ups[position, UP_ROWS - KEYVAL_ROWS :, :] = source[split:, :]

    choose(nearest(here, owner, half), arrived, put_own)
    choose(nearest(here, owner, 1 - half), arrived, put_mirrored)

    third = flat.shape[0] // 3
    one = flat[pl.ds(0, third, stride=3), :]
    two = pltpu.roll(flat[pl.ds(1, third, stride=3), :], 64, 1)
    three = pltpu.roll(flat[pl.ds(2, third, stride=3), :], 64, 1)
    lane = lax.broadcasted_iota(jnp.int32, one.shape, 1)
    left[pl.ds(0, third, stride=2), :] = one
    left[pl.ds(1, third, stride=2), :] = jnp.where(lane < 64, two, three)
    right[pl.ds(0, third, stride=2), :] = pltpu.roll(two, 64, 1)
    right[pl.ds(1, third, stride=2), :] = three
    weight[...] = jnp.concatenate([left[...], right[...]], 1).astype(jnp.bfloat16)


def join(here, owner, arrived):
    depth = D // PIECES
    return pl.pallas_call(
        join_kernel,
        out_shape=(
            jax.ShapeDtypeStruct((depth, 256), jnp.bfloat16),
            jax.ShapeDtypeStruct((2, UP_ROWS, 128), jnp.bfloat16),
        ),
        in_specs=[pl.BlockSpec(memory_space=pltpu.SMEM)] * 2
        + [pl.BlockSpec(memory_space=pltpu.VMEM)] * 4,
        out_specs=(pl.BlockSpec(memory_space=pltpu.VMEM),) * 2,
        scratch_shapes=[
            pltpu.VMEM((2 * DOWN_ROWS, 128), jnp.float32),
            pltpu.VMEM((depth, 128), jnp.float32),
            pltpu.VMEM((depth, 128), jnp.float32),
        ],
        compiler_params=pltpu.CompilerParams(vmem_limit_bytes=16 << 20),
        cost_estimate=pl.CostEstimate(flops=0, bytes_accessed=16 << 20, transcendentals=0),
    )(here, owner, *arrived)


def settle_kernel(here, there, owner, near, far, own, across):
    half = lax.axis_index("ctx") // PIECES
    for number, (wishes, out) in enumerate(((here, own), (there, across))):
        close = nearest(wishes, owner, half)

        @pl.when(close)
        def _():
            out[...] = near[number]

        @pl.when(jnp.logical_not(close))
        def _():
            out[...] = far[number]


def settle(here, there, owner, near, far):
    slab = jax.ShapeDtypeStruct(near.shape[1:], jnp.bfloat16)
    return pl.pallas_call(
        settle_kernel,
        out_shape=(slab, slab),
        in_specs=[pl.BlockSpec(memory_space=pltpu.SMEM)] * 3
        + [pl.BlockSpec(memory_space=pltpu.VMEM)] * 2,
        out_specs=(pl.BlockSpec(memory_space=pltpu.VMEM),) * 2,
        compiler_params=pltpu.CompilerParams(vmem_limit_bytes=16 << 20),
        cost_estimate=pl.CostEstimate(flops=0, bytes_accessed=1 << 20, transcendentals=0),
    )(here, there, owner, near, far)


def narrow_kernel(weight, *refs):
    for block, out in zip(refs[:4], refs[4:]):
        sides, rows, depth = block.shape
        product = jnp.dot(
            block[...].reshape(sides * rows, depth),
            weight[...],
            preferred_element_type=jnp.float32,
        )
        out[...] = product[:, : 3 * ADAPTER_RANK].reshape(out.shape).astype(jnp.bfloat16)


def narrow(weight, dealt):
    sides, rows, depth = dealt[0].shape
    partial_sums = jax.ShapeDtypeStruct((sides, rows, 3 * ADAPTER_RANK), jnp.bfloat16)
    return pl.pallas_call(
        narrow_kernel,
        out_shape=(partial_sums,) * 4,
        in_specs=[pl.BlockSpec(memory_space=pltpu.VMEM)] * 5,
        out_specs=(pl.BlockSpec(memory_space=pltpu.VMEM),) * 4,
        compiler_params=pltpu.CompilerParams(vmem_limit_bytes=16 << 20),
        cost_estimate=pl.CostEstimate(
            flops=2 * 8 * rows * depth * 256, bytes_accessed=2 << 20, transcendentals=0
        ),
    )(weight, *dealt)


def attend_kernel(
    query_block,
    key_same,
    key_other,
    value_same,
    value_other,
    own_rank,
    all_rank,
    up_same,
    up_other,
    cosines,
    sines,
    attended,
    flat_query,
    flat_keyval,
    keys,
    values,
):
    step = pl.program_id(0)
    rows = query_block.shape[0]
    base = lax.axis_index("ctx") * rows
    half = lax.axis_index("ctx") // PIECES
    seat = lax.rem(lax.axis_index("ctx"), PIECES)
    dot = partial(jnp.dot, preferred_element_type=jnp.float32)

    @pl.when(step == 0)
    def _():
        for apart in range(PIECES):
            ups = up_other if apart % 2 else up_same
            for position in range(2):
                piece = ups[apart // 2, position].astype(jnp.float32)
                place = (seat ^ apart) * 2 + position
                first = pl.multiple_of(place * QUERY_ROWS, QUERY_ROWS)
                flat_query[pl.ds(first, QUERY_ROWS), :] = piece[:QUERY_ROWS]
                first = pl.multiple_of(place * KEYVAL_ROWS, KEYVAL_ROWS)
                for side in range(2):
                    begin = QUERY_ROWS + side * KEYVAL_ROWS
                    flat_keyval[side, pl.ds(first, KEYVAL_ROWS), :] = piece[
                        begin : begin + KEYVAL_ROWS
                    ]

    def turned(delta, cosine, sine):
        return delta * cosine + pltpu.roll(delta, HEAD_SIZE // 2, 1) * sine

    def up(flat, first, stride):
        return flat[pl.ds(first, ADAPTER_RANK, stride=stride), :].astype(jnp.bfloat16)

    for side in range(2):
        heads = 2 * KEYVALUE_HEADS
        key_up = up(flat_keyval.at[side], step, heads)
        value_up = up(flat_keyval.at[side], step + KEYVALUE_HEADS, heads)
        for core in range(2):
            rank = all_rank[core, :, side].reshape(PIECES // 2 * rows, 2 * ADAPTER_RANK)
            key_delta = adapter_scale * dot(rank[:, :ADAPTER_RANK], key_up)
            value_delta = adapter_scale * dot(rank[:, ADAPTER_RANK:], value_up)
            for chip in range(PIECES // 2):
                there = seat ^ (2 * chip + core)
                first = ((half ^ side) * PIECES + there) * rows
                span = pl.ds(pl.multiple_of(first, rows), rows)
                part = slice(chip * rows, (chip + 1) * rows)
                delta = turned(key_delta[part], cosines[span, :], sines[span, :])
                full = (key_other if core else key_same)[chip, side].astype(jnp.float32) + delta
                keys[span, :] = full.astype(jnp.bfloat16)
                full = (value_other if core else value_same)[chip, side].astype(jnp.float32)
                values[span, :] = (full + value_delta[part]).astype(jnp.bfloat16)
    here = pl.ds(pl.multiple_of(base, rows), rows)
    cosine = cosines[here, :]
    sine = sines[here, :]
    taken = GROUP // 2
    for first in range(0, GROUP, taken):
        weight = [up(flat_query, step * GROUP + first + head, QH) for head in range(taken)]
        deltas = adapter_scale * dot(own_rank[:, :ADAPTER_RANK], jnp.concatenate(weight, 1))
        queries = []
        for place in range(taken):
            moved = turned(deltas[:, place * HEAD_SIZE : (place + 1) * HEAD_SIZE], cosine, sine)
            span = slice((first + place) * HEAD_SIZE, (first + place + 1) * HEAD_SIZE)
            queries.append(
                (query_block[:, span].astype(jnp.float32) + moved).astype(jnp.bfloat16)
            )
        queries = jnp.concatenate(queries, 0)
        scores = lax.dot_general(
            queries, keys[...], (((1,), (1,)), ((), ())), preferred_element_type=jnp.float32
        )
        row = lax.broadcasted_iota(jnp.int32, scores.shape, 0)
        column = lax.broadcasted_iota(jnp.int32, scores.shape, 1)
        scores = jnp.where(column <= base + lax.rem(row, rows), scores, mask_floor)
        scores = scores - jnp.max(scores, axis=-1, keepdims=True)
        weights = jnp.exp2(scores * (HEAD_SIZE ** (-0.5) * math.log2(math.e)))
        divisor = jnp.sum(weights, axis=-1, keepdims=True)
        result = (dot(weights.astype(jnp.bfloat16), values[...]) / divisor).astype(jnp.bfloat16)
        for place in range(taken):
            span = slice((first + place) * HEAD_SIZE, (first + place + 1) * HEAD_SIZE)
            attended[:, span] = result[place * rows : (place + 1) * rows]


def attend(query_base, base, own_rank, all_rank, ups, cosines, sines):
    rows = query_base.shape[0]
    seq = 4 * PIECES // 2 * rows
    width = GROUP * HEAD_SIZE

    def whole(shape):
        return pl.BlockSpec(shape, lambda h: (0,) * len(shape))

    key_spec = pl.BlockSpec((PIECES // 2, 2, rows, HEAD_SIZE), lambda h: (0, 0, 0, h))
    value_spec = pl.BlockSpec(
        (PIECES // 2, 2, rows, HEAD_SIZE), lambda h: (0, 0, 0, h + KEYVALUE_HEADS)
    )
    return pl.pallas_call(
        attend_kernel,
        grid=(KEYVALUE_HEADS,),
        out_shape=jax.ShapeDtypeStruct((rows, QH * HEAD_SIZE), jnp.bfloat16),
        in_specs=[
            pl.BlockSpec((rows, width), lambda h: (0, h)),
            key_spec,
            key_spec,
            value_spec,
            value_spec,
            whole(own_rank.shape),
            whole(all_rank.shape),
            whole(ups[0].shape),
            whole(ups[1].shape),
            whole(cosines.shape),
            whole(sines.shape),
        ],
        out_specs=pl.BlockSpec((rows, width), lambda h: (0, h)),
        scratch_shapes=[
            pltpu.VMEM((2 * PIECES * QUERY_ROWS, 128), jnp.float32),
            pltpu.VMEM((2, 2 * PIECES * KEYVAL_ROWS, 128), jnp.float32),
            pltpu.VMEM((seq, HEAD_SIZE), jnp.bfloat16),
            pltpu.VMEM((seq, HEAD_SIZE), jnp.bfloat16),
        ],
        compiler_params=pltpu.CompilerParams(vmem_limit_bytes=60 << 20),
        cost_estimate=pl.CostEstimate(
            flops=48 * rows * QH * seq * HEAD_SIZE,
            bytes_accessed=10 << 20,
            transcendentals=rows * QH * seq,
        ),
    )(query_base, base[0], base[1], base[0], base[1], own_rank, all_rank, *ups, cosines, sines)


def widen_kernel(attended_rows, same, other, out_delta, down_out, up_out, attended, sem):
    fetch = pltpu.make_async_copy(attended_rows, attended, sem)
    fetch.start()
    plane = lax.axis_index("groups")
    seat = lax.rem(lax.axis_index("ctx"), PIECES)
    for apart in range(PIECES):
        pieces = other if apart % 2 else same
        for position in range(2):
            piece = pieces[apart // 2, position].astype(jnp.float32)
            place = (seat ^ apart) * 2 + (position ^ plane)
            first = place * 2 * DOWN_OUT_ROWS
            block = piece[:DOWN_OUT_ROWS]
            down_out[pl.ds(first, DOWN_OUT_ROWS, stride=2), :] = block
            down_out[pl.ds(first + 1, DOWN_OUT_ROWS, stride=2), :] = pltpu.roll(block, 64, 1)
            first = pl.multiple_of(place * UP_OUT_ROWS, UP_OUT_ROWS)
            up_out[pl.ds(first, UP_OUT_ROWS), :] = piece[DOWN_OUT_ROWS:]
    dot = partial(jnp.dot, preferred_element_type=jnp.float32)
    fetch.wait()
    rank = dot(attended[...], down_out[...].astype(jnp.bfloat16))[:, :ADAPTER_RANK]
    rank = rank.astype(jnp.bfloat16)
    blocks = D // 128
    for first in range(0, blocks, 4):
        weight = [
            up_out[pl.ds(first + block, ADAPTER_RANK, stride=blocks), :].astype(jnp.bfloat16)
            for block in range(4)
        ]
        delta = adapter_scale * dot(rank, jnp.concatenate(weight, 1))
        out_delta[:, first * 128 : (first + 4) * 128] = delta.astype(jnp.bfloat16)


def widen(attended, same, other):
    return pl.pallas_call(
        widen_kernel,
        out_shape=jax.ShapeDtypeStruct((attended.shape[0], D), jnp.bfloat16),
        in_specs=[pl.BlockSpec(memory_space=pl.ANY)] + [pl.BlockSpec(memory_space=pltpu.VMEM)] * 2,
        out_specs=pl.BlockSpec(memory_space=pltpu.VMEM),
        scratch_shapes=[
            pltpu.VMEM((QH * HEAD_SIZE, 128), jnp.float32),
            pltpu.VMEM((ADAPTER_RANK * D // 128, 128), jnp.float32),
            pltpu.VMEM(attended.shape, attended.dtype),
            pltpu.SemaphoreType.DMA,
        ],
        compiler_params=pltpu.CompilerParams(vmem_limit_bytes=60 << 20),
        cost_estimate=pl.CostEstimate(flops=1 << 27, bytes_accessed=4 << 20, transcendentals=0),
    )(attended, same, other)


def swap(block, mask):
    return lax.ppermute(block, ("groups", "ctx"), [(i, i ^ mask) for i in range(4 * PIECES)])


def direct_shards(
    normed_input, query_base, key_base, value_base, adapter_pool, stretch_adapter, adapter_owner
):
    tok_rows = normed_input.shape[0]
    ctx = lax.axis_size("ctx")
    seq = ctx * tok_rows
    blocks = [list(range(PIECES)), list(range(PIECES, 2 * PIECES))]
    half_dim = HEAD_SIZE // 2
    frequency = rope_base ** (-(jnp.arange(half_dim, dtype=jnp.float32) * 2.0) / HEAD_SIZE)
    angle = jnp.arange(seq, dtype=jnp.int32).astype(jnp.float32)[:, None] * frequency[None, :]
    cosine = jnp.cos(angle)
    sine = jnp.sin(angle)
    cosines = jnp.concatenate([cosine, cosine], 1)
    sines = jnp.concatenate([-sine, sine], 1)

    def after(block, *others):
        return lax.optimization_barrier((block, others))[0]

    def exchange(sent):
        return [swap(block, flip * PIECES) if flip else block for flip, block in enumerate(sent)]

    def along_z(block):
        return jnp.stack([block, swap(block, 4)])

    def along_x(pair):
        quad = jnp.stack([pair, swap(pair, 2)], 1)
        return quad.reshape((PIECES // 2,) + pair.shape[1:])

    elsewhere = swap(stretch_adapter, 2 * PIECES)
    packed = pack_row(adapter_pool, FIRST)
    packed_second = pack_row(adapter_pool, SECOND, packed)
    even, odd = deal(normed_input, packed)
    sibling = swap(odd, 1)
    base = jnp.concatenate([key_base, value_base], 1)
    base = jnp.stack([base, swap(base, PIECES)])

    spread = lax.all_to_all(packed, "ctx", 0, 0, axis_index_groups=blocks)
    spread = after(spread, packed_second, sibling, base)
    sent = pick(spread, stretch_adapter, elsewhere, adapter_owner, (896, KEYVAL_ROWS))
    arrived = exchange(sent)
    dealt = [after(jnp.stack([even[j], sibling[j]]), sent) for j in range(PIECES // 2)]
    dealt = [swap(block, 2 * j) if j else block for j, block in enumerate(dealt)]
    packed_second = after(packed_second, arrived[1])
    spread = lax.all_to_all(packed_second, "ctx", 0, 0, axis_index_groups=blocks)

    weight, ups = join(stretch_adapter, adapter_owner, arrived)
    partial_sums = narrow(after(weight, cosines, sines), dealt)
    back = [swap(block, 2 * j) if j else block for j, block in enumerate(partial_sums)]
    back = sum(block.astype(jnp.float32) for block in back)
    own_rank = swap(after(back[1].astype(jnp.bfloat16), spread), 1)
    own_rank = back[0] + own_rank.astype(jnp.float32)
    own_rank = own_rank.astype(jnp.bfloat16)
    all_rank = own_rank[:, ADAPTER_RANK:]
    base = along_z(after(base, *partial_sums))
    ups = along_z(after(ups, *partial_sums))
    near, far = pick(spread, stretch_adapter, elsewhere, adapter_owner, None)
    far = swap(far, PIECES)
    all_rank = jnp.stack([all_rank, swap(all_rank, PIECES)])
    all_rank = after(all_rank, ups)
    ups = along_x(after(ups, all_rank))
    base = along_x(after(base, all_rank))
    own, across = settle(stretch_adapter, elsewhere, adapter_owner, near, far)
    all_rank = jnp.stack([swap(all_rank, apart) if apart else all_rank for apart in (0, 2, 4, 6)])
    all_rank = after(all_rank, across, ups)
    base = after(base, all_rank)
    ends = jnp.stack([own, swap(across, 2 * PIECES)])
    all_rank = jnp.stack([all_rank, swap(all_rank, 1)])
    ends = jnp.stack([swap(ends, apart) if apart else ends for apart in (0, 2, 4, 6)])
    base = (base, swap(base, 1))
    ups = (ups, swap(ups, 1))
    ends = (ends, swap(ends, 1))

    attended = attend(query_base, base, own_rank, all_rank, ups, cosines, sines)
    return attended, widen(attended, *ends)


def shards(normed_input, query_base, key_base, value_base, adapter_pool, stretch_adapter, owner):
    fits = (
        lax.axis_size("groups") == 2
        and lax.axis_size("ctx") == 2 * PIECES
        and normed_input.shape[0] * PIECES == BLOCK_TOKENS
        and adapter_pool.shape[0] == 1
    )
    plan = direct_shards if fits else spread_shards
    return plan(
        normed_input, query_base, key_base, value_base, adapter_pool, stretch_adapter, owner
    )


def solution(mesh):
    placed = (
        P(("groups", "ctx"), None),
        P(("groups", "ctx"), None),
        P(("groups", "ctx"), None),
        P(("groups", "ctx"), None),
        P("ctx", None),
        P("groups"),
        P(),
    )
    return jax.shard_map(
        shards,
        mesh=mesh,
        in_specs=placed,
        out_specs=(P(("groups", "ctx"), None), P(("groups", "ctx"), None)),
        check_vma=False,
    )
```

```python
from functools import partial
import math

import jax
import jax.numpy as jnp
from jax import lax
from jax.experimental import pallas as pl
from jax.experimental.pallas import tpu as pltpu
from jax.sharding import PartitionSpec as P

D = 8192
QH = 32
KEYVALUE_HEADS = 4
HEAD_SIZE = 128
ADAPTER_RANK = 64
BLOCK_TOKENS = 512
QKV_POOL = 1900544


adapter_scale = 2.0
rope_base = 500000.0
mask_floor = -1e30


def from_partner(block, axis, apart):
    count = lax.axis_size(axis)
    route = []
    for low in range(count):
        high = low | 1 << apart
        if high != low and high < count:
            route += [(low, high), (high, low)]
    return lax.ppermute(block, axis, route)


def rotate(delta, token_positions, heads):
    half_dim = HEAD_SIZE // 2
    frequency = rope_base ** (-(jnp.arange(half_dim, dtype=jnp.float32) * 2.0) / HEAD_SIZE)
    angle = token_positions.astype(jnp.float32)[:, None] * frequency[None, :]
    cosine = jnp.cos(angle)[:, None, :]
    sine_part = jnp.sin(angle)[:, None, :]
    shaped = delta.reshape(delta.shape[0], heads, HEAD_SIZE)
    first_half = shaped[..., :half_dim]
    second_half = shaped[..., half_dim:]
    joined = jnp.concatenate(
        [
            first_half * cosine - second_half * sine_part,
            second_half * cosine + first_half * sine_part,
        ],
        -1,
    )
    return joined.reshape(delta.shape[0], heads * HEAD_SIZE)


def project_heads(
    narrow_product, query_row_block, key_row_block, value_row_block, upper_part, token_positions
):
    query_up_weight = upper_part[: ADAPTER_RANK * QH * HEAD_SIZE].reshape(
        ADAPTER_RANK, QH * HEAD_SIZE
    )
    keyvalue_up_weight = upper_part[ADAPTER_RANK * QH * HEAD_SIZE :].reshape(
        ADAPTER_RANK, 2 * KEYVALUE_HEADS * HEAD_SIZE
    )
    query_correction = adapter_scale * jnp.dot(
        narrow_product[:, :ADAPTER_RANK], query_up_weight, preferred_element_type=jnp.float32
    )
    key_correction = adapter_scale * jnp.dot(
        narrow_product[:, ADAPTER_RANK : 2 * ADAPTER_RANK],
        keyvalue_up_weight[:, : KEYVALUE_HEADS * HEAD_SIZE],
        preferred_element_type=jnp.float32,
    )
    value_correction = adapter_scale * jnp.dot(
        narrow_product[:, 2 * ADAPTER_RANK :],
        keyvalue_up_weight[:, KEYVALUE_HEADS * HEAD_SIZE :],
        preferred_element_type=jnp.float32,
    )
    queries = (
        query_row_block.astype(jnp.float32) + rotate(query_correction, token_positions, QH)
    ).astype(jnp.bfloat16)
    new_keys = (
        key_row_block.astype(jnp.float32) + rotate(key_correction, token_positions, KEYVALUE_HEADS)
    ).astype(jnp.bfloat16)
    new_values = (value_row_block.astype(jnp.float32) + value_correction).astype(jnp.bfloat16)
    return (queries, new_keys, new_values)


def output_delta(attended_rows, out_part):
    down_out = out_part[: QH * HEAD_SIZE * ADAPTER_RANK].reshape(QH * HEAD_SIZE, ADAPTER_RANK)
    raised_output = out_part[QH * HEAD_SIZE * ADAPTER_RANK :].reshape(ADAPTER_RANK, D)
    narrow_product = jnp.dot(attended_rows, down_out, preferred_element_type=jnp.float32).astype(
        jnp.bfloat16
    )
    return (
        adapter_scale * jnp.dot(narrow_product, raised_output, preferred_element_type=jnp.float32)
    ).astype(jnp.bfloat16)


def head_major(query_row_block):
    count_rows = query_row_block.shape[0]
    group_size = QH // KEYVALUE_HEADS
    return (
        query_row_block.reshape(count_rows, KEYVALUE_HEADS, group_size, HEAD_SIZE)
        .transpose(1, 2, 0, 3)
        .reshape(KEYVALUE_HEADS, group_size * count_rows, HEAD_SIZE)
    )


def row_major(head_rows, count_rows):
    group_size = QH // KEYVALUE_HEADS
    return (
        head_rows.reshape(KEYVALUE_HEADS, group_size, count_rows, HEAD_SIZE)
        .transpose(2, 0, 1, 3)
        .reshape(count_rows, QH * HEAD_SIZE)
    )


def online_update(current, queries, query_pos, key_slice, value_slice, key_start):
    run_max, run_sum, run_acc = current
    scores = jnp.einsum(
        "hqd,khd->hqk", queries, key_slice, preferred_element_type=jnp.float32
    ) * HEAD_SIZE ** (-0.5)
    key_pos = key_start + jnp.arange(key_slice.shape[0], dtype=jnp.int32)
    allowed = (query_pos[:, None] >= key_pos[None, :])[None]
    new_max = jnp.maximum(run_max, jnp.max(jnp.where(allowed, scores, mask_floor), axis=-1))
    weights = jnp.where(allowed, jnp.exp(scores - new_max[..., None]), 0.0)
    rescale = jnp.exp(run_max - new_max)
    new_sum = run_sum * rescale + jnp.sum(weights, axis=-1)
    new_acc = run_acc * rescale[..., None] + jnp.einsum(
        "hqk,khd->hqd",
        weights.astype(jnp.bfloat16),
        value_slice,
        preferred_element_type=jnp.float32,
    )
    return (new_max, new_sum, new_acc)


def unchanged(current):
    return current


def fold_keys(carry_state, shard_part, prepared):
    key_row_block, value_row_block = shard_part
    key_count = key_row_block.shape[0]
    sub_width = math.gcd(key_count, 1024)
    key_heads = key_row_block.reshape(key_count // sub_width, sub_width, KEYVALUE_HEADS, HEAD_SIZE)
    value_heads = value_row_block.reshape(
        key_count // sub_width, sub_width, KEYVALUE_HEADS, HEAD_SIZE
    )

    def one_step(sub_index, carried):
        key_start = sub_index * sub_width
        key_slice = lax.dynamic_index_in_dim(key_heads, sub_index, 0, keepdims=False)
        value_slice = lax.dynamic_index_in_dim(value_heads, sub_index, 0, keepdims=False)
        updated = []
        for (queries, query_pos), running in zip(prepared, carried):
            advance = partial(
                online_update,
                queries=queries,
                query_pos=query_pos,
                key_slice=key_slice,
                value_slice=value_slice,
                key_start=key_start,
            )
            updated.append(lax.cond(key_start <= jnp.max(query_pos), advance, unchanged, running))
        return tuple(updated)

    return lax.fori_loop(0, key_count // sub_width, one_step, carry_state)


def finish_block(result, count_rows):
    run_max, run_sum, run_acc = result
    divisor = jnp.where(run_sum > 0.0, run_sum, 1.0)
    return row_major(run_acc / divisor[..., None], count_rows).astype(jnp.bfloat16)


def spread_shards(
    normed_input, query_base, key_base, value_base, adapter_pool, stretch_adapter, adapter_owner
):
    cycle_size = lax.axis_size("ctx")
    my_index = lax.axis_index("ctx")
    tok_rows = normed_input.shape[0]
    token_positions = my_index * tok_rows + jnp.arange(tok_rows, dtype=jnp.int32)
    device_ids = jnp.arange(cycle_size, dtype=jnp.int32)
    stretch_of = device_ids * tok_rows // BLOCK_TOKENS
    stretch_ids = jnp.arange(stretch_adapter.shape[0], dtype=jnp.int32)
    adapter_of = jnp.sum(
        jnp.where(stretch_of[:, None] == stretch_ids[None, :], stretch_adapter[None, :], 0), axis=1
    )
    adapter_ids = jnp.arange(adapter_owner.shape[0], dtype=jnp.int32)
    slot_of = jnp.sum(
        jnp.where(adapter_of[:, None] == adapter_ids[None, :], adapter_owner[None, :], 0), axis=1
    )
    down_size = 3 * ADAPTER_RANK * D
    group_count = BLOCK_TOKENS // tok_rows
    levels = group_count.bit_length() - 1
    local_index = my_index % group_count
    col_width = D // group_count
    piece_len = down_size // (group_count * cycle_size)
    pool_rows = adapter_pool.shape[0]
    down_shaped = adapter_pool[:, :down_size].reshape(pool_rows, group_count, cycle_size, piece_len)
    spread_down = lax.all_to_all(down_shaped, "ctx", split_axis=2, concat_axis=0, tiled=True)
    flat_down = spread_down.reshape(-1, piece_len)
    wanted = jnp.take(flat_down, slot_of * group_count + device_ids % group_count, axis=0)[
        :, None, :
    ]
    down_slice = lax.all_to_all(wanted, "ctx", split_axis=0, concat_axis=1, tiled=True).reshape(
        col_width, 3 * ADAPTER_RANK
    )
    spread_rest = lax.all_to_all(
        adapter_pool[:, down_size:], "ctx", split_axis=1, concat_axis=0, tiled=True
    )
    rest_row = lax.all_to_all(
        jnp.take(spread_rest, slot_of, axis=0), "ctx", split_axis=0, concat_axis=1, tiled=True
    )[0]
    upper_part = rest_row[: QKV_POOL - down_size]
    out_part = rest_row[QKV_POOL - down_size :]
    pieces = normed_input.reshape(tok_rows, group_count, col_width)
    slice_order = jnp.bitwise_xor(local_index, jnp.arange(group_count, dtype=jnp.int32))
    moving = jnp.take(pieces, slice_order, axis=1).transpose(1, 0, 2)
    for level in range(levels):
        shaped = moving.reshape(group_count >> level + 1, 2, 1 << level, tok_rows, col_width)
        arrived = from_partner(shaped[:, 1], "ctx", level)
        moving = jnp.stack([shaped[:, 0], arrived], 1).reshape(group_count, tok_rows, col_width)
    partial_rows = jnp.dot(
        moving.reshape(group_count * tok_rows, col_width),
        down_slice,
        preferred_element_type=jnp.float32,
    ).reshape(group_count, tok_rows, 3 * ADAPTER_RANK)
    for level in reversed(range(levels)):
        halves = partial_rows.reshape(2, partial_rows.shape[0] // 2, tok_rows, 3 * ADAPTER_RANK)
        partial_rows = halves[0] + from_partner(
            halves[1].astype(jnp.bfloat16), "ctx", level
        ).astype(jnp.float32)
    narrow_product = partial_rows[0].astype(jnp.bfloat16)
    queries, new_keys, new_values = project_heads(
        narrow_product, query_base, key_base, value_base, upper_part, token_positions
    )
    group_size = QH // KEYVALUE_HEADS
    blocks = [(queries, token_positions)]
    prepared = [
        (head_major(block_q), jnp.tile(block_pos, group_size)) for block_q, block_pos in blocks
    ]
    initial = tuple(
        (
            (
                jnp.full((KEYVALUE_HEADS, head_q.shape[1]), mask_floor, jnp.float32),
                jnp.zeros((KEYVALUE_HEADS, head_q.shape[1]), jnp.float32),
                jnp.zeros((KEYVALUE_HEADS, head_q.shape[1], HEAD_SIZE), jnp.float32),
            )
            for head_q, block_pos in prepared
        )
    )
    finals = fold_keys(
        initial,
        (
            lax.all_gather(new_keys, "ctx", axis=0, tiled=True),
            lax.all_gather(new_values, "ctx", axis=0, tiled=True),
        ),
        prepared,
    )
    attended = finish_block(finals[0], tok_rows)
    out_delta = output_delta(attended, out_part)
    return (attended, out_delta)


PIECES = 8
GROUP = QH // KEYVALUE_HEADS
FIRST = ((0, 12288), (12288, 2048), (14336, 512))
SECOND = ((14848, 2048), (16896, 4096))
DOWN_ROWS, QUERY_ROWS, KEYVAL_ROWS, DOWN_OUT_ROWS, UP_OUT_ROWS = 768, 128, 32, 128, 256
UP_ROWS = QUERY_ROWS + 2 * KEYVAL_ROWS


def pack_kernel(sections, pool, *refs):
    out, buffers, sems = refs[-3:]
    plane = lax.axis_index("groups")
    slabs, slab_rows = out.shape[:2]

    def copies(slab):
        listed = []
        offset = 0
        for first, rows in sections:
            share = rows // (2 * PIECES)
            begin = first + (slab * 2 + plane) * share
            listed.append(
                pltpu.make_async_copy(
                    pool.at[:, pl.ds(pl.multiple_of(begin * 128, 2048), share * 128)],
                    buffers.at[slab, :, pl.ds(offset, share * 128)],
                    sems.at[slab, len(listed)],
                )
            )
            offset += share * 128
        return listed

    for slab in range(slabs):
        for copy in copies(slab):
            copy.start()

    def step(slab, carried):
        for copy in copies(slab):
            copy.wait()

        def chunk(index, inner):
            line = buffers[slab, :, pl.ds(pl.multiple_of(index * 2048, 2048), 2048)]
            block = line.astype(jnp.float32).reshape(16, 128).astype(jnp.bfloat16)
            out[slab, pl.ds(pl.multiple_of(index * 16, 16), 16), :] = block
            return inner

        lax.fori_loop(0, slab_rows // 16, chunk, 0, unroll=8)
        return carried

    lax.fori_loop(0, slabs, step, 0)


def pack_row(pool, sections, *after):
    slab_rows = sum(rows for _, rows in sections) // (2 * PIECES)
    return pl.pallas_call(
        partial(pack_kernel, sections),
        out_shape=jax.ShapeDtypeStruct((PIECES, slab_rows, 128), jnp.bfloat16),
        in_specs=[pl.BlockSpec(memory_space=pl.ANY)] * (1 + len(after)),
        out_specs=pl.BlockSpec(memory_space=pltpu.VMEM),
        scratch_shapes=[
            pltpu.VMEM((PIECES, 1, slab_rows * 128), jnp.bfloat16),
            pltpu.SemaphoreType.DMA((PIECES, len(sections))),
        ],
        compiler_params=pltpu.CompilerParams(vmem_limit_bytes=60 << 20),
        cost_estimate=pl.CostEstimate(flops=0, bytes_accessed=8 << 20, transcendentals=0),
    )(pool, *after)


def pick_kernel(mirrored, here, there, owner, spread, *refs):
    sems = refs[-1]
    outs = refs[:4] if len(refs) > 3 else [refs[flip % 2].at[flip // 2] for flip in range(4)]
    half = lax.axis_index("ctx") // PIECES
    rows = spread.shape[1]
    copies = []
    for flip, out in enumerate(outs):
        wishes = there if flip >= 2 else here
        block = half ^ (flip & 1)
        row = lax.rem(owner[wishes[block]], PIECES)
        copies.append(
            pltpu.make_async_copy(spread.at[row], out.at[pl.ds(0, rows)], sems.at[flip, 0])
        )
        if mirrored is not None:
            first, count = mirrored
            row = lax.rem(owner[wishes[1 - block]], PIECES)
            copies.append(
                pltpu.make_async_copy(
                    spread.at[row, pl.ds(first, count)],
                    out.at[pl.ds(rows, count)],
                    sems.at[flip, 1],
                )
            )
    for copy in copies:
        copy.start()
    for copy in copies:
        copy.wait()


def pick(spread, here, there, owner, mirrored):
    rows = spread.shape[1] + (mirrored[1] if mirrored else 0)
    shape, count = ((rows, 128), 4) if mirrored else ((2, rows, 128), 2)
    slab = jax.ShapeDtypeStruct(shape, jnp.bfloat16)
    return pl.pallas_call(
        partial(pick_kernel, mirrored),
        out_shape=(slab,) * count,
        in_specs=[pl.BlockSpec(memory_space=pltpu.SMEM)] * 3 + [pl.BlockSpec(memory_space=pl.ANY)],
        out_specs=(pl.BlockSpec(memory_space=pltpu.VMEM),) * count,
        scratch_shapes=[pltpu.SemaphoreType.DMA((4, 2))],
        compiler_params=pltpu.CompilerParams(vmem_limit_bytes=16 << 20),
        cost_estimate=pl.CostEstimate(flops=0, bytes_accessed=2 << 20, transcendentals=0),
    )(here, there, owner, spread)


def deal_kernel(rows, even, odd, sems):
    seat = lax.rem(lax.axis_index("ctx"), PIECES)
    width = rows.shape[1] // PIECES
    copies = []
    for apart in range(PIECES):
        first = pl.multiple_of((seat ^ apart) * width, width)
        target = (odd if apart % 2 else even).at[apart // 2]
        copies.append(
            pltpu.make_async_copy(rows.at[:, pl.ds(first, width)], target, sems.at[apart])
        )
    for copy in copies:
        copy.start()
    for copy in copies:
        copy.wait()


def deal(rows, *after):
    slab = jax.ShapeDtypeStruct((PIECES // 2, rows.shape[0], rows.shape[1] // PIECES), rows.dtype)

    def kernel(rows, *refs):
        deal_kernel(rows, *refs[-3:])

    return pl.pallas_call(
        kernel,
        out_shape=(slab, slab),
        in_specs=[pl.BlockSpec(memory_space=pl.ANY)] * (1 + len(after)),
        out_specs=(pl.BlockSpec(memory_space=pltpu.VMEM),) * 2,
        scratch_shapes=[pltpu.SemaphoreType.DMA((PIECES,))],
        compiler_params=pltpu.CompilerParams(vmem_limit_bytes=16 << 20),
        cost_estimate=pl.CostEstimate(flops=0, bytes_accessed=2 << 20, transcendentals=0),
    )(rows, *after)


def nearest(here, owner, block):
    half = lax.axis_index("ctx") // PIECES
    return owner[here[block]] // PIECES == half


def choose(close, arrived, put):
    plane = lax.axis_index("groups")

    @pl.when(close)
    def _():
        put(arrived[0], plane)
        put(arrived[2], 1 - plane)

    @pl.when(jnp.logical_not(close))
    def _():
        put(arrived[1], plane)
        put(arrived[3], 1 - plane)


def join_kernel(here, owner, *refs):
    arrived, (weight, ups), (flat, left, right) = refs[:4], refs[4:6], refs[6:]
    half = lax.axis_index("ctx") // PIECES
    split = DOWN_ROWS + QUERY_ROWS + KEYVAL_ROWS

    def put_own(source, position):
        first = pl.multiple_of(position * DOWN_ROWS, DOWN_ROWS)
        flat[pl.ds(first, DOWN_ROWS), :] = source[:DOWN_ROWS, :].astype(jnp.float32)
        ups[position, : UP_ROWS - KEYVAL_ROWS, :] = source[DOWN_ROWS:split, :]

    def put_mirrored(source, position):
        ups[position, UP_ROWS - KEYVAL_ROWS :, :] = source[split:, :]

    choose(nearest(here, owner, half), arrived, put_own)
    choose(nearest(here, owner, 1 - half), arrived, put_mirrored)

    third = flat.shape[0] // 3
    one = flat[pl.ds(0, third, stride=3), :]
    two = pltpu.roll(flat[pl.ds(1, third, stride=3), :], 64, 1)
    three = pltpu.roll(flat[pl.ds(2, third, stride=3), :], 64, 1)
    lane = lax.broadcasted_iota(jnp.int32, one.shape, 1)
    left[pl.ds(0, third, stride=2), :] = one
    left[pl.ds(1, third, stride=2), :] = jnp.where(lane < 64, two, three)
    right[pl.ds(0, third, stride=2), :] = pltpu.roll(two, 64, 1)
    right[pl.ds(1, third, stride=2), :] = three
    weight[...] = jnp.concatenate([left[...], right[...]], 1).astype(jnp.bfloat16)


def join(here, owner, arrived):
    depth = D // PIECES
    return pl.pallas_call(
        join_kernel,
        out_shape=(
            jax.ShapeDtypeStruct((depth, 256), jnp.bfloat16),
            jax.ShapeDtypeStruct((2, UP_ROWS, 128), jnp.bfloat16),
        ),
        in_specs=[pl.BlockSpec(memory_space=pltpu.SMEM)] * 2
        + [pl.BlockSpec(memory_space=pltpu.VMEM)] * 4,
        out_specs=(pl.BlockSpec(memory_space=pltpu.VMEM),) * 2,
        scratch_shapes=[
            pltpu.VMEM((2 * DOWN_ROWS, 128), jnp.float32),
            pltpu.VMEM((depth, 128), jnp.float32),
            pltpu.VMEM((depth, 128), jnp.float32),
        ],
        compiler_params=pltpu.CompilerParams(vmem_limit_bytes=16 << 20),
        cost_estimate=pl.CostEstimate(flops=0, bytes_accessed=96 << 20, transcendentals=0),
    )(here, owner, *arrived)


def settle_kernel(here, there, owner, near, far, own, across):
    half = lax.axis_index("ctx") // PIECES
    for number, (wishes, out) in enumerate(((here, own), (there, across))):
        close = nearest(wishes, owner, half)

        @pl.when(close)
        def _():
            out[...] = near[number]

        @pl.when(jnp.logical_not(close))
        def _():
            out[...] = far[number]


def settle(here, there, owner, near, far):
    slab = jax.ShapeDtypeStruct(near.shape[1:], jnp.bfloat16)
    return pl.pallas_call(
        settle_kernel,
        out_shape=(slab, slab),
        in_specs=[pl.BlockSpec(memory_space=pltpu.SMEM)] * 3
        + [pl.BlockSpec(memory_space=pltpu.VMEM)] * 2,
        out_specs=(pl.BlockSpec(memory_space=pltpu.VMEM),) * 2,
        compiler_params=pltpu.CompilerParams(vmem_limit_bytes=16 << 20),
        cost_estimate=pl.CostEstimate(flops=0, bytes_accessed=1 << 20, transcendentals=0),
    )(here, there, owner, near, far)


def narrow_kernel(weight, *refs):
    for block, out in zip(refs[:4], refs[4:]):
        sides, rows, depth = block.shape
        product = jnp.dot(
            block[...].reshape(sides * rows, depth),
            weight[...],
            preferred_element_type=jnp.float32,
        )
        out[...] = product[:, : 3 * ADAPTER_RANK].reshape(out.shape).astype(jnp.bfloat16)


def narrow(weight, dealt):
    sides, rows, depth = dealt[0].shape
    partial_sums = jax.ShapeDtypeStruct((sides, rows, 3 * ADAPTER_RANK), jnp.bfloat16)
    return pl.pallas_call(
        narrow_kernel,
        out_shape=(partial_sums,) * 4,
        in_specs=[pl.BlockSpec(memory_space=pltpu.VMEM)] * 5,
        out_specs=(pl.BlockSpec(memory_space=pltpu.VMEM),) * 4,
        compiler_params=pltpu.CompilerParams(vmem_limit_bytes=16 << 20),
        cost_estimate=pl.CostEstimate(
            flops=2 * 8 * rows * depth * 256, bytes_accessed=2 << 20, transcendentals=0
        ),
    )(weight, *dealt)


def attend_kernel(
    query_block,
    key_same,
    key_other,
    value_same,
    value_other,
    own_rank,
    all_rank,
    up_same,
    up_other,
    cosines,
    sines,
    attended,
    flat_query,
    flat_keyval,
    keys,
    values,
):
    step = pl.program_id(0)
    rows = query_block.shape[0]
    base = lax.axis_index("ctx") * rows
    half = lax.axis_index("ctx") // PIECES
    seat = lax.rem(lax.axis_index("ctx"), PIECES)
    dot = partial(jnp.dot, preferred_element_type=jnp.float32)

    @pl.when(step == 0)
    def _():
        for apart in range(PIECES):
            ups = up_other if apart % 2 else up_same
            for position in range(2):
                piece = ups[apart // 2, position].astype(jnp.float32)
                place = (seat ^ apart) * 2 + position
                first = pl.multiple_of(place * QUERY_ROWS, QUERY_ROWS)
                flat_query[pl.ds(first, QUERY_ROWS), :] = piece[:QUERY_ROWS]
                first = pl.multiple_of(place * KEYVAL_ROWS, KEYVAL_ROWS)
                for side in range(2):
                    begin = QUERY_ROWS + side * KEYVAL_ROWS
                    flat_keyval[side, pl.ds(first, KEYVAL_ROWS), :] = piece[
                        begin : begin + KEYVAL_ROWS
                    ]

    def turned(delta, cosine, sine):
        return delta * cosine + pltpu.roll(delta, HEAD_SIZE // 2, 1) * sine

    def up(flat, first, stride):
        return flat[pl.ds(first, ADAPTER_RANK, stride=stride), :].astype(jnp.bfloat16)

    for side in range(2):
        heads = 2 * KEYVALUE_HEADS
        key_up = up(flat_keyval.at[side], step, heads)
        value_up = up(flat_keyval.at[side], step + KEYVALUE_HEADS, heads)
        for core in range(2):
            rank = all_rank[core, :, side].reshape(PIECES // 2 * rows, 2 * ADAPTER_RANK)
            key_delta = adapter_scale * dot(rank[:, :ADAPTER_RANK], key_up)
            value_delta = adapter_scale * dot(rank[:, ADAPTER_RANK:], value_up)
            for chip in range(PIECES // 2):
                there = seat ^ (2 * chip + core)
                first = ((half ^ side) * PIECES + there) * rows
                span = pl.ds(pl.multiple_of(first, rows), rows)
                part = slice(chip * rows, (chip + 1) * rows)
                delta = turned(key_delta[part], cosines[span, :], sines[span, :])
                full = (key_other if core else key_same)[chip, side].astype(jnp.float32) + delta
                keys[span, :] = full.astype(jnp.bfloat16)
                full = (value_other if core else value_same)[chip, side].astype(jnp.float32)
                values[span, :] = (full + value_delta[part]).astype(jnp.bfloat16)
    here = pl.ds(pl.multiple_of(base, rows), rows)
    cosine = cosines[here, :]
    sine = sines[here, :]
    taken = GROUP // 2
    for first in range(0, GROUP, taken):
        weight = [up(flat_query, step * GROUP + first + head, QH) for head in range(taken)]
        deltas = adapter_scale * dot(own_rank[:, :ADAPTER_RANK], jnp.concatenate(weight, 1))
        queries = []
        for place in range(taken):
            moved = turned(deltas[:, place * HEAD_SIZE : (place + 1) * HEAD_SIZE], cosine, sine)
            span = slice((first + place) * HEAD_SIZE, (first + place + 1) * HEAD_SIZE)
            queries.append(
                (query_block[:, span].astype(jnp.float32) + moved).astype(jnp.bfloat16)
            )
        queries = jnp.concatenate(queries, 0)
        scores = lax.dot_general(
            queries, keys[...], (((1,), (1,)), ((), ())), preferred_element_type=jnp.float32
        )
        row = lax.broadcasted_iota(jnp.int32, scores.shape, 0)
        column = lax.broadcasted_iota(jnp.int32, scores.shape, 1)
        scores = jnp.where(column <= base + lax.rem(row, rows), scores, mask_floor)
        scores = scores - jnp.max(scores, axis=-1, keepdims=True)
        weights = jnp.exp2(scores * (HEAD_SIZE ** (-0.5) * math.log2(math.e)))
        divisor = jnp.sum(weights, axis=-1, keepdims=True)
        result = (dot(weights.astype(jnp.bfloat16), values[...]) / divisor).astype(jnp.bfloat16)
        for place in range(taken):
            span = slice((first + place) * HEAD_SIZE, (first + place + 1) * HEAD_SIZE)
            attended[:, span] = result[place * rows : (place + 1) * rows]


def attend(query_base, base, own_rank, all_rank, ups, cosines, sines):
    rows = query_base.shape[0]
    seq = 4 * PIECES // 2 * rows
    width = GROUP * HEAD_SIZE

    def whole(shape):
        return pl.BlockSpec(shape, lambda h: (0,) * len(shape))

    key_spec = pl.BlockSpec((PIECES // 2, 2, rows, HEAD_SIZE), lambda h: (0, 0, 0, h))
    value_spec = pl.BlockSpec(
        (PIECES // 2, 2, rows, HEAD_SIZE), lambda h: (0, 0, 0, h + KEYVALUE_HEADS)
    )
    return pl.pallas_call(
        attend_kernel,
        grid=(KEYVALUE_HEADS,),
        out_shape=jax.ShapeDtypeStruct((rows, QH * HEAD_SIZE), jnp.bfloat16),
        in_specs=[
            pl.BlockSpec((rows, width), lambda h: (0, h)),
            key_spec,
            key_spec,
            value_spec,
            value_spec,
            whole(own_rank.shape),
            whole(all_rank.shape),
            whole(ups[0].shape),
            whole(ups[1].shape),
            whole(cosines.shape),
            whole(sines.shape),
        ],
        out_specs=pl.BlockSpec((rows, width), lambda h: (0, h)),
        scratch_shapes=[
            pltpu.VMEM((2 * PIECES * QUERY_ROWS, 128), jnp.float32),
            pltpu.VMEM((2, 2 * PIECES * KEYVAL_ROWS, 128), jnp.float32),
            pltpu.VMEM((seq, HEAD_SIZE), jnp.bfloat16),
            pltpu.VMEM((seq, HEAD_SIZE), jnp.bfloat16),
        ],
        compiler_params=pltpu.CompilerParams(vmem_limit_bytes=60 << 20),
        cost_estimate=pl.CostEstimate(
            flops=48 * rows * QH * seq * HEAD_SIZE,
            bytes_accessed=10 << 20,
            transcendentals=rows * QH * seq,
        ),
    )(query_base, base[0], base[1], base[0], base[1], own_rank, all_rank, *ups, cosines, sines)


def widen_kernel(attended, same, other, out_delta, down_out, up_out):
    plane = lax.axis_index("groups")
    seat = lax.rem(lax.axis_index("ctx"), PIECES)
    for apart in range(PIECES):
        pieces = other if apart % 2 else same
        for position in range(2):
            piece = pieces[apart // 2, position].astype(jnp.float32)
            place = (seat ^ apart) * 2 + (position ^ plane)
            first = place * 2 * DOWN_OUT_ROWS
            block = piece[:DOWN_OUT_ROWS]
            down_out[pl.ds(first, DOWN_OUT_ROWS, stride=2), :] = block
            down_out[pl.ds(first + 1, DOWN_OUT_ROWS, stride=2), :] = pltpu.roll(block, 64, 1)
            first = pl.multiple_of(place * UP_OUT_ROWS, UP_OUT_ROWS)
            up_out[pl.ds(first, UP_OUT_ROWS), :] = piece[DOWN_OUT_ROWS:]
    dot = partial(jnp.dot, preferred_element_type=jnp.float32)
    rank = dot(attended[...], down_out[...].astype(jnp.bfloat16))[:, :ADAPTER_RANK]
    rank = rank.astype(jnp.bfloat16)
    blocks = D // 128
    for first in range(0, blocks, 4):
        weight = [
            up_out[pl.ds(first + block, ADAPTER_RANK, stride=blocks), :].astype(jnp.bfloat16)
            for block in range(4)
        ]
        delta = adapter_scale * dot(rank, jnp.concatenate(weight, 1))
        out_delta[:, first * 128 : (first + 4) * 128] = delta.astype(jnp.bfloat16)


def widen(attended, same, other):
    return pl.pallas_call(
        widen_kernel,
        out_shape=jax.ShapeDtypeStruct((attended.shape[0], D), jnp.bfloat16),
        in_specs=[pl.BlockSpec(memory_space=pltpu.VMEM)] * 3,
        out_specs=pl.BlockSpec(memory_space=pltpu.VMEM),
        scratch_shapes=[
            pltpu.VMEM((QH * HEAD_SIZE, 128), jnp.float32),
            pltpu.VMEM((ADAPTER_RANK * D // 128, 128), jnp.float32),
        ],
        compiler_params=pltpu.CompilerParams(vmem_limit_bytes=32 << 20),
        cost_estimate=pl.CostEstimate(flops=1 << 27, bytes_accessed=4 << 20, transcendentals=0),
    )(attended, same, other)


def swap(block, mask):
    return lax.ppermute(block, ("groups", "ctx"), [(i, i ^ mask) for i in range(4 * PIECES)])


def direct_shards(
    normed_input, query_base, key_base, value_base, adapter_pool, stretch_adapter, adapter_owner
):
    tok_rows = normed_input.shape[0]
    ctx = lax.axis_size("ctx")
    seq = ctx * tok_rows
    blocks = [list(range(PIECES)), list(range(PIECES, 2 * PIECES))]
    half_dim = HEAD_SIZE // 2
    frequency = rope_base ** (-(jnp.arange(half_dim, dtype=jnp.float32) * 2.0) / HEAD_SIZE)
    angle = jnp.arange(seq, dtype=jnp.int32).astype(jnp.float32)[:, None] * frequency[None, :]
    cosine = jnp.cos(angle)
    sine = jnp.sin(angle)
    cosines = jnp.concatenate([cosine, cosine], 1)
    sines = jnp.concatenate([-sine, sine], 1)

    def after(block, *others):
        return lax.optimization_barrier((block, others))[0]

    def exchange(sent):
        return [swap(block, flip * PIECES) if flip else block for flip, block in enumerate(sent)]

    def along_z(block):
        return jnp.stack([block, swap(block, 4)])

    def along_x(pair):
        quad = jnp.stack([pair, swap(pair, 2)], 1)
        return quad.reshape((PIECES // 2,) + pair.shape[1:])

    elsewhere = swap(stretch_adapter, 2 * PIECES)
    packed = pack_row(adapter_pool, FIRST)
    packed_second = pack_row(adapter_pool, SECOND, packed)
    even, odd = deal(normed_input, packed)
    sibling = swap(odd, 1)
    base = jnp.concatenate([key_base, value_base], 1)
    base = along_x(along_z(jnp.stack([base, swap(base, PIECES)])))

    spread = lax.all_to_all(packed, "ctx", 0, 0, axis_index_groups=blocks)
    spread = after(spread, packed_second, sibling, base)
    sent = pick(spread, stretch_adapter, elsewhere, adapter_owner, (896, KEYVAL_ROWS))
    arrived = exchange(sent)
    dealt = [after(jnp.stack([even[j], sibling[j]]), sent) for j in range(PIECES // 2)]
    dealt = [swap(block, 2 * j) if j else block for j, block in enumerate(dealt)]
    packed_second = after(packed_second, sent)
    spread = lax.all_to_all(packed_second, "ctx", 0, 0, axis_index_groups=blocks)

    weight, ups = join(stretch_adapter, adapter_owner, arrived)
    partial_sums = narrow(after(weight, spread, cosines, sines), dealt)
    back = [swap(block, 2 * j) if j else block for j, block in enumerate(partial_sums)]
    back = sum(block.astype(jnp.float32) for block in back)
    own_rank = swap(back[1].astype(jnp.bfloat16), 1)
    own_rank = back[0] + own_rank.astype(jnp.float32)
    own_rank = own_rank.astype(jnp.bfloat16)
    ups = along_z(after(ups, *partial_sums))
    near, far = pick(
        after(spread, *partial_sums), stretch_adapter, elsewhere, adapter_owner, None
    )
    far = swap(far, PIECES)
    base = after(base, *partial_sums)
    base = (base, swap(base, 1))
    all_rank = after(own_rank[:, ADAPTER_RANK:], ups)
    all_rank = jnp.stack([all_rank, swap(all_rank, PIECES)])
    own, across = settle(stretch_adapter, elsewhere, adapter_owner, near, far)
    all_rank = after(all_rank, across)
    ups = along_x(after(ups, all_rank))
    ends = jnp.stack([own, swap(across, 2 * PIECES)])
    all_rank = jnp.stack([swap(all_rank, apart) if apart else all_rank for apart in (0, 2, 4, 6)])
    all_rank = after(all_rank, ups, ends)
    ends = jnp.stack([swap(ends, apart) if apart else ends for apart in (0, 2, 4, 6)])
    all_rank = jnp.stack([all_rank, swap(all_rank, 1)])
    ups = (ups, swap(ups, 1))
    ends = (ends, swap(ends, 1))

    attended = attend(query_base, base, own_rank, all_rank, ups, cosines, sines)
    return attended, widen(attended, *ends)


def shards(normed_input, query_base, key_base, value_base, adapter_pool, stretch_adapter, owner):
    fits = (
        lax.axis_size("groups") == 2
        and lax.axis_size("ctx") == 2 * PIECES
        and normed_input.shape[0] * PIECES == BLOCK_TOKENS
        and adapter_pool.shape[0] == 1
    )
    plan = direct_shards if fits else spread_shards
    return plan(
        normed_input, query_base, key_base, value_base, adapter_pool, stretch_adapter, owner
    )


def solution(mesh):
    placed = (
        P(("groups", "ctx"), None),
        P(("groups", "ctx"), None),
        P(("groups", "ctx"), None),
        P(("groups", "ctx"), None),
        P("ctx", None),
        P("groups"),
        P(),
    )
    return jax.shard_map(
        shards,
        mesh=mesh,
        in_specs=placed,
        out_specs=(P(("groups", "ctx"), None), P(("groups", "ctx"), None)),
        check_vma=False,
    )
```

```python
from functools import partial
import math

import jax
import jax.numpy as jnp
from jax import lax
from jax.experimental import pallas as pl
from jax.experimental.pallas import tpu as pltpu
from jax.sharding import PartitionSpec as P

D = 8192
QH = 32
KEYVALUE_HEADS = 4
HEAD_SIZE = 128
ADAPTER_RANK = 64
BLOCK_TOKENS = 512
QKV_POOL = 1900544


adapter_scale = 2.0
rope_base = 500000.0
mask_floor = -1e30


def from_partner(block, axis, apart):
    count = lax.axis_size(axis)
    route = []
    for low in range(count):
        high = low | 1 << apart
        if high != low and high < count:
            route += [(low, high), (high, low)]
    return lax.ppermute(block, axis, route)


def rotate(delta, token_positions, heads):
    half_dim = HEAD_SIZE // 2
    frequency = rope_base ** (-(jnp.arange(half_dim, dtype=jnp.float32) * 2.0) / HEAD_SIZE)
    angle = token_positions.astype(jnp.float32)[:, None] * frequency[None, :]
    cosine = jnp.cos(angle)[:, None, :]
    sine_part = jnp.sin(angle)[:, None, :]
    shaped = delta.reshape(delta.shape[0], heads, HEAD_SIZE)
    first_half = shaped[..., :half_dim]
    second_half = shaped[..., half_dim:]
    joined = jnp.concatenate(
        [
            first_half * cosine - second_half * sine_part,
            second_half * cosine + first_half * sine_part,
        ],
        -1,
    )
    return joined.reshape(delta.shape[0], heads * HEAD_SIZE)


def project_heads(
    narrow_product, query_row_block, key_row_block, value_row_block, upper_part, token_positions
):
    query_up_weight = upper_part[: ADAPTER_RANK * QH * HEAD_SIZE].reshape(
        ADAPTER_RANK, QH * HEAD_SIZE
    )
    keyvalue_up_weight = upper_part[ADAPTER_RANK * QH * HEAD_SIZE :].reshape(
        ADAPTER_RANK, 2 * KEYVALUE_HEADS * HEAD_SIZE
    )
    query_correction = adapter_scale * jnp.dot(
        narrow_product[:, :ADAPTER_RANK], query_up_weight, preferred_element_type=jnp.float32
    )
    key_correction = adapter_scale * jnp.dot(
        narrow_product[:, ADAPTER_RANK : 2 * ADAPTER_RANK],
        keyvalue_up_weight[:, : KEYVALUE_HEADS * HEAD_SIZE],
        preferred_element_type=jnp.float32,
    )
    value_correction = adapter_scale * jnp.dot(
        narrow_product[:, 2 * ADAPTER_RANK :],
        keyvalue_up_weight[:, KEYVALUE_HEADS * HEAD_SIZE :],
        preferred_element_type=jnp.float32,
    )
    queries = (
        query_row_block.astype(jnp.float32) + rotate(query_correction, token_positions, QH)
    ).astype(jnp.bfloat16)
    new_keys = (
        key_row_block.astype(jnp.float32) + rotate(key_correction, token_positions, KEYVALUE_HEADS)
    ).astype(jnp.bfloat16)
    new_values = (value_row_block.astype(jnp.float32) + value_correction).astype(jnp.bfloat16)
    return (queries, new_keys, new_values)


def output_delta(attended_rows, out_part):
    down_out = out_part[: QH * HEAD_SIZE * ADAPTER_RANK].reshape(QH * HEAD_SIZE, ADAPTER_RANK)
    raised_output = out_part[QH * HEAD_SIZE * ADAPTER_RANK :].reshape(ADAPTER_RANK, D)
    narrow_product = jnp.dot(attended_rows, down_out, preferred_element_type=jnp.float32).astype(
        jnp.bfloat16
    )
    return (
        adapter_scale * jnp.dot(narrow_product, raised_output, preferred_element_type=jnp.float32)
    ).astype(jnp.bfloat16)


def head_major(query_row_block):
    count_rows = query_row_block.shape[0]
    group_size = QH // KEYVALUE_HEADS
    return (
        query_row_block.reshape(count_rows, KEYVALUE_HEADS, group_size, HEAD_SIZE)
        .transpose(1, 2, 0, 3)
        .reshape(KEYVALUE_HEADS, group_size * count_rows, HEAD_SIZE)
    )


def row_major(head_rows, count_rows):
    group_size = QH // KEYVALUE_HEADS
    return (
        head_rows.reshape(KEYVALUE_HEADS, group_size, count_rows, HEAD_SIZE)
        .transpose(2, 0, 1, 3)
        .reshape(count_rows, QH * HEAD_SIZE)
    )


def online_update(current, queries, query_pos, key_slice, value_slice, key_start):
    run_max, run_sum, run_acc = current
    scores = jnp.einsum(
        "hqd,khd->hqk", queries, key_slice, preferred_element_type=jnp.float32
    ) * HEAD_SIZE ** (-0.5)
    key_pos = key_start + jnp.arange(key_slice.shape[0], dtype=jnp.int32)
    allowed = (query_pos[:, None] >= key_pos[None, :])[None]
    new_max = jnp.maximum(run_max, jnp.max(jnp.where(allowed, scores, mask_floor), axis=-1))
    weights = jnp.where(allowed, jnp.exp(scores - new_max[..., None]), 0.0)
    rescale = jnp.exp(run_max - new_max)
    new_sum = run_sum * rescale + jnp.sum(weights, axis=-1)
    new_acc = run_acc * rescale[..., None] + jnp.einsum(
        "hqk,khd->hqd",
        weights.astype(jnp.bfloat16),
        value_slice,
        preferred_element_type=jnp.float32,
    )
    return (new_max, new_sum, new_acc)


def unchanged(current):
    return current


def fold_keys(carry_state, shard_part, prepared):
    key_row_block, value_row_block = shard_part
    key_count = key_row_block.shape[0]
    sub_width = math.gcd(key_count, 1024)
    key_heads = key_row_block.reshape(key_count // sub_width, sub_width, KEYVALUE_HEADS, HEAD_SIZE)
    value_heads = value_row_block.reshape(
        key_count // sub_width, sub_width, KEYVALUE_HEADS, HEAD_SIZE
    )

    def one_step(sub_index, carried):
        key_start = sub_index * sub_width
        key_slice = lax.dynamic_index_in_dim(key_heads, sub_index, 0, keepdims=False)
        value_slice = lax.dynamic_index_in_dim(value_heads, sub_index, 0, keepdims=False)
        updated = []
        for (queries, query_pos), running in zip(prepared, carried):
            advance = partial(
                online_update,
                queries=queries,
                query_pos=query_pos,
                key_slice=key_slice,
                value_slice=value_slice,
                key_start=key_start,
            )
            updated.append(lax.cond(key_start <= jnp.max(query_pos), advance, unchanged, running))
        return tuple(updated)

    return lax.fori_loop(0, key_count // sub_width, one_step, carry_state)


def finish_block(result, count_rows):
    run_max, run_sum, run_acc = result
    divisor = jnp.where(run_sum > 0.0, run_sum, 1.0)
    return row_major(run_acc / divisor[..., None], count_rows).astype(jnp.bfloat16)


def spread_shards(
    normed_input, query_base, key_base, value_base, adapter_pool, stretch_adapter, adapter_owner
):
    cycle_size = lax.axis_size("ctx")
    my_index = lax.axis_index("ctx")
    tok_rows = normed_input.shape[0]
    token_positions = my_index * tok_rows + jnp.arange(tok_rows, dtype=jnp.int32)
    device_ids = jnp.arange(cycle_size, dtype=jnp.int32)
    stretch_of = device_ids * tok_rows // BLOCK_TOKENS
    stretch_ids = jnp.arange(stretch_adapter.shape[0], dtype=jnp.int32)
    adapter_of = jnp.sum(
        jnp.where(stretch_of[:, None] == stretch_ids[None, :], stretch_adapter[None, :], 0), axis=1
    )
    adapter_ids = jnp.arange(adapter_owner.shape[0], dtype=jnp.int32)
    slot_of = jnp.sum(
        jnp.where(adapter_of[:, None] == adapter_ids[None, :], adapter_owner[None, :], 0), axis=1
    )
    down_size = 3 * ADAPTER_RANK * D
    group_count = BLOCK_TOKENS // tok_rows
    levels = group_count.bit_length() - 1
    local_index = my_index % group_count
    col_width = D // group_count
    piece_len = down_size // (group_count * cycle_size)
    pool_rows = adapter_pool.shape[0]
    down_shaped = adapter_pool[:, :down_size].reshape(pool_rows, group_count, cycle_size, piece_len)
    spread_down = lax.all_to_all(down_shaped, "ctx", split_axis=2, concat_axis=0, tiled=True)
    flat_down = spread_down.reshape(-1, piece_len)
    wanted = jnp.take(flat_down, slot_of * group_count + device_ids % group_count, axis=0)[
        :, None, :
    ]
    down_slice = lax.all_to_all(wanted, "ctx", split_axis=0, concat_axis=1, tiled=True).reshape(
        col_width, 3 * ADAPTER_RANK
    )
    spread_rest = lax.all_to_all(
        adapter_pool[:, down_size:], "ctx", split_axis=1, concat_axis=0, tiled=True
    )
    rest_row = lax.all_to_all(
        jnp.take(spread_rest, slot_of, axis=0), "ctx", split_axis=0, concat_axis=1, tiled=True
    )[0]
    upper_part = rest_row[: QKV_POOL - down_size]
    out_part = rest_row[QKV_POOL - down_size :]
    pieces = normed_input.reshape(tok_rows, group_count, col_width)
    slice_order = jnp.bitwise_xor(local_index, jnp.arange(group_count, dtype=jnp.int32))
    moving = jnp.take(pieces, slice_order, axis=1).transpose(1, 0, 2)
    for level in range(levels):
        shaped = moving.reshape(group_count >> level + 1, 2, 1 << level, tok_rows, col_width)
        arrived = from_partner(shaped[:, 1], "ctx", level)
        moving = jnp.stack([shaped[:, 0], arrived], 1).reshape(group_count, tok_rows, col_width)
    partial_rows = jnp.dot(
        moving.reshape(group_count * tok_rows, col_width),
        down_slice,
        preferred_element_type=jnp.float32,
    ).reshape(group_count, tok_rows, 3 * ADAPTER_RANK)
    for level in reversed(range(levels)):
        halves = partial_rows.reshape(2, partial_rows.shape[0] // 2, tok_rows, 3 * ADAPTER_RANK)
        partial_rows = halves[0] + from_partner(
            halves[1].astype(jnp.bfloat16), "ctx", level
        ).astype(jnp.float32)
    narrow_product = partial_rows[0].astype(jnp.bfloat16)
    queries, new_keys, new_values = project_heads(
        narrow_product, query_base, key_base, value_base, upper_part, token_positions
    )
    group_size = QH // KEYVALUE_HEADS
    blocks = [(queries, token_positions)]
    prepared = [
        (head_major(block_q), jnp.tile(block_pos, group_size)) for block_q, block_pos in blocks
    ]
    initial = tuple(
        (
            (
                jnp.full((KEYVALUE_HEADS, head_q.shape[1]), mask_floor, jnp.float32),
                jnp.zeros((KEYVALUE_HEADS, head_q.shape[1]), jnp.float32),
                jnp.zeros((KEYVALUE_HEADS, head_q.shape[1], HEAD_SIZE), jnp.float32),
            )
            for head_q, block_pos in prepared
        )
    )
    finals = fold_keys(
        initial,
        (
            lax.all_gather(new_keys, "ctx", axis=0, tiled=True),
            lax.all_gather(new_values, "ctx", axis=0, tiled=True),
        ),
        prepared,
    )
    attended = finish_block(finals[0], tok_rows)
    out_delta = output_delta(attended, out_part)
    return (attended, out_delta)


PIECES = 8
GROUP = QH // KEYVALUE_HEADS
FIRST = ((0, 12288), (12288, 2048), (14336, 512))
SECOND = ((14848, 2048), (16896, 4096))
DOWN_ROWS, QUERY_ROWS, KEYVAL_ROWS, DOWN_OUT_ROWS, UP_OUT_ROWS = 768, 128, 32, 128, 256
UP_ROWS = QUERY_ROWS + 2 * KEYVAL_ROWS


def pack_kernel(sections, pool, *refs):
    out, buffers, sems = refs[-3:]
    plane = lax.axis_index("groups")
    slabs, slab_rows = out.shape[:2]

    def copies(slab):
        listed = []
        offset = 0
        for first, rows in sections:
            share = rows // (2 * PIECES)
            begin = first + (slab * 2 + plane) * share
            listed.append(
                pltpu.make_async_copy(
                    pool.at[:, pl.ds(pl.multiple_of(begin * 128, 2048), share * 128)],
                    buffers.at[slab, :, pl.ds(offset, share * 128)],
                    sems.at[slab, len(listed)],
                )
            )
            offset += share * 128
        return listed

    for slab in range(slabs):
        for copy in copies(slab):
            copy.start()

    def step(slab, carried):
        for copy in copies(slab):
            copy.wait()

        def chunk(index, inner):
            line = buffers[slab, :, pl.ds(pl.multiple_of(index * 2048, 2048), 2048)]
            block = line.astype(jnp.float32).reshape(16, 128).astype(jnp.bfloat16)
            out[slab, pl.ds(pl.multiple_of(index * 16, 16), 16), :] = block
            return inner

        lax.fori_loop(0, slab_rows // 16, chunk, 0, unroll=8)
        return carried

    lax.fori_loop(0, slabs, step, 0)


def pack_row(pool, sections, *after):
    slab_rows = sum(rows for _, rows in sections) // (2 * PIECES)
    return pl.pallas_call(
        partial(pack_kernel, sections),
        out_shape=jax.ShapeDtypeStruct((PIECES, slab_rows, 128), jnp.bfloat16),
        in_specs=[pl.BlockSpec(memory_space=pl.ANY)] * (1 + len(after)),
        out_specs=pl.BlockSpec(memory_space=pltpu.VMEM),
        scratch_shapes=[
            pltpu.VMEM((PIECES, 1, slab_rows * 128), jnp.bfloat16),
            pltpu.SemaphoreType.DMA((PIECES, len(sections))),
        ],
        compiler_params=pltpu.CompilerParams(vmem_limit_bytes=60 << 20),
        cost_estimate=pl.CostEstimate(flops=0, bytes_accessed=8 << 20, transcendentals=0),
    )(pool, *after)


def pick_kernel(mirrored, here, there, owner, spread, *refs):
    sems = refs[-1]
    outs = refs[:4] if len(refs) > 3 else [refs[flip % 2].at[flip // 2] for flip in range(4)]
    half = lax.axis_index("ctx") // PIECES
    rows = spread.shape[1]
    copies = []
    for flip, out in enumerate(outs):
        wishes = there if flip >= 2 else here
        block = half ^ (flip & 1)
        row = lax.rem(owner[wishes[block]], PIECES)
        copies.append(
            pltpu.make_async_copy(spread.at[row], out.at[pl.ds(0, rows)], sems.at[flip, 0])
        )
        if mirrored is not None:
            first, count = mirrored
            row = lax.rem(owner[wishes[1 - block]], PIECES)
            copies.append(
                pltpu.make_async_copy(
                    spread.at[row, pl.ds(first, count)],
                    out.at[pl.ds(rows, count)],
                    sems.at[flip, 1],
                )
            )
    for copy in copies:
        copy.start()
    for copy in copies:
        copy.wait()


def pick(spread, here, there, owner, mirrored):
    rows = spread.shape[1] + (mirrored[1] if mirrored else 0)
    shape, count = ((rows, 128), 4) if mirrored else ((2, rows, 128), 2)
    slab = jax.ShapeDtypeStruct(shape, jnp.bfloat16)
    return pl.pallas_call(
        partial(pick_kernel, mirrored),
        out_shape=(slab,) * count,
        in_specs=[pl.BlockSpec(memory_space=pltpu.SMEM)] * 3 + [pl.BlockSpec(memory_space=pl.ANY)],
        out_specs=(pl.BlockSpec(memory_space=pltpu.VMEM),) * count,
        scratch_shapes=[pltpu.SemaphoreType.DMA((4, 2))],
        compiler_params=pltpu.CompilerParams(vmem_limit_bytes=16 << 20),
        cost_estimate=pl.CostEstimate(flops=0, bytes_accessed=2 << 20, transcendentals=0),
    )(here, there, owner, spread)


def deal_kernel(rows, even, odd, sems):
    seat = lax.rem(lax.axis_index("ctx"), PIECES)
    width = rows.shape[1] // PIECES
    copies = []
    for apart in range(PIECES):
        first = pl.multiple_of((seat ^ apart) * width, width)
        target = (odd if apart % 2 else even).at[apart // 2]
        copies.append(
            pltpu.make_async_copy(rows.at[:, pl.ds(first, width)], target, sems.at[apart])
        )
    for copy in copies:
        copy.start()
    for copy in copies:
        copy.wait()


def deal(rows, *after):
    slab = jax.ShapeDtypeStruct((PIECES // 2, rows.shape[0], rows.shape[1] // PIECES), rows.dtype)

    def kernel(rows, *refs):
        deal_kernel(rows, *refs[-3:])

    return pl.pallas_call(
        kernel,
        out_shape=(slab, slab),
        in_specs=[pl.BlockSpec(memory_space=pl.ANY)] * (1 + len(after)),
        out_specs=(pl.BlockSpec(memory_space=pltpu.VMEM),) * 2,
        scratch_shapes=[pltpu.SemaphoreType.DMA((PIECES,))],
        compiler_params=pltpu.CompilerParams(vmem_limit_bytes=16 << 20),
        cost_estimate=pl.CostEstimate(flops=0, bytes_accessed=2 << 20, transcendentals=0),
    )(rows, *after)


def nearest(here, owner, block):
    half = lax.axis_index("ctx") // PIECES
    return owner[here[block]] // PIECES == half


def choose(close, arrived, put):
    plane = lax.axis_index("groups")

    @pl.when(close)
    def _():
        put(arrived[0], plane)
        put(arrived[2], 1 - plane)

    @pl.when(jnp.logical_not(close))
    def _():
        put(arrived[1], plane)
        put(arrived[3], 1 - plane)


def join_kernel(here, owner, *refs):
    arrived, (weight, ups), (flat, left, right) = refs[:4], refs[4:6], refs[6:]
    half = lax.axis_index("ctx") // PIECES
    split = DOWN_ROWS + QUERY_ROWS + KEYVAL_ROWS

    def put_own(source, position):
        first = pl.multiple_of(position * DOWN_ROWS, DOWN_ROWS)
        flat[pl.ds(first, DOWN_ROWS), :] = source[:DOWN_ROWS, :].astype(jnp.float32)
        ups[position, : UP_ROWS - KEYVAL_ROWS, :] = source[DOWN_ROWS:split, :]

    def put_mirrored(source, position):
        ups[position, UP_ROWS - KEYVAL_ROWS :, :] = source[split:, :]

    choose(nearest(here, owner, half), arrived, put_own)
    choose(nearest(here, owner, 1 - half), arrived, put_mirrored)

    third = flat.shape[0] // 3
    one = flat[pl.ds(0, third, stride=3), :]
    two = pltpu.roll(flat[pl.ds(1, third, stride=3), :], 64, 1)
    three = pltpu.roll(flat[pl.ds(2, third, stride=3), :], 64, 1)
    lane = lax.broadcasted_iota(jnp.int32, one.shape, 1)
    left[pl.ds(0, third, stride=2), :] = one
    left[pl.ds(1, third, stride=2), :] = jnp.where(lane < 64, two, three)
    right[pl.ds(0, third, stride=2), :] = pltpu.roll(two, 64, 1)
    right[pl.ds(1, third, stride=2), :] = three
    weight[...] = jnp.concatenate([left[...], right[...]], 1).astype(jnp.bfloat16)


def join(here, owner, arrived):
    depth = D // PIECES
    return pl.pallas_call(
        join_kernel,
        out_shape=(
            jax.ShapeDtypeStruct((depth, 256), jnp.bfloat16),
            jax.ShapeDtypeStruct((2, UP_ROWS, 128), jnp.bfloat16),
        ),
        in_specs=[pl.BlockSpec(memory_space=pltpu.SMEM)] * 2
        + [pl.BlockSpec(memory_space=pltpu.VMEM)] * 4,
        out_specs=(pl.BlockSpec(memory_space=pltpu.VMEM),) * 2,
        scratch_shapes=[
            pltpu.VMEM((2 * DOWN_ROWS, 128), jnp.float32),
            pltpu.VMEM((depth, 128), jnp.float32),
            pltpu.VMEM((depth, 128), jnp.float32),
        ],
        compiler_params=pltpu.CompilerParams(vmem_limit_bytes=16 << 20),
        cost_estimate=pl.CostEstimate(flops=0, bytes_accessed=96 << 20, transcendentals=0),
    )(here, owner, *arrived)


def settle_kernel(here, there, owner, near, far, own, across):
    half = lax.axis_index("ctx") // PIECES
    for number, (wishes, out) in enumerate(((here, own), (there, across))):
        close = nearest(wishes, owner, half)

        @pl.when(close)
        def _():
            out[...] = near[number]

        @pl.when(jnp.logical_not(close))
        def _():
            out[...] = far[number]


def settle(here, there, owner, near, far):
    slab = jax.ShapeDtypeStruct(near.shape[1:], jnp.bfloat16)
    return pl.pallas_call(
        settle_kernel,
        out_shape=(slab, slab),
        in_specs=[pl.BlockSpec(memory_space=pltpu.SMEM)] * 3
        + [pl.BlockSpec(memory_space=pltpu.VMEM)] * 2,
        out_specs=(pl.BlockSpec(memory_space=pltpu.VMEM),) * 2,
        compiler_params=pltpu.CompilerParams(vmem_limit_bytes=16 << 20),
        cost_estimate=pl.CostEstimate(flops=0, bytes_accessed=1 << 20, transcendentals=0),
    )(here, there, owner, near, far)


def narrow_kernel(weight, *refs):
    for block, out in zip(refs[:4], refs[4:]):
        sides, rows, depth = block.shape
        product = jnp.dot(
            block[...].reshape(sides * rows, depth),
            weight[...],
            preferred_element_type=jnp.float32,
        )
        out[...] = product[:, : 3 * ADAPTER_RANK].reshape(out.shape).astype(jnp.bfloat16)


def narrow(weight, dealt):
    sides, rows, depth = dealt[0].shape
    partial_sums = jax.ShapeDtypeStruct((sides, rows, 3 * ADAPTER_RANK), jnp.bfloat16)
    return pl.pallas_call(
        narrow_kernel,
        out_shape=(partial_sums,) * 4,
        in_specs=[pl.BlockSpec(memory_space=pltpu.VMEM)] * 5,
        out_specs=(pl.BlockSpec(memory_space=pltpu.VMEM),) * 4,
        compiler_params=pltpu.CompilerParams(vmem_limit_bytes=16 << 20),
        cost_estimate=pl.CostEstimate(
            flops=2 * 8 * rows * depth * 256, bytes_accessed=2 << 20, transcendentals=0
        ),
    )(weight, *dealt)


def attend_kernel(
    first_head,
    query_block,
    key_same,
    key_other,
    value_same,
    value_other,
    own_rank,
    all_rank,
    up_same,
    up_other,
    cosines,
    sines,
    *refs,
):
    attended, flat_query, flat_keyval, keys, values = refs[-5:]
    step = pl.program_id(0) + first_head
    rows = query_block.shape[0]
    base = lax.axis_index("ctx") * rows
    half = lax.axis_index("ctx") // PIECES
    seat = lax.rem(lax.axis_index("ctx"), PIECES)
    dot = partial(jnp.dot, preferred_element_type=jnp.float32)

    @pl.when(pl.program_id(0) == 0)
    def _():
        for apart in range(PIECES):
            ups = up_other if apart % 2 else up_same
            for position in range(2):
                piece = ups[apart // 2, position].astype(jnp.float32)
                place = (seat ^ apart) * 2 + position
                first = pl.multiple_of(place * QUERY_ROWS, QUERY_ROWS)
                flat_query[pl.ds(first, QUERY_ROWS), :] = piece[:QUERY_ROWS]
                first = pl.multiple_of(place * KEYVAL_ROWS, KEYVAL_ROWS)
                for side in range(2):
                    begin = QUERY_ROWS + side * KEYVAL_ROWS
                    flat_keyval[side, pl.ds(first, KEYVAL_ROWS), :] = piece[
                        begin : begin + KEYVAL_ROWS
                    ]

    def turned(delta, cosine, sine):
        return delta * cosine + pltpu.roll(delta, HEAD_SIZE // 2, 1) * sine

    def up(flat, first, stride):
        return flat[pl.ds(first, ADAPTER_RANK, stride=stride), :].astype(jnp.bfloat16)

    for side in range(2):
        heads = 2 * KEYVALUE_HEADS
        key_up = up(flat_keyval.at[side], step, heads)
        value_up = up(flat_keyval.at[side], step + KEYVALUE_HEADS, heads)
        for core in range(2):
            rank = all_rank[core, :, side].reshape(PIECES // 2 * rows, 2 * ADAPTER_RANK)
            key_delta = adapter_scale * dot(rank[:, :ADAPTER_RANK], key_up)
            value_delta = adapter_scale * dot(rank[:, ADAPTER_RANK:], value_up)
            for chip in range(PIECES // 2):
                there = seat ^ (2 * chip + core)
                first = ((half ^ side) * PIECES + there) * rows
                span = pl.ds(pl.multiple_of(first, rows), rows)
                part = slice(chip * rows, (chip + 1) * rows)
                delta = turned(key_delta[part], cosines[span, :], sines[span, :])
                full = (key_other if core else key_same)[chip, side].astype(jnp.float32) + delta
                keys[span, :] = full.astype(jnp.bfloat16)
                full = (value_other if core else value_same)[chip, side].astype(jnp.float32)
                values[span, :] = (full + value_delta[part]).astype(jnp.bfloat16)
    here = pl.ds(pl.multiple_of(base, rows), rows)
    cosine = cosines[here, :]
    sine = sines[here, :]
    taken = GROUP // 2
    for first in range(0, GROUP, taken):
        weight = [up(flat_query, step * GROUP + first + head, QH) for head in range(taken)]
        deltas = adapter_scale * dot(own_rank[:, :ADAPTER_RANK], jnp.concatenate(weight, 1))
        queries = []
        for place in range(taken):
            moved = turned(deltas[:, place * HEAD_SIZE : (place + 1) * HEAD_SIZE], cosine, sine)
            span = slice((first + place) * HEAD_SIZE, (first + place + 1) * HEAD_SIZE)
            queries.append(
                (query_block[:, span].astype(jnp.float32) + moved).astype(jnp.bfloat16)
            )
        queries = jnp.concatenate(queries, 0)
        scores = lax.dot_general(
            queries, keys[...], (((1,), (1,)), ((), ())), preferred_element_type=jnp.float32
        )
        row = lax.broadcasted_iota(jnp.int32, scores.shape, 0)
        column = lax.broadcasted_iota(jnp.int32, scores.shape, 1)
        scores = jnp.where(column <= base + lax.rem(row, rows), scores, mask_floor)
        scores = scores - jnp.max(scores, axis=-1, keepdims=True)
        weights = jnp.exp2(scores * (HEAD_SIZE ** (-0.5) * math.log2(math.e)))
        divisor = jnp.sum(weights, axis=-1, keepdims=True)
        result = (dot(weights.astype(jnp.bfloat16), values[...]) / divisor).astype(jnp.bfloat16)
        for place in range(taken):
            span = slice((first + place) * HEAD_SIZE, (first + place + 1) * HEAD_SIZE)
            attended[:, span] = result[place * rows : (place + 1) * rows]


def attend(first_head, heads, before, query_base, base, own_rank, all_rank, ups, cosines, sines):
    rows = query_base.shape[0]
    seq = 4 * PIECES // 2 * rows
    width = GROUP * HEAD_SIZE

    def whole(shape):
        return pl.BlockSpec(shape, lambda h: (0,) * len(shape))

    key_spec = pl.BlockSpec((PIECES // 2, 2, rows, HEAD_SIZE), lambda h: (0, 0, 0, h + first_head))
    value_spec = pl.BlockSpec(
        (PIECES // 2, 2, rows, HEAD_SIZE), lambda h: (0, 0, 0, h + first_head + KEYVALUE_HEADS)
    )
    operands = (query_base, base[0], base[1], base[0], base[1], own_rank, all_rank, *ups)
    operands += (cosines, sines) + (() if before is None else (before,))
    query_spec = pl.BlockSpec((rows, width), lambda h: (0, h + first_head))
    return pl.pallas_call(
        partial(attend_kernel, first_head),
        grid=(heads,),
        out_shape=jax.ShapeDtypeStruct((rows, QH * HEAD_SIZE), jnp.bfloat16),
        in_specs=[
            query_spec,
            key_spec,
            key_spec,
            value_spec,
            value_spec,
            whole(own_rank.shape),
            whole(all_rank.shape),
            whole(ups[0].shape),
            whole(ups[1].shape),
            whole(cosines.shape),
            whole(sines.shape),
        ]
        + [pl.BlockSpec(memory_space=pl.ANY)] * (len(operands) - 11),
        out_specs=query_spec,
        input_output_aliases={} if before is None else {len(operands) - 1: 0},
        scratch_shapes=[
            pltpu.VMEM((2 * PIECES * QUERY_ROWS, 128), jnp.float32),
            pltpu.VMEM((2, 2 * PIECES * KEYVAL_ROWS, 128), jnp.float32),
            pltpu.VMEM((seq, HEAD_SIZE), jnp.bfloat16),
            pltpu.VMEM((seq, HEAD_SIZE), jnp.bfloat16),
        ],
        compiler_params=pltpu.CompilerParams(vmem_limit_bytes=60 << 20),
        cost_estimate=pl.CostEstimate(
            flops=12 * heads * rows * QH * seq * HEAD_SIZE,
            bytes_accessed=10 << 20,
            transcendentals=heads * rows * GROUP * seq,
        ),
    )(*operands)


def widen_kernel(attended, same, other, out_delta, down_out, up_out):
    plane = lax.axis_index("groups")
    seat = lax.rem(lax.axis_index("ctx"), PIECES)
    for apart in range(PIECES):
        pieces = other if apart % 2 else same
        for position in range(2):
            piece = pieces[apart // 2, position].astype(jnp.float32)
            place = (seat ^ apart) * 2 + (position ^ plane)
            first = place * 2 * DOWN_OUT_ROWS
            block = piece[:DOWN_OUT_ROWS]
            down_out[pl.ds(first, DOWN_OUT_ROWS, stride=2), :] = block
            down_out[pl.ds(first + 1, DOWN_OUT_ROWS, stride=2), :] = pltpu.roll(block, 64, 1)
            first = pl.multiple_of(place * UP_OUT_ROWS, UP_OUT_ROWS)
            up_out[pl.ds(first, UP_OUT_ROWS), :] = piece[DOWN_OUT_ROWS:]
    dot = partial(jnp.dot, preferred_element_type=jnp.float32)
    rank = dot(attended[...], down_out[...].astype(jnp.bfloat16))[:, :ADAPTER_RANK]
    rank = rank.astype(jnp.bfloat16)
    blocks = D // 128
    for first in range(0, blocks, 4):
        weight = [
            up_out[pl.ds(first + block, ADAPTER_RANK, stride=blocks), :].astype(jnp.bfloat16)
            for block in range(4)
        ]
        delta = adapter_scale * dot(rank, jnp.concatenate(weight, 1))
        out_delta[:, first * 128 : (first + 4) * 128] = delta.astype(jnp.bfloat16)


def widen(attended, same, other):
    return pl.pallas_call(
        widen_kernel,
        out_shape=jax.ShapeDtypeStruct((attended.shape[0], D), jnp.bfloat16),
        in_specs=[pl.BlockSpec(memory_space=pltpu.VMEM)] * 3,
        out_specs=pl.BlockSpec(memory_space=pltpu.VMEM),
        scratch_shapes=[
            pltpu.VMEM((QH * HEAD_SIZE, 128), jnp.float32),
            pltpu.VMEM((ADAPTER_RANK * D // 128, 128), jnp.float32),
        ],
        compiler_params=pltpu.CompilerParams(vmem_limit_bytes=32 << 20),
        cost_estimate=pl.CostEstimate(flops=1 << 27, bytes_accessed=4 << 20, transcendentals=0),
    )(attended, same, other)


def swap(block, mask):
    return lax.ppermute(block, ("groups", "ctx"), [(i, i ^ mask) for i in range(4 * PIECES)])


def direct_shards(
    normed_input, query_base, key_base, value_base, adapter_pool, stretch_adapter, adapter_owner
):
    tok_rows = normed_input.shape[0]
    ctx = lax.axis_size("ctx")
    seq = ctx * tok_rows
    blocks = [list(range(PIECES)), list(range(PIECES, 2 * PIECES))]
    half_dim = HEAD_SIZE // 2
    frequency = rope_base ** (-(jnp.arange(half_dim, dtype=jnp.float32) * 2.0) / HEAD_SIZE)
    angle = jnp.arange(seq, dtype=jnp.int32).astype(jnp.float32)[:, None] * frequency[None, :]
    cosine = jnp.cos(angle)
    sine = jnp.sin(angle)
    cosines = jnp.concatenate([cosine, cosine], 1)
    sines = jnp.concatenate([-sine, sine], 1)

    def after(block, *others):
        return lax.optimization_barrier((block, others))[0]

    def exchange(sent):
        return [swap(block, flip * PIECES) if flip else block for flip, block in enumerate(sent)]

    def along_z(block):
        return jnp.stack([block, swap(block, 4)])

    def along_x(pair):
        quad = jnp.stack([pair, swap(pair, 2)], 1)
        return quad.reshape((PIECES // 2,) + pair.shape[1:])

    elsewhere = swap(stretch_adapter, 2 * PIECES)
    packed = pack_row(adapter_pool, FIRST)
    packed_second = pack_row(adapter_pool, SECOND, packed)
    even, odd = deal(normed_input, packed)
    sibling = swap(odd, 1)
    base = jnp.concatenate([key_base, value_base], 1)
    base = jnp.stack([base, swap(base, PIECES)])
    packed = after(packed, base)

    spread = lax.all_to_all(packed, "ctx", 0, 0, axis_index_groups=blocks)
    spread = after(spread, packed_second, sibling)
    sent = pick(spread, stretch_adapter, elsewhere, adapter_owner, (896, KEYVAL_ROWS))
    arrived = exchange(sent)
    dealt = [after(jnp.stack([even[j], sibling[j]]), sent) for j in range(PIECES // 2)]
    dealt = [swap(block, 2 * j) if j else block for j, block in enumerate(dealt)]
    base = along_z(after(base, sent))

    weight, ups = join(stretch_adapter, adapter_owner, arrived)
    partial_sums = narrow(after(weight, base, cosines, sines), dealt)
    packed_second = after(packed_second, *partial_sums)
    spread = lax.all_to_all(packed_second, "ctx", 0, 0, axis_index_groups=blocks)
    back = [swap(block, 2 * j) if j else block for j, block in enumerate(partial_sums)]
    back = sum(block.astype(jnp.float32) for block in back)
    own_rank = swap(back[1].astype(jnp.bfloat16), 1)
    own_rank = back[0] + own_rank.astype(jnp.float32)
    own_rank = own_rank.astype(jnp.bfloat16)
    ups = along_z(after(ups, *partial_sums))
    base = along_x(base)
    all_rank = after(own_rank[:, ADAPTER_RANK:], ups)
    near, far = pick(after(spread, all_rank), stretch_adapter, elsewhere, adapter_owner, None)
    far = swap(far, PIECES)
    all_rank = jnp.stack([all_rank, swap(all_rank, PIECES)])
    all_rank = after(all_rank, base)
    ups = along_x(after(ups, all_rank))
    base = (base, swap(after(base, all_rank), 1))
    all_rank = jnp.stack([swap(all_rank, apart) if apart else all_rank for apart in (0, 2, 4, 6)])
    all_rank = after(all_rank, ups, near)
    ups = (ups, swap(ups, 1))
    all_rank = jnp.stack([all_rank, swap(all_rank, 1)])

    far = after(far, all_rank)
    own, across = settle(stretch_adapter, elsewhere, adapter_owner, near, far)
    ends = jnp.stack([own, swap(across, 2 * PIECES)])
    shared = (query_base, base, own_rank, all_rank, ups, cosines, sines)
    attended = attend(0, 1, None, *shared)
    ends = after(ends, attended)
    ends = jnp.stack([swap(ends, apart) if apart else ends for apart in (0, 2, 4, 6)])
    attended = attend(1, KEYVALUE_HEADS - 1, attended, *shared)
    ends = after(ends, attended)
    return attended, widen(attended, ends, swap(ends, 1))


def shards(normed_input, query_base, key_base, value_base, adapter_pool, stretch_adapter, owner):
    fits = (
        lax.axis_size("groups") == 2
        and lax.axis_size("ctx") == 2 * PIECES
        and normed_input.shape[0] * PIECES == BLOCK_TOKENS
        and adapter_pool.shape[0] == 1
    )
    plan = direct_shards if fits else spread_shards
    return plan(
        normed_input, query_base, key_base, value_base, adapter_pool, stretch_adapter, owner
    )


def solution(mesh):
    placed = (
        P(("groups", "ctx"), None),
        P(("groups", "ctx"), None),
        P(("groups", "ctx"), None),
        P(("groups", "ctx"), None),
        P("ctx", None),
        P("groups"),
        P(),
    )
    return jax.shard_map(
        shards,
        mesh=mesh,
        in_specs=placed,
        out_specs=(P(("groups", "ctx"), None), P(("groups", "ctx"), None)),
        check_vma=False,
    )
```

```python
from functools import partial
import math

import jax
import jax.numpy as jnp
from jax import lax
from jax.experimental import pallas as pl
from jax.experimental.pallas import tpu as pltpu
from jax.sharding import PartitionSpec as P

D = 8192
QH = 32
KEYVALUE_HEADS = 4
HEAD_SIZE = 128
ADAPTER_RANK = 64
BLOCK_TOKENS = 512
QKV_POOL = 1900544


adapter_scale = 2.0
rope_base = 500000.0
mask_floor = -1e30


def from_partner(block, axis, apart):
    count = lax.axis_size(axis)
    route = []
    for low in range(count):
        high = low | 1 << apart
        if high != low and high < count:
            route += [(low, high), (high, low)]
    return lax.ppermute(block, axis, route)


def rotate(delta, token_positions, heads):
    half_dim = HEAD_SIZE // 2
    frequency = rope_base ** (-(jnp.arange(half_dim, dtype=jnp.float32) * 2.0) / HEAD_SIZE)
    angle = token_positions.astype(jnp.float32)[:, None] * frequency[None, :]
    cosine = jnp.cos(angle)[:, None, :]
    sine_part = jnp.sin(angle)[:, None, :]
    shaped = delta.reshape(delta.shape[0], heads, HEAD_SIZE)
    first_half = shaped[..., :half_dim]
    second_half = shaped[..., half_dim:]
    joined = jnp.concatenate(
        [
            first_half * cosine - second_half * sine_part,
            second_half * cosine + first_half * sine_part,
        ],
        -1,
    )
    return joined.reshape(delta.shape[0], heads * HEAD_SIZE)


def project_heads(
    narrow_product, query_row_block, key_row_block, value_row_block, upper_part, token_positions
):
    query_up_weight = upper_part[: ADAPTER_RANK * QH * HEAD_SIZE].reshape(
        ADAPTER_RANK, QH * HEAD_SIZE
    )
    keyvalue_up_weight = upper_part[ADAPTER_RANK * QH * HEAD_SIZE :].reshape(
        ADAPTER_RANK, 2 * KEYVALUE_HEADS * HEAD_SIZE
    )
    query_correction = adapter_scale * jnp.dot(
        narrow_product[:, :ADAPTER_RANK], query_up_weight, preferred_element_type=jnp.float32
    )
    key_correction = adapter_scale * jnp.dot(
        narrow_product[:, ADAPTER_RANK : 2 * ADAPTER_RANK],
        keyvalue_up_weight[:, : KEYVALUE_HEADS * HEAD_SIZE],
        preferred_element_type=jnp.float32,
    )
    value_correction = adapter_scale * jnp.dot(
        narrow_product[:, 2 * ADAPTER_RANK :],
        keyvalue_up_weight[:, KEYVALUE_HEADS * HEAD_SIZE :],
        preferred_element_type=jnp.float32,
    )
    queries = (
        query_row_block.astype(jnp.float32) + rotate(query_correction, token_positions, QH)
    ).astype(jnp.bfloat16)
    new_keys = (
        key_row_block.astype(jnp.float32) + rotate(key_correction, token_positions, KEYVALUE_HEADS)
    ).astype(jnp.bfloat16)
    new_values = (value_row_block.astype(jnp.float32) + value_correction).astype(jnp.bfloat16)
    return (queries, new_keys, new_values)


def output_delta(attended_rows, out_part):
    down_out = out_part[: QH * HEAD_SIZE * ADAPTER_RANK].reshape(QH * HEAD_SIZE, ADAPTER_RANK)
    raised_output = out_part[QH * HEAD_SIZE * ADAPTER_RANK :].reshape(ADAPTER_RANK, D)
    narrow_product = jnp.dot(attended_rows, down_out, preferred_element_type=jnp.float32).astype(
        jnp.bfloat16
    )
    return (
        adapter_scale * jnp.dot(narrow_product, raised_output, preferred_element_type=jnp.float32)
    ).astype(jnp.bfloat16)


def head_major(query_row_block):
    count_rows = query_row_block.shape[0]
    group_size = QH // KEYVALUE_HEADS
    return (
        query_row_block.reshape(count_rows, KEYVALUE_HEADS, group_size, HEAD_SIZE)
        .transpose(1, 2, 0, 3)
        .reshape(KEYVALUE_HEADS, group_size * count_rows, HEAD_SIZE)
    )


def row_major(head_rows, count_rows):
    group_size = QH // KEYVALUE_HEADS
    return (
        head_rows.reshape(KEYVALUE_HEADS, group_size, count_rows, HEAD_SIZE)
        .transpose(2, 0, 1, 3)
        .reshape(count_rows, QH * HEAD_SIZE)
    )


def online_update(current, queries, query_pos, key_slice, value_slice, key_start):
    run_max, run_sum, run_acc = current
    scores = jnp.einsum(
        "hqd,khd->hqk", queries, key_slice, preferred_element_type=jnp.float32
    ) * HEAD_SIZE ** (-0.5)
    key_pos = key_start + jnp.arange(key_slice.shape[0], dtype=jnp.int32)
    allowed = (query_pos[:, None] >= key_pos[None, :])[None]
    new_max = jnp.maximum(run_max, jnp.max(jnp.where(allowed, scores, mask_floor), axis=-1))
    weights = jnp.where(allowed, jnp.exp(scores - new_max[..., None]), 0.0)
    rescale = jnp.exp(run_max - new_max)
    new_sum = run_sum * rescale + jnp.sum(weights, axis=-1)
    new_acc = run_acc * rescale[..., None] + jnp.einsum(
        "hqk,khd->hqd",
        weights.astype(jnp.bfloat16),
        value_slice,
        preferred_element_type=jnp.float32,
    )
    return (new_max, new_sum, new_acc)


def unchanged(current):
    return current


def fold_keys(carry_state, shard_part, prepared):
    key_row_block, value_row_block = shard_part
    key_count = key_row_block.shape[0]
    sub_width = math.gcd(key_count, 1024)
    key_heads = key_row_block.reshape(key_count // sub_width, sub_width, KEYVALUE_HEADS, HEAD_SIZE)
    value_heads = value_row_block.reshape(
        key_count // sub_width, sub_width, KEYVALUE_HEADS, HEAD_SIZE
    )

    def one_step(sub_index, carried):
        key_start = sub_index * sub_width
        key_slice = lax.dynamic_index_in_dim(key_heads, sub_index, 0, keepdims=False)
        value_slice = lax.dynamic_index_in_dim(value_heads, sub_index, 0, keepdims=False)
        updated = []
        for (queries, query_pos), running in zip(prepared, carried):
            advance = partial(
                online_update,
                queries=queries,
                query_pos=query_pos,
                key_slice=key_slice,
                value_slice=value_slice,
                key_start=key_start,
            )
            updated.append(lax.cond(key_start <= jnp.max(query_pos), advance, unchanged, running))
        return tuple(updated)

    return lax.fori_loop(0, key_count // sub_width, one_step, carry_state)


def finish_block(result, count_rows):
    run_max, run_sum, run_acc = result
    divisor = jnp.where(run_sum > 0.0, run_sum, 1.0)
    return row_major(run_acc / divisor[..., None], count_rows).astype(jnp.bfloat16)


def spread_shards(
    normed_input, query_base, key_base, value_base, adapter_pool, stretch_adapter, adapter_owner
):
    cycle_size = lax.axis_size("ctx")
    my_index = lax.axis_index("ctx")
    tok_rows = normed_input.shape[0]
    token_positions = my_index * tok_rows + jnp.arange(tok_rows, dtype=jnp.int32)
    device_ids = jnp.arange(cycle_size, dtype=jnp.int32)
    stretch_of = device_ids * tok_rows // BLOCK_TOKENS
    stretch_ids = jnp.arange(stretch_adapter.shape[0], dtype=jnp.int32)
    adapter_of = jnp.sum(
        jnp.where(stretch_of[:, None] == stretch_ids[None, :], stretch_adapter[None, :], 0), axis=1
    )
    adapter_ids = jnp.arange(adapter_owner.shape[0], dtype=jnp.int32)
    slot_of = jnp.sum(
        jnp.where(adapter_of[:, None] == adapter_ids[None, :], adapter_owner[None, :], 0), axis=1
    )
    down_size = 3 * ADAPTER_RANK * D
    group_count = BLOCK_TOKENS // tok_rows
    levels = group_count.bit_length() - 1
    local_index = my_index % group_count
    col_width = D // group_count
    piece_len = down_size // (group_count * cycle_size)
    pool_rows = adapter_pool.shape[0]
    down_shaped = adapter_pool[:, :down_size].reshape(pool_rows, group_count, cycle_size, piece_len)
    spread_down = lax.all_to_all(down_shaped, "ctx", split_axis=2, concat_axis=0, tiled=True)
    flat_down = spread_down.reshape(-1, piece_len)
    wanted = jnp.take(flat_down, slot_of * group_count + device_ids % group_count, axis=0)[
        :, None, :
    ]
    down_slice = lax.all_to_all(wanted, "ctx", split_axis=0, concat_axis=1, tiled=True).reshape(
        col_width, 3 * ADAPTER_RANK
    )
    spread_rest = lax.all_to_all(
        adapter_pool[:, down_size:], "ctx", split_axis=1, concat_axis=0, tiled=True
    )
    rest_row = lax.all_to_all(
        jnp.take(spread_rest, slot_of, axis=0), "ctx", split_axis=0, concat_axis=1, tiled=True
    )[0]
    upper_part = rest_row[: QKV_POOL - down_size]
    out_part = rest_row[QKV_POOL - down_size :]
    pieces = normed_input.reshape(tok_rows, group_count, col_width)
    slice_order = jnp.bitwise_xor(local_index, jnp.arange(group_count, dtype=jnp.int32))
    moving = jnp.take(pieces, slice_order, axis=1).transpose(1, 0, 2)
    for level in range(levels):
        shaped = moving.reshape(group_count >> level + 1, 2, 1 << level, tok_rows, col_width)
        arrived = from_partner(shaped[:, 1], "ctx", level)
        moving = jnp.stack([shaped[:, 0], arrived], 1).reshape(group_count, tok_rows, col_width)
    partial_rows = jnp.dot(
        moving.reshape(group_count * tok_rows, col_width),
        down_slice,
        preferred_element_type=jnp.float32,
    ).reshape(group_count, tok_rows, 3 * ADAPTER_RANK)
    for level in reversed(range(levels)):
        halves = partial_rows.reshape(2, partial_rows.shape[0] // 2, tok_rows, 3 * ADAPTER_RANK)
        partial_rows = halves[0] + from_partner(
            halves[1].astype(jnp.bfloat16), "ctx", level
        ).astype(jnp.float32)
    narrow_product = partial_rows[0].astype(jnp.bfloat16)
    queries, new_keys, new_values = project_heads(
        narrow_product, query_base, key_base, value_base, upper_part, token_positions
    )
    group_size = QH // KEYVALUE_HEADS
    blocks = [(queries, token_positions)]
    prepared = [
        (head_major(block_q), jnp.tile(block_pos, group_size)) for block_q, block_pos in blocks
    ]
    initial = tuple(
        (
            (
                jnp.full((KEYVALUE_HEADS, head_q.shape[1]), mask_floor, jnp.float32),
                jnp.zeros((KEYVALUE_HEADS, head_q.shape[1]), jnp.float32),
                jnp.zeros((KEYVALUE_HEADS, head_q.shape[1], HEAD_SIZE), jnp.float32),
            )
            for head_q, block_pos in prepared
        )
    )
    finals = fold_keys(
        initial,
        (
            lax.all_gather(new_keys, "ctx", axis=0, tiled=True),
            lax.all_gather(new_values, "ctx", axis=0, tiled=True),
        ),
        prepared,
    )
    attended = finish_block(finals[0], tok_rows)
    out_delta = output_delta(attended, out_part)
    return (attended, out_delta)


PIECES = 8
GROUP = QH // KEYVALUE_HEADS
SECTIONS = ((0, 12288), (12288, 2048), (14336, 512), (14848, 2048), (16896, 4096))
DOWN_ROWS, QUERY_ROWS, KEYVAL_ROWS, DOWN_OUT_ROWS, UP_OUT_ROWS = 768, 128, 32, 128, 256
UP_ROWS = QUERY_ROWS + 2 * KEYVAL_ROWS
FIRST_ROWS = DOWN_ROWS + QUERY_ROWS + KEYVAL_ROWS


def pack_kernel(sections, pool, *refs):
    out, buffers, sems = refs[-3:]
    plane = lax.axis_index("groups")
    slabs, slab_rows = out.shape[:2]

    def copies(slab):
        listed = []
        offset = 0
        for first, rows in sections:
            share = rows // (2 * PIECES)
            begin = first + (slab * 2 + plane) * share
            listed.append(
                pltpu.make_async_copy(
                    pool.at[:, pl.ds(pl.multiple_of(begin * 128, 2048), share * 128)],
                    buffers.at[slab, :, pl.ds(offset, share * 128)],
                    sems.at[slab, len(listed)],
                )
            )
            offset += share * 128
        return listed

    for slab in range(slabs):
        for copy in copies(slab):
            copy.start()

    def step(slab, carried):
        for copy in copies(slab):
            copy.wait()

        def chunk(index, inner):
            line = buffers[slab, :, pl.ds(pl.multiple_of(index * 2048, 2048), 2048)]
            block = line.astype(jnp.float32).reshape(16, 128).astype(jnp.bfloat16)
            out[slab, pl.ds(pl.multiple_of(index * 16, 16), 16), :] = block
            return inner

        lax.fori_loop(0, slab_rows // 16, chunk, 0, unroll=8)
        return carried

    lax.fori_loop(0, slabs, step, 0)


def pack_row(pool, sections, *after):
    slab_rows = sum(rows for _, rows in sections) // (2 * PIECES)
    return pl.pallas_call(
        partial(pack_kernel, sections),
        out_shape=jax.ShapeDtypeStruct((PIECES, slab_rows, 128), jnp.bfloat16),
        in_specs=[pl.BlockSpec(memory_space=pl.ANY)] * (1 + len(after)),
        out_specs=pl.BlockSpec(memory_space=pltpu.VMEM),
        scratch_shapes=[
            pltpu.VMEM((PIECES, 1, slab_rows * 128), jnp.bfloat16),
            pltpu.SemaphoreType.DMA((PIECES, len(sections))),
        ],
        compiler_params=pltpu.CompilerParams(vmem_limit_bytes=60 << 20),
        cost_estimate=pl.CostEstimate(flops=0, bytes_accessed=8 << 20, transcendentals=0),
    )(pool, *after)


def pick_kernel(here, there, owner, spread, *refs):
    outs, lasts, sems = refs[:4], refs[4:6], refs[6]
    half = lax.axis_index("ctx") // PIECES
    last = spread.shape[1] - FIRST_ROWS
    copies = []
    for flip, out in enumerate(outs):
        wishes = there if flip >= 2 else here
        block = half ^ (flip & 1)
        row = lax.rem(owner[wishes[block]], PIECES)
        mirrored = lax.rem(owner[wishes[1 - block]], PIECES)
        pairs = (
            (spread.at[row, pl.ds(0, FIRST_ROWS)], out.at[pl.ds(0, FIRST_ROWS)]),
            (
                spread.at[mirrored, pl.ds(FIRST_ROWS - KEYVAL_ROWS, KEYVAL_ROWS)],
                out.at[pl.ds(FIRST_ROWS, KEYVAL_ROWS)],
            ),
            (spread.at[row, pl.ds(FIRST_ROWS, last)], lasts[flip % 2].at[flip // 2]),
        )
        for number, (source, target) in enumerate(pairs):
            copies.append(pltpu.make_async_copy(source, target, sems.at[flip, number]))
    for copy in copies:
        copy.start()
    for copy in copies:
        copy.wait()


def pick(spread, here, there, owner):
    last = spread.shape[1] - FIRST_ROWS
    first_shape = jax.ShapeDtypeStruct((FIRST_ROWS + KEYVAL_ROWS, 128), jnp.bfloat16)
    last_shape = jax.ShapeDtypeStruct((2, last, 128), jnp.bfloat16)
    outs = pl.pallas_call(
        pick_kernel,
        out_shape=(first_shape,) * 4 + (last_shape,) * 2,
        in_specs=[pl.BlockSpec(memory_space=pltpu.SMEM)] * 3 + [pl.BlockSpec(memory_space=pl.ANY)],
        out_specs=(pl.BlockSpec(memory_space=pltpu.VMEM),) * 6,
        scratch_shapes=[pltpu.SemaphoreType.DMA((4, 3))],
        compiler_params=pltpu.CompilerParams(vmem_limit_bytes=16 << 20),
        cost_estimate=pl.CostEstimate(flops=0, bytes_accessed=3 << 20, transcendentals=0),
    )(here, there, owner, spread)
    return outs[:4], outs[4], outs[5]


def deal_kernel(rows, even, odd, sems):
    seat = lax.rem(lax.axis_index("ctx"), PIECES)
    width = rows.shape[1] // PIECES
    copies = []
    for apart in range(PIECES):
        first = pl.multiple_of((seat ^ apart) * width, width)
        target = (odd if apart % 2 else even).at[apart // 2]
        copies.append(
            pltpu.make_async_copy(rows.at[:, pl.ds(first, width)], target, sems.at[apart])
        )
    for copy in copies:
        copy.start()
    for copy in copies:
        copy.wait()


def deal(rows, *after):
    slab = jax.ShapeDtypeStruct((PIECES // 2, rows.shape[0], rows.shape[1] // PIECES), rows.dtype)

    def kernel(rows, *refs):
        deal_kernel(rows, *refs[-3:])

    return pl.pallas_call(
        kernel,
        out_shape=(slab, slab),
        in_specs=[pl.BlockSpec(memory_space=pl.ANY)] * (1 + len(after)),
        out_specs=(pl.BlockSpec(memory_space=pltpu.VMEM),) * 2,
        scratch_shapes=[pltpu.SemaphoreType.DMA((PIECES,))],
        compiler_params=pltpu.CompilerParams(vmem_limit_bytes=16 << 20),
        cost_estimate=pl.CostEstimate(flops=0, bytes_accessed=2 << 20, transcendentals=0),
    )(rows, *after)


def nearest(here, owner, block):
    half = lax.axis_index("ctx") // PIECES
    return owner[here[block]] // PIECES == half


def choose(close, arrived, put):
    plane = lax.axis_index("groups")

    @pl.when(close)
    def _():
        put(arrived[0], plane)
        put(arrived[2], 1 - plane)

    @pl.when(jnp.logical_not(close))
    def _():
        put(arrived[1], plane)
        put(arrived[3], 1 - plane)


def join_kernel(here, owner, *refs):
    arrived, (weight, ups), (flat, left, right) = refs[:4], refs[4:6], refs[6:]
    half = lax.axis_index("ctx") // PIECES
    split = DOWN_ROWS + QUERY_ROWS + KEYVAL_ROWS

    def put_own(source, position):
        first = pl.multiple_of(position * DOWN_ROWS, DOWN_ROWS)
        flat[pl.ds(first, DOWN_ROWS), :] = source[:DOWN_ROWS, :].astype(jnp.float32)
        ups[position, : UP_ROWS - KEYVAL_ROWS, :] = source[DOWN_ROWS:split, :]

    def put_mirrored(source, position):
        ups[position, UP_ROWS - KEYVAL_ROWS :, :] = source[split:, :]

    choose(nearest(here, owner, half), arrived, put_own)
    choose(nearest(here, owner, 1 - half), arrived, put_mirrored)

    third = flat.shape[0] // 3
    one = flat[pl.ds(0, third, stride=3), :]
    two = pltpu.roll(flat[pl.ds(1, third, stride=3), :], 64, 1)
    three = pltpu.roll(flat[pl.ds(2, third, stride=3), :], 64, 1)
    lane = lax.broadcasted_iota(jnp.int32, one.shape, 1)
    left[pl.ds(0, third, stride=2), :] = one
    left[pl.ds(1, third, stride=2), :] = jnp.where(lane < 64, two, three)
    right[pl.ds(0, third, stride=2), :] = pltpu.roll(two, 64, 1)
    right[pl.ds(1, third, stride=2), :] = three
    weight[...] = jnp.concatenate([left[...], right[...]], 1).astype(jnp.bfloat16)


def join(here, owner, arrived):
    depth = D // PIECES
    return pl.pallas_call(
        join_kernel,
        out_shape=(
            jax.ShapeDtypeStruct((depth, 256), jnp.bfloat16),
            jax.ShapeDtypeStruct((2, UP_ROWS, 128), jnp.bfloat16),
        ),
        in_specs=[pl.BlockSpec(memory_space=pltpu.SMEM)] * 2
        + [pl.BlockSpec(memory_space=pltpu.VMEM)] * 4,
        out_specs=(pl.BlockSpec(memory_space=pltpu.VMEM),) * 2,
        scratch_shapes=[
            pltpu.VMEM((2 * DOWN_ROWS, 128), jnp.float32),
            pltpu.VMEM((depth, 128), jnp.float32),
            pltpu.VMEM((depth, 128), jnp.float32),
        ],
        compiler_params=pltpu.CompilerParams(vmem_limit_bytes=16 << 20),
        cost_estimate=pl.CostEstimate(flops=0, bytes_accessed=96 << 20, transcendentals=0),
    )(here, owner, *arrived)


def settle_kernel(here, there, owner, near, far, own, across):
    half = lax.axis_index("ctx") // PIECES
    for number, (wishes, out) in enumerate(((here, own), (there, across))):
        close = nearest(wishes, owner, half)

        @pl.when(close)
        def _():
            out[...] = near[number]

        @pl.when(jnp.logical_not(close))
        def _():
            out[...] = far[number]


def settle(here, there, owner, near, far):
    slab = jax.ShapeDtypeStruct(near.shape[1:], jnp.bfloat16)
    return pl.pallas_call(
        settle_kernel,
        out_shape=(slab, slab),
        in_specs=[pl.BlockSpec(memory_space=pltpu.SMEM)] * 3
        + [pl.BlockSpec(memory_space=pltpu.VMEM)] * 2,
        out_specs=(pl.BlockSpec(memory_space=pltpu.VMEM),) * 2,
        compiler_params=pltpu.CompilerParams(vmem_limit_bytes=16 << 20),
        cost_estimate=pl.CostEstimate(flops=0, bytes_accessed=1 << 20, transcendentals=0),
    )(here, there, owner, near, far)


def narrow_kernel(weight, *refs):
    for block, out in zip(refs[:4], refs[4:]):
        sides, rows, depth = block.shape
        product = jnp.dot(
            block[...].reshape(sides * rows, depth),
            weight[...],
            preferred_element_type=jnp.float32,
        )
        out[...] = product[:, : 3 * ADAPTER_RANK].reshape(out.shape).astype(jnp.bfloat16)


def narrow(weight, dealt):
    sides, rows, depth = dealt[0].shape
    partial_sums = jax.ShapeDtypeStruct((sides, rows, 3 * ADAPTER_RANK), jnp.bfloat16)
    return pl.pallas_call(
        narrow_kernel,
        out_shape=(partial_sums,) * 4,
        in_specs=[pl.BlockSpec(memory_space=pltpu.VMEM)] * 5,
        out_specs=(pl.BlockSpec(memory_space=pltpu.VMEM),) * 4,
        compiler_params=pltpu.CompilerParams(vmem_limit_bytes=16 << 20),
        cost_estimate=pl.CostEstimate(
            flops=2 * 8 * rows * depth * 256, bytes_accessed=2 << 20, transcendentals=0
        ),
    )(weight, *dealt)


def attend_kernel(
    first_head,
    query_block,
    key_same,
    key_other,
    value_same,
    value_other,
    own_rank,
    all_rank,
    up_same,
    up_other,
    cosines,
    sines,
    *refs,
):
    attended, flat_query, flat_keyval, keys, values = refs[-5:]
    step = pl.program_id(0) + first_head
    rows = query_block.shape[0]
    base = lax.axis_index("ctx") * rows
    half = lax.axis_index("ctx") // PIECES
    seat = lax.rem(lax.axis_index("ctx"), PIECES)
    dot = partial(jnp.dot, preferred_element_type=jnp.float32)

    @pl.when(pl.program_id(0) == 0)
    def _():
        for apart in range(PIECES):
            ups = up_other if apart % 2 else up_same
            for position in range(2):
                piece = ups[apart // 2, position].astype(jnp.float32)
                place = (seat ^ apart) * 2 + position
                first = pl.multiple_of(place * QUERY_ROWS, QUERY_ROWS)
                flat_query[pl.ds(first, QUERY_ROWS), :] = piece[:QUERY_ROWS]
                first = pl.multiple_of(place * KEYVAL_ROWS, KEYVAL_ROWS)
                for side in range(2):
                    begin = QUERY_ROWS + side * KEYVAL_ROWS
                    flat_keyval[side, pl.ds(first, KEYVAL_ROWS), :] = piece[
                        begin : begin + KEYVAL_ROWS
                    ]

    def turned(delta, cosine, sine):
        return delta * cosine + pltpu.roll(delta, HEAD_SIZE // 2, 1) * sine

    def up(flat, first, stride):
        return flat[pl.ds(first, ADAPTER_RANK, stride=stride), :].astype(jnp.bfloat16)

    for side in range(2):
        heads = 2 * KEYVALUE_HEADS
        key_up = up(flat_keyval.at[side], step, heads)
        value_up = up(flat_keyval.at[side], step + KEYVALUE_HEADS, heads)
        for core in range(2):
            rank = all_rank[core, :, side].reshape(PIECES // 2 * rows, 2 * ADAPTER_RANK)
            key_delta = adapter_scale * dot(rank[:, :ADAPTER_RANK], key_up)
            value_delta = adapter_scale * dot(rank[:, ADAPTER_RANK:], value_up)
            for chip in range(PIECES // 2):
                there = seat ^ (2 * chip + core)
                first = ((half ^ side) * PIECES + there) * rows
                span = pl.ds(pl.multiple_of(first, rows), rows)
                part = slice(chip * rows, (chip + 1) * rows)
                delta = turned(key_delta[part], cosines[span, :], sines[span, :])
                full = (key_other if core else key_same)[chip, side].astype(jnp.float32) + delta
                keys[span, :] = full.astype(jnp.bfloat16)
                full = (value_other if core else value_same)[chip, side].astype(jnp.float32)
                values[span, :] = (full + value_delta[part]).astype(jnp.bfloat16)
    here = pl.ds(pl.multiple_of(base, rows), rows)
    cosine = cosines[here, :]
    sine = sines[here, :]
    taken = GROUP // 2
    for first in range(0, GROUP, taken):
        weight = [up(flat_query, step * GROUP + first + head, QH) for head in range(taken)]
        deltas = adapter_scale * dot(own_rank[:, :ADAPTER_RANK], jnp.concatenate(weight, 1))
        queries = []
        for place in range(taken):
            moved = turned(deltas[:, place * HEAD_SIZE : (place + 1) * HEAD_SIZE], cosine, sine)
            span = slice((first + place) * HEAD_SIZE, (first + place + 1) * HEAD_SIZE)
            queries.append(
                (query_block[:, span].astype(jnp.float32) + moved).astype(jnp.bfloat16)
            )
        queries = jnp.concatenate(queries, 0)
        scores = lax.dot_general(
            queries, keys[...], (((1,), (1,)), ((), ())), preferred_element_type=jnp.float32
        )
        row = lax.broadcasted_iota(jnp.int32, scores.shape, 0)
        column = lax.broadcasted_iota(jnp.int32, scores.shape, 1)
        scores = jnp.where(column <= base + lax.rem(row, rows), scores, mask_floor)
        scores = scores - jnp.max(scores, axis=-1, keepdims=True)
        weights = jnp.exp2(scores * (HEAD_SIZE ** (-0.5) * math.log2(math.e)))
        divisor = jnp.sum(weights, axis=-1, keepdims=True)
        result = (dot(weights.astype(jnp.bfloat16), values[...]) / divisor).astype(jnp.bfloat16)
        for place in range(taken):
            span = slice((first + place) * HEAD_SIZE, (first + place + 1) * HEAD_SIZE)
            attended[:, span] = result[place * rows : (place + 1) * rows]


def attend(first_head, heads, before, query_base, base, own_rank, all_rank, ups, cosines, sines):
    rows = query_base.shape[0]
    seq = 4 * PIECES // 2 * rows
    width = GROUP * HEAD_SIZE

    def whole(shape):
        return pl.BlockSpec(shape, lambda h: (0,) * len(shape))

    key_spec = pl.BlockSpec((PIECES // 2, 2, rows, HEAD_SIZE), lambda h: (0, 0, 0, h + first_head))
    value_spec = pl.BlockSpec(
        (PIECES // 2, 2, rows, HEAD_SIZE), lambda h: (0, 0, 0, h + first_head + KEYVALUE_HEADS)
    )
    operands = (query_base, base[0], base[1], base[0], base[1], own_rank, all_rank, *ups)
    operands += (cosines, sines) + (() if before is None else (before,))
    query_spec = pl.BlockSpec((rows, width), lambda h: (0, h + first_head))
    return pl.pallas_call(
        partial(attend_kernel, first_head),
        grid=(heads,),
        out_shape=jax.ShapeDtypeStruct((rows, QH * HEAD_SIZE), jnp.bfloat16),
        in_specs=[
            query_spec,
            key_spec,
            key_spec,
            value_spec,
            value_spec,
            whole(own_rank.shape),
            whole(all_rank.shape),
            whole(ups[0].shape),
            whole(ups[1].shape),
            whole(cosines.shape),
            whole(sines.shape),
        ]
        + [pl.BlockSpec(memory_space=pl.ANY)] * (len(operands) - 11),
        out_specs=query_spec,
        input_output_aliases={} if before is None else {len(operands) - 1: 0},
        scratch_shapes=[
            pltpu.VMEM((2 * PIECES * QUERY_ROWS, 128), jnp.float32),
            pltpu.VMEM((2, 2 * PIECES * KEYVAL_ROWS, 128), jnp.float32),
            pltpu.VMEM((seq, HEAD_SIZE), jnp.bfloat16),
            pltpu.VMEM((seq, HEAD_SIZE), jnp.bfloat16),
        ],
        compiler_params=pltpu.CompilerParams(vmem_limit_bytes=60 << 20),
        cost_estimate=pl.CostEstimate(
            flops=12 * heads * rows * QH * seq * HEAD_SIZE,
            bytes_accessed=10 << 20,
            transcendentals=heads * rows * GROUP * seq,
        ),
    )(*operands)


def widen_kernel(attended, same, other, out_delta, down_out, up_out):
    plane = lax.axis_index("groups")
    seat = lax.rem(lax.axis_index("ctx"), PIECES)
    for apart in range(PIECES):
        pieces = other if apart % 2 else same
        for position in range(2):
            piece = pieces[apart // 2, position].astype(jnp.float32)
            place = (seat ^ apart) * 2 + (position ^ plane)
            first = place * 2 * DOWN_OUT_ROWS
            block = piece[:DOWN_OUT_ROWS]
            down_out[pl.ds(first, DOWN_OUT_ROWS, stride=2), :] = block
            down_out[pl.ds(first + 1, DOWN_OUT_ROWS, stride=2), :] = pltpu.roll(block, 64, 1)
            first = pl.multiple_of(place * UP_OUT_ROWS, UP_OUT_ROWS)
            up_out[pl.ds(first, UP_OUT_ROWS), :] = piece[DOWN_OUT_ROWS:]
    dot = partial(jnp.dot, preferred_element_type=jnp.float32)
    rank = dot(attended[...], down_out[...].astype(jnp.bfloat16))[:, :ADAPTER_RANK]
    rank = rank.astype(jnp.bfloat16)
    blocks = D // 128
    for first in range(0, blocks, 4):
        weight = [
            up_out[pl.ds(first + block, ADAPTER_RANK, stride=blocks), :].astype(jnp.bfloat16)
            for block in range(4)
        ]
        delta = adapter_scale * dot(rank, jnp.concatenate(weight, 1))
        out_delta[:, first * 128 : (first + 4) * 128] = delta.astype(jnp.bfloat16)


def widen(attended, same, other):
    return pl.pallas_call(
        widen_kernel,
        out_shape=jax.ShapeDtypeStruct((attended.shape[0], D), jnp.bfloat16),
        in_specs=[pl.BlockSpec(memory_space=pltpu.VMEM)] * 3,
        out_specs=pl.BlockSpec(memory_space=pltpu.VMEM),
        scratch_shapes=[
            pltpu.VMEM((QH * HEAD_SIZE, 128), jnp.float32),
            pltpu.VMEM((ADAPTER_RANK * D // 128, 128), jnp.float32),
        ],
        compiler_params=pltpu.CompilerParams(vmem_limit_bytes=32 << 20),
        cost_estimate=pl.CostEstimate(flops=1 << 27, bytes_accessed=4 << 20, transcendentals=0),
    )(attended, same, other)


def swap(block, mask):
    return lax.ppermute(block, ("groups", "ctx"), [(i, i ^ mask) for i in range(4 * PIECES)])


def direct_shards(
    normed_input, query_base, key_base, value_base, adapter_pool, stretch_adapter, adapter_owner
):
    tok_rows = normed_input.shape[0]
    ctx = lax.axis_size("ctx")
    seq = ctx * tok_rows
    blocks = [list(range(PIECES)), list(range(PIECES, 2 * PIECES))]
    half_dim = HEAD_SIZE // 2
    frequency = rope_base ** (-(jnp.arange(half_dim, dtype=jnp.float32) * 2.0) / HEAD_SIZE)
    angle = jnp.arange(seq, dtype=jnp.int32).astype(jnp.float32)[:, None] * frequency[None, :]
    cosine = jnp.cos(angle)
    sine = jnp.sin(angle)
    cosines = jnp.concatenate([cosine, cosine], 1)
    sines = jnp.concatenate([-sine, sine], 1)

    def after(block, *others):
        return lax.optimization_barrier((block, others))[0]

    def exchange(sent):
        across = swap(sent[2], 2 * PIECES)
        return [sent[0], swap(sent[1], PIECES), across, swap(sent[3], 3 * PIECES)]

    def along_z(block):
        return jnp.stack([block, swap(block, 4)])

    def along_x(pair):
        quad = jnp.stack([pair, swap(pair, 2)], 1)
        return quad.reshape((PIECES // 2,) + pair.shape[1:])

    elsewhere = swap(stretch_adapter, 2 * PIECES)
    packed = pack_row(adapter_pool, SECTIONS)
    even, odd = deal(normed_input, packed)
    sibling = swap(odd, 1)
    base = jnp.concatenate([key_base, value_base], 1)
    base = jnp.stack([base, swap(base, PIECES)])

    spread = lax.all_to_all(packed, "ctx", 0, 0, axis_index_groups=blocks)
    spread = after(spread, sibling, base, cosines, sines)
    sent, near, far = pick(spread, stretch_adapter, elsewhere, adapter_owner)
    arrived = exchange(sent)
    dealt = [after(jnp.stack([even[j], sibling[j]]), sent) for j in range(PIECES // 2)]
    dealt = [swap(block, 2 * j) if j else block for j, block in enumerate(dealt)]

    weight, ups = join(stretch_adapter, adapter_owner, arrived)
    far = swap(after(far, weight), PIECES)
    partial_sums = narrow(weight, dealt)
    back = [swap(block, 2 * j) if j else block for j, block in enumerate(partial_sums)]
    back = sum(block.astype(jnp.float32) for block in back)
    own_rank = swap(after(back[1].astype(jnp.bfloat16), far), 1)
    own_rank = back[0] + own_rank.astype(jnp.float32)
    own_rank = own_rank.astype(jnp.bfloat16)
    ups = along_z(after(ups, *partial_sums))
    base = along_z(after(base, *partial_sums))
    all_rank = own_rank[:, ADAPTER_RANK:]
    base = along_x(after(base, own_rank))
    own, across = settle(
        stretch_adapter, elsewhere, adapter_owner, near, after(far, own_rank)
    )
    ends = jnp.stack([own, swap(across, 2 * PIECES)])
    all_rank = jnp.stack([all_rank, swap(all_rank, PIECES)])
    all_rank = after(all_rank, ups)
    ups = along_x(after(ups, all_rank))
    all_rank = jnp.stack([swap(all_rank, apart) if apart else all_rank for apart in (0, 2, 4, 6)])
    base = after(base, all_rank)
    base = (base, swap(base, 1))
    all_rank = after(all_rank, ups, ends)
    ups = (ups, swap(ups, 1))
    all_rank = jnp.stack([all_rank, swap(all_rank, 1)])

    shared = (query_base, base, own_rank, all_rank, ups, cosines, sines)
    attended = attend(0, 1, None, *shared)
    ends = after(ends, attended)
    ends = jnp.stack([swap(ends, apart) if apart else ends for apart in (0, 2, 4, 6)])
    attended = attend(1, KEYVALUE_HEADS - 1, attended, *shared)
    ends = after(ends, attended)
    return attended, widen(attended, ends, swap(ends, 1))


def shards(normed_input, query_base, key_base, value_base, adapter_pool, stretch_adapter, owner):
    fits = (
        lax.axis_size("groups") == 2
        and lax.axis_size("ctx") == 2 * PIECES
        and normed_input.shape[0] * PIECES == BLOCK_TOKENS
        and adapter_pool.shape[0] == 1
    )
    plan = direct_shards if fits else spread_shards
    return plan(
        normed_input, query_base, key_base, value_base, adapter_pool, stretch_adapter, owner
    )


def solution(mesh):
    placed = (
        P(("groups", "ctx"), None),
        P(("groups", "ctx"), None),
        P(("groups", "ctx"), None),
        P(("groups", "ctx"), None),
        P("ctx", None),
        P("groups"),
        P(),
    )
    return jax.shard_map(
        shards,
        mesh=mesh,
        in_specs=placed,
        out_specs=(P(("groups", "ctx"), None), P(("groups", "ctx"), None)),
        check_vma=False,
    )
```

```python
from functools import partial
import math

import jax
import jax.numpy as jnp
from jax import lax
from jax.experimental import pallas as pl
from jax.experimental.pallas import tpu as pltpu
from jax.sharding import PartitionSpec as P

D = 8192
QH = 32
KEYVALUE_HEADS = 4
HEAD_SIZE = 128
ADAPTER_RANK = 64
BLOCK_TOKENS = 512
QKV_POOL = 1900544


adapter_scale = 2.0
rope_base = 500000.0
mask_floor = -1e30


def from_partner(block, axis, apart):
    count = lax.axis_size(axis)
    route = []
    for low in range(count):
        high = low | 1 << apart
        if high != low and high < count:
            route += [(low, high), (high, low)]
    return lax.ppermute(block, axis, route)


def rotate(delta, token_positions, heads):
    half_dim = HEAD_SIZE // 2
    frequency = rope_base ** (-(jnp.arange(half_dim, dtype=jnp.float32) * 2.0) / HEAD_SIZE)
    angle = token_positions.astype(jnp.float32)[:, None] * frequency[None, :]
    cosine = jnp.cos(angle)[:, None, :]
    sine_part = jnp.sin(angle)[:, None, :]
    shaped = delta.reshape(delta.shape[0], heads, HEAD_SIZE)
    first_half = shaped[..., :half_dim]
    second_half = shaped[..., half_dim:]
    joined = jnp.concatenate(
        [
            first_half * cosine - second_half * sine_part,
            second_half * cosine + first_half * sine_part,
        ],
        -1,
    )
    return joined.reshape(delta.shape[0], heads * HEAD_SIZE)


def project_heads(
    narrow_product, query_row_block, key_row_block, value_row_block, upper_part, token_positions
):
    query_up_weight = upper_part[: ADAPTER_RANK * QH * HEAD_SIZE].reshape(
        ADAPTER_RANK, QH * HEAD_SIZE
    )
    keyvalue_up_weight = upper_part[ADAPTER_RANK * QH * HEAD_SIZE :].reshape(
        ADAPTER_RANK, 2 * KEYVALUE_HEADS * HEAD_SIZE
    )
    query_correction = adapter_scale * jnp.dot(
        narrow_product[:, :ADAPTER_RANK], query_up_weight, preferred_element_type=jnp.float32
    )
    key_correction = adapter_scale * jnp.dot(
        narrow_product[:, ADAPTER_RANK : 2 * ADAPTER_RANK],
        keyvalue_up_weight[:, : KEYVALUE_HEADS * HEAD_SIZE],
        preferred_element_type=jnp.float32,
    )
    value_correction = adapter_scale * jnp.dot(
        narrow_product[:, 2 * ADAPTER_RANK :],
        keyvalue_up_weight[:, KEYVALUE_HEADS * HEAD_SIZE :],
        preferred_element_type=jnp.float32,
    )
    queries = (
        query_row_block.astype(jnp.float32) + rotate(query_correction, token_positions, QH)
    ).astype(jnp.bfloat16)
    new_keys = (
        key_row_block.astype(jnp.float32) + rotate(key_correction, token_positions, KEYVALUE_HEADS)
    ).astype(jnp.bfloat16)
    new_values = (value_row_block.astype(jnp.float32) + value_correction).astype(jnp.bfloat16)
    return (queries, new_keys, new_values)


def output_delta(attended_rows, out_part):
    down_out = out_part[: QH * HEAD_SIZE * ADAPTER_RANK].reshape(QH * HEAD_SIZE, ADAPTER_RANK)
    raised_output = out_part[QH * HEAD_SIZE * ADAPTER_RANK :].reshape(ADAPTER_RANK, D)
    narrow_product = jnp.dot(attended_rows, down_out, preferred_element_type=jnp.float32).astype(
        jnp.bfloat16
    )
    return (
        adapter_scale * jnp.dot(narrow_product, raised_output, preferred_element_type=jnp.float32)
    ).astype(jnp.bfloat16)


def head_major(query_row_block):
    count_rows = query_row_block.shape[0]
    group_size = QH // KEYVALUE_HEADS
    return (
        query_row_block.reshape(count_rows, KEYVALUE_HEADS, group_size, HEAD_SIZE)
        .transpose(1, 2, 0, 3)
        .reshape(KEYVALUE_HEADS, group_size * count_rows, HEAD_SIZE)
    )


def row_major(head_rows, count_rows):
    group_size = QH // KEYVALUE_HEADS
    return (
        head_rows.reshape(KEYVALUE_HEADS, group_size, count_rows, HEAD_SIZE)
        .transpose(2, 0, 1, 3)
        .reshape(count_rows, QH * HEAD_SIZE)
    )


def online_update(current, queries, query_pos, key_slice, value_slice, key_start):
    run_max, run_sum, run_acc = current
    scores = jnp.einsum(
        "hqd,khd->hqk", queries, key_slice, preferred_element_type=jnp.float32
    ) * HEAD_SIZE ** (-0.5)
    key_pos = key_start + jnp.arange(key_slice.shape[0], dtype=jnp.int32)
    allowed = (query_pos[:, None] >= key_pos[None, :])[None]
    new_max = jnp.maximum(run_max, jnp.max(jnp.where(allowed, scores, mask_floor), axis=-1))
    weights = jnp.where(allowed, jnp.exp(scores - new_max[..., None]), 0.0)
    rescale = jnp.exp(run_max - new_max)
    new_sum = run_sum * rescale + jnp.sum(weights, axis=-1)
    new_acc = run_acc * rescale[..., None] + jnp.einsum(
        "hqk,khd->hqd",
        weights.astype(jnp.bfloat16),
        value_slice,
        preferred_element_type=jnp.float32,
    )
    return (new_max, new_sum, new_acc)


def unchanged(current):
    return current


def fold_keys(carry_state, shard_part, prepared):
    key_row_block, value_row_block = shard_part
    key_count = key_row_block.shape[0]
    sub_width = math.gcd(key_count, 1024)
    key_heads = key_row_block.reshape(key_count // sub_width, sub_width, KEYVALUE_HEADS, HEAD_SIZE)
    value_heads = value_row_block.reshape(
        key_count // sub_width, sub_width, KEYVALUE_HEADS, HEAD_SIZE
    )

    def one_step(sub_index, carried):
        key_start = sub_index * sub_width
        key_slice = lax.dynamic_index_in_dim(key_heads, sub_index, 0, keepdims=False)
        value_slice = lax.dynamic_index_in_dim(value_heads, sub_index, 0, keepdims=False)
        updated = []
        for (queries, query_pos), running in zip(prepared, carried):
            advance = partial(
                online_update,
                queries=queries,
                query_pos=query_pos,
                key_slice=key_slice,
                value_slice=value_slice,
                key_start=key_start,
            )
            updated.append(lax.cond(key_start <= jnp.max(query_pos), advance, unchanged, running))
        return tuple(updated)

    return lax.fori_loop(0, key_count // sub_width, one_step, carry_state)


def finish_block(result, count_rows):
    run_max, run_sum, run_acc = result
    divisor = jnp.where(run_sum > 0.0, run_sum, 1.0)
    return row_major(run_acc / divisor[..., None], count_rows).astype(jnp.bfloat16)


def spread_shards(
    normed_input, query_base, key_base, value_base, adapter_pool, stretch_adapter, adapter_owner
):
    cycle_size = lax.axis_size("ctx")
    my_index = lax.axis_index("ctx")
    tok_rows = normed_input.shape[0]
    token_positions = my_index * tok_rows + jnp.arange(tok_rows, dtype=jnp.int32)
    device_ids = jnp.arange(cycle_size, dtype=jnp.int32)
    stretch_of = device_ids * tok_rows // BLOCK_TOKENS
    stretch_ids = jnp.arange(stretch_adapter.shape[0], dtype=jnp.int32)
    adapter_of = jnp.sum(
        jnp.where(stretch_of[:, None] == stretch_ids[None, :], stretch_adapter[None, :], 0), axis=1
    )
    adapter_ids = jnp.arange(adapter_owner.shape[0], dtype=jnp.int32)
    slot_of = jnp.sum(
        jnp.where(adapter_of[:, None] == adapter_ids[None, :], adapter_owner[None, :], 0), axis=1
    )
    down_size = 3 * ADAPTER_RANK * D
    group_count = BLOCK_TOKENS // tok_rows
    levels = group_count.bit_length() - 1
    local_index = my_index % group_count
    col_width = D // group_count
    piece_len = down_size // (group_count * cycle_size)
    pool_rows = adapter_pool.shape[0]
    down_shaped = adapter_pool[:, :down_size].reshape(pool_rows, group_count, cycle_size, piece_len)
    spread_down = lax.all_to_all(down_shaped, "ctx", split_axis=2, concat_axis=0, tiled=True)
    flat_down = spread_down.reshape(-1, piece_len)
    wanted = jnp.take(flat_down, slot_of * group_count + device_ids % group_count, axis=0)[
        :, None, :
    ]
    down_slice = lax.all_to_all(wanted, "ctx", split_axis=0, concat_axis=1, tiled=True).reshape(
        col_width, 3 * ADAPTER_RANK
    )
    spread_rest = lax.all_to_all(
        adapter_pool[:, down_size:], "ctx", split_axis=1, concat_axis=0, tiled=True
    )
    rest_row = lax.all_to_all(
        jnp.take(spread_rest, slot_of, axis=0), "ctx", split_axis=0, concat_axis=1, tiled=True
    )[0]
    upper_part = rest_row[: QKV_POOL - down_size]
    out_part = rest_row[QKV_POOL - down_size :]
    pieces = normed_input.reshape(tok_rows, group_count, col_width)
    slice_order = jnp.bitwise_xor(local_index, jnp.arange(group_count, dtype=jnp.int32))
    moving = jnp.take(pieces, slice_order, axis=1).transpose(1, 0, 2)
    for level in range(levels):
        shaped = moving.reshape(group_count >> level + 1, 2, 1 << level, tok_rows, col_width)
        arrived = from_partner(shaped[:, 1], "ctx", level)
        moving = jnp.stack([shaped[:, 0], arrived], 1).reshape(group_count, tok_rows, col_width)
    partial_rows = jnp.dot(
        moving.reshape(group_count * tok_rows, col_width),
        down_slice,
        preferred_element_type=jnp.float32,
    ).reshape(group_count, tok_rows, 3 * ADAPTER_RANK)
    for level in reversed(range(levels)):
        halves = partial_rows.reshape(2, partial_rows.shape[0] // 2, tok_rows, 3 * ADAPTER_RANK)
        partial_rows = halves[0] + from_partner(
            halves[1].astype(jnp.bfloat16), "ctx", level
        ).astype(jnp.float32)
    narrow_product = partial_rows[0].astype(jnp.bfloat16)
    queries, new_keys, new_values = project_heads(
        narrow_product, query_base, key_base, value_base, upper_part, token_positions
    )
    group_size = QH // KEYVALUE_HEADS
    blocks = [(queries, token_positions)]
    prepared = [
        (head_major(block_q), jnp.tile(block_pos, group_size)) for block_q, block_pos in blocks
    ]
    initial = tuple(
        (
            (
                jnp.full((KEYVALUE_HEADS, head_q.shape[1]), mask_floor, jnp.float32),
                jnp.zeros((KEYVALUE_HEADS, head_q.shape[1]), jnp.float32),
                jnp.zeros((KEYVALUE_HEADS, head_q.shape[1], HEAD_SIZE), jnp.float32),
            )
            for head_q, block_pos in prepared
        )
    )
    finals = fold_keys(
        initial,
        (
            lax.all_gather(new_keys, "ctx", axis=0, tiled=True),
            lax.all_gather(new_values, "ctx", axis=0, tiled=True),
        ),
        prepared,
    )
    attended = finish_block(finals[0], tok_rows)
    out_delta = output_delta(attended, out_part)
    return (attended, out_delta)


PIECES = 8
GROUP = QH // KEYVALUE_HEADS
SECTIONS = ((0, 12288), (12288, 2048), (14336, 512), (14848, 2048), (16896, 4096))
DOWN_ROWS, QUERY_ROWS, KEYVAL_ROWS, DOWN_OUT_ROWS, UP_OUT_ROWS = 768, 128, 32, 128, 256
UP_ROWS = QUERY_ROWS + 2 * KEYVAL_ROWS
FIRST_ROWS = DOWN_ROWS + QUERY_ROWS + KEYVAL_ROWS


def pack_kernel(sections, pool, *refs):
    out, buffers, sems = refs[-3:]
    plane = lax.axis_index("groups")
    slabs, slab_rows = out.shape[:2]

    def copies(slab):
        listed = []
        offset = 0
        for first, rows in sections:
            share = rows // (2 * PIECES)
            begin = first + (slab * 2 + plane) * share
            listed.append(
                pltpu.make_async_copy(
                    pool.at[:, pl.ds(pl.multiple_of(begin * 128, 2048), share * 128)],
                    buffers.at[slab, :, pl.ds(offset, share * 128)],
                    sems.at[slab, len(listed)],
                )
            )
            offset += share * 128
        return listed

    for slab in range(slabs):
        for copy in copies(slab):
            copy.start()

    def step(slab, carried):
        for copy in copies(slab):
            copy.wait()

        def chunk(index, inner):
            line = buffers[slab, :, pl.ds(pl.multiple_of(index * 2048, 2048), 2048)]
            block = line.astype(jnp.float32).reshape(16, 128).astype(jnp.bfloat16)
            out[slab, pl.ds(pl.multiple_of(index * 16, 16), 16), :] = block
            return inner

        lax.fori_loop(0, slab_rows // 16, chunk, 0, unroll=8)
        return carried

    lax.fori_loop(0, slabs, step, 0)


def pack_row(pool, sections, *after):
    slab_rows = sum(rows for _, rows in sections) // (2 * PIECES)
    return pl.pallas_call(
        partial(pack_kernel, sections),
        out_shape=jax.ShapeDtypeStruct((PIECES, slab_rows, 128), jnp.bfloat16),
        in_specs=[pl.BlockSpec(memory_space=pl.ANY)] * (1 + len(after)),
        out_specs=pl.BlockSpec(memory_space=pltpu.VMEM),
        scratch_shapes=[
            pltpu.VMEM((PIECES, 1, slab_rows * 128), jnp.bfloat16),
            pltpu.SemaphoreType.DMA((PIECES, len(sections))),
        ],
        compiler_params=pltpu.CompilerParams(vmem_limit_bytes=60 << 20),
        cost_estimate=pl.CostEstimate(flops=0, bytes_accessed=8 << 20, transcendentals=0),
    )(pool, *after)


def pick_kernel(here, there, owner, spread, *refs):
    outs, lasts, sems = refs[:4], refs[4:6], refs[6]
    half = lax.axis_index("ctx") // PIECES
    last = spread.shape[1] - FIRST_ROWS
    copies = []
    for flip, out in enumerate(outs):
        wishes = there if flip >= 2 else here
        block = half ^ (flip & 1)
        row = lax.rem(owner[wishes[block]], PIECES)
        mirrored = lax.rem(owner[wishes[1 - block]], PIECES)
        pairs = (
            (spread.at[row, pl.ds(0, FIRST_ROWS)], out.at[pl.ds(0, FIRST_ROWS)]),
            (
                spread.at[mirrored, pl.ds(FIRST_ROWS - KEYVAL_ROWS, KEYVAL_ROWS)],
                out.at[pl.ds(FIRST_ROWS, KEYVAL_ROWS)],
            ),
            (spread.at[row, pl.ds(FIRST_ROWS, last)], lasts[flip % 2].at[flip // 2]),
        )
        for number, (source, target) in enumerate(pairs):
            copies.append(pltpu.make_async_copy(source, target, sems.at[flip, number]))
    for copy in copies:
        copy.start()
    for copy in copies:
        copy.wait()


def pick(spread, here, there, owner):
    last = spread.shape[1] - FIRST_ROWS
    first_shape = jax.ShapeDtypeStruct((FIRST_ROWS + KEYVAL_ROWS, 128), jnp.bfloat16)
    last_shape = jax.ShapeDtypeStruct((2, last, 128), jnp.bfloat16)
    outs = pl.pallas_call(
        pick_kernel,
        out_shape=(first_shape,) * 4 + (last_shape,) * 2,
        in_specs=[pl.BlockSpec(memory_space=pltpu.SMEM)] * 3 + [pl.BlockSpec(memory_space=pl.ANY)],
        out_specs=(pl.BlockSpec(memory_space=pltpu.VMEM),) * 6,
        scratch_shapes=[pltpu.SemaphoreType.DMA((4, 3))],
        compiler_params=pltpu.CompilerParams(vmem_limit_bytes=16 << 20),
        cost_estimate=pl.CostEstimate(flops=0, bytes_accessed=3 << 20, transcendentals=0),
    )(here, there, owner, spread)
    return outs[:4], outs[4], outs[5]


def deal_kernel(rows, even, odd, sems):
    seat = lax.rem(lax.axis_index("ctx"), PIECES)
    width = rows.shape[1] // PIECES
    copies = []
    for apart in range(PIECES):
        first = pl.multiple_of((seat ^ apart) * width, width)
        target = (odd if apart % 2 else even).at[apart // 2]
        copies.append(
            pltpu.make_async_copy(rows.at[:, pl.ds(first, width)], target, sems.at[apart])
        )
    for copy in copies:
        copy.start()
    for copy in copies:
        copy.wait()


def deal(rows, *after):
    slab = jax.ShapeDtypeStruct((PIECES // 2, rows.shape[0], rows.shape[1] // PIECES), rows.dtype)

    def kernel(rows, *refs):
        deal_kernel(rows, *refs[-3:])

    return pl.pallas_call(
        kernel,
        out_shape=(slab, slab),
        in_specs=[pl.BlockSpec(memory_space=pl.ANY)] * (1 + len(after)),
        out_specs=(pl.BlockSpec(memory_space=pltpu.VMEM),) * 2,
        scratch_shapes=[pltpu.SemaphoreType.DMA((PIECES,))],
        compiler_params=pltpu.CompilerParams(vmem_limit_bytes=16 << 20),
        cost_estimate=pl.CostEstimate(flops=0, bytes_accessed=2 << 20, transcendentals=0),
    )(rows, *after)


def nearest(here, owner, block):
    half = lax.axis_index("ctx") // PIECES
    return owner[here[block]] // PIECES == half


def choose(close, arrived, put):
    plane = lax.axis_index("groups")

    @pl.when(close)
    def _():
        put(arrived[0], plane)
        put(arrived[2], 1 - plane)

    @pl.when(jnp.logical_not(close))
    def _():
        put(arrived[1], plane)
        put(arrived[3], 1 - plane)


def join_kernel(here, owner, *refs):
    arrived, (weight, ups), (flat, left, right) = refs[:4], refs[4:6], refs[6:]
    half = lax.axis_index("ctx") // PIECES
    split = DOWN_ROWS + QUERY_ROWS + KEYVAL_ROWS

    def put_own(source, position):
        first = pl.multiple_of(position * DOWN_ROWS, DOWN_ROWS)
        flat[pl.ds(first, DOWN_ROWS), :] = source[:DOWN_ROWS, :].astype(jnp.float32)
        ups[position, : UP_ROWS - KEYVAL_ROWS, :] = source[DOWN_ROWS:split, :]

    def put_mirrored(source, position):
        ups[position, UP_ROWS - KEYVAL_ROWS :, :] = source[split:, :]

    choose(nearest(here, owner, half), arrived, put_own)
    choose(nearest(here, owner, 1 - half), arrived, put_mirrored)

    third = flat.shape[0] // 3
    one = flat[pl.ds(0, third, stride=3), :]
    two = pltpu.roll(flat[pl.ds(1, third, stride=3), :], 64, 1)
    three = pltpu.roll(flat[pl.ds(2, third, stride=3), :], 64, 1)
    lane = lax.broadcasted_iota(jnp.int32, one.shape, 1)
    left[pl.ds(0, third, stride=2), :] = one
    left[pl.ds(1, third, stride=2), :] = jnp.where(lane < 64, two, three)
    right[pl.ds(0, third, stride=2), :] = pltpu.roll(two, 64, 1)
    right[pl.ds(1, third, stride=2), :] = three
    weight[...] = jnp.concatenate([left[...], right[...]], 1).astype(jnp.bfloat16)


def join(here, owner, arrived):
    depth = D // PIECES
    return pl.pallas_call(
        join_kernel,
        out_shape=(
            jax.ShapeDtypeStruct((depth, 256), jnp.bfloat16),
            jax.ShapeDtypeStruct((2, UP_ROWS, 128), jnp.bfloat16),
        ),
        in_specs=[pl.BlockSpec(memory_space=pltpu.SMEM)] * 2
        + [pl.BlockSpec(memory_space=pltpu.VMEM)] * 4,
        out_specs=(pl.BlockSpec(memory_space=pltpu.VMEM),) * 2,
        scratch_shapes=[
            pltpu.VMEM((2 * DOWN_ROWS, 128), jnp.float32),
            pltpu.VMEM((depth, 128), jnp.float32),
            pltpu.VMEM((depth, 128), jnp.float32),
        ],
        compiler_params=pltpu.CompilerParams(vmem_limit_bytes=16 << 20),
        cost_estimate=pl.CostEstimate(flops=0, bytes_accessed=96 << 20, transcendentals=0),
    )(here, owner, *arrived)


def settle_kernel(here, there, owner, near, far, own, across):
    half = lax.axis_index("ctx") // PIECES
    for number, (wishes, out) in enumerate(((here, own), (there, across))):
        close = nearest(wishes, owner, half)

        @pl.when(close)
        def _():
            out[...] = near[number]

        @pl.when(jnp.logical_not(close))
        def _():
            out[...] = far[number]


def settle(here, there, owner, near, far):
    slab = jax.ShapeDtypeStruct(near.shape[1:], jnp.bfloat16)
    return pl.pallas_call(
        settle_kernel,
        out_shape=(slab, slab),
        in_specs=[pl.BlockSpec(memory_space=pltpu.SMEM)] * 3
        + [pl.BlockSpec(memory_space=pltpu.VMEM)] * 2,
        out_specs=(pl.BlockSpec(memory_space=pltpu.VMEM),) * 2,
        compiler_params=pltpu.CompilerParams(vmem_limit_bytes=16 << 20),
        cost_estimate=pl.CostEstimate(flops=0, bytes_accessed=1 << 20, transcendentals=0),
    )(here, there, owner, near, far)


def narrow_kernel(weight, *refs):
    for block, out in zip(refs[:4], refs[4:]):
        sides, rows, depth = block.shape
        product = jnp.dot(
            block[...].reshape(sides * rows, depth),
            weight[...],
            preferred_element_type=jnp.float32,
        )
        out[...] = product[:, : 3 * ADAPTER_RANK].reshape(out.shape).astype(jnp.bfloat16)


def narrow(weight, dealt):
    sides, rows, depth = dealt[0].shape
    partial_sums = jax.ShapeDtypeStruct((sides, rows, 3 * ADAPTER_RANK), jnp.bfloat16)
    return pl.pallas_call(
        narrow_kernel,
        out_shape=(partial_sums,) * 4,
        in_specs=[pl.BlockSpec(memory_space=pltpu.VMEM)] * 5,
        out_specs=(pl.BlockSpec(memory_space=pltpu.VMEM),) * 4,
        compiler_params=pltpu.CompilerParams(vmem_limit_bytes=16 << 20),
        cost_estimate=pl.CostEstimate(
            flops=2 * 8 * rows * depth * 256, bytes_accessed=2 << 20, transcendentals=0
        ),
    )(weight, *dealt)


def attend_kernel(
    first_head,
    query_block,
    key_same,
    key_other,
    value_same,
    value_other,
    own_rank,
    all_rank,
    up_same,
    up_other,
    cosines,
    sines,
    *refs,
):
    attended, flat_query, flat_keyval, keys, values = refs[-5:]
    step = pl.program_id(0) + first_head
    rows = query_block.shape[0]
    base = lax.axis_index("ctx") * rows
    half = lax.axis_index("ctx") // PIECES
    seat = lax.rem(lax.axis_index("ctx"), PIECES)
    dot = partial(jnp.dot, preferred_element_type=jnp.float32)

    @pl.when(pl.program_id(0) == 0)
    def _():
        for apart in range(PIECES):
            ups = up_other if apart % 2 else up_same
            for position in range(2):
                piece = ups[apart // 2, position].astype(jnp.float32)
                place = (seat ^ apart) * 2 + position
                first = pl.multiple_of(place * QUERY_ROWS, QUERY_ROWS)
                flat_query[pl.ds(first, QUERY_ROWS), :] = piece[:QUERY_ROWS]
                first = pl.multiple_of(place * KEYVAL_ROWS, KEYVAL_ROWS)
                for side in range(2):
                    begin = QUERY_ROWS + side * KEYVAL_ROWS
                    flat_keyval[side, pl.ds(first, KEYVAL_ROWS), :] = piece[
                        begin : begin + KEYVAL_ROWS
                    ]

    def turned(delta, cosine, sine):
        return delta * cosine + pltpu.roll(delta, HEAD_SIZE // 2, 1) * sine

    def up(flat, first, stride):
        return flat[pl.ds(first, ADAPTER_RANK, stride=stride), :].astype(jnp.bfloat16)

    for side in range(2):
        heads = 2 * KEYVALUE_HEADS
        key_up = up(flat_keyval.at[side], step, heads)
        value_up = up(flat_keyval.at[side], step + KEYVALUE_HEADS, heads)
        for core in range(2):
            rank = all_rank[core, :, side].reshape(PIECES // 2 * rows, 2 * ADAPTER_RANK)
            key_delta = adapter_scale * dot(rank[:, :ADAPTER_RANK], key_up)
            value_delta = adapter_scale * dot(rank[:, ADAPTER_RANK:], value_up)
            for chip in range(PIECES // 2):
                there = seat ^ (2 * chip + core)
                first = ((half ^ side) * PIECES + there) * rows
                span = pl.ds(pl.multiple_of(first, rows), rows)
                part = slice(chip * rows, (chip + 1) * rows)
                delta = turned(key_delta[part], cosines[span, :], sines[span, :])
                full = (key_other if core else key_same)[chip, side].astype(jnp.float32) + delta
                keys[span, :] = full.astype(jnp.bfloat16)
                full = (value_other if core else value_same)[chip, side].astype(jnp.float32)
                values[span, :] = (full + value_delta[part]).astype(jnp.bfloat16)
    here = pl.ds(pl.multiple_of(base, rows), rows)
    cosine = cosines[here, :]
    sine = sines[here, :]
    taken = GROUP // 2
    for first in range(0, GROUP, taken):
        weight = [up(flat_query, step * GROUP + first + head, QH) for head in range(taken)]
        deltas = adapter_scale * dot(own_rank[:, :ADAPTER_RANK], jnp.concatenate(weight, 1))
        queries = []
        for place in range(taken):
            moved = turned(deltas[:, place * HEAD_SIZE : (place + 1) * HEAD_SIZE], cosine, sine)
            span = slice((first + place) * HEAD_SIZE, (first + place + 1) * HEAD_SIZE)
            queries.append(
                (query_block[:, span].astype(jnp.float32) + moved).astype(jnp.bfloat16)
            )
        queries = jnp.concatenate(queries, 0)
        scores = lax.dot_general(
            queries, keys[...], (((1,), (1,)), ((), ())), preferred_element_type=jnp.float32
        )
        row = lax.broadcasted_iota(jnp.int32, scores.shape, 0)
        column = lax.broadcasted_iota(jnp.int32, scores.shape, 1)
        scores = jnp.where(column <= base + lax.rem(row, rows), scores, mask_floor)
        scores = scores - jnp.max(scores, axis=-1, keepdims=True)
        weights = jnp.exp2(scores * (HEAD_SIZE ** (-0.5) * math.log2(math.e)))
        divisor = jnp.sum(weights, axis=-1, keepdims=True)
        result = (dot(weights.astype(jnp.bfloat16), values[...]) / divisor).astype(jnp.bfloat16)
        for place in range(taken):
            span = slice((first + place) * HEAD_SIZE, (first + place + 1) * HEAD_SIZE)
            attended[:, span] = result[place * rows : (place + 1) * rows]


def attend(first_head, heads, before, query_base, base, own_rank, all_rank, ups, cosines, sines):
    rows = query_base.shape[0]
    seq = 4 * PIECES // 2 * rows
    width = GROUP * HEAD_SIZE

    def whole(shape):
        return pl.BlockSpec(shape, lambda h: (0,) * len(shape))

    key_spec = pl.BlockSpec((PIECES // 2, 2, rows, HEAD_SIZE), lambda h: (0, 0, 0, h + first_head))
    value_spec = pl.BlockSpec(
        (PIECES // 2, 2, rows, HEAD_SIZE), lambda h: (0, 0, 0, h + first_head + KEYVALUE_HEADS)
    )
    operands = (query_base, base[0], base[1], base[0], base[1], own_rank, all_rank, *ups)
    operands += (cosines, sines) + (() if before is None else (before,))
    query_spec = pl.BlockSpec((rows, width), lambda h: (0, h + first_head))
    return pl.pallas_call(
        partial(attend_kernel, first_head),
        grid=(heads,),
        out_shape=jax.ShapeDtypeStruct((rows, QH * HEAD_SIZE), jnp.bfloat16),
        in_specs=[
            query_spec,
            key_spec,
            key_spec,
            value_spec,
            value_spec,
            whole(own_rank.shape),
            whole(all_rank.shape),
            whole(ups[0].shape),
            whole(ups[1].shape),
            whole(cosines.shape),
            whole(sines.shape),
        ]
        + [pl.BlockSpec(memory_space=pl.ANY)] * (len(operands) - 11),
        out_specs=query_spec,
        input_output_aliases={} if before is None else {len(operands) - 1: 0},
        scratch_shapes=[
            pltpu.VMEM((2 * PIECES * QUERY_ROWS, 128), jnp.float32),
            pltpu.VMEM((2, 2 * PIECES * KEYVAL_ROWS, 128), jnp.float32),
            pltpu.VMEM((seq, HEAD_SIZE), jnp.bfloat16),
            pltpu.VMEM((seq, HEAD_SIZE), jnp.bfloat16),
        ],
        compiler_params=pltpu.CompilerParams(vmem_limit_bytes=60 << 20),
        cost_estimate=pl.CostEstimate(
            flops=12 * heads * rows * QH * seq * HEAD_SIZE,
            bytes_accessed=10 << 20,
            transcendentals=heads * rows * GROUP * seq,
        ),
    )(*operands)


def widen_kernel(attended_rows, same, other, out_delta, down_out, up_out, attended, sem):
    fetch = pltpu.make_async_copy(attended_rows, attended, sem)
    fetch.start()
    plane = lax.axis_index("groups")
    seat = lax.rem(lax.axis_index("ctx"), PIECES)
    for apart in range(PIECES):
        pieces = other if apart % 2 else same
        for position in range(2):
            piece = pieces[apart // 2, position].astype(jnp.float32)
            place = (seat ^ apart) * 2 + (position ^ plane)
            first = place * 2 * DOWN_OUT_ROWS
            block = piece[:DOWN_OUT_ROWS]
            down_out[pl.ds(first, DOWN_OUT_ROWS, stride=2), :] = block
            down_out[pl.ds(first + 1, DOWN_OUT_ROWS, stride=2), :] = pltpu.roll(block, 64, 1)
            first = pl.multiple_of(place * UP_OUT_ROWS, UP_OUT_ROWS)
            up_out[pl.ds(first, UP_OUT_ROWS), :] = piece[DOWN_OUT_ROWS:]
    dot = partial(jnp.dot, preferred_element_type=jnp.float32)
    fetch.wait()
    rank = dot(attended[...], down_out[...].astype(jnp.bfloat16))[:, :ADAPTER_RANK]
    rank = rank.astype(jnp.bfloat16)
    blocks = D // 128
    for first in range(0, blocks, 4):
        weight = [
            up_out[pl.ds(first + block, ADAPTER_RANK, stride=blocks), :].astype(jnp.bfloat16)
            for block in range(4)
        ]
        delta = adapter_scale * dot(rank, jnp.concatenate(weight, 1))
        out_delta[:, first * 128 : (first + 4) * 128] = delta.astype(jnp.bfloat16)


def widen(attended, same, other):
    return pl.pallas_call(
        widen_kernel,
        out_shape=jax.ShapeDtypeStruct((attended.shape[0], D), jnp.bfloat16),
        in_specs=[pl.BlockSpec(memory_space=pl.ANY)] + [pl.BlockSpec(memory_space=pltpu.VMEM)] * 2,
        out_specs=pl.BlockSpec(memory_space=pltpu.VMEM),
        scratch_shapes=[
            pltpu.VMEM((QH * HEAD_SIZE, 128), jnp.float32),
            pltpu.VMEM((ADAPTER_RANK * D // 128, 128), jnp.float32),
            pltpu.VMEM(attended.shape, attended.dtype),
            pltpu.SemaphoreType.DMA,
        ],
        compiler_params=pltpu.CompilerParams(vmem_limit_bytes=32 << 20),
        cost_estimate=pl.CostEstimate(flops=1 << 27, bytes_accessed=4 << 20, transcendentals=0),
    )(attended, same, other)


def swap(block, mask):
    return lax.ppermute(block, ("groups", "ctx"), [(i, i ^ mask) for i in range(4 * PIECES)])


def direct_shards(
    normed_input, query_base, key_base, value_base, adapter_pool, stretch_adapter, adapter_owner
):
    tok_rows = normed_input.shape[0]
    ctx = lax.axis_size("ctx")
    seq = ctx * tok_rows
    blocks = [list(range(PIECES)), list(range(PIECES, 2 * PIECES))]
    half_dim = HEAD_SIZE // 2
    frequency = rope_base ** (-(jnp.arange(half_dim, dtype=jnp.float32) * 2.0) / HEAD_SIZE)
    angle = jnp.arange(seq, dtype=jnp.int32).astype(jnp.float32)[:, None] * frequency[None, :]
    cosine = jnp.cos(angle)
    sine = jnp.sin(angle)
    cosines = jnp.concatenate([cosine, cosine], 1)
    sines = jnp.concatenate([-sine, sine], 1)

    def after(block, *others):
        return lax.optimization_barrier((block, others))[0]

    def exchange(sent):
        across = swap(sent[2], 2 * PIECES)
        return [sent[0], swap(sent[1], PIECES), across, swap(sent[3], 3 * PIECES)]

    def along_z(block):
        return jnp.stack([block, swap(block, 4)])

    def along_x(pair):
        quad = jnp.stack([pair, swap(pair, 2)], 1)
        return quad.reshape((PIECES // 2,) + pair.shape[1:])

    elsewhere = swap(stretch_adapter, 2 * PIECES)
    packed = pack_row(adapter_pool, SECTIONS)
    even, odd = deal(normed_input, packed)
    sibling = swap(odd, 1)
    base = jnp.concatenate([key_base, value_base], 1)
    base = jnp.stack([base, swap(base, PIECES)])

    spread = lax.all_to_all(packed, "ctx", 0, 0, axis_index_groups=blocks)
    spread = after(spread, sibling, base, cosines, sines)
    sent, near, far = pick(spread, stretch_adapter, elsewhere, adapter_owner)
    arrived = exchange(sent)
    dealt = [after(jnp.stack([even[j], sibling[j]]), sent) for j in range(PIECES // 2)]
    dealt = [swap(block, 2 * j) if j else block for j, block in enumerate(dealt)]

    weight, ups = join(stretch_adapter, adapter_owner, arrived)
    base = along_z(after(base, arrived[1]))
    partial_sums = narrow(after(weight, base), dealt)
    back = [swap(block, 2 * j) if j else block for j, block in enumerate(partial_sums)]
    back = sum(block.astype(jnp.float32) for block in back)
    ups = along_z(after(ups, *partial_sums))
    own_rank = swap(after(back[1].astype(jnp.bfloat16), ups), 1)
    own_rank = back[0] + own_rank.astype(jnp.float32)
    own_rank = own_rank.astype(jnp.bfloat16)
    base = along_x(after(base, *partial_sums))
    all_rank = own_rank[:, ADAPTER_RANK:]
    ups = along_x(after(ups, own_rank))
    all_rank = jnp.stack([all_rank, swap(all_rank, PIECES)])
    all_rank = after(all_rank, ups)
    far = swap(after(far, all_rank), PIECES)
    all_rank = jnp.stack([swap(all_rank, apart) if apart else all_rank for apart in (0, 2, 4, 6)])
    base = after(base, all_rank)
    base = (base, swap(base, 1))
    ups = (ups, swap(after(ups, all_rank), 1))
    all_rank = jnp.stack([all_rank, swap(all_rank, 1)])

    shared = (query_base, base, own_rank, all_rank, ups, cosines, sines)
    attended = attend(0, 1, None, *shared)
    far = after(far, attended)
    own, across = settle(stretch_adapter, elsewhere, adapter_owner, near, far)
    ends = jnp.stack([own, swap(across, 2 * PIECES)])
    ends = jnp.stack([swap(ends, apart) if apart else ends for apart in (0, 2, 4, 6)])
    attended = attend(1, KEYVALUE_HEADS - 1, attended, *shared)
    ends = after(ends, attended)
    return attended, widen(attended, ends, swap(ends, 1))


def shards(normed_input, query_base, key_base, value_base, adapter_pool, stretch_adapter, owner):
    fits = (
        lax.axis_size("groups") == 2
        and lax.axis_size("ctx") == 2 * PIECES
        and normed_input.shape[0] * PIECES == BLOCK_TOKENS
        and adapter_pool.shape[0] == 1
    )
    plan = direct_shards if fits else spread_shards
    return plan(
        normed_input, query_base, key_base, value_base, adapter_pool, stretch_adapter, owner
    )


def solution(mesh):
    placed = (
        P(("groups", "ctx"), None),
        P(("groups", "ctx"), None),
        P(("groups", "ctx"), None),
        P(("groups", "ctx"), None),
        P("ctx", None),
        P("groups"),
        P(),
    )
    return jax.shard_map(
        shards,
        mesh=mesh,
        in_specs=placed,
        out_specs=(P(("groups", "ctx"), None), P(("groups", "ctx"), None)),
        check_vma=False,
    )
```

```python
from functools import partial
import math

import jax
import jax.numpy as jnp
from jax import lax
from jax.experimental import pallas as pl
from jax.experimental.pallas import tpu as pltpu
from jax.sharding import PartitionSpec as P

D = 8192
QH = 32
KEYVALUE_HEADS = 4
HEAD_SIZE = 128
ADAPTER_RANK = 64
BLOCK_TOKENS = 512
QKV_POOL = 1900544


adapter_scale = 2.0
rope_base = 500000.0
mask_floor = -1e30


def from_partner(block, axis, apart):
    count = lax.axis_size(axis)
    route = []
    for low in range(count):
        high = low | 1 << apart
        if high != low and high < count:
            route += [(low, high), (high, low)]
    return lax.ppermute(block, axis, route)


def rotate(delta, token_positions, heads):
    half_dim = HEAD_SIZE // 2
    frequency = rope_base ** (-(jnp.arange(half_dim, dtype=jnp.float32) * 2.0) / HEAD_SIZE)
    angle = token_positions.astype(jnp.float32)[:, None] * frequency[None, :]
    cosine = jnp.cos(angle)[:, None, :]
    sine_part = jnp.sin(angle)[:, None, :]
    shaped = delta.reshape(delta.shape[0], heads, HEAD_SIZE)
    first_half = shaped[..., :half_dim]
    second_half = shaped[..., half_dim:]
    joined = jnp.concatenate(
        [
            first_half * cosine - second_half * sine_part,
            second_half * cosine + first_half * sine_part,
        ],
        -1,
    )
    return joined.reshape(delta.shape[0], heads * HEAD_SIZE)


def project_heads(
    narrow_product, query_row_block, key_row_block, value_row_block, upper_part, token_positions
):
    query_up_weight = upper_part[: ADAPTER_RANK * QH * HEAD_SIZE].reshape(
        ADAPTER_RANK, QH * HEAD_SIZE
    )
    keyvalue_up_weight = upper_part[ADAPTER_RANK * QH * HEAD_SIZE :].reshape(
        ADAPTER_RANK, 2 * KEYVALUE_HEADS * HEAD_SIZE
    )
    query_correction = adapter_scale * jnp.dot(
        narrow_product[:, :ADAPTER_RANK], query_up_weight, preferred_element_type=jnp.float32
    )
    key_correction = adapter_scale * jnp.dot(
        narrow_product[:, ADAPTER_RANK : 2 * ADAPTER_RANK],
        keyvalue_up_weight[:, : KEYVALUE_HEADS * HEAD_SIZE],
        preferred_element_type=jnp.float32,
    )
    value_correction = adapter_scale * jnp.dot(
        narrow_product[:, 2 * ADAPTER_RANK :],
        keyvalue_up_weight[:, KEYVALUE_HEADS * HEAD_SIZE :],
        preferred_element_type=jnp.float32,
    )
    queries = (
        query_row_block.astype(jnp.float32) + rotate(query_correction, token_positions, QH)
    ).astype(jnp.bfloat16)
    new_keys = (
        key_row_block.astype(jnp.float32) + rotate(key_correction, token_positions, KEYVALUE_HEADS)
    ).astype(jnp.bfloat16)
    new_values = (value_row_block.astype(jnp.float32) + value_correction).astype(jnp.bfloat16)
    return (queries, new_keys, new_values)


def output_delta(attended_rows, out_part):
    down_out = out_part[: QH * HEAD_SIZE * ADAPTER_RANK].reshape(QH * HEAD_SIZE, ADAPTER_RANK)
    raised_output = out_part[QH * HEAD_SIZE * ADAPTER_RANK :].reshape(ADAPTER_RANK, D)
    narrow_product = jnp.dot(attended_rows, down_out, preferred_element_type=jnp.float32).astype(
        jnp.bfloat16
    )
    return (
        adapter_scale * jnp.dot(narrow_product, raised_output, preferred_element_type=jnp.float32)
    ).astype(jnp.bfloat16)


def head_major(query_row_block):
    count_rows = query_row_block.shape[0]
    group_size = QH // KEYVALUE_HEADS
    return (
        query_row_block.reshape(count_rows, KEYVALUE_HEADS, group_size, HEAD_SIZE)
        .transpose(1, 2, 0, 3)
        .reshape(KEYVALUE_HEADS, group_size * count_rows, HEAD_SIZE)
    )


def row_major(head_rows, count_rows):
    group_size = QH // KEYVALUE_HEADS
    return (
        head_rows.reshape(KEYVALUE_HEADS, group_size, count_rows, HEAD_SIZE)
        .transpose(2, 0, 1, 3)
        .reshape(count_rows, QH * HEAD_SIZE)
    )


def online_update(current, queries, query_pos, key_slice, value_slice, key_start):
    run_max, run_sum, run_acc = current
    scores = jnp.einsum(
        "hqd,khd->hqk", queries, key_slice, preferred_element_type=jnp.float32
    ) * HEAD_SIZE ** (-0.5)
    key_pos = key_start + jnp.arange(key_slice.shape[0], dtype=jnp.int32)
    allowed = (query_pos[:, None] >= key_pos[None, :])[None]
    new_max = jnp.maximum(run_max, jnp.max(jnp.where(allowed, scores, mask_floor), axis=-1))
    weights = jnp.where(allowed, jnp.exp(scores - new_max[..., None]), 0.0)
    rescale = jnp.exp(run_max - new_max)
    new_sum = run_sum * rescale + jnp.sum(weights, axis=-1)
    new_acc = run_acc * rescale[..., None] + jnp.einsum(
        "hqk,khd->hqd",
        weights.astype(jnp.bfloat16),
        value_slice,
        preferred_element_type=jnp.float32,
    )
    return (new_max, new_sum, new_acc)


def unchanged(current):
    return current


def fold_keys(carry_state, shard_part, prepared):
    key_row_block, value_row_block = shard_part
    key_count = key_row_block.shape[0]
    sub_width = math.gcd(key_count, 1024)
    key_heads = key_row_block.reshape(key_count // sub_width, sub_width, KEYVALUE_HEADS, HEAD_SIZE)
    value_heads = value_row_block.reshape(
        key_count // sub_width, sub_width, KEYVALUE_HEADS, HEAD_SIZE
    )

    def one_step(sub_index, carried):
        key_start = sub_index * sub_width
        key_slice = lax.dynamic_index_in_dim(key_heads, sub_index, 0, keepdims=False)
        value_slice = lax.dynamic_index_in_dim(value_heads, sub_index, 0, keepdims=False)
        updated = []
        for (queries, query_pos), running in zip(prepared, carried):
            advance = partial(
                online_update,
                queries=queries,
                query_pos=query_pos,
                key_slice=key_slice,
                value_slice=value_slice,
                key_start=key_start,
            )
            updated.append(lax.cond(key_start <= jnp.max(query_pos), advance, unchanged, running))
        return tuple(updated)

    return lax.fori_loop(0, key_count // sub_width, one_step, carry_state)


def finish_block(result, count_rows):
    run_max, run_sum, run_acc = result
    divisor = jnp.where(run_sum > 0.0, run_sum, 1.0)
    return row_major(run_acc / divisor[..., None], count_rows).astype(jnp.bfloat16)


def spread_shards(
    normed_input, query_base, key_base, value_base, adapter_pool, stretch_adapter, adapter_owner
):
    cycle_size = lax.axis_size("ctx")
    my_index = lax.axis_index("ctx")
    tok_rows = normed_input.shape[0]
    token_positions = my_index * tok_rows + jnp.arange(tok_rows, dtype=jnp.int32)
    device_ids = jnp.arange(cycle_size, dtype=jnp.int32)
    stretch_of = device_ids * tok_rows // BLOCK_TOKENS
    stretch_ids = jnp.arange(stretch_adapter.shape[0], dtype=jnp.int32)
    adapter_of = jnp.sum(
        jnp.where(stretch_of[:, None] == stretch_ids[None, :], stretch_adapter[None, :], 0), axis=1
    )
    adapter_ids = jnp.arange(adapter_owner.shape[0], dtype=jnp.int32)
    slot_of = jnp.sum(
        jnp.where(adapter_of[:, None] == adapter_ids[None, :], adapter_owner[None, :], 0), axis=1
    )
    down_size = 3 * ADAPTER_RANK * D
    group_count = BLOCK_TOKENS // tok_rows
    levels = group_count.bit_length() - 1
    local_index = my_index % group_count
    col_width = D // group_count
    piece_len = down_size // (group_count * cycle_size)
    pool_rows = adapter_pool.shape[0]
    down_shaped = adapter_pool[:, :down_size].reshape(pool_rows, group_count, cycle_size, piece_len)
    spread_down = lax.all_to_all(down_shaped, "ctx", split_axis=2, concat_axis=0, tiled=True)
    flat_down = spread_down.reshape(-1, piece_len)
    wanted = jnp.take(flat_down, slot_of * group_count + device_ids % group_count, axis=0)[
        :, None, :
    ]
    down_slice = lax.all_to_all(wanted, "ctx", split_axis=0, concat_axis=1, tiled=True).reshape(
        col_width, 3 * ADAPTER_RANK
    )
    spread_rest = lax.all_to_all(
        adapter_pool[:, down_size:], "ctx", split_axis=1, concat_axis=0, tiled=True
    )
    rest_row = lax.all_to_all(
        jnp.take(spread_rest, slot_of, axis=0), "ctx", split_axis=0, concat_axis=1, tiled=True
    )[0]
    upper_part = rest_row[: QKV_POOL - down_size]
    out_part = rest_row[QKV_POOL - down_size :]
    pieces = normed_input.reshape(tok_rows, group_count, col_width)
    slice_order = jnp.bitwise_xor(local_index, jnp.arange(group_count, dtype=jnp.int32))
    moving = jnp.take(pieces, slice_order, axis=1).transpose(1, 0, 2)
    for level in range(levels):
        shaped = moving.reshape(group_count >> level + 1, 2, 1 << level, tok_rows, col_width)
        arrived = from_partner(shaped[:, 1], "ctx", level)
        moving = jnp.stack([shaped[:, 0], arrived], 1).reshape(group_count, tok_rows, col_width)
    partial_rows = jnp.dot(
        moving.reshape(group_count * tok_rows, col_width),
        down_slice,
        preferred_element_type=jnp.float32,
    ).reshape(group_count, tok_rows, 3 * ADAPTER_RANK)
    for level in reversed(range(levels)):
        halves = partial_rows.reshape(2, partial_rows.shape[0] // 2, tok_rows, 3 * ADAPTER_RANK)
        partial_rows = halves[0] + from_partner(
            halves[1].astype(jnp.bfloat16), "ctx", level
        ).astype(jnp.float32)
    narrow_product = partial_rows[0].astype(jnp.bfloat16)
    queries, new_keys, new_values = project_heads(
        narrow_product, query_base, key_base, value_base, upper_part, token_positions
    )
    group_size = QH // KEYVALUE_HEADS
    blocks = [(queries, token_positions)]
    prepared = [
        (head_major(block_q), jnp.tile(block_pos, group_size)) for block_q, block_pos in blocks
    ]
    initial = tuple(
        (
            (
                jnp.full((KEYVALUE_HEADS, head_q.shape[1]), mask_floor, jnp.float32),
                jnp.zeros((KEYVALUE_HEADS, head_q.shape[1]), jnp.float32),
                jnp.zeros((KEYVALUE_HEADS, head_q.shape[1], HEAD_SIZE), jnp.float32),
            )
            for head_q, block_pos in prepared
        )
    )
    finals = fold_keys(
        initial,
        (
            lax.all_gather(new_keys, "ctx", axis=0, tiled=True),
            lax.all_gather(new_values, "ctx", axis=0, tiled=True),
        ),
        prepared,
    )
    attended = finish_block(finals[0], tok_rows)
    out_delta = output_delta(attended, out_part)
    return (attended, out_delta)


PIECES = 8
GROUP = QH // KEYVALUE_HEADS
SECTIONS = ((0, 12288), (12288, 2048), (14336, 512), (14848, 2048), (16896, 4096))
DOWN_ROWS, QUERY_ROWS, KEYVAL_ROWS, DOWN_OUT_ROWS, UP_OUT_ROWS = 768, 128, 32, 128, 256
UP_ROWS = QUERY_ROWS + 2 * KEYVAL_ROWS
FIRST_ROWS = DOWN_ROWS + QUERY_ROWS + KEYVAL_ROWS


def pack_kernel(sections, pool, *refs):
    out, buffers, sems = refs[-3:]
    plane = lax.axis_index("groups")
    slabs, slab_rows = out.shape[:2]

    def copies(slab):
        listed = []
        offset = 0
        for first, rows in sections:
            share = rows // (2 * PIECES)
            begin = first + (slab * 2 + plane) * share
            listed.append(
                pltpu.make_async_copy(
                    pool.at[:, pl.ds(pl.multiple_of(begin * 128, 2048), share * 128)],
                    buffers.at[slab, :, pl.ds(offset, share * 128)],
                    sems.at[slab, len(listed)],
                )
            )
            offset += share * 128
        return listed

    for slab in range(slabs):
        for copy in copies(slab):
            copy.start()

    def step(slab, carried):
        for copy in copies(slab):
            copy.wait()

        def chunk(index, inner):
            line = buffers[slab, :, pl.ds(pl.multiple_of(index * 2048, 2048), 2048)]
            block = line.astype(jnp.float32).reshape(16, 128).astype(jnp.bfloat16)
            out[slab, pl.ds(pl.multiple_of(index * 16, 16), 16), :] = block
            return inner

        lax.fori_loop(0, slab_rows // 16, chunk, 0, unroll=8)
        return carried

    lax.fori_loop(0, slabs, step, 0)


def pack_row(pool, sections, *after):
    slab_rows = sum(rows for _, rows in sections) // (2 * PIECES)
    return pl.pallas_call(
        partial(pack_kernel, sections),
        out_shape=jax.ShapeDtypeStruct((PIECES, slab_rows, 128), jnp.bfloat16),
        in_specs=[pl.BlockSpec(memory_space=pl.ANY)] * (1 + len(after)),
        out_specs=pl.BlockSpec(memory_space=pltpu.VMEM),
        scratch_shapes=[
            pltpu.VMEM((PIECES, 1, slab_rows * 128), jnp.bfloat16),
            pltpu.SemaphoreType.DMA((PIECES, len(sections))),
        ],
        compiler_params=pltpu.CompilerParams(vmem_limit_bytes=60 << 20),
        cost_estimate=pl.CostEstimate(flops=0, bytes_accessed=8 << 20, transcendentals=0),
    )(pool, *after)


def pick_kernel(here, there, owner, spread, *refs):
    outs, lasts, sems = refs[:4], refs[4:6], refs[6]
    half = lax.axis_index("ctx") // PIECES
    last = spread.shape[1] - FIRST_ROWS
    copies = []
    for flip, out in enumerate(outs):
        wishes = there if flip >= 2 else here
        block = half ^ (flip & 1)
        row = lax.rem(owner[wishes[block]], PIECES)
        mirrored = lax.rem(owner[wishes[1 - block]], PIECES)
        pairs = (
            (spread.at[row, pl.ds(0, FIRST_ROWS)], out.at[pl.ds(0, FIRST_ROWS)]),
            (
                spread.at[mirrored, pl.ds(FIRST_ROWS - KEYVAL_ROWS, KEYVAL_ROWS)],
                out.at[pl.ds(FIRST_ROWS, KEYVAL_ROWS)],
            ),
            (spread.at[row, pl.ds(FIRST_ROWS, last)], lasts[flip % 2].at[flip // 2]),
        )
        for number, (source, target) in enumerate(pairs):
            copies.append(pltpu.make_async_copy(source, target, sems.at[flip, number]))
    for copy in copies:
        copy.start()
    for copy in copies:
        copy.wait()


def pick(spread, here, there, owner):
    last = spread.shape[1] - FIRST_ROWS
    first_shape = jax.ShapeDtypeStruct((FIRST_ROWS + KEYVAL_ROWS, 128), jnp.bfloat16)
    last_shape = jax.ShapeDtypeStruct((2, last, 128), jnp.bfloat16)
    outs = pl.pallas_call(
        pick_kernel,
        out_shape=(first_shape,) * 4 + (last_shape,) * 2,
        in_specs=[pl.BlockSpec(memory_space=pltpu.SMEM)] * 3 + [pl.BlockSpec(memory_space=pl.ANY)],
        out_specs=(pl.BlockSpec(memory_space=pltpu.VMEM),) * 6,
        scratch_shapes=[pltpu.SemaphoreType.DMA((4, 3))],
        compiler_params=pltpu.CompilerParams(vmem_limit_bytes=16 << 20),
        cost_estimate=pl.CostEstimate(flops=0, bytes_accessed=3 << 20, transcendentals=0),
    )(here, there, owner, spread)
    return outs[:4], outs[4], outs[5]


def deal_kernel(rows, even, odd, sems):
    seat = lax.rem(lax.axis_index("ctx"), PIECES)
    width = rows.shape[1] // PIECES
    copies = []
    for apart in range(PIECES):
        first = pl.multiple_of((seat ^ apart) * width, width)
        target = (odd if apart % 2 else even).at[apart // 2]
        copies.append(
            pltpu.make_async_copy(rows.at[:, pl.ds(first, width)], target, sems.at[apart])
        )
    for copy in copies:
        copy.start()
    for copy in copies:
        copy.wait()


def deal(rows, *after):
    slab = jax.ShapeDtypeStruct((PIECES // 2, rows.shape[0], rows.shape[1] // PIECES), rows.dtype)

    def kernel(rows, *refs):
        deal_kernel(rows, *refs[-3:])

    return pl.pallas_call(
        kernel,
        out_shape=(slab, slab),
        in_specs=[pl.BlockSpec(memory_space=pl.ANY)] * (1 + len(after)),
        out_specs=(pl.BlockSpec(memory_space=pltpu.VMEM),) * 2,
        scratch_shapes=[pltpu.SemaphoreType.DMA((PIECES,))],
        compiler_params=pltpu.CompilerParams(vmem_limit_bytes=16 << 20),
        cost_estimate=pl.CostEstimate(flops=0, bytes_accessed=2 << 20, transcendentals=0),
    )(rows, *after)


def nearest(here, owner, block):
    half = lax.axis_index("ctx") // PIECES
    return owner[here[block]] // PIECES == half


def choose(close, arrived, put):
    plane = lax.axis_index("groups")

    @pl.when(close)
    def _():
        put(arrived[0], plane)
        put(arrived[2], 1 - plane)

    @pl.when(jnp.logical_not(close))
    def _():
        put(arrived[1], plane)
        put(arrived[3], 1 - plane)


def join_kernel(here, owner, *refs):
    arrived, (weight, ups), (flat, left, right) = refs[:4], refs[4:6], refs[6:]
    half = lax.axis_index("ctx") // PIECES
    split = DOWN_ROWS + QUERY_ROWS + KEYVAL_ROWS

    def put_own(source, position):
        first = pl.multiple_of(position * DOWN_ROWS, DOWN_ROWS)
        flat[pl.ds(first, DOWN_ROWS), :] = source[:DOWN_ROWS, :].astype(jnp.float32)
        ups[position, : UP_ROWS - KEYVAL_ROWS, :] = source[DOWN_ROWS:split, :]

    def put_mirrored(source, position):
        ups[position, UP_ROWS - KEYVAL_ROWS :, :] = source[split:, :]

    choose(nearest(here, owner, half), arrived, put_own)
    choose(nearest(here, owner, 1 - half), arrived, put_mirrored)

    third = flat.shape[0] // 3
    one = flat[pl.ds(0, third, stride=3), :]
    two = pltpu.roll(flat[pl.ds(1, third, stride=3), :], 64, 1)
    three = pltpu.roll(flat[pl.ds(2, third, stride=3), :], 64, 1)
    lane = lax.broadcasted_iota(jnp.int32, one.shape, 1)
    left[pl.ds(0, third, stride=2), :] = one
    left[pl.ds(1, third, stride=2), :] = jnp.where(lane < 64, two, three)
    right[pl.ds(0, third, stride=2), :] = pltpu.roll(two, 64, 1)
    right[pl.ds(1, third, stride=2), :] = three
    weight[...] = jnp.concatenate([left[...], right[...]], 1).astype(jnp.bfloat16)


def join(here, owner, arrived):
    depth = D // PIECES
    return pl.pallas_call(
        join_kernel,
        out_shape=(
            jax.ShapeDtypeStruct((depth, 256), jnp.bfloat16),
            jax.ShapeDtypeStruct((2, UP_ROWS, 128), jnp.bfloat16),
        ),
        in_specs=[pl.BlockSpec(memory_space=pltpu.SMEM)] * 2
        + [pl.BlockSpec(memory_space=pltpu.VMEM)] * 4,
        out_specs=(pl.BlockSpec(memory_space=pltpu.VMEM),) * 2,
        scratch_shapes=[
            pltpu.VMEM((2 * DOWN_ROWS, 128), jnp.float32),
            pltpu.VMEM((depth, 128), jnp.float32),
            pltpu.VMEM((depth, 128), jnp.float32),
        ],
        compiler_params=pltpu.CompilerParams(vmem_limit_bytes=16 << 20),
        cost_estimate=pl.CostEstimate(flops=0, bytes_accessed=96 << 20, transcendentals=0),
    )(here, owner, *arrived)


def settle_kernel(here, there, owner, near, far, own, across):
    half = lax.axis_index("ctx") // PIECES
    for number, (wishes, out) in enumerate(((here, own), (there, across))):
        close = nearest(wishes, owner, half)

        @pl.when(close)
        def _():
            out[...] = near[number]

        @pl.when(jnp.logical_not(close))
        def _():
            out[...] = far[number]


def settle(here, there, owner, near, far):
    slab = jax.ShapeDtypeStruct(near.shape[1:], jnp.bfloat16)
    return pl.pallas_call(
        settle_kernel,
        out_shape=(slab, slab),
        in_specs=[pl.BlockSpec(memory_space=pltpu.SMEM)] * 3
        + [pl.BlockSpec(memory_space=pltpu.VMEM)] * 2,
        out_specs=(pl.BlockSpec(memory_space=pltpu.VMEM),) * 2,
        compiler_params=pltpu.CompilerParams(vmem_limit_bytes=16 << 20),
        cost_estimate=pl.CostEstimate(flops=0, bytes_accessed=1 << 20, transcendentals=0),
    )(here, there, owner, near, far)


def narrow_kernel(weight, *refs):
    for block, out in zip(refs[:4], refs[4:]):
        sides, rows, depth = block.shape
        product = jnp.dot(
            block[...].reshape(sides * rows, depth),
            weight[...],
            preferred_element_type=jnp.float32,
        )
        out[...] = product[:, : 3 * ADAPTER_RANK].reshape(out.shape).astype(jnp.bfloat16)


def narrow(weight, dealt):
    sides, rows, depth = dealt[0].shape
    partial_sums = jax.ShapeDtypeStruct((sides, rows, 3 * ADAPTER_RANK), jnp.bfloat16)
    return pl.pallas_call(
        narrow_kernel,
        out_shape=(partial_sums,) * 4,
        in_specs=[pl.BlockSpec(memory_space=pltpu.VMEM)] * 5,
        out_specs=(pl.BlockSpec(memory_space=pltpu.VMEM),) * 4,
        compiler_params=pltpu.CompilerParams(vmem_limit_bytes=16 << 20),
        cost_estimate=pl.CostEstimate(
            flops=2 * 8 * rows * depth * 256, bytes_accessed=2 << 20, transcendentals=0
        ),
    )(weight, *dealt)


def attend_kernel(
    first_head,
    query_block,
    key_same,
    key_other,
    value_same,
    value_other,
    own_rank,
    all_rank,
    up_same,
    up_other,
    cosines,
    sines,
    *refs,
):
    attended, flat_query, flat_keyval, keys, values = refs[-5:]
    step = pl.program_id(0) + first_head
    rows = query_block.shape[0]
    base = lax.axis_index("ctx") * rows
    half = lax.axis_index("ctx") // PIECES
    seat = lax.rem(lax.axis_index("ctx"), PIECES)
    dot = partial(jnp.dot, preferred_element_type=jnp.float32)

    @pl.when(pl.program_id(0) == 0)
    def _():
        for apart in range(PIECES):
            ups = up_other if apart % 2 else up_same
            for position in range(2):
                piece = ups[apart // 2, position].astype(jnp.float32)
                place = (seat ^ apart) * 2 + position
                first = pl.multiple_of(place * QUERY_ROWS, QUERY_ROWS)
                flat_query[pl.ds(first, QUERY_ROWS), :] = piece[:QUERY_ROWS]
                first = pl.multiple_of(place * KEYVAL_ROWS, KEYVAL_ROWS)
                for side in range(2):
                    begin = QUERY_ROWS + side * KEYVAL_ROWS
                    flat_keyval[side, pl.ds(first, KEYVAL_ROWS), :] = piece[
                        begin : begin + KEYVAL_ROWS
                    ]

    def turned(delta, cosine, sine):
        return delta * cosine + pltpu.roll(delta, HEAD_SIZE // 2, 1) * sine

    def up(flat, first, stride):
        return flat[pl.ds(first, ADAPTER_RANK, stride=stride), :].astype(jnp.bfloat16)

    for side in range(2):
        heads = 2 * KEYVALUE_HEADS
        key_up = up(flat_keyval.at[side], step, heads)
        value_up = up(flat_keyval.at[side], step + KEYVALUE_HEADS, heads)
        for core in range(2):
            rank = all_rank[core, :, side].reshape(PIECES // 2 * rows, 2 * ADAPTER_RANK)
            key_delta = adapter_scale * dot(rank[:, :ADAPTER_RANK], key_up)
            value_delta = adapter_scale * dot(rank[:, ADAPTER_RANK:], value_up)
            for chip in range(PIECES // 2):
                there = seat ^ (2 * chip + core)
                first = ((half ^ side) * PIECES + there) * rows
                span = pl.ds(pl.multiple_of(first, rows), rows)
                part = slice(chip * rows, (chip + 1) * rows)
                delta = turned(key_delta[part], cosines[span, :], sines[span, :])
                full = (key_other if core else key_same)[chip, side].astype(jnp.float32) + delta
                keys[span, :] = full.astype(jnp.bfloat16)
                full = (value_other if core else value_same)[chip, side].astype(jnp.float32)
                values[span, :] = (full + value_delta[part]).astype(jnp.bfloat16)
    here = pl.ds(pl.multiple_of(base, rows), rows)
    cosine = cosines[here, :]
    sine = sines[here, :]
    taken = GROUP // 2
    for first in range(0, GROUP, taken):
        weight = [up(flat_query, step * GROUP + first + head, QH) for head in range(taken)]
        deltas = adapter_scale * dot(own_rank[:, :ADAPTER_RANK], jnp.concatenate(weight, 1))
        queries = []
        for place in range(taken):
            moved = turned(deltas[:, place * HEAD_SIZE : (place + 1) * HEAD_SIZE], cosine, sine)
            span = slice((first + place) * HEAD_SIZE, (first + place + 1) * HEAD_SIZE)
            queries.append(
                (query_block[:, span].astype(jnp.float32) + moved).astype(jnp.bfloat16)
            )
        queries = jnp.concatenate(queries, 0)
        scores = lax.dot_general(
            queries, keys[...], (((1,), (1,)), ((), ())), preferred_element_type=jnp.float32
        )
        row = lax.broadcasted_iota(jnp.int32, scores.shape, 0)
        column = lax.broadcasted_iota(jnp.int32, scores.shape, 1)
        scores = jnp.where(column <= base + lax.rem(row, rows), scores, mask_floor)
        scores = scores - jnp.max(scores, axis=-1, keepdims=True)
        weights = jnp.exp2(scores * (HEAD_SIZE ** (-0.5) * math.log2(math.e)))
        divisor = jnp.sum(weights, axis=-1, keepdims=True)
        result = (dot(weights.astype(jnp.bfloat16), values[...]) / divisor).astype(jnp.bfloat16)
        for place in range(taken):
            span = slice((first + place) * HEAD_SIZE, (first + place + 1) * HEAD_SIZE)
            attended[:, span] = result[place * rows : (place + 1) * rows]


def attend(first_head, heads, before, query_base, base, own_rank, all_rank, ups, cosines, sines):
    rows = query_base.shape[0]
    seq = 4 * PIECES // 2 * rows
    width = GROUP * HEAD_SIZE

    def whole(shape):
        return pl.BlockSpec(shape, lambda h: (0,) * len(shape))

    key_spec = pl.BlockSpec((PIECES // 2, 2, rows, HEAD_SIZE), lambda h: (0, 0, 0, h + first_head))
    value_spec = pl.BlockSpec(
        (PIECES // 2, 2, rows, HEAD_SIZE), lambda h: (0, 0, 0, h + first_head + KEYVALUE_HEADS)
    )
    operands = (query_base, base[0], base[1], base[0], base[1], own_rank, all_rank, *ups)
    operands += (cosines, sines) + (() if before is None else (before,))
    query_spec = pl.BlockSpec((rows, width), lambda h: (0, h + first_head))
    return pl.pallas_call(
        partial(attend_kernel, first_head),
        grid=(heads,),
        out_shape=jax.ShapeDtypeStruct((rows, QH * HEAD_SIZE), jnp.bfloat16),
        in_specs=[
            query_spec,
            key_spec,
            key_spec,
            value_spec,
            value_spec,
            whole(own_rank.shape),
            whole(all_rank.shape),
            whole(ups[0].shape),
            whole(ups[1].shape),
            whole(cosines.shape),
            whole(sines.shape),
        ]
        + [pl.BlockSpec(memory_space=pl.ANY)] * (len(operands) - 11),
        out_specs=query_spec,
        input_output_aliases={} if before is None else {len(operands) - 1: 0},
        scratch_shapes=[
            pltpu.VMEM((2 * PIECES * QUERY_ROWS, 128), jnp.float32),
            pltpu.VMEM((2, 2 * PIECES * KEYVAL_ROWS, 128), jnp.float32),
            pltpu.VMEM((seq, HEAD_SIZE), jnp.bfloat16),
            pltpu.VMEM((seq, HEAD_SIZE), jnp.bfloat16),
        ],
        compiler_params=pltpu.CompilerParams(vmem_limit_bytes=60 << 20),
        cost_estimate=pl.CostEstimate(
            flops=12 * heads * rows * QH * seq * HEAD_SIZE,
            bytes_accessed=10 << 20,
            transcendentals=heads * rows * GROUP * seq,
        ),
    )(*operands)


def widen_kernel(attended_rows, same, other, out_delta, down_out, up_out, attended, sem):
    fetch = pltpu.make_async_copy(attended_rows, attended, sem)
    fetch.start()
    plane = lax.axis_index("groups")
    seat = lax.rem(lax.axis_index("ctx"), PIECES)
    for apart in range(PIECES):
        pieces = other if apart % 2 else same
        for position in range(2):
            piece = pieces[apart // 2, position].astype(jnp.float32)
            place = (seat ^ apart) * 2 + (position ^ plane)
            first = place * 2 * DOWN_OUT_ROWS
            block = piece[:DOWN_OUT_ROWS]
            down_out[pl.ds(first, DOWN_OUT_ROWS, stride=2), :] = block
            down_out[pl.ds(first + 1, DOWN_OUT_ROWS, stride=2), :] = pltpu.roll(block, 64, 1)
            first = pl.multiple_of(place * UP_OUT_ROWS, UP_OUT_ROWS)
            up_out[pl.ds(first, UP_OUT_ROWS), :] = piece[DOWN_OUT_ROWS:]
    dot = partial(jnp.dot, preferred_element_type=jnp.float32)
    fetch.wait()
    rank = dot(attended[...], down_out[...].astype(jnp.bfloat16))[:, :ADAPTER_RANK]
    rank = rank.astype(jnp.bfloat16)
    blocks = D // 128
    for first in range(0, blocks, 4):
        weight = [
            up_out[pl.ds(first + block, ADAPTER_RANK, stride=blocks), :].astype(jnp.bfloat16)
            for block in range(4)
        ]
        delta = adapter_scale * dot(rank, jnp.concatenate(weight, 1))
        out_delta[:, first * 128 : (first + 4) * 128] = delta.astype(jnp.bfloat16)


def widen(attended, same, other):
    return pl.pallas_call(
        widen_kernel,
        out_shape=jax.ShapeDtypeStruct((attended.shape[0], D), jnp.bfloat16),
        in_specs=[pl.BlockSpec(memory_space=pl.ANY)] + [pl.BlockSpec(memory_space=pltpu.VMEM)] * 2,
        out_specs=pl.BlockSpec(memory_space=pltpu.VMEM),
        scratch_shapes=[
            pltpu.VMEM((QH * HEAD_SIZE, 128), jnp.float32),
            pltpu.VMEM((ADAPTER_RANK * D // 128, 128), jnp.float32),
            pltpu.VMEM(attended.shape, attended.dtype),
            pltpu.SemaphoreType.DMA,
        ],
        compiler_params=pltpu.CompilerParams(vmem_limit_bytes=32 << 20),
        cost_estimate=pl.CostEstimate(flops=1 << 27, bytes_accessed=4 << 20, transcendentals=0),
    )(attended, same, other)


def swap(block, mask):
    return lax.ppermute(block, ("groups", "ctx"), [(i, i ^ mask) for i in range(4 * PIECES)])


def direct_shards(
    normed_input, query_base, key_base, value_base, adapter_pool, stretch_adapter, adapter_owner
):
    tok_rows = normed_input.shape[0]
    ctx = lax.axis_size("ctx")
    seq = ctx * tok_rows
    blocks = [list(range(PIECES)), list(range(PIECES, 2 * PIECES))]
    half_dim = HEAD_SIZE // 2
    frequency = rope_base ** (-(jnp.arange(half_dim, dtype=jnp.float32) * 2.0) / HEAD_SIZE)
    angle = jnp.arange(seq, dtype=jnp.int32).astype(jnp.float32)[:, None] * frequency[None, :]
    cosine = jnp.cos(angle)
    sine = jnp.sin(angle)
    cosines = jnp.concatenate([cosine, cosine], 1)
    sines = jnp.concatenate([-sine, sine], 1)

    def after(block, *others):
        return lax.optimization_barrier((block, others))[0]

    def exchange(sent):
        across = swap(sent[2], 2 * PIECES)
        return [sent[0], swap(sent[1], PIECES), across, swap(sent[3], 3 * PIECES)]

    def along_z(block):
        return jnp.stack([block, swap(block, 4)])

    def along_x(pair):
        quad = jnp.stack([pair, swap(pair, 2)], 1)
        return quad.reshape((PIECES // 2,) + pair.shape[1:])

    elsewhere = swap(stretch_adapter, 2 * PIECES)
    packed = pack_row(adapter_pool, SECTIONS)
    even, odd = deal(normed_input, packed)
    sibling = swap(odd, 1)
    base = jnp.concatenate([key_base, value_base], 1)
    base = jnp.stack([base, swap(base, PIECES)])

    spread = lax.all_to_all(packed, "ctx", 0, 0, axis_index_groups=blocks)
    spread = after(spread, sibling, base, cosines, sines)
    sent, near, far = pick(spread, stretch_adapter, elsewhere, adapter_owner)
    arrived = exchange(sent)
    dealt = [after(jnp.stack([even[j], sibling[j]]), sent) for j in range(PIECES // 2)]
    dealt = [swap(block, 2 * j) if j else block for j, block in enumerate(dealt)]

    weight, ups = join(stretch_adapter, adapter_owner, arrived)
    partial_sums = narrow(weight, dealt)
    back = [swap(block, 2 * j) if j else block for j, block in enumerate(partial_sums)]
    back = sum(block.astype(jnp.float32) for block in back)
    base = after(base, *partial_sums)
    base = [base, swap(base, 2), swap(base, 4)]
    own_rank = swap(after(back[1].astype(jnp.bfloat16), *base), 1)
    own_rank = back[0] + own_rank.astype(jnp.float32)
    own_rank = own_rank.astype(jnp.bfloat16)
    base = jnp.stack(base + [swap(after(base[2], own_rank), 2)])
    all_rank = own_rank[:, ADAPTER_RANK:]
    ups = along_z(after(ups, own_rank))
    all_rank = jnp.stack([all_rank, swap(all_rank, PIECES)])
    all_rank = after(all_rank, ups)
    ups = along_x(after(ups, all_rank))
    far = swap(after(far, all_rank), PIECES)
    all_rank = jnp.stack([swap(all_rank, apart) if apart else all_rank for apart in (0, 2, 4, 6)])
    base = after(base, all_rank)
    base = (base, swap(base, 1))
    all_rank = after(all_rank, ups)
    ups = (ups, swap(ups, 1))
    all_rank = jnp.stack([all_rank, swap(all_rank, 1)])

    shared = (query_base, base, own_rank, all_rank, ups, cosines, sines)
    attended = attend(0, 1, None, *shared)
    far = after(far, attended)
    own, across = settle(stretch_adapter, elsewhere, adapter_owner, near, far)
    ends = jnp.stack([own, swap(across, 2 * PIECES)])
    ends = jnp.stack([swap(ends, apart) if apart else ends for apart in (0, 2, 4, 6)])
    attended = attend(1, KEYVALUE_HEADS - 1, attended, *shared)
    ends = after(ends, attended)
    return attended, widen(attended, ends, swap(ends, 1))


def shards(normed_input, query_base, key_base, value_base, adapter_pool, stretch_adapter, owner):
    fits = (
        lax.axis_size("groups") == 2
        and lax.axis_size("ctx") == 2 * PIECES
        and normed_input.shape[0] * PIECES == BLOCK_TOKENS
        and adapter_pool.shape[0] == 1
    )
    plan = direct_shards if fits else spread_shards
    return plan(
        normed_input, query_base, key_base, value_base, adapter_pool, stretch_adapter, owner
    )


def solution(mesh):
    placed = (
        P(("groups", "ctx"), None),
        P(("groups", "ctx"), None),
        P(("groups", "ctx"), None),
        P(("groups", "ctx"), None),
        P("ctx", None),
        P("groups"),
        P(),
    )
    return jax.shard_map(
        shards,
        mesh=mesh,
        in_specs=placed,
        out_specs=(P(("groups", "ctx"), None), P(("groups", "ctx"), None)),
        check_vma=False,
    )
```

```python
from functools import partial
import math

import jax
import jax.numpy as jnp
from jax import lax
from jax.experimental import pallas as pl
from jax.experimental.pallas import tpu as pltpu
from jax.sharding import PartitionSpec as P

D = 8192
QH = 32
KEYVALUE_HEADS = 4
HEAD_SIZE = 128
ADAPTER_RANK = 64
BLOCK_TOKENS = 512
QKV_POOL = 1900544


adapter_scale = 2.0
rope_base = 500000.0
mask_floor = -1e30


def from_partner(block, axis, apart):
    count = lax.axis_size(axis)
    route = []
    for low in range(count):
        high = low | 1 << apart
        if high != low and high < count:
            route += [(low, high), (high, low)]
    return lax.ppermute(block, axis, route)


def rotate(delta, token_positions, heads):
    half_dim = HEAD_SIZE // 2
    frequency = rope_base ** (-(jnp.arange(half_dim, dtype=jnp.float32) * 2.0) / HEAD_SIZE)
    angle = token_positions.astype(jnp.float32)[:, None] * frequency[None, :]
    cosine = jnp.cos(angle)[:, None, :]
    sine_part = jnp.sin(angle)[:, None, :]
    shaped = delta.reshape(delta.shape[0], heads, HEAD_SIZE)
    first_half = shaped[..., :half_dim]
    second_half = shaped[..., half_dim:]
    joined = jnp.concatenate(
        [
            first_half * cosine - second_half * sine_part,
            second_half * cosine + first_half * sine_part,
        ],
        -1,
    )
    return joined.reshape(delta.shape[0], heads * HEAD_SIZE)


def project_heads(
    narrow_product, query_row_block, key_row_block, value_row_block, upper_part, token_positions
):
    query_up_weight = upper_part[: ADAPTER_RANK * QH * HEAD_SIZE].reshape(
        ADAPTER_RANK, QH * HEAD_SIZE
    )
    keyvalue_up_weight = upper_part[ADAPTER_RANK * QH * HEAD_SIZE :].reshape(
        ADAPTER_RANK, 2 * KEYVALUE_HEADS * HEAD_SIZE
    )
    query_correction = adapter_scale * jnp.dot(
        narrow_product[:, :ADAPTER_RANK], query_up_weight, preferred_element_type=jnp.float32
    )
    key_correction = adapter_scale * jnp.dot(
        narrow_product[:, ADAPTER_RANK : 2 * ADAPTER_RANK],
        keyvalue_up_weight[:, : KEYVALUE_HEADS * HEAD_SIZE],
        preferred_element_type=jnp.float32,
    )
    value_correction = adapter_scale * jnp.dot(
        narrow_product[:, 2 * ADAPTER_RANK :],
        keyvalue_up_weight[:, KEYVALUE_HEADS * HEAD_SIZE :],
        preferred_element_type=jnp.float32,
    )
    queries = (
        query_row_block.astype(jnp.float32) + rotate(query_correction, token_positions, QH)
    ).astype(jnp.bfloat16)
    new_keys = (
        key_row_block.astype(jnp.float32) + rotate(key_correction, token_positions, KEYVALUE_HEADS)
    ).astype(jnp.bfloat16)
    new_values = (value_row_block.astype(jnp.float32) + value_correction).astype(jnp.bfloat16)
    return (queries, new_keys, new_values)


def output_delta(attended_rows, out_part):
    down_out = out_part[: QH * HEAD_SIZE * ADAPTER_RANK].reshape(QH * HEAD_SIZE, ADAPTER_RANK)
    raised_output = out_part[QH * HEAD_SIZE * ADAPTER_RANK :].reshape(ADAPTER_RANK, D)
    narrow_product = jnp.dot(attended_rows, down_out, preferred_element_type=jnp.float32).astype(
        jnp.bfloat16
    )
    return (
        adapter_scale * jnp.dot(narrow_product, raised_output, preferred_element_type=jnp.float32)
    ).astype(jnp.bfloat16)


def head_major(query_row_block):
    count_rows = query_row_block.shape[0]
    group_size = QH // KEYVALUE_HEADS
    return (
        query_row_block.reshape(count_rows, KEYVALUE_HEADS, group_size, HEAD_SIZE)
        .transpose(1, 2, 0, 3)
        .reshape(KEYVALUE_HEADS, group_size * count_rows, HEAD_SIZE)
    )


def row_major(head_rows, count_rows):
    group_size = QH // KEYVALUE_HEADS
    return (
        head_rows.reshape(KEYVALUE_HEADS, group_size, count_rows, HEAD_SIZE)
        .transpose(2, 0, 1, 3)
        .reshape(count_rows, QH * HEAD_SIZE)
    )


def online_update(current, queries, query_pos, key_slice, value_slice, key_start):
    run_max, run_sum, run_acc = current
    scores = jnp.einsum(
        "hqd,khd->hqk", queries, key_slice, preferred_element_type=jnp.float32
    ) * HEAD_SIZE ** (-0.5)
    key_pos = key_start + jnp.arange(key_slice.shape[0], dtype=jnp.int32)
    allowed = (query_pos[:, None] >= key_pos[None, :])[None]
    new_max = jnp.maximum(run_max, jnp.max(jnp.where(allowed, scores, mask_floor), axis=-1))
    weights = jnp.where(allowed, jnp.exp(scores - new_max[..., None]), 0.0)
    rescale = jnp.exp(run_max - new_max)
    new_sum = run_sum * rescale + jnp.sum(weights, axis=-1)
    new_acc = run_acc * rescale[..., None] + jnp.einsum(
        "hqk,khd->hqd",
        weights.astype(jnp.bfloat16),
        value_slice,
        preferred_element_type=jnp.float32,
    )
    return (new_max, new_sum, new_acc)


def unchanged(current):
    return current


def fold_keys(carry_state, shard_part, prepared):
    key_row_block, value_row_block = shard_part
    key_count = key_row_block.shape[0]
    sub_width = math.gcd(key_count, 1024)
    key_heads = key_row_block.reshape(key_count // sub_width, sub_width, KEYVALUE_HEADS, HEAD_SIZE)
    value_heads = value_row_block.reshape(
        key_count // sub_width, sub_width, KEYVALUE_HEADS, HEAD_SIZE
    )

    def one_step(sub_index, carried):
        key_start = sub_index * sub_width
        key_slice = lax.dynamic_index_in_dim(key_heads, sub_index, 0, keepdims=False)
        value_slice = lax.dynamic_index_in_dim(value_heads, sub_index, 0, keepdims=False)
        updated = []
        for (queries, query_pos), running in zip(prepared, carried):
            advance = partial(
                online_update,
                queries=queries,
                query_pos=query_pos,
                key_slice=key_slice,
                value_slice=value_slice,
                key_start=key_start,
            )
            updated.append(lax.cond(key_start <= jnp.max(query_pos), advance, unchanged, running))
        return tuple(updated)

    return lax.fori_loop(0, key_count // sub_width, one_step, carry_state)


def finish_block(result, count_rows):
    run_max, run_sum, run_acc = result
    divisor = jnp.where(run_sum > 0.0, run_sum, 1.0)
    return row_major(run_acc / divisor[..., None], count_rows).astype(jnp.bfloat16)


def spread_shards(
    normed_input, query_base, key_base, value_base, adapter_pool, stretch_adapter, adapter_owner
):
    cycle_size = lax.axis_size("ctx")
    my_index = lax.axis_index("ctx")
    tok_rows = normed_input.shape[0]
    token_positions = my_index * tok_rows + jnp.arange(tok_rows, dtype=jnp.int32)
    device_ids = jnp.arange(cycle_size, dtype=jnp.int32)
    stretch_of = device_ids * tok_rows // BLOCK_TOKENS
    stretch_ids = jnp.arange(stretch_adapter.shape[0], dtype=jnp.int32)
    adapter_of = jnp.sum(
        jnp.where(stretch_of[:, None] == stretch_ids[None, :], stretch_adapter[None, :], 0), axis=1
    )
    adapter_ids = jnp.arange(adapter_owner.shape[0], dtype=jnp.int32)
    slot_of = jnp.sum(
        jnp.where(adapter_of[:, None] == adapter_ids[None, :], adapter_owner[None, :], 0), axis=1
    )
    down_size = 3 * ADAPTER_RANK * D
    group_count = BLOCK_TOKENS // tok_rows
    levels = group_count.bit_length() - 1
    local_index = my_index % group_count
    col_width = D // group_count
    piece_len = down_size // (group_count * cycle_size)
    pool_rows = adapter_pool.shape[0]
    down_shaped = adapter_pool[:, :down_size].reshape(pool_rows, group_count, cycle_size, piece_len)
    spread_down = lax.all_to_all(down_shaped, "ctx", split_axis=2, concat_axis=0, tiled=True)
    flat_down = spread_down.reshape(-1, piece_len)
    wanted = jnp.take(flat_down, slot_of * group_count + device_ids % group_count, axis=0)[
        :, None, :
    ]
    down_slice = lax.all_to_all(wanted, "ctx", split_axis=0, concat_axis=1, tiled=True).reshape(
        col_width, 3 * ADAPTER_RANK
    )
    spread_rest = lax.all_to_all(
        adapter_pool[:, down_size:], "ctx", split_axis=1, concat_axis=0, tiled=True
    )
    rest_row = lax.all_to_all(
        jnp.take(spread_rest, slot_of, axis=0), "ctx", split_axis=0, concat_axis=1, tiled=True
    )[0]
    upper_part = rest_row[: QKV_POOL - down_size]
    out_part = rest_row[QKV_POOL - down_size :]
    pieces = normed_input.reshape(tok_rows, group_count, col_width)
    slice_order = jnp.bitwise_xor(local_index, jnp.arange(group_count, dtype=jnp.int32))
    moving = jnp.take(pieces, slice_order, axis=1).transpose(1, 0, 2)
    for level in range(levels):
        shaped = moving.reshape(group_count >> level + 1, 2, 1 << level, tok_rows, col_width)
        arrived = from_partner(shaped[:, 1], "ctx", level)
        moving = jnp.stack([shaped[:, 0], arrived], 1).reshape(group_count, tok_rows, col_width)
    partial_rows = jnp.dot(
        moving.reshape(group_count * tok_rows, col_width),
        down_slice,
        preferred_element_type=jnp.float32,
    ).reshape(group_count, tok_rows, 3 * ADAPTER_RANK)
    for level in reversed(range(levels)):
        halves = partial_rows.reshape(2, partial_rows.shape[0] // 2, tok_rows, 3 * ADAPTER_RANK)
        partial_rows = halves[0] + from_partner(
            halves[1].astype(jnp.bfloat16), "ctx", level
        ).astype(jnp.float32)
    narrow_product = partial_rows[0].astype(jnp.bfloat16)
    queries, new_keys, new_values = project_heads(
        narrow_product, query_base, key_base, value_base, upper_part, token_positions
    )
    group_size = QH // KEYVALUE_HEADS
    blocks = [(queries, token_positions)]
    prepared = [
        (head_major(block_q), jnp.tile(block_pos, group_size)) for block_q, block_pos in blocks
    ]
    initial = tuple(
        (
            (
                jnp.full((KEYVALUE_HEADS, head_q.shape[1]), mask_floor, jnp.float32),
                jnp.zeros((KEYVALUE_HEADS, head_q.shape[1]), jnp.float32),
                jnp.zeros((KEYVALUE_HEADS, head_q.shape[1], HEAD_SIZE), jnp.float32),
            )
            for head_q, block_pos in prepared
        )
    )
    finals = fold_keys(
        initial,
        (
            lax.all_gather(new_keys, "ctx", axis=0, tiled=True),
            lax.all_gather(new_values, "ctx", axis=0, tiled=True),
        ),
        prepared,
    )
    attended = finish_block(finals[0], tok_rows)
    out_delta = output_delta(attended, out_part)
    return (attended, out_delta)


PIECES = 8
GROUP = QH // KEYVALUE_HEADS
SECTIONS = ((0, 12288), (12288, 2048), (14336, 512), (14848, 2048), (16896, 4096))
DOWN_ROWS, QUERY_ROWS, KEYVAL_ROWS, DOWN_OUT_ROWS, UP_OUT_ROWS = 768, 128, 32, 128, 256
UP_ROWS = QUERY_ROWS + 2 * KEYVAL_ROWS
FIRST_ROWS = DOWN_ROWS + QUERY_ROWS + KEYVAL_ROWS


def pack_kernel(sections, pool, *refs):
    out, buffers, sems = refs[-3:]
    plane = lax.axis_index("groups")
    slabs, slab_rows = out.shape[:2]

    def copies(slab):
        listed = []
        offset = 0
        for first, rows in sections:
            share = rows // (2 * PIECES)
            begin = first + (slab * 2 + plane) * share
            listed.append(
                pltpu.make_async_copy(
                    pool.at[:, pl.ds(pl.multiple_of(begin * 128, 2048), share * 128)],
                    buffers.at[slab, :, pl.ds(offset, share * 128)],
                    sems.at[slab, len(listed)],
                )
            )
            offset += share * 128
        return listed

    for slab in range(slabs):
        for copy in copies(slab):
            copy.start()

    def step(slab, carried):
        for copy in copies(slab):
            copy.wait()

        def chunk(index, inner):
            line = buffers[slab, :, pl.ds(pl.multiple_of(index * 4096, 4096), 4096)]
            out[slab, pl.ds(pl.multiple_of(index * 32, 32), 32), :] = line.reshape(32, 128)
            return inner

        lax.fori_loop(0, slab_rows // 32, chunk, 0, unroll=4)
        return carried

    lax.fori_loop(0, slabs, step, 0)


def pack_row(pool, sections, *after):
    slab_rows = sum(rows for _, rows in sections) // (2 * PIECES)
    return pl.pallas_call(
        partial(pack_kernel, sections),
        out_shape=jax.ShapeDtypeStruct((PIECES, slab_rows, 128), jnp.bfloat16),
        in_specs=[pl.BlockSpec(memory_space=pl.ANY)] * (1 + len(after)),
        out_specs=pl.BlockSpec(memory_space=pltpu.VMEM),
        scratch_shapes=[
            pltpu.VMEM((PIECES, 1, slab_rows * 128), jnp.bfloat16),
            pltpu.SemaphoreType.DMA((PIECES, len(sections))),
        ],
        compiler_params=pltpu.CompilerParams(vmem_limit_bytes=60 << 20),
        cost_estimate=pl.CostEstimate(flops=0, bytes_accessed=8 << 20, transcendentals=0),
    )(pool, *after)


def pick_kernel(here, there, owner, spread, *refs):
    outs, lasts, sems = refs[:4], refs[4:6], refs[6]
    half = lax.axis_index("ctx") // PIECES
    last = spread.shape[1] - FIRST_ROWS
    copies = []
    for flip, out in enumerate(outs):
        wishes = there if flip >= 2 else here
        block = half ^ (flip & 1)
        row = lax.rem(owner[wishes[block]], PIECES)
        mirrored = lax.rem(owner[wishes[1 - block]], PIECES)
        pairs = (
            (spread.at[row, pl.ds(0, FIRST_ROWS)], out.at[pl.ds(0, FIRST_ROWS)]),
            (
                spread.at[mirrored, pl.ds(FIRST_ROWS - KEYVAL_ROWS, KEYVAL_ROWS)],
                out.at[pl.ds(FIRST_ROWS, KEYVAL_ROWS)],
            ),
            (spread.at[row, pl.ds(FIRST_ROWS, last)], lasts[flip % 2].at[flip // 2]),
        )
        for number, (source, target) in enumerate(pairs):
            copies.append(pltpu.make_async_copy(source, target, sems.at[flip, number]))
    for copy in copies:
        copy.start()
    for copy in copies:
        copy.wait()


def pick(spread, here, there, owner):
    last = spread.shape[1] - FIRST_ROWS
    first_shape = jax.ShapeDtypeStruct((FIRST_ROWS + KEYVAL_ROWS, 128), jnp.bfloat16)
    last_shape = jax.ShapeDtypeStruct((2, last, 128), jnp.bfloat16)
    outs = pl.pallas_call(
        pick_kernel,
        out_shape=(first_shape,) * 4 + (last_shape,) * 2,
        in_specs=[pl.BlockSpec(memory_space=pltpu.SMEM)] * 3 + [pl.BlockSpec(memory_space=pl.ANY)],
        out_specs=(pl.BlockSpec(memory_space=pltpu.VMEM),) * 6,
        scratch_shapes=[pltpu.SemaphoreType.DMA((4, 3))],
        compiler_params=pltpu.CompilerParams(vmem_limit_bytes=16 << 20),
        cost_estimate=pl.CostEstimate(flops=0, bytes_accessed=3 << 20, transcendentals=0),
    )(here, there, owner, spread)
    return outs[:4], outs[4], outs[5]


def deal_kernel(rows, even, odd, sems):
    seat = lax.rem(lax.axis_index("ctx"), PIECES)
    width = rows.shape[1] // PIECES
    copies = []
    for apart in range(PIECES):
        first = pl.multiple_of((seat ^ apart) * width, width)
        target = (odd if apart % 2 else even).at[apart // 2]
        copies.append(
            pltpu.make_async_copy(rows.at[:, pl.ds(first, width)], target, sems.at[apart])
        )
    for copy in copies:
        copy.start()
    for copy in copies:
        copy.wait()


def deal(rows, *after):
    slab = jax.ShapeDtypeStruct((PIECES // 2, rows.shape[0], rows.shape[1] // PIECES), rows.dtype)

    def kernel(rows, *refs):
        deal_kernel(rows, *refs[-3:])

    return pl.pallas_call(
        kernel,
        out_shape=(slab, slab),
        in_specs=[pl.BlockSpec(memory_space=pl.ANY)] * (1 + len(after)),
        out_specs=(pl.BlockSpec(memory_space=pltpu.VMEM),) * 2,
        scratch_shapes=[pltpu.SemaphoreType.DMA((PIECES,))],
        compiler_params=pltpu.CompilerParams(vmem_limit_bytes=16 << 20),
        cost_estimate=pl.CostEstimate(flops=0, bytes_accessed=2 << 20, transcendentals=0),
    )(rows, *after)


def nearest(here, owner, block):
    half = lax.axis_index("ctx") // PIECES
    return owner[here[block]] // PIECES == half


def choose(close, arrived, put):
    plane = lax.axis_index("groups")

    @pl.when(close)
    def _():
        put(arrived[0], plane)
        put(arrived[2], 1 - plane)

    @pl.when(jnp.logical_not(close))
    def _():
        put(arrived[1], plane)
        put(arrived[3], 1 - plane)


def join_kernel(here, owner, *refs):
    arrived, (weight, ups), (flat, left, right) = refs[:4], refs[4:6], refs[6:]
    half = lax.axis_index("ctx") // PIECES
    split = DOWN_ROWS + QUERY_ROWS + KEYVAL_ROWS

    def put_own(source, position):
        first = pl.multiple_of(position * DOWN_ROWS, DOWN_ROWS)
        flat[pl.ds(first, DOWN_ROWS), :] = source[:DOWN_ROWS, :].astype(jnp.float32)
        ups[position, : UP_ROWS - KEYVAL_ROWS, :] = source[DOWN_ROWS:split, :]

    def put_mirrored(source, position):
        ups[position, UP_ROWS - KEYVAL_ROWS :, :] = source[split:, :]

    choose(nearest(here, owner, half), arrived, put_own)
    choose(nearest(here, owner, 1 - half), arrived, put_mirrored)

    third = flat.shape[0] // 3
    one = flat[pl.ds(0, third, stride=3), :]
    two = pltpu.roll(flat[pl.ds(1, third, stride=3), :], 64, 1)
    three = pltpu.roll(flat[pl.ds(2, third, stride=3), :], 64, 1)
    lane = lax.broadcasted_iota(jnp.int32, one.shape, 1)
    left[pl.ds(0, third, stride=2), :] = one
    left[pl.ds(1, third, stride=2), :] = jnp.where(lane < 64, two, three)
    right[pl.ds(0, third, stride=2), :] = pltpu.roll(two, 64, 1)
    right[pl.ds(1, third, stride=2), :] = three
    weight[...] = jnp.concatenate([left[...], right[...]], 1).astype(jnp.bfloat16)


def join(here, owner, arrived):
    depth = D // PIECES
    return pl.pallas_call(
        join_kernel,
        out_shape=(
            jax.ShapeDtypeStruct((depth, 256), jnp.bfloat16),
            jax.ShapeDtypeStruct((2, UP_ROWS, 128), jnp.bfloat16),
        ),
        in_specs=[pl.BlockSpec(memory_space=pltpu.SMEM)] * 2
        + [pl.BlockSpec(memory_space=pltpu.VMEM)] * 4,
        out_specs=(pl.BlockSpec(memory_space=pltpu.VMEM),) * 2,
        scratch_shapes=[
            pltpu.VMEM((2 * DOWN_ROWS, 128), jnp.float32),
            pltpu.VMEM((depth, 128), jnp.float32),
            pltpu.VMEM((depth, 128), jnp.float32),
        ],
        compiler_params=pltpu.CompilerParams(vmem_limit_bytes=16 << 20),
        cost_estimate=pl.CostEstimate(flops=0, bytes_accessed=96 << 20, transcendentals=0),
    )(here, owner, *arrived)


def settle_kernel(here, there, owner, near, far, own, across):
    half = lax.axis_index("ctx") // PIECES
    for number, (wishes, out) in enumerate(((here, own), (there, across))):
        close = nearest(wishes, owner, half)

        @pl.when(close)
        def _():
            out[...] = near[number]

        @pl.when(jnp.logical_not(close))
        def _():
            out[...] = far[number]


def settle(here, there, owner, near, far):
    slab = jax.ShapeDtypeStruct(near.shape[1:], jnp.bfloat16)
    return pl.pallas_call(
        settle_kernel,
        out_shape=(slab, slab),
        in_specs=[pl.BlockSpec(memory_space=pltpu.SMEM)] * 3
        + [pl.BlockSpec(memory_space=pltpu.VMEM)] * 2,
        out_specs=(pl.BlockSpec(memory_space=pltpu.VMEM),) * 2,
        compiler_params=pltpu.CompilerParams(vmem_limit_bytes=16 << 20),
        cost_estimate=pl.CostEstimate(flops=0, bytes_accessed=1 << 20, transcendentals=0),
    )(here, there, owner, near, far)


def narrow_kernel(weight, *refs):
    for block, out in zip(refs[:4], refs[4:]):
        sides, rows, depth = block.shape
        product = jnp.dot(
            block[...].reshape(sides * rows, depth),
            weight[...],
            preferred_element_type=jnp.float32,
        )
        out[...] = product[:, : 3 * ADAPTER_RANK].reshape(out.shape).astype(jnp.bfloat16)


def narrow(weight, dealt):
    sides, rows, depth = dealt[0].shape
    partial_sums = jax.ShapeDtypeStruct((sides, rows, 3 * ADAPTER_RANK), jnp.bfloat16)
    return pl.pallas_call(
        narrow_kernel,
        out_shape=(partial_sums,) * 4,
        in_specs=[pl.BlockSpec(memory_space=pltpu.VMEM)] * 5,
        out_specs=(pl.BlockSpec(memory_space=pltpu.VMEM),) * 4,
        compiler_params=pltpu.CompilerParams(vmem_limit_bytes=16 << 20),
        cost_estimate=pl.CostEstimate(
            flops=2 * 8 * rows * depth * 256, bytes_accessed=2 << 20, transcendentals=0
        ),
    )(weight, *dealt)


def attend_kernel(
    first_head,
    query_block,
    key_same,
    key_other,
    value_same,
    value_other,
    own_rank,
    all_rank,
    up_same,
    up_other,
    cosines,
    sines,
    *refs,
):
    attended, flat_query, flat_keyval, keys, values = refs[-5:]
    step = pl.program_id(0) + first_head
    rows = query_block.shape[0]
    base = lax.axis_index("ctx") * rows
    half = lax.axis_index("ctx") // PIECES
    seat = lax.rem(lax.axis_index("ctx"), PIECES)
    dot = partial(jnp.dot, preferred_element_type=jnp.float32)

    @pl.when(pl.program_id(0) == 0)
    def _():
        for apart in range(PIECES):
            ups = up_other if apart % 2 else up_same
            for position in range(2):
                piece = ups[apart // 2, position].astype(jnp.float32)
                place = (seat ^ apart) * 2 + position
                first = pl.multiple_of(place * QUERY_ROWS, QUERY_ROWS)
                flat_query[pl.ds(first, QUERY_ROWS), :] = piece[:QUERY_ROWS]
                first = pl.multiple_of(place * KEYVAL_ROWS, KEYVAL_ROWS)
                for side in range(2):
                    begin = QUERY_ROWS + side * KEYVAL_ROWS
                    flat_keyval[side, pl.ds(first, KEYVAL_ROWS), :] = piece[
                        begin : begin + KEYVAL_ROWS
                    ]

    def turned(delta, cosine, sine):
        return delta * cosine + pltpu.roll(delta, HEAD_SIZE // 2, 1) * sine

    def up(flat, first, stride):
        return flat[pl.ds(first, ADAPTER_RANK, stride=stride), :].astype(jnp.bfloat16)

    for side in range(2):
        heads = 2 * KEYVALUE_HEADS
        key_up = up(flat_keyval.at[side], step, heads)
        value_up = up(flat_keyval.at[side], step + KEYVALUE_HEADS, heads)
        for core in range(2):
            rank = all_rank[core, :, side].reshape(PIECES // 2 * rows, 2 * ADAPTER_RANK)
            key_delta = adapter_scale * dot(rank[:, :ADAPTER_RANK], key_up)
            value_delta = adapter_scale * dot(rank[:, ADAPTER_RANK:], value_up)
            for chip in range(PIECES // 2):
                there = seat ^ (2 * chip + core)
                first = ((half ^ side) * PIECES + there) * rows
                span = pl.ds(pl.multiple_of(first, rows), rows)
                part = slice(chip * rows, (chip + 1) * rows)
                delta = turned(key_delta[part], cosines[span, :], sines[span, :])
                full = (key_other if core else key_same)[chip, side].astype(jnp.float32) + delta
                keys[span, :] = full.astype(jnp.bfloat16)
                full = (value_other if core else value_same)[chip, side].astype(jnp.float32)
                values[span, :] = (full + value_delta[part]).astype(jnp.bfloat16)
    here = pl.ds(pl.multiple_of(base, rows), rows)
    cosine = cosines[here, :]
    sine = sines[here, :]
    taken = GROUP // 2
    for first in range(0, GROUP, taken):
        weight = [up(flat_query, step * GROUP + first + head, QH) for head in range(taken)]
        deltas = adapter_scale * dot(own_rank[:, :ADAPTER_RANK], jnp.concatenate(weight, 1))
        queries = []
        for place in range(taken):
            moved = turned(deltas[:, place * HEAD_SIZE : (place + 1) * HEAD_SIZE], cosine, sine)
            span = slice((first + place) * HEAD_SIZE, (first + place + 1) * HEAD_SIZE)
            queries.append(
                (query_block[:, span].astype(jnp.float32) + moved).astype(jnp.bfloat16)
            )
        queries = jnp.concatenate(queries, 0)
        scores = lax.dot_general(
            queries, keys[...], (((1,), (1,)), ((), ())), preferred_element_type=jnp.float32
        )
        row = lax.broadcasted_iota(jnp.int32, scores.shape, 0)
        column = lax.broadcasted_iota(jnp.int32, scores.shape, 1)
        scores = jnp.where(column <= base + lax.rem(row, rows), scores, mask_floor)
        scores = scores - jnp.max(scores, axis=-1, keepdims=True)
        weights = jnp.exp2(scores * (HEAD_SIZE ** (-0.5) * math.log2(math.e)))
        divisor = jnp.sum(weights, axis=-1, keepdims=True)
        result = (dot(weights.astype(jnp.bfloat16), values[...]) / divisor).astype(jnp.bfloat16)
        for place in range(taken):
            span = slice((first + place) * HEAD_SIZE, (first + place + 1) * HEAD_SIZE)
            attended[:, span] = result[place * rows : (place + 1) * rows]


def attend(first_head, heads, before, query_base, base, own_rank, all_rank, ups, cosines, sines):
    rows = query_base.shape[0]
    seq = 4 * PIECES // 2 * rows
    width = GROUP * HEAD_SIZE

    def whole(shape):
        return pl.BlockSpec(shape, lambda h: (0,) * len(shape))

    key_spec = pl.BlockSpec((PIECES // 2, 2, rows, HEAD_SIZE), lambda h: (0, 0, 0, h + first_head))
    value_spec = pl.BlockSpec(
        (PIECES // 2, 2, rows, HEAD_SIZE), lambda h: (0, 0, 0, h + first_head + KEYVALUE_HEADS)
    )
    operands = (query_base, base[0], base[1], base[0], base[1], own_rank, all_rank, *ups)
    operands += (cosines, sines) + (() if before is None else (before,))
    query_spec = pl.BlockSpec((rows, width), lambda h: (0, h + first_head))
    return pl.pallas_call(
        partial(attend_kernel, first_head),
        grid=(heads,),
        out_shape=jax.ShapeDtypeStruct((rows, QH * HEAD_SIZE), jnp.bfloat16),
        in_specs=[
            query_spec,
            key_spec,
            key_spec,
            value_spec,
            value_spec,
            whole(own_rank.shape),
            whole(all_rank.shape),
            whole(ups[0].shape),
            whole(ups[1].shape),
            whole(cosines.shape),
            whole(sines.shape),
        ]
        + [pl.BlockSpec(memory_space=pl.ANY)] * (len(operands) - 11),
        out_specs=query_spec,
        input_output_aliases={} if before is None else {len(operands) - 1: 0},
        scratch_shapes=[
            pltpu.VMEM((2 * PIECES * QUERY_ROWS, 128), jnp.float32),
            pltpu.VMEM((2, 2 * PIECES * KEYVAL_ROWS, 128), jnp.float32),
            pltpu.VMEM((seq, HEAD_SIZE), jnp.bfloat16),
            pltpu.VMEM((seq, HEAD_SIZE), jnp.bfloat16),
        ],
        compiler_params=pltpu.CompilerParams(vmem_limit_bytes=60 << 20),
        cost_estimate=pl.CostEstimate(
            flops=12 * heads * rows * QH * seq * HEAD_SIZE,
            bytes_accessed=10 << 20,
            transcendentals=heads * rows * GROUP * seq,
        ),
    )(*operands)


def widen_kernel(attended_rows, same, other, out_delta, down_out, up_out, attended, sem):
    fetch = pltpu.make_async_copy(attended_rows, attended, sem)
    fetch.start()
    plane = lax.axis_index("groups")
    seat = lax.rem(lax.axis_index("ctx"), PIECES)
    for apart in range(PIECES):
        pieces = other if apart % 2 else same
        for position in range(2):
            piece = pieces[apart // 2, position].astype(jnp.float32)
            place = (seat ^ apart) * 2 + (position ^ plane)
            first = place * 2 * DOWN_OUT_ROWS
            block = piece[:DOWN_OUT_ROWS]
            down_out[pl.ds(first, DOWN_OUT_ROWS, stride=2), :] = block
            down_out[pl.ds(first + 1, DOWN_OUT_ROWS, stride=2), :] = pltpu.roll(block, 64, 1)
            first = pl.multiple_of(place * UP_OUT_ROWS, UP_OUT_ROWS)
            up_out[pl.ds(first, UP_OUT_ROWS), :] = piece[DOWN_OUT_ROWS:]
    dot = partial(jnp.dot, preferred_element_type=jnp.float32)
    fetch.wait()
    rank = dot(attended[...], down_out[...].astype(jnp.bfloat16))[:, :ADAPTER_RANK]
    rank = rank.astype(jnp.bfloat16)
    blocks = D // 128
    for first in range(0, blocks, 4):
        weight = [
            up_out[pl.ds(first + block, ADAPTER_RANK, stride=blocks), :].astype(jnp.bfloat16)
            for block in range(4)
        ]
        delta = adapter_scale * dot(rank, jnp.concatenate(weight, 1))
        out_delta[:, first * 128 : (first + 4) * 128] = delta.astype(jnp.bfloat16)


def widen(attended, same, other):
    return pl.pallas_call(
        widen_kernel,
        out_shape=jax.ShapeDtypeStruct((attended.shape[0], D), jnp.bfloat16),
        in_specs=[pl.BlockSpec(memory_space=pl.ANY)] + [pl.BlockSpec(memory_space=pltpu.VMEM)] * 2,
        out_specs=pl.BlockSpec(memory_space=pltpu.VMEM),
        scratch_shapes=[
            pltpu.VMEM((QH * HEAD_SIZE, 128), jnp.float32),
            pltpu.VMEM((ADAPTER_RANK * D // 128, 128), jnp.float32),
            pltpu.VMEM(attended.shape, attended.dtype),
            pltpu.SemaphoreType.DMA,
        ],
        compiler_params=pltpu.CompilerParams(vmem_limit_bytes=32 << 20),
        cost_estimate=pl.CostEstimate(flops=1 << 27, bytes_accessed=4 << 20, transcendentals=0),
    )(attended, same, other)


def swap(block, mask):
    return lax.ppermute(block, ("groups", "ctx"), [(i, i ^ mask) for i in range(4 * PIECES)])


def direct_shards(
    normed_input, query_base, key_base, value_base, adapter_pool, stretch_adapter, adapter_owner
):
    tok_rows = normed_input.shape[0]
    ctx = lax.axis_size("ctx")
    seq = ctx * tok_rows
    blocks = [list(range(PIECES)), list(range(PIECES, 2 * PIECES))]
    half_dim = HEAD_SIZE // 2
    frequency = rope_base ** (-(jnp.arange(half_dim, dtype=jnp.float32) * 2.0) / HEAD_SIZE)
    angle = jnp.arange(seq, dtype=jnp.int32).astype(jnp.float32)[:, None] * frequency[None, :]
    cosine = jnp.cos(angle)
    sine = jnp.sin(angle)
    cosines = jnp.concatenate([cosine, cosine], 1)
    sines = jnp.concatenate([-sine, sine], 1)

    def after(block, *others):
        return lax.optimization_barrier((block, others))[0]

    def exchange(sent):
        across = swap(sent[2], 2 * PIECES)
        return [sent[0], swap(sent[1], PIECES), across, swap(sent[3], 3 * PIECES)]

    elsewhere = swap(stretch_adapter, 2 * PIECES)
    packed = pack_row(adapter_pool, SECTIONS)
    even, odd = deal(normed_input, packed)
    sibling = swap(odd, 1)
    base = jnp.concatenate([key_base, value_base], 1)
    base = jnp.stack([base, swap(base, PIECES)])

    spread = lax.all_to_all(packed, "ctx", 0, 0, axis_index_groups=blocks)
    spread = after(spread, sibling, base, cosines, sines)
    sent, near, far = pick(spread, stretch_adapter, elsewhere, adapter_owner)
    arrived = exchange(sent)
    dealt = [after(jnp.stack([even[j], sibling[j]]), sent) for j in range(PIECES // 2)]
    dealt = [swap(block, 2 * j) if j else block for j, block in enumerate(dealt)]

    weight, ups = join(stretch_adapter, adapter_owner, arrived)
    far = swap(after(far, weight), PIECES)
    partial_sums = narrow(weight, dealt)
    back = [swap(block, 2 * j) if j else block for j, block in enumerate(partial_sums)]
    back = sum(block.astype(jnp.float32) for block in back)
    base = after(base, *partial_sums)
    base = [base, swap(base, 2), swap(base, 4)]
    own_rank = swap(after(back[1].astype(jnp.bfloat16), far, *base), 1)
    own_rank = back[0] + own_rank.astype(jnp.float32)
    own_rank = own_rank.astype(jnp.bfloat16)
    base = jnp.stack(base + [swap(after(base[2], own_rank), 2)])
    all_rank = own_rank[:, ADAPTER_RANK:]
    ups = jnp.stack([ups, swap(after(ups, own_rank), 2)])
    all_rank = jnp.stack([all_rank, swap(all_rank, PIECES)])
    own, across = settle(stretch_adapter, elsewhere, adapter_owner, near, after(far, own_rank))
    ends = jnp.stack([own, swap(across, 2 * PIECES)])
    all_rank = after(all_rank, ups)
    ups = jnp.stack([ups, swap(after(ups, all_rank), 4)])
    ups = ups.reshape((PIECES // 2,) + ups.shape[2:])
    all_rank = jnp.stack([swap(all_rank, apart) if apart else all_rank for apart in (0, 2, 4, 6)])
    base = after(base, all_rank)
    base = (base, swap(base, 1))
    all_rank = after(all_rank, ups, across)
    ups = (ups, swap(ups, 1))
    all_rank = jnp.stack([all_rank, swap(all_rank, 1)])

    shared = (query_base, base, own_rank, all_rank, ups, cosines, sines)
    attended = attend(0, 1, None, *shared)
    ends = after(ends, attended)
    ends = jnp.stack([swap(ends, apart) if apart else ends for apart in (0, 2, 4, 6)])
    attended = attend(1, KEYVALUE_HEADS - 1, attended, *shared)
    ends = after(ends, attended)
    return attended, widen(attended, ends, swap(ends, 1))


def shards(normed_input, query_base, key_base, value_base, adapter_pool, stretch_adapter, owner):
    fits = (
        lax.axis_size("groups") == 2
        and lax.axis_size("ctx") == 2 * PIECES
        and normed_input.shape[0] * PIECES == BLOCK_TOKENS
        and adapter_pool.shape[0] == 1
    )
    plan = direct_shards if fits else spread_shards
    return plan(
        normed_input, query_base, key_base, value_base, adapter_pool, stretch_adapter, owner
    )


def solution(mesh):
    placed = (
        P(("groups", "ctx"), None),
        P(("groups", "ctx"), None),
        P(("groups", "ctx"), None),
        P(("groups", "ctx"), None),
        P("ctx", None),
        P("groups"),
        P(),
    )
    return jax.shard_map(
        shards,
        mesh=mesh,
        in_specs=placed,
        out_specs=(P(("groups", "ctx"), None), P(("groups", "ctx"), None)),
        check_vma=False,
    )
```

```python
from functools import partial
import math

import jax
import jax.numpy as jnp
from jax import lax
from jax.experimental import pallas as pl
from jax.experimental.pallas import tpu as pltpu
from jax.sharding import PartitionSpec as P

D = 8192
QH = 32
KEYVALUE_HEADS = 4
HEAD_SIZE = 128
ADAPTER_RANK = 64
BLOCK_TOKENS = 512
QKV_POOL = 1900544


adapter_scale = 2.0
rope_base = 500000.0
mask_floor = -1e30


def from_partner(block, axis, apart):
    count = lax.axis_size(axis)
    route = []
    for low in range(count):
        high = low | 1 << apart
        if high != low and high < count:
            route += [(low, high), (high, low)]
    return lax.ppermute(block, axis, route)


def rotate(delta, token_positions, heads):
    half_dim = HEAD_SIZE // 2
    frequency = rope_base ** (-(jnp.arange(half_dim, dtype=jnp.float32) * 2.0) / HEAD_SIZE)
    angle = token_positions.astype(jnp.float32)[:, None] * frequency[None, :]
    cosine = jnp.cos(angle)[:, None, :]
    sine_part = jnp.sin(angle)[:, None, :]
    shaped = delta.reshape(delta.shape[0], heads, HEAD_SIZE)
    first_half = shaped[..., :half_dim]
    second_half = shaped[..., half_dim:]
    joined = jnp.concatenate(
        [
            first_half * cosine - second_half * sine_part,
            second_half * cosine + first_half * sine_part,
        ],
        -1,
    )
    return joined.reshape(delta.shape[0], heads * HEAD_SIZE)


def project_heads(
    narrow_product, query_row_block, key_row_block, value_row_block, upper_part, token_positions
):
    query_up_weight = upper_part[: ADAPTER_RANK * QH * HEAD_SIZE].reshape(
        ADAPTER_RANK, QH * HEAD_SIZE
    )
    keyvalue_up_weight = upper_part[ADAPTER_RANK * QH * HEAD_SIZE :].reshape(
        ADAPTER_RANK, 2 * KEYVALUE_HEADS * HEAD_SIZE
    )
    query_correction = adapter_scale * jnp.dot(
        narrow_product[:, :ADAPTER_RANK], query_up_weight, preferred_element_type=jnp.float32
    )
    key_correction = adapter_scale * jnp.dot(
        narrow_product[:, ADAPTER_RANK : 2 * ADAPTER_RANK],
        keyvalue_up_weight[:, : KEYVALUE_HEADS * HEAD_SIZE],
        preferred_element_type=jnp.float32,
    )
    value_correction = adapter_scale * jnp.dot(
        narrow_product[:, 2 * ADAPTER_RANK :],
        keyvalue_up_weight[:, KEYVALUE_HEADS * HEAD_SIZE :],
        preferred_element_type=jnp.float32,
    )
    queries = (
        query_row_block.astype(jnp.float32) + rotate(query_correction, token_positions, QH)
    ).astype(jnp.bfloat16)
    new_keys = (
        key_row_block.astype(jnp.float32) + rotate(key_correction, token_positions, KEYVALUE_HEADS)
    ).astype(jnp.bfloat16)
    new_values = (value_row_block.astype(jnp.float32) + value_correction).astype(jnp.bfloat16)
    return (queries, new_keys, new_values)


def output_delta(attended_rows, out_part):
    down_out = out_part[: QH * HEAD_SIZE * ADAPTER_RANK].reshape(QH * HEAD_SIZE, ADAPTER_RANK)
    raised_output = out_part[QH * HEAD_SIZE * ADAPTER_RANK :].reshape(ADAPTER_RANK, D)
    narrow_product = jnp.dot(attended_rows, down_out, preferred_element_type=jnp.float32).astype(
        jnp.bfloat16
    )
    return (
        adapter_scale * jnp.dot(narrow_product, raised_output, preferred_element_type=jnp.float32)
    ).astype(jnp.bfloat16)


def head_major(query_row_block):
    count_rows = query_row_block.shape[0]
    group_size = QH // KEYVALUE_HEADS
    return (
        query_row_block.reshape(count_rows, KEYVALUE_HEADS, group_size, HEAD_SIZE)
        .transpose(1, 2, 0, 3)
        .reshape(KEYVALUE_HEADS, group_size * count_rows, HEAD_SIZE)
    )


def row_major(head_rows, count_rows):
    group_size = QH // KEYVALUE_HEADS
    return (
        head_rows.reshape(KEYVALUE_HEADS, group_size, count_rows, HEAD_SIZE)
        .transpose(2, 0, 1, 3)
        .reshape(count_rows, QH * HEAD_SIZE)
    )


def online_update(current, queries, query_pos, key_slice, value_slice, key_start):
    run_max, run_sum, run_acc = current
    scores = jnp.einsum(
        "hqd,khd->hqk", queries, key_slice, preferred_element_type=jnp.float32
    ) * HEAD_SIZE ** (-0.5)
    key_pos = key_start + jnp.arange(key_slice.shape[0], dtype=jnp.int32)
    allowed = (query_pos[:, None] >= key_pos[None, :])[None]
    new_max = jnp.maximum(run_max, jnp.max(jnp.where(allowed, scores, mask_floor), axis=-1))
    weights = jnp.where(allowed, jnp.exp(scores - new_max[..., None]), 0.0)
    rescale = jnp.exp(run_max - new_max)
    new_sum = run_sum * rescale + jnp.sum(weights, axis=-1)
    new_acc = run_acc * rescale[..., None] + jnp.einsum(
        "hqk,khd->hqd",
        weights.astype(jnp.bfloat16),
        value_slice,
        preferred_element_type=jnp.float32,
    )
    return (new_max, new_sum, new_acc)


def unchanged(current):
    return current


def fold_keys(carry_state, shard_part, prepared):
    key_row_block, value_row_block = shard_part
    key_count = key_row_block.shape[0]
    sub_width = math.gcd(key_count, 1024)
    key_heads = key_row_block.reshape(key_count // sub_width, sub_width, KEYVALUE_HEADS, HEAD_SIZE)
    value_heads = value_row_block.reshape(
        key_count // sub_width, sub_width, KEYVALUE_HEADS, HEAD_SIZE
    )

    def one_step(sub_index, carried):
        key_start = sub_index * sub_width
        key_slice = lax.dynamic_index_in_dim(key_heads, sub_index, 0, keepdims=False)
        value_slice = lax.dynamic_index_in_dim(value_heads, sub_index, 0, keepdims=False)
        updated = []
        for (queries, query_pos), running in zip(prepared, carried):
            advance = partial(
                online_update,
                queries=queries,
                query_pos=query_pos,
                key_slice=key_slice,
                value_slice=value_slice,
                key_start=key_start,
            )
            updated.append(lax.cond(key_start <= jnp.max(query_pos), advance, unchanged, running))
        return tuple(updated)

    return lax.fori_loop(0, key_count // sub_width, one_step, carry_state)


def finish_block(result, count_rows):
    run_max, run_sum, run_acc = result
    divisor = jnp.where(run_sum > 0.0, run_sum, 1.0)
    return row_major(run_acc / divisor[..., None], count_rows).astype(jnp.bfloat16)


def spread_shards(
    normed_input, query_base, key_base, value_base, adapter_pool, stretch_adapter, adapter_owner
):
    cycle_size = lax.axis_size("ctx")
    my_index = lax.axis_index("ctx")
    tok_rows = normed_input.shape[0]
    token_positions = my_index * tok_rows + jnp.arange(tok_rows, dtype=jnp.int32)
    device_ids = jnp.arange(cycle_size, dtype=jnp.int32)
    stretch_of = device_ids * tok_rows // BLOCK_TOKENS
    stretch_ids = jnp.arange(stretch_adapter.shape[0], dtype=jnp.int32)
    adapter_of = jnp.sum(
        jnp.where(stretch_of[:, None] == stretch_ids[None, :], stretch_adapter[None, :], 0), axis=1
    )
    adapter_ids = jnp.arange(adapter_owner.shape[0], dtype=jnp.int32)
    slot_of = jnp.sum(
        jnp.where(adapter_of[:, None] == adapter_ids[None, :], adapter_owner[None, :], 0), axis=1
    )
    down_size = 3 * ADAPTER_RANK * D
    group_count = BLOCK_TOKENS // tok_rows
    levels = group_count.bit_length() - 1
    local_index = my_index % group_count
    col_width = D // group_count
    piece_len = down_size // (group_count * cycle_size)
    pool_rows = adapter_pool.shape[0]
    down_shaped = adapter_pool[:, :down_size].reshape(pool_rows, group_count, cycle_size, piece_len)
    spread_down = lax.all_to_all(down_shaped, "ctx", split_axis=2, concat_axis=0, tiled=True)
    flat_down = spread_down.reshape(-1, piece_len)
    wanted = jnp.take(flat_down, slot_of * group_count + device_ids % group_count, axis=0)[
        :, None, :
    ]
    down_slice = lax.all_to_all(wanted, "ctx", split_axis=0, concat_axis=1, tiled=True).reshape(
        col_width, 3 * ADAPTER_RANK
    )
    spread_rest = lax.all_to_all(
        adapter_pool[:, down_size:], "ctx", split_axis=1, concat_axis=0, tiled=True
    )
    rest_row = lax.all_to_all(
        jnp.take(spread_rest, slot_of, axis=0), "ctx", split_axis=0, concat_axis=1, tiled=True
    )[0]
    upper_part = rest_row[: QKV_POOL - down_size]
    out_part = rest_row[QKV_POOL - down_size :]
    pieces = normed_input.reshape(tok_rows, group_count, col_width)
    slice_order = jnp.bitwise_xor(local_index, jnp.arange(group_count, dtype=jnp.int32))
    moving = jnp.take(pieces, slice_order, axis=1).transpose(1, 0, 2)
    for level in range(levels):
        shaped = moving.reshape(group_count >> level + 1, 2, 1 << level, tok_rows, col_width)
        arrived = from_partner(shaped[:, 1], "ctx", level)
        moving = jnp.stack([shaped[:, 0], arrived], 1).reshape(group_count, tok_rows, col_width)
    partial_rows = jnp.dot(
        moving.reshape(group_count * tok_rows, col_width),
        down_slice,
        preferred_element_type=jnp.float32,
    ).reshape(group_count, tok_rows, 3 * ADAPTER_RANK)
    for level in reversed(range(levels)):
        halves = partial_rows.reshape(2, partial_rows.shape[0] // 2, tok_rows, 3 * ADAPTER_RANK)
        partial_rows = halves[0] + from_partner(
            halves[1].astype(jnp.bfloat16), "ctx", level
        ).astype(jnp.float32)
    narrow_product = partial_rows[0].astype(jnp.bfloat16)
    queries, new_keys, new_values = project_heads(
        narrow_product, query_base, key_base, value_base, upper_part, token_positions
    )
    group_size = QH // KEYVALUE_HEADS
    blocks = [(queries, token_positions)]
    prepared = [
        (head_major(block_q), jnp.tile(block_pos, group_size)) for block_q, block_pos in blocks
    ]
    initial = tuple(
        (
            (
                jnp.full((KEYVALUE_HEADS, head_q.shape[1]), mask_floor, jnp.float32),
                jnp.zeros((KEYVALUE_HEADS, head_q.shape[1]), jnp.float32),
                jnp.zeros((KEYVALUE_HEADS, head_q.shape[1], HEAD_SIZE), jnp.float32),
            )
            for head_q, block_pos in prepared
        )
    )
    finals = fold_keys(
        initial,
        (
            lax.all_gather(new_keys, "ctx", axis=0, tiled=True),
            lax.all_gather(new_values, "ctx", axis=0, tiled=True),
        ),
        prepared,
    )
    attended = finish_block(finals[0], tok_rows)
    out_delta = output_delta(attended, out_part)
    return (attended, out_delta)


PIECES = 8
GROUP = QH // KEYVALUE_HEADS
SECTIONS = ((0, 12288), (12288, 2048), (14336, 512), (14848, 2048), (16896, 4096))
DOWN_ROWS, QUERY_ROWS, KEYVAL_ROWS, DOWN_OUT_ROWS, UP_OUT_ROWS = 768, 128, 32, 128, 256
UP_ROWS = QUERY_ROWS + 2 * KEYVAL_ROWS
FIRST_ROWS = DOWN_ROWS + QUERY_ROWS + KEYVAL_ROWS


def pack_kernel(sections, pool, *refs):
    out, buffers, sems = refs[-3:]
    plane = lax.axis_index("groups")
    slabs, slab_rows = out.shape[:2]

    def copies(slab):
        listed = []
        offset = 0
        for first, rows in sections:
            share = rows // (2 * PIECES)
            begin = first + (slab * 2 + plane) * share
            listed.append(
                pltpu.make_async_copy(
                    pool.at[:, pl.ds(pl.multiple_of(begin * 128, 2048), share * 128)],
                    buffers.at[slab, :, pl.ds(offset, share * 128)],
                    sems.at[slab, len(listed)],
                )
            )
            offset += share * 128
        return listed

    for slab in range(slabs):
        for copy in copies(slab):
            copy.start()

    def step(slab, carried):
        for copy in copies(slab):
            copy.wait()

        def chunk(index, inner):
            line = buffers[slab, :, pl.ds(pl.multiple_of(index * 2048, 2048), 2048)]
            block = line.astype(jnp.float32).reshape(16, 128).astype(jnp.bfloat16)
            out[slab, pl.ds(pl.multiple_of(index * 16, 16), 16), :] = block
            return inner

        lax.fori_loop(0, slab_rows // 16, chunk, 0, unroll=8)
        return carried

    lax.fori_loop(0, slabs, step, 0)


def pack_row(pool, sections, *after):
    slab_rows = sum(rows for _, rows in sections) // (2 * PIECES)
    return pl.pallas_call(
        partial(pack_kernel, sections),
        out_shape=jax.ShapeDtypeStruct((PIECES, slab_rows, 128), jnp.bfloat16),
        in_specs=[pl.BlockSpec(memory_space=pl.ANY)] * (1 + len(after)),
        out_specs=pl.BlockSpec(memory_space=pltpu.VMEM),
        scratch_shapes=[
            pltpu.VMEM((PIECES, 1, slab_rows * 128), jnp.bfloat16),
            pltpu.SemaphoreType.DMA((PIECES, len(sections))),
        ],
        compiler_params=pltpu.CompilerParams(vmem_limit_bytes=60 << 20),
        cost_estimate=pl.CostEstimate(flops=0, bytes_accessed=8 << 20, transcendentals=0),
    )(pool, *after)


def pick_kernel(here, there, owner, spread, *refs):
    outs, lasts, sems = refs[:4], refs[4:6], refs[6]
    half = lax.axis_index("ctx") // PIECES
    last = spread.shape[1] - FIRST_ROWS
    copies = []
    for flip, out in enumerate(outs):
        wishes = there if flip >= 2 else here
        block = half ^ (flip & 1)
        row = lax.rem(owner[wishes[block]], PIECES)
        mirrored = lax.rem(owner[wishes[1 - block]], PIECES)
        pairs = (
            (spread.at[row, pl.ds(0, FIRST_ROWS)], out.at[pl.ds(0, FIRST_ROWS)]),
            (
                spread.at[mirrored, pl.ds(FIRST_ROWS - KEYVAL_ROWS, KEYVAL_ROWS)],
                out.at[pl.ds(FIRST_ROWS, KEYVAL_ROWS)],
            ),
            (spread.at[row, pl.ds(FIRST_ROWS, last)], lasts[flip % 2].at[flip // 2]),
        )
        for number, (source, target) in enumerate(pairs):
            copies.append(pltpu.make_async_copy(source, target, sems.at[flip, number]))
    for copy in copies:
        copy.start()
    for copy in copies:
        copy.wait()


def pick(spread, here, there, owner):
    last = spread.shape[1] - FIRST_ROWS
    first_shape = jax.ShapeDtypeStruct((FIRST_ROWS + KEYVAL_ROWS, 128), jnp.bfloat16)
    last_shape = jax.ShapeDtypeStruct((2, last, 128), jnp.bfloat16)
    outs = pl.pallas_call(
        pick_kernel,
        out_shape=(first_shape,) * 4 + (last_shape,) * 2,
        in_specs=[pl.BlockSpec(memory_space=pltpu.SMEM)] * 3 + [pl.BlockSpec(memory_space=pl.ANY)],
        out_specs=(pl.BlockSpec(memory_space=pltpu.VMEM),) * 6,
        scratch_shapes=[pltpu.SemaphoreType.DMA((4, 3))],
        compiler_params=pltpu.CompilerParams(vmem_limit_bytes=16 << 20),
        cost_estimate=pl.CostEstimate(flops=0, bytes_accessed=3 << 20, transcendentals=0),
    )(here, there, owner, spread)
    return outs[:4], outs[4], outs[5]


def deal_kernel(rows, even, odd, sems):
    seat = lax.rem(lax.axis_index("ctx"), PIECES)
    width = rows.shape[1] // PIECES
    copies = []
    for apart in range(PIECES):
        first = pl.multiple_of((seat ^ apart) * width, width)
        target = (odd if apart % 2 else even).at[apart // 2]
        copies.append(
            pltpu.make_async_copy(rows.at[:, pl.ds(first, width)], target, sems.at[apart])
        )
    for copy in copies:
        copy.start()
    for copy in copies:
        copy.wait()


def deal(rows, *after):
    slab = jax.ShapeDtypeStruct((PIECES // 2, rows.shape[0], rows.shape[1] // PIECES), rows.dtype)

    def kernel(rows, *refs):
        deal_kernel(rows, *refs[-3:])

    return pl.pallas_call(
        kernel,
        out_shape=(slab, slab),
        in_specs=[pl.BlockSpec(memory_space=pl.ANY)] * (1 + len(after)),
        out_specs=(pl.BlockSpec(memory_space=pltpu.VMEM),) * 2,
        scratch_shapes=[pltpu.SemaphoreType.DMA((PIECES,))],
        compiler_params=pltpu.CompilerParams(vmem_limit_bytes=16 << 20),
        cost_estimate=pl.CostEstimate(flops=0, bytes_accessed=2 << 20, transcendentals=0),
    )(rows, *after)


def nearest(here, owner, block):
    half = lax.axis_index("ctx") // PIECES
    return owner[here[block]] // PIECES == half


def choose(close, arrived, put):
    plane = lax.axis_index("groups")

    @pl.when(close)
    def _():
        put(arrived[0], plane)
        put(arrived[2], 1 - plane)

    @pl.when(jnp.logical_not(close))
    def _():
        put(arrived[1], plane)
        put(arrived[3], 1 - plane)


def join_kernel(here, owner, *refs):
    arrived, (weight, ups), (flat, left, right) = refs[:4], refs[4:6], refs[6:]
    half = lax.axis_index("ctx") // PIECES
    split = DOWN_ROWS + QUERY_ROWS + KEYVAL_ROWS

    def put_own(source, position):
        first = pl.multiple_of(position * DOWN_ROWS, DOWN_ROWS)
        flat[pl.ds(first, DOWN_ROWS), :] = source[:DOWN_ROWS, :].astype(jnp.float32)
        ups[position, : UP_ROWS - KEYVAL_ROWS, :] = source[DOWN_ROWS:split, :]

    def put_mirrored(source, position):
        ups[position, UP_ROWS - KEYVAL_ROWS :, :] = source[split:, :]

    choose(nearest(here, owner, half), arrived, put_own)
    choose(nearest(here, owner, 1 - half), arrived, put_mirrored)

    third = flat.shape[0] // 3
    one = flat[pl.ds(0, third, stride=3), :]
    two = pltpu.roll(flat[pl.ds(1, third, stride=3), :], 64, 1)
    three = pltpu.roll(flat[pl.ds(2, third, stride=3), :], 64, 1)
    lane = lax.broadcasted_iota(jnp.int32, one.shape, 1)
    left[pl.ds(0, third, stride=2), :] = one
    left[pl.ds(1, third, stride=2), :] = jnp.where(lane < 64, two, three)
    right[pl.ds(0, third, stride=2), :] = pltpu.roll(two, 64, 1)
    right[pl.ds(1, third, stride=2), :] = three
    weight[...] = jnp.concatenate([left[...], right[...]], 1).astype(jnp.bfloat16)


def join(here, owner, arrived):
    depth = D // PIECES
    return pl.pallas_call(
        join_kernel,
        out_shape=(
            jax.ShapeDtypeStruct((depth, 256), jnp.bfloat16),
            jax.ShapeDtypeStruct((2, UP_ROWS, 128), jnp.bfloat16),
        ),
        in_specs=[pl.BlockSpec(memory_space=pltpu.SMEM)] * 2
        + [pl.BlockSpec(memory_space=pltpu.VMEM)] * 4,
        out_specs=(pl.BlockSpec(memory_space=pltpu.VMEM),) * 2,
        scratch_shapes=[
            pltpu.VMEM((2 * DOWN_ROWS, 128), jnp.float32),
            pltpu.VMEM((depth, 128), jnp.float32),
            pltpu.VMEM((depth, 128), jnp.float32),
        ],
        compiler_params=pltpu.CompilerParams(vmem_limit_bytes=16 << 20),
        cost_estimate=pl.CostEstimate(flops=0, bytes_accessed=96 << 20, transcendentals=0),
    )(here, owner, *arrived)


def settle_kernel(here, there, owner, near, far, own, across):
    half = lax.axis_index("ctx") // PIECES
    for number, (wishes, out) in enumerate(((here, own), (there, across))):
        close = nearest(wishes, owner, half)

        @pl.when(close)
        def _():
            out[...] = near[number]

        @pl.when(jnp.logical_not(close))
        def _():
            out[...] = far[number]


def settle(here, there, owner, near, far):
    slab = jax.ShapeDtypeStruct(near.shape[1:], jnp.bfloat16)
    return pl.pallas_call(
        settle_kernel,
        out_shape=(slab, slab),
        in_specs=[pl.BlockSpec(memory_space=pltpu.SMEM)] * 3
        + [pl.BlockSpec(memory_space=pltpu.VMEM)] * 2,
        out_specs=(pl.BlockSpec(memory_space=pltpu.VMEM),) * 2,
        compiler_params=pltpu.CompilerParams(vmem_limit_bytes=16 << 20),
        cost_estimate=pl.CostEstimate(flops=0, bytes_accessed=1 << 20, transcendentals=0),
    )(here, there, owner, near, far)


def narrow_kernel(weight, *refs):
    for block, out in zip(refs[:4], refs[4:]):
        sides, rows, depth = block.shape
        product = jnp.dot(
            block[...].reshape(sides * rows, depth),
            weight[...],
            preferred_element_type=jnp.float32,
        )
        out[...] = product[:, : 3 * ADAPTER_RANK].reshape(out.shape).astype(jnp.bfloat16)


def narrow(weight, dealt):
    sides, rows, depth = dealt[0].shape
    partial_sums = jax.ShapeDtypeStruct((sides, rows, 3 * ADAPTER_RANK), jnp.bfloat16)
    return pl.pallas_call(
        narrow_kernel,
        out_shape=(partial_sums,) * 4,
        in_specs=[pl.BlockSpec(memory_space=pltpu.VMEM)] * 5,
        out_specs=(pl.BlockSpec(memory_space=pltpu.VMEM),) * 4,
        compiler_params=pltpu.CompilerParams(vmem_limit_bytes=16 << 20),
        cost_estimate=pl.CostEstimate(
            flops=2 * 8 * rows * depth * 256, bytes_accessed=2 << 20, transcendentals=0
        ),
    )(weight, *dealt)


def attend_kernel(
    first_head,
    query_block,
    key_same,
    key_other,
    value_same,
    value_other,
    own_rank,
    rows_same,
    rows_other,
    cosines,
    sines,
    *refs,
):
    attended, flat_query, flat_keyval, keys, values = refs[-5:]
    step = pl.program_id(0) + first_head
    rows = query_block.shape[0]
    base = lax.axis_index("ctx") * rows
    half = lax.axis_index("ctx") // PIECES
    seat = lax.rem(lax.axis_index("ctx"), PIECES)
    dot = partial(jnp.dot, preferred_element_type=jnp.float32)

    @pl.when(pl.program_id(0) == 0)
    def _():
        for apart in range(PIECES):
            source = rows_other if apart % 2 else rows_same
            for position in range(2):
                begin = PIECES * rows + (apart // 2 * 2 + position) * UP_ROWS
                piece = source[begin : begin + UP_ROWS, :].astype(jnp.float32)
                place = (seat ^ apart) * 2 + position
                first = pl.multiple_of(place * QUERY_ROWS, QUERY_ROWS)
                flat_query[pl.ds(first, QUERY_ROWS), :] = piece[:QUERY_ROWS]
                first = pl.multiple_of(place * KEYVAL_ROWS, KEYVAL_ROWS)
                for side in range(2):
                    begin = QUERY_ROWS + side * KEYVAL_ROWS
                    flat_keyval[side, pl.ds(first, KEYVAL_ROWS), :] = piece[
                        begin : begin + KEYVAL_ROWS
                    ]

    def turned(delta, cosine, sine):
        return delta * cosine + pltpu.roll(delta, HEAD_SIZE // 2, 1) * sine

    def up(flat, first, stride):
        return flat[pl.ds(first, ADAPTER_RANK, stride=stride), :].astype(jnp.bfloat16)

    for side in range(2):
        heads = 2 * KEYVALUE_HEADS
        key_up = up(flat_keyval.at[side], step, heads)
        value_up = up(flat_keyval.at[side], step + KEYVALUE_HEADS, heads)
        for core in range(2):
            source = rows_other if core else rows_same
            rank = [
                source[(2 * chip + side) * rows : (2 * chip + side + 1) * rows, :]
                for chip in range(PIECES // 2)
            ]
            rank = jnp.concatenate(rank, 0)
            key_delta = adapter_scale * dot(rank[:, :ADAPTER_RANK], key_up)
            value_delta = adapter_scale * dot(rank[:, ADAPTER_RANK:], value_up)
            for chip in range(PIECES // 2):
                there = seat ^ (2 * chip + core)
                first = ((half ^ side) * PIECES + there) * rows
                span = pl.ds(pl.multiple_of(first, rows), rows)
                part = slice(chip * rows, (chip + 1) * rows)
                delta = turned(key_delta[part], cosines[span, :], sines[span, :])
                full = (key_other if core else key_same)[chip, side].astype(jnp.float32) + delta
                keys[span, :] = full.astype(jnp.bfloat16)
                full = (value_other if core else value_same)[chip, side].astype(jnp.float32)
                values[span, :] = (full + value_delta[part]).astype(jnp.bfloat16)
    here = pl.ds(pl.multiple_of(base, rows), rows)
    cosine = cosines[here, :]
    sine = sines[here, :]
    taken = GROUP // 2
    limit = lax.broadcasted_iota(jnp.int32, (rows, 1), 0) + base
    limit = jnp.concatenate([limit] * taken, 0)
    for first in range(0, GROUP, taken):
        weight = [up(flat_query, step * GROUP + first + head, QH) for head in range(taken)]
        deltas = adapter_scale * dot(own_rank[:, :ADAPTER_RANK], jnp.concatenate(weight, 1))
        queries = []
        for place in range(taken):
            moved = turned(deltas[:, place * HEAD_SIZE : (place + 1) * HEAD_SIZE], cosine, sine)
            span = slice((first + place) * HEAD_SIZE, (first + place + 1) * HEAD_SIZE)
            queries.append(
                (query_block[:, span].astype(jnp.float32) + moved).astype(jnp.bfloat16)
            )
        queries = jnp.concatenate(queries, 0)
        scores = lax.dot_general(
            queries, keys[...], (((1,), (1,)), ((), ())), preferred_element_type=jnp.float32
        )
        column = lax.broadcasted_iota(jnp.int32, scores.shape, 1)
        scores = jnp.where(column <= limit, scores, mask_floor)
        scores = scores - jnp.max(scores, axis=-1, keepdims=True)
        weights = jnp.exp2(scores * (HEAD_SIZE ** (-0.5) * math.log2(math.e)))
        divisor = jnp.sum(weights, axis=-1, keepdims=True)
        result = (dot(weights.astype(jnp.bfloat16), values[...]) / divisor).astype(jnp.bfloat16)
        for place in range(taken):
            span = slice((first + place) * HEAD_SIZE, (first + place + 1) * HEAD_SIZE)
            attended[:, span] = result[place * rows : (place + 1) * rows]


def attend(first_head, heads, before, query_base, base, own_rank, gathered, cosines, sines):
    rows = query_base.shape[0]
    seq = 4 * PIECES // 2 * rows
    width = GROUP * HEAD_SIZE

    def whole(shape):
        return pl.BlockSpec(shape, lambda h: (0,) * len(shape))

    key_spec = pl.BlockSpec((PIECES // 2, 2, rows, HEAD_SIZE), lambda h: (0, 0, 0, h + first_head))
    value_spec = pl.BlockSpec(
        (PIECES // 2, 2, rows, HEAD_SIZE), lambda h: (0, 0, 0, h + first_head + KEYVALUE_HEADS)
    )
    operands = (query_base, base[0], base[1], base[0], base[1], own_rank, *gathered)
    operands += (cosines, sines) + (() if before is None else (before,))
    query_spec = pl.BlockSpec((rows, width), lambda h: (0, h + first_head))
    return pl.pallas_call(
        partial(attend_kernel, first_head),
        grid=(heads,),
        out_shape=jax.ShapeDtypeStruct((rows, QH * HEAD_SIZE), jnp.bfloat16),
        in_specs=[
            query_spec,
            key_spec,
            key_spec,
            value_spec,
            value_spec,
            whole(own_rank.shape),
            whole(gathered[0].shape),
            whole(gathered[1].shape),
            whole(cosines.shape),
            whole(sines.shape),
        ]
        + [pl.BlockSpec(memory_space=pl.ANY)] * (len(operands) - 10),
        out_specs=query_spec,
        input_output_aliases={} if before is None else {len(operands) - 1: 0},
        scratch_shapes=[
            pltpu.VMEM((2 * PIECES * QUERY_ROWS, 128), jnp.float32),
            pltpu.VMEM((2, 2 * PIECES * KEYVAL_ROWS, 128), jnp.float32),
            pltpu.VMEM((seq, HEAD_SIZE), jnp.bfloat16),
            pltpu.VMEM((seq, HEAD_SIZE), jnp.bfloat16),
        ],
        compiler_params=pltpu.CompilerParams(vmem_limit_bytes=60 << 20),
        cost_estimate=pl.CostEstimate(
            flops=12 * heads * rows * QH * seq * HEAD_SIZE,
            bytes_accessed=10 << 20,
            transcendentals=heads * rows * GROUP * seq,
        ),
    )(*operands)


def widen_kernel(attended, same, other, out_delta, down_out, up_out):
    plane = lax.axis_index("groups")
    seat = lax.rem(lax.axis_index("ctx"), PIECES)
    for apart in range(PIECES):
        pieces = other if apart % 2 else same
        for position in range(2):
            piece = pieces[apart // 2, position].astype(jnp.float32)
            place = (seat ^ apart) * 2 + (position ^ plane)
            first = place * 2 * DOWN_OUT_ROWS
            block = piece[:DOWN_OUT_ROWS]
            down_out[pl.ds(first, DOWN_OUT_ROWS, stride=2), :] = block
            down_out[pl.ds(first + 1, DOWN_OUT_ROWS, stride=2), :] = pltpu.roll(block, 64, 1)
            first = pl.multiple_of(place * UP_OUT_ROWS, UP_OUT_ROWS)
            up_out[pl.ds(first, UP_OUT_ROWS), :] = piece[DOWN_OUT_ROWS:]
    dot = partial(jnp.dot, preferred_element_type=jnp.float32)
    rank = dot(attended[...], down_out[...].astype(jnp.bfloat16))[:, :ADAPTER_RANK]
    rank = rank.astype(jnp.bfloat16)
    blocks = D // 128
    for first in range(0, blocks, 4):
        weight = [
            up_out[pl.ds(first + block, ADAPTER_RANK, stride=blocks), :].astype(jnp.bfloat16)
            for block in range(4)
        ]
        delta = adapter_scale * dot(rank, jnp.concatenate(weight, 1))
        out_delta[:, first * 128 : (first + 4) * 128] = delta.astype(jnp.bfloat16)


def widen(attended, same, other):
    return pl.pallas_call(
        widen_kernel,
        out_shape=jax.ShapeDtypeStruct((attended.shape[0], D), jnp.bfloat16),
        in_specs=[pl.BlockSpec(memory_space=pltpu.VMEM)] * 3,
        out_specs=pl.BlockSpec(memory_space=pltpu.VMEM),
        scratch_shapes=[
            pltpu.VMEM((QH * HEAD_SIZE, 128), jnp.float32),
            pltpu.VMEM((ADAPTER_RANK * D // 128, 128), jnp.float32),
        ],
        compiler_params=pltpu.CompilerParams(vmem_limit_bytes=32 << 20),
        cost_estimate=pl.CostEstimate(flops=1 << 27, bytes_accessed=4 << 20, transcendentals=0),
    )(attended, same, other)


def swap(block, mask):
    return lax.ppermute(block, ("groups", "ctx"), [(i, i ^ mask) for i in range(4 * PIECES)])


def direct_shards(
    normed_input, query_base, key_base, value_base, adapter_pool, stretch_adapter, adapter_owner
):
    tok_rows = normed_input.shape[0]
    ctx = lax.axis_size("ctx")
    seq = ctx * tok_rows
    blocks = [list(range(PIECES)), list(range(PIECES, 2 * PIECES))]
    half_dim = HEAD_SIZE // 2
    frequency = rope_base ** (-(jnp.arange(half_dim, dtype=jnp.float32) * 2.0) / HEAD_SIZE)
    angle = jnp.arange(seq, dtype=jnp.int32).astype(jnp.float32)[:, None] * frequency[None, :]
    cosine = jnp.cos(angle)
    sine = jnp.sin(angle)
    cosines = jnp.concatenate([cosine, cosine], 1)
    sines = jnp.concatenate([-sine, sine], 1)

    def after(block, *others):
        return lax.optimization_barrier((block, others))[0]

    def exchange(sent):
        across = swap(sent[2], 2 * PIECES)
        return [sent[0], swap(sent[1], PIECES), across, swap(sent[3], 3 * PIECES)]

    def along_z(block):
        return jnp.stack([block, swap(block, 4)])

    def along_x(pair):
        quad = jnp.stack([pair, swap(pair, 2)], 1)
        return quad.reshape((PIECES // 2,) + pair.shape[1:])

    elsewhere = swap(stretch_adapter, 2 * PIECES)
    packed = pack_row(adapter_pool, SECTIONS)
    even, odd = deal(normed_input, packed)
    sibling = swap(odd, 1)
    base = jnp.concatenate([key_base, value_base], 1)
    base = jnp.stack([base, swap(base, PIECES)])

    spread = lax.all_to_all(packed, "ctx", 0, 0, axis_index_groups=blocks)
    spread = after(spread, sibling, base, cosines, sines)
    sent, near, far = pick(spread, stretch_adapter, elsewhere, adapter_owner)
    arrived = exchange(sent)
    dealt = [after(jnp.stack([even[j], sibling[j]]), sent) for j in range(PIECES // 2)]
    dealt = [swap(block, 2 * j) if j else block for j, block in enumerate(dealt)]

    weight, ups = join(stretch_adapter, adapter_owner, arrived)
    far = swap(after(far, weight), PIECES)
    partial_sums = narrow(weight, dealt)
    back = [swap(block, 2 * j) if j else block for j, block in enumerate(partial_sums)]
    back = sum(block.astype(jnp.float32) for block in back)
    own_rank = swap(after(back[1].astype(jnp.bfloat16), far), 1)
    own_rank = back[0] + own_rank.astype(jnp.float32)
    own_rank = own_rank.astype(jnp.bfloat16)
    ups = along_z(after(ups, *partial_sums))
    base = along_z(after(base, *partial_sums))
    all_rank = own_rank[:, ADAPTER_RANK:]
    base = along_x(after(base, own_rank))
    own, across = settle(
        stretch_adapter, elsewhere, adapter_owner, near, after(far, own_rank)
    )
    ends = jnp.stack([own, swap(across, 2 * PIECES)])
    all_rank = jnp.stack([all_rank, swap(all_rank, PIECES)])
    all_rank = after(all_rank, ups)
    ups = along_x(after(ups, all_rank))
    all_rank = jnp.stack([swap(all_rank, apart) if apart else all_rank for apart in (0, 2, 4, 6)])
    base = after(base, all_rank)
    base = (base, swap(base, 1))
    gathered = jnp.concatenate([all_rank.reshape(-1, 128), ups.reshape(-1, 128)])
    gathered = after(gathered, ends)
    gathered = (gathered, swap(gathered, 1))

    shared = (query_base, base, own_rank, gathered, cosines, sines)
    attended = attend(0, 1, None, *shared)
    ends = after(ends, attended)
    ends = jnp.stack([swap(ends, apart) if apart else ends for apart in (0, 2, 4, 6)])
    attended = attend(1, KEYVALUE_HEADS - 1, attended, *shared)
    ends = after(ends, attended)
    return attended, widen(attended, ends, swap(ends, 1))


def shards(normed_input, query_base, key_base, value_base, adapter_pool, stretch_adapter, owner):
    fits = (
        lax.axis_size("groups") == 2
        and lax.axis_size("ctx") == 2 * PIECES
        and normed_input.shape[0] * PIECES == BLOCK_TOKENS
        and adapter_pool.shape[0] == 1
    )
    plan = direct_shards if fits else spread_shards
    return plan(
        normed_input, query_base, key_base, value_base, adapter_pool, stretch_adapter, owner
    )


def solution(mesh):
    placed = (
        P(("groups", "ctx"), None),
        P(("groups", "ctx"), None),
        P(("groups", "ctx"), None),
        P(("groups", "ctx"), None),
        P("ctx", None),
        P("groups"),
        P(),
    )
    return jax.shard_map(
        shards,
        mesh=mesh,
        in_specs=placed,
        out_specs=(P(("groups", "ctx"), None), P(("groups", "ctx"), None)),
        check_vma=False,
    )
```

```python
from functools import partial
import math

import jax
import jax.numpy as jnp
from jax import lax
from jax.experimental import pallas as pl
from jax.experimental.pallas import tpu as pltpu
from jax.sharding import PartitionSpec as P

D = 8192
QH = 32
KEYVALUE_HEADS = 4
HEAD_SIZE = 128
ADAPTER_RANK = 64
BLOCK_TOKENS = 512
QKV_POOL = 1900544


adapter_scale = 2.0
rope_base = 500000.0
mask_floor = -1e30


def from_partner(block, axis, apart):
    count = lax.axis_size(axis)
    route = []
    for low in range(count):
        high = low | 1 << apart
        if high != low and high < count:
            route += [(low, high), (high, low)]
    return lax.ppermute(block, axis, route)


def rotate(delta, token_positions, heads):
    half_dim = HEAD_SIZE // 2
    frequency = rope_base ** (-(jnp.arange(half_dim, dtype=jnp.float32) * 2.0) / HEAD_SIZE)
    angle = token_positions.astype(jnp.float32)[:, None] * frequency[None, :]
    cosine = jnp.cos(angle)[:, None, :]
    sine_part = jnp.sin(angle)[:, None, :]
    shaped = delta.reshape(delta.shape[0], heads, HEAD_SIZE)
    first_half = shaped[..., :half_dim]
    second_half = shaped[..., half_dim:]
    joined = jnp.concatenate(
        [
            first_half * cosine - second_half * sine_part,
            second_half * cosine + first_half * sine_part,
        ],
        -1,
    )
    return joined.reshape(delta.shape[0], heads * HEAD_SIZE)


def project_heads(
    narrow_product, query_row_block, key_row_block, value_row_block, upper_part, token_positions
):
    query_up_weight = upper_part[: ADAPTER_RANK * QH * HEAD_SIZE].reshape(
        ADAPTER_RANK, QH * HEAD_SIZE
    )
    keyvalue_up_weight = upper_part[ADAPTER_RANK * QH * HEAD_SIZE :].reshape(
        ADAPTER_RANK, 2 * KEYVALUE_HEADS * HEAD_SIZE
    )
    query_correction = adapter_scale * jnp.dot(
        narrow_product[:, :ADAPTER_RANK], query_up_weight, preferred_element_type=jnp.float32
    )
    key_correction = adapter_scale * jnp.dot(
        narrow_product[:, ADAPTER_RANK : 2 * ADAPTER_RANK],
        keyvalue_up_weight[:, : KEYVALUE_HEADS * HEAD_SIZE],
        preferred_element_type=jnp.float32,
    )
    value_correction = adapter_scale * jnp.dot(
        narrow_product[:, 2 * ADAPTER_RANK :],
        keyvalue_up_weight[:, KEYVALUE_HEADS * HEAD_SIZE :],
        preferred_element_type=jnp.float32,
    )
    queries = (
        query_row_block.astype(jnp.float32) + rotate(query_correction, token_positions, QH)
    ).astype(jnp.bfloat16)
    new_keys = (
        key_row_block.astype(jnp.float32) + rotate(key_correction, token_positions, KEYVALUE_HEADS)
    ).astype(jnp.bfloat16)
    new_values = (value_row_block.astype(jnp.float32) + value_correction).astype(jnp.bfloat16)
    return (queries, new_keys, new_values)


def output_delta(attended_rows, out_part):
    down_out = out_part[: QH * HEAD_SIZE * ADAPTER_RANK].reshape(QH * HEAD_SIZE, ADAPTER_RANK)
    raised_output = out_part[QH * HEAD_SIZE * ADAPTER_RANK :].reshape(ADAPTER_RANK, D)
    narrow_product = jnp.dot(attended_rows, down_out, preferred_element_type=jnp.float32).astype(
        jnp.bfloat16
    )
    return (
        adapter_scale * jnp.dot(narrow_product, raised_output, preferred_element_type=jnp.float32)
    ).astype(jnp.bfloat16)


def head_major(query_row_block):
    count_rows = query_row_block.shape[0]
    group_size = QH // KEYVALUE_HEADS
    return (
        query_row_block.reshape(count_rows, KEYVALUE_HEADS, group_size, HEAD_SIZE)
        .transpose(1, 2, 0, 3)
        .reshape(KEYVALUE_HEADS, group_size * count_rows, HEAD_SIZE)
    )


def row_major(head_rows, count_rows):
    group_size = QH // KEYVALUE_HEADS
    return (
        head_rows.reshape(KEYVALUE_HEADS, group_size, count_rows, HEAD_SIZE)
        .transpose(2, 0, 1, 3)
        .reshape(count_rows, QH * HEAD_SIZE)
    )


def online_update(current, queries, query_pos, key_slice, value_slice, key_start):
    run_max, run_sum, run_acc = current
    scores = jnp.einsum(
        "hqd,khd->hqk", queries, key_slice, preferred_element_type=jnp.float32
    ) * HEAD_SIZE ** (-0.5)
    key_pos = key_start + jnp.arange(key_slice.shape[0], dtype=jnp.int32)
    allowed = (query_pos[:, None] >= key_pos[None, :])[None]
    new_max = jnp.maximum(run_max, jnp.max(jnp.where(allowed, scores, mask_floor), axis=-1))
    weights = jnp.where(allowed, jnp.exp(scores - new_max[..., None]), 0.0)
    rescale = jnp.exp(run_max - new_max)
    new_sum = run_sum * rescale + jnp.sum(weights, axis=-1)
    new_acc = run_acc * rescale[..., None] + jnp.einsum(
        "hqk,khd->hqd",
        weights.astype(jnp.bfloat16),
        value_slice,
        preferred_element_type=jnp.float32,
    )
    return (new_max, new_sum, new_acc)


def unchanged(current):
    return current


def fold_keys(carry_state, shard_part, prepared):
    key_row_block, value_row_block = shard_part
    key_count = key_row_block.shape[0]
    sub_width = math.gcd(key_count, 1024)
    key_heads = key_row_block.reshape(key_count // sub_width, sub_width, KEYVALUE_HEADS, HEAD_SIZE)
    value_heads = value_row_block.reshape(
        key_count // sub_width, sub_width, KEYVALUE_HEADS, HEAD_SIZE
    )

    def one_step(sub_index, carried):
        key_start = sub_index * sub_width
        key_slice = lax.dynamic_index_in_dim(key_heads, sub_index, 0, keepdims=False)
        value_slice = lax.dynamic_index_in_dim(value_heads, sub_index, 0, keepdims=False)
        updated = []
        for (queries, query_pos), running in zip(prepared, carried):
            advance = partial(
                online_update,
                queries=queries,
                query_pos=query_pos,
                key_slice=key_slice,
                value_slice=value_slice,
                key_start=key_start,
            )
            updated.append(lax.cond(key_start <= jnp.max(query_pos), advance, unchanged, running))
        return tuple(updated)

    return lax.fori_loop(0, key_count // sub_width, one_step, carry_state)


def finish_block(result, count_rows):
    run_max, run_sum, run_acc = result
    divisor = jnp.where(run_sum > 0.0, run_sum, 1.0)
    return row_major(run_acc / divisor[..., None], count_rows).astype(jnp.bfloat16)


def spread_shards(
    normed_input, query_base, key_base, value_base, adapter_pool, stretch_adapter, adapter_owner
):
    cycle_size = lax.axis_size("ctx")
    my_index = lax.axis_index("ctx")
    tok_rows = normed_input.shape[0]
    token_positions = my_index * tok_rows + jnp.arange(tok_rows, dtype=jnp.int32)
    device_ids = jnp.arange(cycle_size, dtype=jnp.int32)
    stretch_of = device_ids * tok_rows // BLOCK_TOKENS
    stretch_ids = jnp.arange(stretch_adapter.shape[0], dtype=jnp.int32)
    adapter_of = jnp.sum(
        jnp.where(stretch_of[:, None] == stretch_ids[None, :], stretch_adapter[None, :], 0), axis=1
    )
    adapter_ids = jnp.arange(adapter_owner.shape[0], dtype=jnp.int32)
    slot_of = jnp.sum(
        jnp.where(adapter_of[:, None] == adapter_ids[None, :], adapter_owner[None, :], 0), axis=1
    )
    down_size = 3 * ADAPTER_RANK * D
    group_count = BLOCK_TOKENS // tok_rows
    levels = group_count.bit_length() - 1
    local_index = my_index % group_count
    col_width = D // group_count
    piece_len = down_size // (group_count * cycle_size)
    pool_rows = adapter_pool.shape[0]
    down_shaped = adapter_pool[:, :down_size].reshape(pool_rows, group_count, cycle_size, piece_len)
    spread_down = lax.all_to_all(down_shaped, "ctx", split_axis=2, concat_axis=0, tiled=True)
    flat_down = spread_down.reshape(-1, piece_len)
    wanted = jnp.take(flat_down, slot_of * group_count + device_ids % group_count, axis=0)[
        :, None, :
    ]
    down_slice = lax.all_to_all(wanted, "ctx", split_axis=0, concat_axis=1, tiled=True).reshape(
        col_width, 3 * ADAPTER_RANK
    )
    spread_rest = lax.all_to_all(
        adapter_pool[:, down_size:], "ctx", split_axis=1, concat_axis=0, tiled=True
    )
    rest_row = lax.all_to_all(
        jnp.take(spread_rest, slot_of, axis=0), "ctx", split_axis=0, concat_axis=1, tiled=True
    )[0]
    upper_part = rest_row[: QKV_POOL - down_size]
    out_part = rest_row[QKV_POOL - down_size :]
    pieces = normed_input.reshape(tok_rows, group_count, col_width)
    slice_order = jnp.bitwise_xor(local_index, jnp.arange(group_count, dtype=jnp.int32))
    moving = jnp.take(pieces, slice_order, axis=1).transpose(1, 0, 2)
    for level in range(levels):
        shaped = moving.reshape(group_count >> level + 1, 2, 1 << level, tok_rows, col_width)
        arrived = from_partner(shaped[:, 1], "ctx", level)
        moving = jnp.stack([shaped[:, 0], arrived], 1).reshape(group_count, tok_rows, col_width)
    partial_rows = jnp.dot(
        moving.reshape(group_count * tok_rows, col_width),
        down_slice,
        preferred_element_type=jnp.float32,
    ).reshape(group_count, tok_rows, 3 * ADAPTER_RANK)
    for level in reversed(range(levels)):
        halves = partial_rows.reshape(2, partial_rows.shape[0] // 2, tok_rows, 3 * ADAPTER_RANK)
        partial_rows = halves[0] + from_partner(
            halves[1].astype(jnp.bfloat16), "ctx", level
        ).astype(jnp.float32)
    narrow_product = partial_rows[0].astype(jnp.bfloat16)
    queries, new_keys, new_values = project_heads(
        narrow_product, query_base, key_base, value_base, upper_part, token_positions
    )
    group_size = QH // KEYVALUE_HEADS
    blocks = [(queries, token_positions)]
    prepared = [
        (head_major(block_q), jnp.tile(block_pos, group_size)) for block_q, block_pos in blocks
    ]
    initial = tuple(
        (
            (
                jnp.full((KEYVALUE_HEADS, head_q.shape[1]), mask_floor, jnp.float32),
                jnp.zeros((KEYVALUE_HEADS, head_q.shape[1]), jnp.float32),
                jnp.zeros((KEYVALUE_HEADS, head_q.shape[1], HEAD_SIZE), jnp.float32),
            )
            for head_q, block_pos in prepared
        )
    )
    finals = fold_keys(
        initial,
        (
            lax.all_gather(new_keys, "ctx", axis=0, tiled=True),
            lax.all_gather(new_values, "ctx", axis=0, tiled=True),
        ),
        prepared,
    )
    attended = finish_block(finals[0], tok_rows)
    out_delta = output_delta(attended, out_part)
    return (attended, out_delta)


PIECES = 8
GROUP = QH // KEYVALUE_HEADS
SECTIONS = ((0, 12288), (12288, 2048), (14336, 512), (14848, 2048), (16896, 4096))
DOWN_ROWS, QUERY_ROWS, KEYVAL_ROWS, DOWN_OUT_ROWS, UP_OUT_ROWS = 768, 128, 32, 128, 256
UP_ROWS = QUERY_ROWS + 2 * KEYVAL_ROWS
FIRST_ROWS = DOWN_ROWS + QUERY_ROWS + KEYVAL_ROWS


def pack_kernel(sections, pool, *refs):
    out, buffers, sems = refs[-3:]
    plane = lax.axis_index("groups")
    slabs, slab_rows = out.shape[:2]

    def copies(slab):
        listed = []
        offset = 0
        for first, rows in sections:
            share = rows // (2 * PIECES)
            begin = first + (slab * 2 + plane) * share
            listed.append(
                pltpu.make_async_copy(
                    pool.at[:, pl.ds(pl.multiple_of(begin * 128, 2048), share * 128)],
                    buffers.at[slab, :, pl.ds(offset, share * 128)],
                    sems.at[slab, len(listed)],
                )
            )
            offset += share * 128
        return listed

    for slab in range(slabs):
        for copy in copies(slab):
            copy.start()

    def step(slab, carried):
        for copy in copies(slab):
            copy.wait()

        def chunk(index, inner):
            line = buffers[slab, :, pl.ds(pl.multiple_of(index * 2048, 2048), 2048)]
            block = line.astype(jnp.float32).reshape(16, 128).astype(jnp.bfloat16)
            out[slab, pl.ds(pl.multiple_of(index * 16, 16), 16), :] = block
            return inner

        lax.fori_loop(0, slab_rows // 16, chunk, 0, unroll=8)
        return carried

    lax.fori_loop(0, slabs, step, 0)


def pack_row(pool, sections, *after):
    slab_rows = sum(rows for _, rows in sections) // (2 * PIECES)
    return pl.pallas_call(
        partial(pack_kernel, sections),
        out_shape=jax.ShapeDtypeStruct((PIECES, slab_rows, 128), jnp.bfloat16),
        in_specs=[pl.BlockSpec(memory_space=pl.ANY)] * (1 + len(after)),
        out_specs=pl.BlockSpec(memory_space=pltpu.VMEM),
        scratch_shapes=[
            pltpu.VMEM((PIECES, 1, slab_rows * 128), jnp.bfloat16),
            pltpu.SemaphoreType.DMA((PIECES, len(sections))),
        ],
        compiler_params=pltpu.CompilerParams(vmem_limit_bytes=60 << 20),
        cost_estimate=pl.CostEstimate(flops=0, bytes_accessed=8 << 20, transcendentals=0),
    )(pool, *after)


def pick_kernel(here, there, owner, spread, *refs):
    outs, lasts, sems = refs[:4], refs[4:6], refs[6]
    half = lax.axis_index("ctx") // PIECES
    last = spread.shape[1] - FIRST_ROWS
    copies = []
    for flip, out in enumerate(outs):
        wishes = there if flip >= 2 else here
        block = half ^ (flip & 1)
        row = lax.rem(owner[wishes[block]], PIECES)
        mirrored = lax.rem(owner[wishes[1 - block]], PIECES)
        pairs = (
            (spread.at[row, pl.ds(0, FIRST_ROWS)], out.at[pl.ds(0, FIRST_ROWS)]),
            (
                spread.at[mirrored, pl.ds(FIRST_ROWS - KEYVAL_ROWS, KEYVAL_ROWS)],
                out.at[pl.ds(FIRST_ROWS, KEYVAL_ROWS)],
            ),
            (spread.at[row, pl.ds(FIRST_ROWS, last)], lasts[flip % 2].at[flip // 2]),
        )
        for number, (source, target) in enumerate(pairs):
            copies.append(pltpu.make_async_copy(source, target, sems.at[flip, number]))
    for copy in copies:
        copy.start()
    for copy in copies:
        copy.wait()


def pick(spread, here, there, owner):
    last = spread.shape[1] - FIRST_ROWS
    first_shape = jax.ShapeDtypeStruct((FIRST_ROWS + KEYVAL_ROWS, 128), jnp.bfloat16)
    last_shape = jax.ShapeDtypeStruct((2, last, 128), jnp.bfloat16)
    outs = pl.pallas_call(
        pick_kernel,
        out_shape=(first_shape,) * 4 + (last_shape,) * 2,
        in_specs=[pl.BlockSpec(memory_space=pltpu.SMEM)] * 3 + [pl.BlockSpec(memory_space=pl.ANY)],
        out_specs=(pl.BlockSpec(memory_space=pltpu.VMEM),) * 6,
        scratch_shapes=[pltpu.SemaphoreType.DMA((4, 3))],
        compiler_params=pltpu.CompilerParams(vmem_limit_bytes=16 << 20),
        cost_estimate=pl.CostEstimate(flops=0, bytes_accessed=3 << 20, transcendentals=0),
    )(here, there, owner, spread)
    return outs[:4], outs[4], outs[5]


def deal_kernel(rows, even, odd, sems):
    seat = lax.rem(lax.axis_index("ctx"), PIECES)
    width = rows.shape[1] // PIECES
    copies = []
    for apart in range(PIECES):
        first = pl.multiple_of((seat ^ apart) * width, width)
        target = (odd if apart % 2 else even).at[apart // 2]
        copies.append(
            pltpu.make_async_copy(rows.at[:, pl.ds(first, width)], target, sems.at[apart])
        )
    for copy in copies:
        copy.start()
    for copy in copies:
        copy.wait()


def deal(rows, *after):
    slab = jax.ShapeDtypeStruct((PIECES // 2, rows.shape[0], rows.shape[1] // PIECES), rows.dtype)

    def kernel(rows, *refs):
        deal_kernel(rows, *refs[-3:])

    return pl.pallas_call(
        kernel,
        out_shape=(slab, slab),
        in_specs=[pl.BlockSpec(memory_space=pl.ANY)] * (1 + len(after)),
        out_specs=(pl.BlockSpec(memory_space=pltpu.VMEM),) * 2,
        scratch_shapes=[pltpu.SemaphoreType.DMA((PIECES,))],
        compiler_params=pltpu.CompilerParams(vmem_limit_bytes=16 << 20),
        cost_estimate=pl.CostEstimate(flops=0, bytes_accessed=2 << 20, transcendentals=0),
    )(rows, *after)


def nearest(here, owner, block):
    half = lax.axis_index("ctx") // PIECES
    return owner[here[block]] // PIECES == half


def choose(close, arrived, put):
    plane = lax.axis_index("groups")

    @pl.when(close)
    def _():
        put(arrived[0], plane)
        put(arrived[2], 1 - plane)

    @pl.when(jnp.logical_not(close))
    def _():
        put(arrived[1], plane)
        put(arrived[3], 1 - plane)


def join_kernel(here, owner, *refs):
    arrived, (weight, ups), (flat, left, right) = refs[:4], refs[4:6], refs[6:]
    half = lax.axis_index("ctx") // PIECES
    split = DOWN_ROWS + QUERY_ROWS + KEYVAL_ROWS

    def put_own(source, position):
        first = pl.multiple_of(position * DOWN_ROWS, DOWN_ROWS)
        flat[pl.ds(first, DOWN_ROWS), :] = source[:DOWN_ROWS, :].astype(jnp.float32)
        ups[position, : UP_ROWS - KEYVAL_ROWS, :] = source[DOWN_ROWS:split, :]

    def put_mirrored(source, position):
        ups[position, UP_ROWS - KEYVAL_ROWS :, :] = source[split:, :]

    choose(nearest(here, owner, half), arrived, put_own)
    choose(nearest(here, owner, 1 - half), arrived, put_mirrored)

    third = flat.shape[0] // 3
    one = flat[pl.ds(0, third, stride=3), :]
    two = pltpu.roll(flat[pl.ds(1, third, stride=3), :], 64, 1)
    three = pltpu.roll(flat[pl.ds(2, third, stride=3), :], 64, 1)
    lane = lax.broadcasted_iota(jnp.int32, one.shape, 1)
    left[pl.ds(0, third, stride=2), :] = one
    left[pl.ds(1, third, stride=2), :] = jnp.where(lane < 64, two, three)
    right[pl.ds(0, third, stride=2), :] = pltpu.roll(two, 64, 1)
    right[pl.ds(1, third, stride=2), :] = three
    weight[...] = jnp.concatenate([left[...], right[...]], 1).astype(jnp.bfloat16)


def join(here, owner, arrived):
    depth = D // PIECES
    return pl.pallas_call(
        join_kernel,
        out_shape=(
            jax.ShapeDtypeStruct((depth, 256), jnp.bfloat16),
            jax.ShapeDtypeStruct((2, UP_ROWS, 128), jnp.bfloat16),
        ),
        in_specs=[pl.BlockSpec(memory_space=pltpu.SMEM)] * 2
        + [pl.BlockSpec(memory_space=pltpu.VMEM)] * 4,
        out_specs=(pl.BlockSpec(memory_space=pltpu.VMEM),) * 2,
        scratch_shapes=[
            pltpu.VMEM((2 * DOWN_ROWS, 128), jnp.float32),
            pltpu.VMEM((depth, 128), jnp.float32),
            pltpu.VMEM((depth, 128), jnp.float32),
        ],
        compiler_params=pltpu.CompilerParams(vmem_limit_bytes=16 << 20),
        cost_estimate=pl.CostEstimate(flops=0, bytes_accessed=96 << 20, transcendentals=0),
    )(here, owner, *arrived)


def settle_kernel(here, there, owner, near, far, own, across):
    half = lax.axis_index("ctx") // PIECES
    for number, (wishes, out) in enumerate(((here, own), (there, across))):
        close = nearest(wishes, owner, half)

        @pl.when(close)
        def _():
            out[...] = near[number]

        @pl.when(jnp.logical_not(close))
        def _():
            out[...] = far[number]


def settle(here, there, owner, near, far):
    slab = jax.ShapeDtypeStruct(near.shape[1:], jnp.bfloat16)
    return pl.pallas_call(
        settle_kernel,
        out_shape=(slab, slab),
        in_specs=[pl.BlockSpec(memory_space=pltpu.SMEM)] * 3
        + [pl.BlockSpec(memory_space=pltpu.VMEM)] * 2,
        out_specs=(pl.BlockSpec(memory_space=pltpu.VMEM),) * 2,
        compiler_params=pltpu.CompilerParams(vmem_limit_bytes=16 << 20),
        cost_estimate=pl.CostEstimate(flops=0, bytes_accessed=1 << 20, transcendentals=0),
    )(here, there, owner, near, far)


def narrow_kernel(weight, *refs):
    for block, out in zip(refs[:4], refs[4:]):
        sides, rows, depth = block.shape
        product = jnp.dot(
            block[...].reshape(sides * rows, depth),
            weight[...],
            preferred_element_type=jnp.float32,
        )
        out[...] = product[:, : 3 * ADAPTER_RANK].reshape(out.shape).astype(jnp.bfloat16)


def narrow(weight, dealt):
    sides, rows, depth = dealt[0].shape
    partial_sums = jax.ShapeDtypeStruct((sides, rows, 3 * ADAPTER_RANK), jnp.bfloat16)
    return pl.pallas_call(
        narrow_kernel,
        out_shape=(partial_sums,) * 4,
        in_specs=[pl.BlockSpec(memory_space=pltpu.VMEM)] * 5,
        out_specs=(pl.BlockSpec(memory_space=pltpu.VMEM),) * 4,
        compiler_params=pltpu.CompilerParams(vmem_limit_bytes=16 << 20),
        cost_estimate=pl.CostEstimate(
            flops=2 * 8 * rows * depth * 256, bytes_accessed=2 << 20, transcendentals=0
        ),
    )(weight, *dealt)


def attend_kernel(
    first_head,
    query_block,
    key_same,
    key_other,
    value_same,
    value_other,
    own_rank,
    rows_same,
    rows_other,
    cosines,
    sines,
    *refs,
):
    attended, flat_query, flat_keyval, keys, values = refs[-5:]
    step = pl.program_id(0) + first_head
    rows = query_block.shape[0]
    base = lax.axis_index("ctx") * rows
    half = lax.axis_index("ctx") // PIECES
    seat = lax.rem(lax.axis_index("ctx"), PIECES)
    dot = partial(jnp.dot, preferred_element_type=jnp.float32)

    @pl.when(pl.program_id(0) == 0)
    def _():
        for apart in range(PIECES):
            source = rows_other if apart % 2 else rows_same
            for position in range(2):
                begin = PIECES * rows + (apart // 2 * 2 + position) * UP_ROWS
                piece = source[begin : begin + UP_ROWS, :].astype(jnp.float32)
                place = (seat ^ apart) * 2 + position
                first = pl.multiple_of(place * QUERY_ROWS, QUERY_ROWS)
                flat_query[pl.ds(first, QUERY_ROWS), :] = piece[:QUERY_ROWS]
                first = pl.multiple_of(place * KEYVAL_ROWS, KEYVAL_ROWS)
                for side in range(2):
                    begin = QUERY_ROWS + side * KEYVAL_ROWS
                    flat_keyval[side, pl.ds(first, KEYVAL_ROWS), :] = piece[
                        begin : begin + KEYVAL_ROWS
                    ]

    def turned(delta, cosine, sine):
        return delta * cosine + pltpu.roll(delta, HEAD_SIZE // 2, 1) * sine

    def up(flat, first, stride):
        return flat[pl.ds(first, ADAPTER_RANK, stride=stride), :].astype(jnp.bfloat16)

    for side in range(2):
        heads = 2 * KEYVALUE_HEADS
        key_up = up(flat_keyval.at[side], step, heads)
        value_up = up(flat_keyval.at[side], step + KEYVALUE_HEADS, heads)
        for core in range(2):
            source = rows_other if core else rows_same
            rank = [
                source[(2 * chip + side) * rows : (2 * chip + side + 1) * rows, :]
                for chip in range(PIECES // 2)
            ]
            rank = jnp.concatenate(rank, 0)
            key_delta = adapter_scale * dot(rank[:, :ADAPTER_RANK], key_up)
            value_delta = adapter_scale * dot(rank[:, ADAPTER_RANK:], value_up)
            for chip in range(PIECES // 2):
                there = seat ^ (2 * chip + core)
                first = ((half ^ side) * PIECES + there) * rows
                span = pl.ds(pl.multiple_of(first, rows), rows)
                part = slice(chip * rows, (chip + 1) * rows)
                delta = turned(key_delta[part], cosines[span, :], sines[span, :])
                full = (key_other if core else key_same)[chip, side].astype(jnp.float32) + delta
                keys[span, :] = full.astype(jnp.bfloat16)
                full = (value_other if core else value_same)[chip, side].astype(jnp.float32)
                values[span, :] = (full + value_delta[part]).astype(jnp.bfloat16)
    here = pl.ds(pl.multiple_of(base, rows), rows)
    cosine = cosines[here, :]
    sine = sines[here, :]
    taken = GROUP
    limit = lax.broadcasted_iota(jnp.int32, (rows, 1), 0) + base
    limit = jnp.concatenate([limit] * taken, 0)
    for first in range(0, GROUP, taken):
        weight = [up(flat_query, step * GROUP + first + head, QH) for head in range(taken)]
        deltas = adapter_scale * dot(own_rank[:, :ADAPTER_RANK], jnp.concatenate(weight, 1))
        queries = []
        for place in range(taken):
            moved = turned(deltas[:, place * HEAD_SIZE : (place + 1) * HEAD_SIZE], cosine, sine)
            span = slice((first + place) * HEAD_SIZE, (first + place + 1) * HEAD_SIZE)
            queries.append(
                (query_block[:, span].astype(jnp.float32) + moved).astype(jnp.bfloat16)
            )
        queries = jnp.concatenate(queries, 0)
        scores = lax.dot_general(
            queries, keys[...], (((1,), (1,)), ((), ())), preferred_element_type=jnp.float32
        )
        column = lax.broadcasted_iota(jnp.int32, scores.shape, 1)
        scores = jnp.where(column <= limit, scores, mask_floor)
        scores = scores - jnp.max(scores, axis=-1, keepdims=True)
        weights = jnp.exp(scores * HEAD_SIZE ** (-0.5))
        divisor = jnp.sum(weights, axis=-1, keepdims=True)
        result = (dot(weights.astype(jnp.bfloat16), values[...]) / divisor).astype(jnp.bfloat16)
        for place in range(taken):
            span = slice((first + place) * HEAD_SIZE, (first + place + 1) * HEAD_SIZE)
            attended[:, span] = result[place * rows : (place + 1) * rows]


def attend(first_head, heads, before, query_base, base, own_rank, gathered, cosines, sines):
    rows = query_base.shape[0]
    seq = 4 * PIECES // 2 * rows
    width = GROUP * HEAD_SIZE

    def whole(shape):
        return pl.BlockSpec(shape, lambda h: (0,) * len(shape))

    key_spec = pl.BlockSpec((PIECES // 2, 2, rows, HEAD_SIZE), lambda h: (0, 0, 0, h + first_head))
    value_spec = pl.BlockSpec(
        (PIECES // 2, 2, rows, HEAD_SIZE), lambda h: (0, 0, 0, h + first_head + KEYVALUE_HEADS)
    )
    operands = (query_base, base[0], base[1], base[0], base[1], own_rank, *gathered)
    operands += (cosines, sines) + (() if before is None else (before,))
    query_spec = pl.BlockSpec((rows, width), lambda h: (0, h + first_head))
    return pl.pallas_call(
        partial(attend_kernel, first_head),
        grid=(heads,),
        out_shape=jax.ShapeDtypeStruct((rows, QH * HEAD_SIZE), jnp.bfloat16),
        in_specs=[
            query_spec,
            key_spec,
            key_spec,
            value_spec,
            value_spec,
            whole(own_rank.shape),
            whole(gathered[0].shape),
            whole(gathered[1].shape),
            whole(cosines.shape),
            whole(sines.shape),
        ]
        + [pl.BlockSpec(memory_space=pl.ANY)] * (len(operands) - 10),
        out_specs=query_spec,
        input_output_aliases={} if before is None else {len(operands) - 1: 0},
        scratch_shapes=[
            pltpu.VMEM((2 * PIECES * QUERY_ROWS, 128), jnp.float32),
            pltpu.VMEM((2, 2 * PIECES * KEYVAL_ROWS, 128), jnp.float32),
            pltpu.VMEM((seq, HEAD_SIZE), jnp.bfloat16),
            pltpu.VMEM((seq, HEAD_SIZE), jnp.bfloat16),
        ],
        compiler_params=pltpu.CompilerParams(vmem_limit_bytes=32 << 20),
        cost_estimate=pl.CostEstimate(
            flops=12 * heads * rows * QH * seq * HEAD_SIZE,
            bytes_accessed=10 << 20,
            transcendentals=heads * rows * GROUP * seq,
        ),
    )(*operands)


def widen_kernel(attended, same, other, out_delta, down_out, up_out):
    plane = lax.axis_index("groups")
    seat = lax.rem(lax.axis_index("ctx"), PIECES)
    for apart in range(PIECES):
        pieces = other if apart % 2 else same
        for position in range(2):
            piece = pieces[apart // 2, position].astype(jnp.float32)
            place = (seat ^ apart) * 2 + (position ^ plane)
            first = place * 2 * DOWN_OUT_ROWS
            block = piece[:DOWN_OUT_ROWS]
            down_out[pl.ds(first, DOWN_OUT_ROWS, stride=2), :] = block
            down_out[pl.ds(first + 1, DOWN_OUT_ROWS, stride=2), :] = pltpu.roll(block, 64, 1)
            first = pl.multiple_of(place * UP_OUT_ROWS, UP_OUT_ROWS)
            up_out[pl.ds(first, UP_OUT_ROWS), :] = piece[DOWN_OUT_ROWS:]
    dot = partial(jnp.dot, preferred_element_type=jnp.float32)
    rank = dot(attended[...], down_out[...].astype(jnp.bfloat16))[:, :ADAPTER_RANK]
    rank = rank.astype(jnp.bfloat16)
    blocks = D // 128
    for first in range(0, blocks, 4):
        weight = [
            up_out[pl.ds(first + block, ADAPTER_RANK, stride=blocks), :].astype(jnp.bfloat16)
            for block in range(4)
        ]
        delta = adapter_scale * dot(rank, jnp.concatenate(weight, 1))
        out_delta[:, first * 128 : (first + 4) * 128] = delta.astype(jnp.bfloat16)


def widen(attended, same, other):
    return pl.pallas_call(
        widen_kernel,
        out_shape=jax.ShapeDtypeStruct((attended.shape[0], D), jnp.bfloat16),
        in_specs=[pl.BlockSpec(memory_space=pltpu.VMEM)] * 3,
        out_specs=pl.BlockSpec(memory_space=pltpu.VMEM),
        scratch_shapes=[
            pltpu.VMEM((QH * HEAD_SIZE, 128), jnp.float32),
            pltpu.VMEM((ADAPTER_RANK * D // 128, 128), jnp.float32),
        ],
        compiler_params=pltpu.CompilerParams(vmem_limit_bytes=32 << 20),
        cost_estimate=pl.CostEstimate(flops=1 << 27, bytes_accessed=4 << 20, transcendentals=0),
    )(attended, same, other)


def swap(block, mask):
    return lax.ppermute(block, ("groups", "ctx"), [(i, i ^ mask) for i in range(4 * PIECES)])


def direct_shards(
    normed_input, query_base, key_base, value_base, adapter_pool, stretch_adapter, adapter_owner
):
    tok_rows = normed_input.shape[0]
    ctx = lax.axis_size("ctx")
    seq = ctx * tok_rows
    blocks = [list(range(PIECES)), list(range(PIECES, 2 * PIECES))]
    half_dim = HEAD_SIZE // 2
    frequency = rope_base ** (-(jnp.arange(half_dim, dtype=jnp.float32) * 2.0) / HEAD_SIZE)
    angle = jnp.arange(seq, dtype=jnp.int32).astype(jnp.float32)[:, None] * frequency[None, :]
    cosine = jnp.cos(angle)
    sine = jnp.sin(angle)
    cosines = jnp.concatenate([cosine, cosine], 1)
    sines = jnp.concatenate([-sine, sine], 1)

    def after(block, *others):
        return lax.optimization_barrier((block, others))[0]

    def exchange(sent):
        across = swap(sent[2], 2 * PIECES)
        return [sent[0], swap(sent[1], PIECES), across, swap(sent[3], 3 * PIECES)]

    def along_z(block):
        return jnp.stack([block, swap(block, 4)])

    def along_x(pair):
        quad = jnp.stack([pair, swap(pair, 2)], 1)
        return quad.reshape((PIECES // 2,) + pair.shape[1:])

    elsewhere = swap(stretch_adapter, 2 * PIECES)
    packed = pack_row(adapter_pool, SECTIONS)
    even, odd = deal(normed_input, packed)
    sibling = swap(odd, 1)
    base = jnp.concatenate([key_base, value_base], 1)
    base = jnp.stack([base, swap(base, PIECES)])

    spread = lax.all_to_all(packed, "ctx", 0, 0, axis_index_groups=blocks)
    spread = after(spread, sibling, base, cosines, sines)
    sent, near, far = pick(spread, stretch_adapter, elsewhere, adapter_owner)
    arrived = exchange(sent)
    dealt = [after(jnp.stack([even[j], sibling[j]]), sent) for j in range(PIECES // 2)]
    dealt = [swap(block, 2 * j) if j else block for j, block in enumerate(dealt)]

    weight, ups = join(stretch_adapter, adapter_owner, arrived)
    far = swap(after(far, weight), PIECES)
    partial_sums = narrow(weight, dealt)
    back = [swap(block, 2 * j) if j else block for j, block in enumerate(partial_sums)]
    back = sum(block.astype(jnp.float32) for block in back)
    own_rank = swap(after(back[1].astype(jnp.bfloat16), far), 1)
    own_rank = back[0] + own_rank.astype(jnp.float32)
    own_rank = own_rank.astype(jnp.bfloat16)
    ups = along_z(after(ups, *partial_sums))
    base = along_z(after(base, *partial_sums))
    all_rank = own_rank[:, ADAPTER_RANK:]
    base = along_x(after(base, own_rank))
    own, across = settle(
        stretch_adapter, elsewhere, adapter_owner, near, after(far, own_rank)
    )
    ends = jnp.stack([own, swap(across, 2 * PIECES)])
    all_rank = jnp.stack([all_rank, swap(all_rank, PIECES)])
    all_rank = after(all_rank, ups)
    ups = along_x(after(ups, all_rank))
    all_rank = jnp.stack([swap(all_rank, apart) if apart else all_rank for apart in (0, 2, 4, 6)])
    base = after(base, all_rank)
    base = (base, swap(base, 1))
    gathered = jnp.concatenate([all_rank.reshape(-1, 128), ups.reshape(-1, 128)])
    gathered = after(gathered, ends)
    gathered = (gathered, swap(gathered, 1))

    shared = (query_base, base, own_rank, gathered, cosines, sines)
    attended = attend(0, 1, None, *shared)
    ends = after(ends, attended)
    ends = jnp.stack([swap(ends, apart) if apart else ends for apart in (0, 2, 4, 6)])
    attended = attend(1, KEYVALUE_HEADS - 1, attended, *shared)
    ends = after(ends, attended)
    return attended, widen(attended, ends, swap(ends, 1))


def shards(normed_input, query_base, key_base, value_base, adapter_pool, stretch_adapter, owner):
    fits = (
        lax.axis_size("groups") == 2
        and lax.axis_size("ctx") == 2 * PIECES
        and normed_input.shape[0] * PIECES == BLOCK_TOKENS
        and adapter_pool.shape[0] == 1
    )
    plan = direct_shards if fits else spread_shards
    return plan(
        normed_input, query_base, key_base, value_base, adapter_pool, stretch_adapter, owner
    )


def solution(mesh):
    placed = (
        P(("groups", "ctx"), None),
        P(("groups", "ctx"), None),
        P(("groups", "ctx"), None),
        P(("groups", "ctx"), None),
        P("ctx", None),
        P("groups"),
        P(),
    )
    return jax.shard_map(
        shards,
        mesh=mesh,
        in_specs=placed,
        out_specs=(P(("groups", "ctx"), None), P(("groups", "ctx"), None)),
        check_vma=False,
    )
```

```python
from functools import partial
import math

import jax
import jax.numpy as jnp
from jax import lax
from jax.experimental import pallas as pl
from jax.experimental.pallas import tpu as pltpu
from jax.sharding import PartitionSpec as P

D = 8192
QH = 32
KEYVALUE_HEADS = 4
HEAD_SIZE = 128
ADAPTER_RANK = 64
BLOCK_TOKENS = 512
QKV_POOL = 1900544


adapter_scale = 2.0
rope_base = 500000.0
mask_floor = -1e30


def from_partner(block, axis, apart):
    count = lax.axis_size(axis)
    route = []
    for low in range(count):
        high = low | 1 << apart
        if high != low and high < count:
            route += [(low, high), (high, low)]
    return lax.ppermute(block, axis, route)


def rotate(delta, token_positions, heads):
    half_dim = HEAD_SIZE // 2
    frequency = rope_base ** (-(jnp.arange(half_dim, dtype=jnp.float32) * 2.0) / HEAD_SIZE)
    angle = token_positions.astype(jnp.float32)[:, None] * frequency[None, :]
    cosine = jnp.cos(angle)[:, None, :]
    sine_part = jnp.sin(angle)[:, None, :]
    shaped = delta.reshape(delta.shape[0], heads, HEAD_SIZE)
    first_half = shaped[..., :half_dim]
    second_half = shaped[..., half_dim:]
    joined = jnp.concatenate(
        [
            first_half * cosine - second_half * sine_part,
            second_half * cosine + first_half * sine_part,
        ],
        -1,
    )
    return joined.reshape(delta.shape[0], heads * HEAD_SIZE)


def project_heads(
    narrow_product, query_row_block, key_row_block, value_row_block, upper_part, token_positions
):
    query_up_weight = upper_part[: ADAPTER_RANK * QH * HEAD_SIZE].reshape(
        ADAPTER_RANK, QH * HEAD_SIZE
    )
    keyvalue_up_weight = upper_part[ADAPTER_RANK * QH * HEAD_SIZE :].reshape(
        ADAPTER_RANK, 2 * KEYVALUE_HEADS * HEAD_SIZE
    )
    query_correction = adapter_scale * jnp.dot(
        narrow_product[:, :ADAPTER_RANK], query_up_weight, preferred_element_type=jnp.float32
    )
    key_correction = adapter_scale * jnp.dot(
        narrow_product[:, ADAPTER_RANK : 2 * ADAPTER_RANK],
        keyvalue_up_weight[:, : KEYVALUE_HEADS * HEAD_SIZE],
        preferred_element_type=jnp.float32,
    )
    value_correction = adapter_scale * jnp.dot(
        narrow_product[:, 2 * ADAPTER_RANK :],
        keyvalue_up_weight[:, KEYVALUE_HEADS * HEAD_SIZE :],
        preferred_element_type=jnp.float32,
    )
    queries = (
        query_row_block.astype(jnp.float32) + rotate(query_correction, token_positions, QH)
    ).astype(jnp.bfloat16)
    new_keys = (
        key_row_block.astype(jnp.float32) + rotate(key_correction, token_positions, KEYVALUE_HEADS)
    ).astype(jnp.bfloat16)
    new_values = (value_row_block.astype(jnp.float32) + value_correction).astype(jnp.bfloat16)
    return (queries, new_keys, new_values)


def output_delta(attended_rows, out_part):
    down_out = out_part[: QH * HEAD_SIZE * ADAPTER_RANK].reshape(QH * HEAD_SIZE, ADAPTER_RANK)
    raised_output = out_part[QH * HEAD_SIZE * ADAPTER_RANK :].reshape(ADAPTER_RANK, D)
    narrow_product = jnp.dot(attended_rows, down_out, preferred_element_type=jnp.float32).astype(
        jnp.bfloat16
    )
    return (
        adapter_scale * jnp.dot(narrow_product, raised_output, preferred_element_type=jnp.float32)
    ).astype(jnp.bfloat16)


def head_major(query_row_block):
    count_rows = query_row_block.shape[0]
    group_size = QH // KEYVALUE_HEADS
    return (
        query_row_block.reshape(count_rows, KEYVALUE_HEADS, group_size, HEAD_SIZE)
        .transpose(1, 2, 0, 3)
        .reshape(KEYVALUE_HEADS, group_size * count_rows, HEAD_SIZE)
    )


def row_major(head_rows, count_rows):
    group_size = QH // KEYVALUE_HEADS
    return (
        head_rows.reshape(KEYVALUE_HEADS, group_size, count_rows, HEAD_SIZE)
        .transpose(2, 0, 1, 3)
        .reshape(count_rows, QH * HEAD_SIZE)
    )


def online_update(current, queries, query_pos, key_slice, value_slice, key_start):
    run_max, run_sum, run_acc = current
    scores = jnp.einsum(
        "hqd,khd->hqk", queries, key_slice, preferred_element_type=jnp.float32
    ) * HEAD_SIZE ** (-0.5)
    key_pos = key_start + jnp.arange(key_slice.shape[0], dtype=jnp.int32)
    allowed = (query_pos[:, None] >= key_pos[None, :])[None]
    new_max = jnp.maximum(run_max, jnp.max(jnp.where(allowed, scores, mask_floor), axis=-1))
    weights = jnp.where(allowed, jnp.exp(scores - new_max[..., None]), 0.0)
    rescale = jnp.exp(run_max - new_max)
    new_sum = run_sum * rescale + jnp.sum(weights, axis=-1)
    new_acc = run_acc * rescale[..., None] + jnp.einsum(
        "hqk,khd->hqd",
        weights.astype(jnp.bfloat16),
        value_slice,
        preferred_element_type=jnp.float32,
    )
    return (new_max, new_sum, new_acc)


def unchanged(current):
    return current


def fold_keys(carry_state, shard_part, prepared):
    key_row_block, value_row_block = shard_part
    key_count = key_row_block.shape[0]
    sub_width = math.gcd(key_count, 1024)
    key_heads = key_row_block.reshape(key_count // sub_width, sub_width, KEYVALUE_HEADS, HEAD_SIZE)
    value_heads = value_row_block.reshape(
        key_count // sub_width, sub_width, KEYVALUE_HEADS, HEAD_SIZE
    )

    def one_step(sub_index, carried):
        key_start = sub_index * sub_width
        key_slice = lax.dynamic_index_in_dim(key_heads, sub_index, 0, keepdims=False)
        value_slice = lax.dynamic_index_in_dim(value_heads, sub_index, 0, keepdims=False)
        updated = []
        for (queries, query_pos), running in zip(prepared, carried):
            advance = partial(
                online_update,
                queries=queries,
                query_pos=query_pos,
                key_slice=key_slice,
                value_slice=value_slice,
                key_start=key_start,
            )
            updated.append(lax.cond(key_start <= jnp.max(query_pos), advance, unchanged, running))
        return tuple(updated)

    return lax.fori_loop(0, key_count // sub_width, one_step, carry_state)


def finish_block(result, count_rows):
    run_max, run_sum, run_acc = result
    divisor = jnp.where(run_sum > 0.0, run_sum, 1.0)
    return row_major(run_acc / divisor[..., None], count_rows).astype(jnp.bfloat16)


def spread_shards(
    normed_input, query_base, key_base, value_base, adapter_pool, stretch_adapter, adapter_owner
):
    cycle_size = lax.axis_size("ctx")
    my_index = lax.axis_index("ctx")
    tok_rows = normed_input.shape[0]
    token_positions = my_index * tok_rows + jnp.arange(tok_rows, dtype=jnp.int32)
    device_ids = jnp.arange(cycle_size, dtype=jnp.int32)
    stretch_of = device_ids * tok_rows // BLOCK_TOKENS
    stretch_ids = jnp.arange(stretch_adapter.shape[0], dtype=jnp.int32)
    adapter_of = jnp.sum(
        jnp.where(stretch_of[:, None] == stretch_ids[None, :], stretch_adapter[None, :], 0), axis=1
    )
    adapter_ids = jnp.arange(adapter_owner.shape[0], dtype=jnp.int32)
    slot_of = jnp.sum(
        jnp.where(adapter_of[:, None] == adapter_ids[None, :], adapter_owner[None, :], 0), axis=1
    )
    down_size = 3 * ADAPTER_RANK * D
    group_count = BLOCK_TOKENS // tok_rows
    levels = group_count.bit_length() - 1
    local_index = my_index % group_count
    col_width = D // group_count
    piece_len = down_size // (group_count * cycle_size)
    pool_rows = adapter_pool.shape[0]
    down_shaped = adapter_pool[:, :down_size].reshape(pool_rows, group_count, cycle_size, piece_len)
    spread_down = lax.all_to_all(down_shaped, "ctx", split_axis=2, concat_axis=0, tiled=True)
    flat_down = spread_down.reshape(-1, piece_len)
    wanted = jnp.take(flat_down, slot_of * group_count + device_ids % group_count, axis=0)[
        :, None, :
    ]
    down_slice = lax.all_to_all(wanted, "ctx", split_axis=0, concat_axis=1, tiled=True).reshape(
        col_width, 3 * ADAPTER_RANK
    )
    spread_rest = lax.all_to_all(
        adapter_pool[:, down_size:], "ctx", split_axis=1, concat_axis=0, tiled=True
    )
    rest_row = lax.all_to_all(
        jnp.take(spread_rest, slot_of, axis=0), "ctx", split_axis=0, concat_axis=1, tiled=True
    )[0]
    upper_part = rest_row[: QKV_POOL - down_size]
    out_part = rest_row[QKV_POOL - down_size :]
    pieces = normed_input.reshape(tok_rows, group_count, col_width)
    slice_order = jnp.bitwise_xor(local_index, jnp.arange(group_count, dtype=jnp.int32))
    moving = jnp.take(pieces, slice_order, axis=1).transpose(1, 0, 2)
    for level in range(levels):
        shaped = moving.reshape(group_count >> level + 1, 2, 1 << level, tok_rows, col_width)
        arrived = from_partner(shaped[:, 1], "ctx", level)
        moving = jnp.stack([shaped[:, 0], arrived], 1).reshape(group_count, tok_rows, col_width)
    partial_rows = jnp.dot(
        moving.reshape(group_count * tok_rows, col_width),
        down_slice,
        preferred_element_type=jnp.float32,
    ).reshape(group_count, tok_rows, 3 * ADAPTER_RANK)
    for level in reversed(range(levels)):
        halves = partial_rows.reshape(2, partial_rows.shape[0] // 2, tok_rows, 3 * ADAPTER_RANK)
        partial_rows = halves[0] + from_partner(
            halves[1].astype(jnp.bfloat16), "ctx", level
        ).astype(jnp.float32)
    narrow_product = partial_rows[0].astype(jnp.bfloat16)
    queries, new_keys, new_values = project_heads(
        narrow_product, query_base, key_base, value_base, upper_part, token_positions
    )
    group_size = QH // KEYVALUE_HEADS
    blocks = [(queries, token_positions)]
    prepared = [
        (head_major(block_q), jnp.tile(block_pos, group_size)) for block_q, block_pos in blocks
    ]
    initial = tuple(
        (
            (
                jnp.full((KEYVALUE_HEADS, head_q.shape[1]), mask_floor, jnp.float32),
                jnp.zeros((KEYVALUE_HEADS, head_q.shape[1]), jnp.float32),
                jnp.zeros((KEYVALUE_HEADS, head_q.shape[1], HEAD_SIZE), jnp.float32),
            )
            for head_q, block_pos in prepared
        )
    )
    finals = fold_keys(
        initial,
        (
            lax.all_gather(new_keys, "ctx", axis=0, tiled=True),
            lax.all_gather(new_values, "ctx", axis=0, tiled=True),
        ),
        prepared,
    )
    attended = finish_block(finals[0], tok_rows)
    out_delta = output_delta(attended, out_part)
    return (attended, out_delta)


PIECES = 8
GROUP = QH // KEYVALUE_HEADS
SECTIONS = ((0, 12288), (12288, 2048), (14336, 512), (14848, 2048), (16896, 4096))
DOWN_ROWS, QUERY_ROWS, KEYVAL_ROWS, DOWN_OUT_ROWS, UP_OUT_ROWS = 768, 128, 32, 128, 256
UP_ROWS = QUERY_ROWS + 2 * KEYVAL_ROWS
FIRST_ROWS = DOWN_ROWS + QUERY_ROWS + KEYVAL_ROWS


def pack_kernel(sections, pool, *refs):
    out, buffers, sems = refs[-3:]
    plane = lax.axis_index("groups")
    slabs, slab_rows = out.shape[:2]

    def copies(slab):
        listed = []
        offset = 0
        for first, rows in sections:
            share = rows // (2 * PIECES)
            begin = first + (slab * 2 + plane) * share
            listed.append(
                pltpu.make_async_copy(
                    pool.at[:, pl.ds(pl.multiple_of(begin * 128, 2048), share * 128)],
                    buffers.at[slab, :, pl.ds(offset, share * 128)],
                    sems.at[slab, len(listed)],
                )
            )
            offset += share * 128
        return listed

    for slab in range(slabs):
        for copy in copies(slab):
            copy.start()

    def step(slab, carried):
        for copy in copies(slab):
            copy.wait()

        def chunk(index, inner):
            line = buffers[slab, :, pl.ds(pl.multiple_of(index * 2048, 2048), 2048)]
            block = line.astype(jnp.float32).reshape(16, 128).astype(jnp.bfloat16)
            out[slab, pl.ds(pl.multiple_of(index * 16, 16), 16), :] = block
            return inner

        lax.fori_loop(0, slab_rows // 16, chunk, 0, unroll=8)
        return carried

    lax.fori_loop(0, slabs, step, 0)


def pack_row(pool, sections, *after):
    slab_rows = sum(rows for _, rows in sections) // (2 * PIECES)
    return pl.pallas_call(
        partial(pack_kernel, sections),
        out_shape=jax.ShapeDtypeStruct((PIECES, slab_rows, 128), jnp.bfloat16),
        in_specs=[pl.BlockSpec(memory_space=pl.ANY)] * (1 + len(after)),
        out_specs=pl.BlockSpec(memory_space=pltpu.VMEM),
        scratch_shapes=[
            pltpu.VMEM((PIECES, 1, slab_rows * 128), jnp.bfloat16),
            pltpu.SemaphoreType.DMA((PIECES, len(sections))),
        ],
        compiler_params=pltpu.CompilerParams(vmem_limit_bytes=60 << 20),
        cost_estimate=pl.CostEstimate(flops=0, bytes_accessed=8 << 20, transcendentals=0),
    )(pool, *after)


def pick_kernel(here, there, owner, spread, *refs):
    outs, lasts, sems = refs[:4], refs[4:6], refs[6]
    half = lax.axis_index("ctx") // PIECES
    last = spread.shape[1] - FIRST_ROWS
    copies = []
    for flip, out in enumerate(outs):
        wishes = there if flip >= 2 else here
        block = half ^ (flip & 1)
        row = lax.rem(owner[wishes[block]], PIECES)
        mirrored = lax.rem(owner[wishes[1 - block]], PIECES)
        pairs = (
            (spread.at[row, pl.ds(0, FIRST_ROWS)], out.at[pl.ds(0, FIRST_ROWS)]),
            (
                spread.at[mirrored, pl.ds(FIRST_ROWS - KEYVAL_ROWS, KEYVAL_ROWS)],
                out.at[pl.ds(FIRST_ROWS, KEYVAL_ROWS)],
            ),
            (spread.at[row, pl.ds(FIRST_ROWS, last)], lasts[flip % 2].at[flip // 2]),
        )
        for number, (source, target) in enumerate(pairs):
            copies.append(pltpu.make_async_copy(source, target, sems.at[flip, number]))
    for copy in copies:
        copy.start()
    for copy in copies:
        copy.wait()


def pick(spread, here, there, owner):
    last = spread.shape[1] - FIRST_ROWS
    first_shape = jax.ShapeDtypeStruct((FIRST_ROWS + KEYVAL_ROWS, 128), jnp.bfloat16)
    last_shape = jax.ShapeDtypeStruct((2, last, 128), jnp.bfloat16)
    outs = pl.pallas_call(
        pick_kernel,
        out_shape=(first_shape,) * 4 + (last_shape,) * 2,
        in_specs=[pl.BlockSpec(memory_space=pltpu.SMEM)] * 3 + [pl.BlockSpec(memory_space=pl.ANY)],
        out_specs=(pl.BlockSpec(memory_space=pltpu.VMEM),) * 6,
        scratch_shapes=[pltpu.SemaphoreType.DMA((4, 3))],
        compiler_params=pltpu.CompilerParams(vmem_limit_bytes=16 << 20),
        cost_estimate=pl.CostEstimate(flops=0, bytes_accessed=3 << 20, transcendentals=0),
    )(here, there, owner, spread)
    return outs[:4], outs[4], outs[5]


def deal_kernel(rows, even, odd, sems):
    seat = lax.rem(lax.axis_index("ctx"), PIECES)
    width = rows.shape[1] // PIECES
    copies = []
    for apart in range(PIECES):
        first = pl.multiple_of((seat ^ apart) * width, width)
        target = (odd if apart % 2 else even).at[apart // 2]
        copies.append(
            pltpu.make_async_copy(rows.at[:, pl.ds(first, width)], target, sems.at[apart])
        )
    for copy in copies:
        copy.start()
    for copy in copies:
        copy.wait()


def deal(rows, *after):
    slab = jax.ShapeDtypeStruct((PIECES // 2, rows.shape[0], rows.shape[1] // PIECES), rows.dtype)

    def kernel(rows, *refs):
        deal_kernel(rows, *refs[-3:])

    return pl.pallas_call(
        kernel,
        out_shape=(slab, slab),
        in_specs=[pl.BlockSpec(memory_space=pl.ANY)] * (1 + len(after)),
        out_specs=(pl.BlockSpec(memory_space=pltpu.VMEM),) * 2,
        scratch_shapes=[pltpu.SemaphoreType.DMA((PIECES,))],
        compiler_params=pltpu.CompilerParams(vmem_limit_bytes=16 << 20),
        cost_estimate=pl.CostEstimate(flops=0, bytes_accessed=2 << 20, transcendentals=0),
    )(rows, *after)


def nearest(here, owner, block):
    half = lax.axis_index("ctx") // PIECES
    return owner[here[block]] // PIECES == half


def choose(close, arrived, put):
    plane = lax.axis_index("groups")

    @pl.when(close)
    def _():
        put(arrived[0], plane)
        put(arrived[2], 1 - plane)

    @pl.when(jnp.logical_not(close))
    def _():
        put(arrived[1], plane)
        put(arrived[3], 1 - plane)


def join_kernel(here, owner, *refs):
    arrived, (weight, ups), (flat, left, right) = refs[:4], refs[4:6], refs[6:]
    half = lax.axis_index("ctx") // PIECES
    split = DOWN_ROWS + QUERY_ROWS + KEYVAL_ROWS

    def put_own(source, position):
        first = pl.multiple_of(position * DOWN_ROWS, DOWN_ROWS)
        flat[pl.ds(first, DOWN_ROWS), :] = source[:DOWN_ROWS, :].astype(jnp.float32)
        ups[position, : UP_ROWS - KEYVAL_ROWS, :] = source[DOWN_ROWS:split, :]

    def put_mirrored(source, position):
        ups[position, UP_ROWS - KEYVAL_ROWS :, :] = source[split:, :]

    choose(nearest(here, owner, half), arrived, put_own)
    choose(nearest(here, owner, 1 - half), arrived, put_mirrored)

    third = flat.shape[0] // 3
    one = flat[pl.ds(0, third, stride=3), :]
    two = pltpu.roll(flat[pl.ds(1, third, stride=3), :], 64, 1)
    three = pltpu.roll(flat[pl.ds(2, third, stride=3), :], 64, 1)
    lane = lax.broadcasted_iota(jnp.int32, one.shape, 1)
    left[pl.ds(0, third, stride=2), :] = one
    left[pl.ds(1, third, stride=2), :] = jnp.where(lane < 64, two, three)
    right[pl.ds(0, third, stride=2), :] = pltpu.roll(two, 64, 1)
    right[pl.ds(1, third, stride=2), :] = three
    weight[...] = jnp.concatenate([left[...], right[...]], 1).astype(jnp.bfloat16)


def join(here, owner, arrived):
    depth = D // PIECES
    return pl.pallas_call(
        join_kernel,
        out_shape=(
            jax.ShapeDtypeStruct((depth, 256), jnp.bfloat16),
            jax.ShapeDtypeStruct((2, UP_ROWS, 128), jnp.bfloat16),
        ),
        in_specs=[pl.BlockSpec(memory_space=pltpu.SMEM)] * 2
        + [pl.BlockSpec(memory_space=pltpu.VMEM)] * 4,
        out_specs=(pl.BlockSpec(memory_space=pltpu.VMEM),) * 2,
        scratch_shapes=[
            pltpu.VMEM((2 * DOWN_ROWS, 128), jnp.float32),
            pltpu.VMEM((depth, 128), jnp.float32),
            pltpu.VMEM((depth, 128), jnp.float32),
        ],
        compiler_params=pltpu.CompilerParams(vmem_limit_bytes=16 << 20),
        cost_estimate=pl.CostEstimate(flops=0, bytes_accessed=96 << 20, transcendentals=0),
    )(here, owner, *arrived)


def settle_kernel(here, there, owner, near, far, own, across):
    half = lax.axis_index("ctx") // PIECES
    for number, (wishes, out) in enumerate(((here, own), (there, across))):
        close = nearest(wishes, owner, half)

        @pl.when(close)
        def _():
            out[...] = near[number]

        @pl.when(jnp.logical_not(close))
        def _():
            out[...] = far[number]


def settle(here, there, owner, near, far):
    slab = jax.ShapeDtypeStruct(near.shape[1:], jnp.bfloat16)
    return pl.pallas_call(
        settle_kernel,
        out_shape=(slab, slab),
        in_specs=[pl.BlockSpec(memory_space=pltpu.SMEM)] * 3
        + [pl.BlockSpec(memory_space=pltpu.VMEM)] * 2,
        out_specs=(pl.BlockSpec(memory_space=pltpu.VMEM),) * 2,
        compiler_params=pltpu.CompilerParams(vmem_limit_bytes=16 << 20),
        cost_estimate=pl.CostEstimate(flops=0, bytes_accessed=1 << 20, transcendentals=0),
    )(here, there, owner, near, far)


def narrow_kernel(weight, *refs):
    for block, out in zip(refs[:4], refs[4:]):
        sides, rows, depth = block.shape
        product = jnp.dot(
            block[...].reshape(sides * rows, depth),
            weight[...],
            preferred_element_type=jnp.float32,
        )
        out[...] = product[:, : 3 * ADAPTER_RANK].reshape(out.shape).astype(jnp.bfloat16)


def narrow(weight, dealt):
    sides, rows, depth = dealt[0].shape
    partial_sums = jax.ShapeDtypeStruct((sides, rows, 3 * ADAPTER_RANK), jnp.bfloat16)
    return pl.pallas_call(
        narrow_kernel,
        out_shape=(partial_sums,) * 4,
        in_specs=[pl.BlockSpec(memory_space=pltpu.VMEM)] * 5,
        out_specs=(pl.BlockSpec(memory_space=pltpu.VMEM),) * 4,
        compiler_params=pltpu.CompilerParams(vmem_limit_bytes=16 << 20),
        cost_estimate=pl.CostEstimate(
            flops=2 * 8 * rows * depth * 256, bytes_accessed=2 << 20, transcendentals=0
        ),
    )(weight, *dealt)


def attend_kernel(
    first_head,
    query_block,
    key_same,
    key_other,
    value_same,
    value_other,
    own_rank,
    rows_same,
    rows_other,
    cosines,
    sines,
    *refs,
):
    attended, flat_query, flat_keyval, keys, values = refs[-5:]
    step = pl.program_id(0) + first_head
    rows = query_block.shape[0]
    base = lax.axis_index("ctx") * rows
    half = lax.axis_index("ctx") // PIECES
    seat = lax.rem(lax.axis_index("ctx"), PIECES)
    dot = partial(jnp.dot, preferred_element_type=jnp.float32)

    @pl.when(pl.program_id(0) == 0)
    def _():
        for apart in range(PIECES):
            source = rows_other if apart % 2 else rows_same
            for position in range(2):
                begin = PIECES * rows + (apart // 2 * 2 + position) * UP_ROWS
                piece = source[begin : begin + UP_ROWS, :].astype(jnp.float32)
                place = (seat ^ apart) * 2 + position
                first = pl.multiple_of(place * QUERY_ROWS, QUERY_ROWS)
                flat_query[pl.ds(first, QUERY_ROWS), :] = piece[:QUERY_ROWS]
                first = pl.multiple_of(place * KEYVAL_ROWS, KEYVAL_ROWS)
                for side in range(2):
                    begin = QUERY_ROWS + side * KEYVAL_ROWS
                    flat_keyval[side, pl.ds(first, KEYVAL_ROWS), :] = piece[
                        begin : begin + KEYVAL_ROWS
                    ]

    def turned(delta, cosine, sine):
        return delta * cosine + pltpu.roll(delta, HEAD_SIZE // 2, 1) * sine

    def up(flat, first, stride):
        return flat[pl.ds(first, ADAPTER_RANK, stride=stride), :].astype(jnp.bfloat16)

    for side in range(2):
        heads = 2 * KEYVALUE_HEADS
        key_up = up(flat_keyval.at[side], step, heads)
        value_up = up(flat_keyval.at[side], step + KEYVALUE_HEADS, heads)
        for core in range(2):
            source = rows_other if core else rows_same
            rank = [
                source[(2 * chip + side) * rows : (2 * chip + side + 1) * rows, :]
                for chip in range(PIECES // 2)
            ]
            rank = jnp.concatenate(rank, 0)
            key_delta = adapter_scale * dot(rank[:, :ADAPTER_RANK], key_up)
            value_delta = adapter_scale * dot(rank[:, ADAPTER_RANK:], value_up)
            for chip in range(PIECES // 2):
                there = seat ^ (2 * chip + core)
                first = ((half ^ side) * PIECES + there) * rows
                span = pl.ds(pl.multiple_of(first, rows), rows)
                part = slice(chip * rows, (chip + 1) * rows)
                delta = turned(key_delta[part], cosines[span, :], sines[span, :])
                full = (key_other if core else key_same)[chip, side].astype(jnp.float32) + delta
                keys[span, :] = full.astype(jnp.bfloat16)
                full = (value_other if core else value_same)[chip, side].astype(jnp.float32)
                values[span, :] = (full + value_delta[part]).astype(jnp.bfloat16)
    here = pl.ds(pl.multiple_of(base, rows), rows)
    cosine = cosines[here, :]
    sine = sines[here, :]
    taken = GROUP
    limit = lax.broadcasted_iota(jnp.int32, (rows, 1), 0) + base
    limit = jnp.concatenate([limit] * taken, 0)
    for first in range(0, GROUP, taken):
        weight = [up(flat_query, step * GROUP + first + head, QH) for head in range(taken)]
        deltas = adapter_scale * dot(own_rank[:, :ADAPTER_RANK], jnp.concatenate(weight, 1))
        queries = []
        for place in range(taken):
            moved = turned(deltas[:, place * HEAD_SIZE : (place + 1) * HEAD_SIZE], cosine, sine)
            span = slice((first + place) * HEAD_SIZE, (first + place + 1) * HEAD_SIZE)
            queries.append(
                (query_block[:, span].astype(jnp.float32) + moved).astype(jnp.bfloat16)
            )
        queries = jnp.concatenate(queries, 0)
        scores = lax.dot_general(
            queries, keys[...], (((1,), (1,)), ((), ())), preferred_element_type=jnp.float32
        )
        column = lax.broadcasted_iota(jnp.int32, scores.shape, 1)
        scores = jnp.where(column <= limit, scores, mask_floor)
        scores = scores - jnp.max(scores, axis=-1, keepdims=True)
        weights = jnp.exp(scores * HEAD_SIZE ** (-0.5))
        divisor = jnp.sum(weights, axis=-1, keepdims=True)
        result = (dot(weights.astype(jnp.bfloat16), values[...]) / divisor).astype(jnp.bfloat16)
        for place in range(taken):
            span = slice((first + place) * HEAD_SIZE, (first + place + 1) * HEAD_SIZE)
            attended[:, span] = result[place * rows : (place + 1) * rows]


def attend(first_head, heads, before, query_base, base, own_rank, gathered, cosines, sines):
    rows = query_base.shape[0]
    seq = 4 * PIECES // 2 * rows
    width = GROUP * HEAD_SIZE

    def whole(shape):
        return pl.BlockSpec(shape, lambda h: (0,) * len(shape))

    key_spec = pl.BlockSpec((PIECES // 2, 2, rows, HEAD_SIZE), lambda h: (0, 0, 0, h + first_head))
    value_spec = pl.BlockSpec(
        (PIECES // 2, 2, rows, HEAD_SIZE), lambda h: (0, 0, 0, h + first_head + KEYVALUE_HEADS)
    )
    operands = (query_base, base[0], base[1], base[0], base[1], own_rank, *gathered)
    operands += (cosines, sines) + (() if before is None else (before,))
    query_spec = pl.BlockSpec((rows, width), lambda h: (0, h + first_head))
    return pl.pallas_call(
        partial(attend_kernel, first_head),
        grid=(heads,),
        out_shape=jax.ShapeDtypeStruct((rows, QH * HEAD_SIZE), jnp.bfloat16),
        in_specs=[
            query_spec,
            key_spec,
            key_spec,
            value_spec,
            value_spec,
            whole(own_rank.shape),
            whole(gathered[0].shape),
            whole(gathered[1].shape),
            whole(cosines.shape),
            whole(sines.shape),
        ]
        + [pl.BlockSpec(memory_space=pl.ANY)] * (len(operands) - 10),
        out_specs=query_spec,
        input_output_aliases={} if before is None else {len(operands) - 1: 0},
        scratch_shapes=[
            pltpu.VMEM((2 * PIECES * QUERY_ROWS, 128), jnp.float32),
            pltpu.VMEM((2, 2 * PIECES * KEYVAL_ROWS, 128), jnp.float32),
            pltpu.VMEM((seq, HEAD_SIZE), jnp.bfloat16),
            pltpu.VMEM((seq, HEAD_SIZE), jnp.bfloat16),
        ],
        compiler_params=pltpu.CompilerParams(vmem_limit_bytes=32 << 20),
        cost_estimate=pl.CostEstimate(
            flops=12 * heads * rows * QH * seq * HEAD_SIZE,
            bytes_accessed=10 << 20,
            transcendentals=heads * rows * GROUP * seq,
        ),
    )(*operands)


def widen_kernel(attended, same, other, out_delta, down_out, up_out):
    plane = lax.axis_index("groups")
    seat = lax.rem(lax.axis_index("ctx"), PIECES)
    for apart in range(PIECES):
        pieces = other if apart % 2 else same
        for position in range(2):
            piece = pieces[apart // 2, position].astype(jnp.float32)
            place = (seat ^ apart) * 2 + (position ^ plane)
            first = place * 2 * DOWN_OUT_ROWS
            block = piece[:DOWN_OUT_ROWS]
            down_out[pl.ds(first, DOWN_OUT_ROWS, stride=2), :] = block
            down_out[pl.ds(first + 1, DOWN_OUT_ROWS, stride=2), :] = pltpu.roll(block, 64, 1)
            first = pl.multiple_of(place * UP_OUT_ROWS, UP_OUT_ROWS)
            up_out[pl.ds(first, UP_OUT_ROWS), :] = piece[DOWN_OUT_ROWS:]
    dot = partial(jnp.dot, preferred_element_type=jnp.float32)
    rank = dot(attended[...], down_out[...].astype(jnp.bfloat16))[:, :ADAPTER_RANK]
    rank = rank.astype(jnp.bfloat16)
    blocks = D // 128
    for first in range(0, blocks, 4):
        weight = [
            up_out[pl.ds(first + block, ADAPTER_RANK, stride=blocks), :].astype(jnp.bfloat16)
            for block in range(4)
        ]
        delta = adapter_scale * dot(rank, jnp.concatenate(weight, 1))
        out_delta[:, first * 128 : (first + 4) * 128] = delta.astype(jnp.bfloat16)


def widen(attended, same, other):
    return pl.pallas_call(
        widen_kernel,
        out_shape=jax.ShapeDtypeStruct((attended.shape[0], D), jnp.bfloat16),
        in_specs=[pl.BlockSpec(memory_space=pltpu.VMEM)] * 3,
        out_specs=pl.BlockSpec(memory_space=pltpu.VMEM),
        scratch_shapes=[
            pltpu.VMEM((QH * HEAD_SIZE, 128), jnp.float32),
            pltpu.VMEM((ADAPTER_RANK * D // 128, 128), jnp.float32),
        ],
        compiler_params=pltpu.CompilerParams(vmem_limit_bytes=32 << 20),
        cost_estimate=pl.CostEstimate(flops=1 << 27, bytes_accessed=4 << 20, transcendentals=0),
    )(attended, same, other)


def swap(block, mask):
    return lax.ppermute(block, ("groups", "ctx"), [(i, i ^ mask) for i in range(4 * PIECES)])


def direct_shards(
    normed_input, query_base, key_base, value_base, adapter_pool, stretch_adapter, adapter_owner
):
    tok_rows = normed_input.shape[0]
    ctx = lax.axis_size("ctx")
    seq = ctx * tok_rows
    blocks = [list(range(PIECES)), list(range(PIECES, 2 * PIECES))]
    half_dim = HEAD_SIZE // 2
    frequency = rope_base ** (-(jnp.arange(half_dim, dtype=jnp.float32) * 2.0) / HEAD_SIZE)
    angle = jnp.arange(seq, dtype=jnp.int32).astype(jnp.float32)[:, None] * frequency[None, :]
    cosine = jnp.cos(angle)
    sine = jnp.sin(angle)
    cosines = jnp.concatenate([cosine, cosine], 1)
    sines = jnp.concatenate([-sine, sine], 1)

    def after(block, *others):
        return lax.optimization_barrier((block, others))[0]

    def exchange(sent):
        across = swap(sent[2], 2 * PIECES)
        return [sent[0], swap(sent[1], PIECES), across, swap(sent[3], 3 * PIECES)]

    def along_z(block):
        return jnp.stack([block, swap(block, 4)])

    def along_x(pair):
        quad = jnp.stack([pair, swap(pair, 2)], 1)
        return quad.reshape((PIECES // 2,) + pair.shape[1:])

    elsewhere = swap(stretch_adapter, 2 * PIECES)
    packed = pack_row(adapter_pool, SECTIONS)
    even, odd = deal(normed_input, packed)
    sibling = swap(odd, 1)
    base = jnp.concatenate([key_base, value_base], 1)
    base = jnp.stack([base, swap(base, PIECES)])

    spread = lax.all_to_all(packed, "ctx", 0, 0, axis_index_groups=blocks)
    spread = after(spread, sibling, base, cosines, sines)
    sent, near, far = pick(spread, stretch_adapter, elsewhere, adapter_owner)
    arrived = exchange(sent)
    dealt = [after(jnp.stack([even[j], sibling[j]]), sent) for j in range(PIECES // 2)]
    dealt = [swap(block, 2 * j) if j else block for j, block in enumerate(dealt)]

    weight, ups = join(stretch_adapter, adapter_owner, arrived)
    far = swap(after(far, weight), PIECES)
    partial_sums = narrow(weight, dealt)
    back = [swap(block, 2 * j) if j else block for j, block in enumerate(partial_sums)]
    back = after(back, far)
    back = sum(block.astype(jnp.float32) for block in back)
    own_rank = swap(back[1].astype(jnp.bfloat16), 1)
    own_rank = back[0] + own_rank.astype(jnp.float32)
    own_rank = own_rank.astype(jnp.bfloat16)
    ups = along_z(after(ups, *partial_sums))
    base = along_z(after(base, *partial_sums))
    all_rank = own_rank[:, ADAPTER_RANK:]
    base = along_x(after(base, own_rank))
    own, across = settle(
        stretch_adapter, elsewhere, adapter_owner, near, after(far, own_rank)
    )
    ends = jnp.stack([own, swap(across, 2 * PIECES)])
    all_rank = jnp.stack([all_rank, swap(all_rank, PIECES)])
    all_rank = after(all_rank, ups)
    ups = along_x(after(ups, all_rank))
    all_rank = jnp.stack([swap(all_rank, apart) if apart else all_rank for apart in (0, 2, 4, 6)])
    base = after(base, all_rank)
    base = (base, swap(base, 1))
    gathered = jnp.concatenate([all_rank.reshape(-1, 128), ups.reshape(-1, 128)])
    gathered = after(gathered, ends)
    gathered = (gathered, swap(gathered, 1))

    shared = (query_base, base, own_rank, gathered, cosines, sines)
    attended = attend(0, 1, None, *shared)
    ends = after(ends, attended)
    ends = jnp.stack([swap(ends, apart) if apart else ends for apart in (0, 2, 4, 6)])
    attended = attend(1, KEYVALUE_HEADS - 1, attended, *shared)
    ends = after(ends, attended)
    return attended, widen(attended, ends, swap(ends, 1))


def shards(normed_input, query_base, key_base, value_base, adapter_pool, stretch_adapter, owner):
    fits = (
        lax.axis_size("groups") == 2
        and lax.axis_size("ctx") == 2 * PIECES
        and normed_input.shape[0] * PIECES == BLOCK_TOKENS
        and adapter_pool.shape[0] == 1
    )
    plan = direct_shards if fits else spread_shards
    return plan(
        normed_input, query_base, key_base, value_base, adapter_pool, stretch_adapter, owner
    )


def solution(mesh):
    placed = (
        P(("groups", "ctx"), None),
        P(("groups", "ctx"), None),
        P(("groups", "ctx"), None),
        P(("groups", "ctx"), None),
        P("ctx", None),
        P("groups"),
        P(),
    )
    return jax.shard_map(
        shards,
        mesh=mesh,
        in_specs=placed,
        out_specs=(P(("groups", "ctx"), None), P(("groups", "ctx"), None)),
        check_vma=False,
    )
```

```python
from functools import partial
import math

import jax
import jax.numpy as jnp
from jax import lax
from jax.experimental import pallas as pl
from jax.experimental.pallas import tpu as pltpu
from jax.sharding import PartitionSpec as P

D = 8192
QH = 32
KEYVALUE_HEADS = 4
HEAD_SIZE = 128
ADAPTER_RANK = 64
BLOCK_TOKENS = 512
QKV_POOL = 1900544


adapter_scale = 2.0
rope_base = 500000.0
mask_floor = -1e30


def from_partner(block, axis, apart):
    count = lax.axis_size(axis)
    route = []
    for low in range(count):
        high = low | 1 << apart
        if high != low and high < count:
            route += [(low, high), (high, low)]
    return lax.ppermute(block, axis, route)


def rotate(delta, token_positions, heads):
    half_dim = HEAD_SIZE // 2
    frequency = rope_base ** (-(jnp.arange(half_dim, dtype=jnp.float32) * 2.0) / HEAD_SIZE)
    angle = token_positions.astype(jnp.float32)[:, None] * frequency[None, :]
    cosine = jnp.cos(angle)[:, None, :]
    sine_part = jnp.sin(angle)[:, None, :]
    shaped = delta.reshape(delta.shape[0], heads, HEAD_SIZE)
    first_half = shaped[..., :half_dim]
    second_half = shaped[..., half_dim:]
    joined = jnp.concatenate(
        [
            first_half * cosine - second_half * sine_part,
            second_half * cosine + first_half * sine_part,
        ],
        -1,
    )
    return joined.reshape(delta.shape[0], heads * HEAD_SIZE)


def project_heads(
    narrow_product, query_row_block, key_row_block, value_row_block, upper_part, token_positions
):
    query_up_weight = upper_part[: ADAPTER_RANK * QH * HEAD_SIZE].reshape(
        ADAPTER_RANK, QH * HEAD_SIZE
    )
    keyvalue_up_weight = upper_part[ADAPTER_RANK * QH * HEAD_SIZE :].reshape(
        ADAPTER_RANK, 2 * KEYVALUE_HEADS * HEAD_SIZE
    )
    query_correction = adapter_scale * jnp.dot(
        narrow_product[:, :ADAPTER_RANK], query_up_weight, preferred_element_type=jnp.float32
    )
    key_correction = adapter_scale * jnp.dot(
        narrow_product[:, ADAPTER_RANK : 2 * ADAPTER_RANK],
        keyvalue_up_weight[:, : KEYVALUE_HEADS * HEAD_SIZE],
        preferred_element_type=jnp.float32,
    )
    value_correction = adapter_scale * jnp.dot(
        narrow_product[:, 2 * ADAPTER_RANK :],
        keyvalue_up_weight[:, KEYVALUE_HEADS * HEAD_SIZE :],
        preferred_element_type=jnp.float32,
    )
    queries = (
        query_row_block.astype(jnp.float32) + rotate(query_correction, token_positions, QH)
    ).astype(jnp.bfloat16)
    new_keys = (
        key_row_block.astype(jnp.float32) + rotate(key_correction, token_positions, KEYVALUE_HEADS)
    ).astype(jnp.bfloat16)
    new_values = (value_row_block.astype(jnp.float32) + value_correction).astype(jnp.bfloat16)
    return (queries, new_keys, new_values)


def output_delta(attended_rows, out_part):
    down_out = out_part[: QH * HEAD_SIZE * ADAPTER_RANK].reshape(QH * HEAD_SIZE, ADAPTER_RANK)
    raised_output = out_part[QH * HEAD_SIZE * ADAPTER_RANK :].reshape(ADAPTER_RANK, D)
    narrow_product = jnp.dot(attended_rows, down_out, preferred_element_type=jnp.float32).astype(
        jnp.bfloat16
    )
    return (
        adapter_scale * jnp.dot(narrow_product, raised_output, preferred_element_type=jnp.float32)
    ).astype(jnp.bfloat16)


def head_major(query_row_block):
    count_rows = query_row_block.shape[0]
    group_size = QH // KEYVALUE_HEADS
    return (
        query_row_block.reshape(count_rows, KEYVALUE_HEADS, group_size, HEAD_SIZE)
        .transpose(1, 2, 0, 3)
        .reshape(KEYVALUE_HEADS, group_size * count_rows, HEAD_SIZE)
    )


def row_major(head_rows, count_rows):
    group_size = QH // KEYVALUE_HEADS
    return (
        head_rows.reshape(KEYVALUE_HEADS, group_size, count_rows, HEAD_SIZE)
        .transpose(2, 0, 1, 3)
        .reshape(count_rows, QH * HEAD_SIZE)
    )


def online_update(current, queries, query_pos, key_slice, value_slice, key_start):
    run_max, run_sum, run_acc = current
    scores = jnp.einsum(
        "hqd,khd->hqk", queries, key_slice, preferred_element_type=jnp.float32
    ) * HEAD_SIZE ** (-0.5)
    key_pos = key_start + jnp.arange(key_slice.shape[0], dtype=jnp.int32)
    allowed = (query_pos[:, None] >= key_pos[None, :])[None]
    new_max = jnp.maximum(run_max, jnp.max(jnp.where(allowed, scores, mask_floor), axis=-1))
    weights = jnp.where(allowed, jnp.exp(scores - new_max[..., None]), 0.0)
    rescale = jnp.exp(run_max - new_max)
    new_sum = run_sum * rescale + jnp.sum(weights, axis=-1)
    new_acc = run_acc * rescale[..., None] + jnp.einsum(
        "hqk,khd->hqd",
        weights.astype(jnp.bfloat16),
        value_slice,
        preferred_element_type=jnp.float32,
    )
    return (new_max, new_sum, new_acc)


def unchanged(current):
    return current


def fold_keys(carry_state, shard_part, prepared):
    key_row_block, value_row_block = shard_part
    key_count = key_row_block.shape[0]
    sub_width = math.gcd(key_count, 1024)
    key_heads = key_row_block.reshape(key_count // sub_width, sub_width, KEYVALUE_HEADS, HEAD_SIZE)
    value_heads = value_row_block.reshape(
        key_count // sub_width, sub_width, KEYVALUE_HEADS, HEAD_SIZE
    )

    def one_step(sub_index, carried):
        key_start = sub_index * sub_width
        key_slice = lax.dynamic_index_in_dim(key_heads, sub_index, 0, keepdims=False)
        value_slice = lax.dynamic_index_in_dim(value_heads, sub_index, 0, keepdims=False)
        updated = []
        for (queries, query_pos), running in zip(prepared, carried):
            advance = partial(
                online_update,
                queries=queries,
                query_pos=query_pos,
                key_slice=key_slice,
                value_slice=value_slice,
                key_start=key_start,
            )
            updated.append(lax.cond(key_start <= jnp.max(query_pos), advance, unchanged, running))
        return tuple(updated)

    return lax.fori_loop(0, key_count // sub_width, one_step, carry_state)


def finish_block(result, count_rows):
    run_max, run_sum, run_acc = result
    divisor = jnp.where(run_sum > 0.0, run_sum, 1.0)
    return row_major(run_acc / divisor[..., None], count_rows).astype(jnp.bfloat16)


def spread_shards(
    normed_input, query_base, key_base, value_base, adapter_pool, stretch_adapter, adapter_owner
):
    cycle_size = lax.axis_size("ctx")
    my_index = lax.axis_index("ctx")
    tok_rows = normed_input.shape[0]
    token_positions = my_index * tok_rows + jnp.arange(tok_rows, dtype=jnp.int32)
    device_ids = jnp.arange(cycle_size, dtype=jnp.int32)
    stretch_of = device_ids * tok_rows // BLOCK_TOKENS
    stretch_ids = jnp.arange(stretch_adapter.shape[0], dtype=jnp.int32)
    adapter_of = jnp.sum(
        jnp.where(stretch_of[:, None] == stretch_ids[None, :], stretch_adapter[None, :], 0), axis=1
    )
    adapter_ids = jnp.arange(adapter_owner.shape[0], dtype=jnp.int32)
    slot_of = jnp.sum(
        jnp.where(adapter_of[:, None] == adapter_ids[None, :], adapter_owner[None, :], 0), axis=1
    )
    down_size = 3 * ADAPTER_RANK * D
    group_count = BLOCK_TOKENS // tok_rows
    levels = group_count.bit_length() - 1
    local_index = my_index % group_count
    col_width = D // group_count
    piece_len = down_size // (group_count * cycle_size)
    pool_rows = adapter_pool.shape[0]
    down_shaped = adapter_pool[:, :down_size].reshape(pool_rows, group_count, cycle_size, piece_len)
    spread_down = lax.all_to_all(down_shaped, "ctx", split_axis=2, concat_axis=0, tiled=True)
    flat_down = spread_down.reshape(-1, piece_len)
    wanted = jnp.take(flat_down, slot_of * group_count + device_ids % group_count, axis=0)[
        :, None, :
    ]
    down_slice = lax.all_to_all(wanted, "ctx", split_axis=0, concat_axis=1, tiled=True).reshape(
        col_width, 3 * ADAPTER_RANK
    )
    spread_rest = lax.all_to_all(
        adapter_pool[:, down_size:], "ctx", split_axis=1, concat_axis=0, tiled=True
    )
    rest_row = lax.all_to_all(
        jnp.take(spread_rest, slot_of, axis=0), "ctx", split_axis=0, concat_axis=1, tiled=True
    )[0]
    upper_part = rest_row[: QKV_POOL - down_size]
    out_part = rest_row[QKV_POOL - down_size :]
    pieces = normed_input.reshape(tok_rows, group_count, col_width)
    slice_order = jnp.bitwise_xor(local_index, jnp.arange(group_count, dtype=jnp.int32))
    moving = jnp.take(pieces, slice_order, axis=1).transpose(1, 0, 2)
    for level in range(levels):
        shaped = moving.reshape(group_count >> level + 1, 2, 1 << level, tok_rows, col_width)
        arrived = from_partner(shaped[:, 1], "ctx", level)
        moving = jnp.stack([shaped[:, 0], arrived], 1).reshape(group_count, tok_rows, col_width)
    partial_rows = jnp.dot(
        moving.reshape(group_count * tok_rows, col_width),
        down_slice,
        preferred_element_type=jnp.float32,
    ).reshape(group_count, tok_rows, 3 * ADAPTER_RANK)
    for level in reversed(range(levels)):
        halves = partial_rows.reshape(2, partial_rows.shape[0] // 2, tok_rows, 3 * ADAPTER_RANK)
        partial_rows = halves[0] + from_partner(
            halves[1].astype(jnp.bfloat16), "ctx", level
        ).astype(jnp.float32)
    narrow_product = partial_rows[0].astype(jnp.bfloat16)
    queries, new_keys, new_values = project_heads(
        narrow_product, query_base, key_base, value_base, upper_part, token_positions
    )
    group_size = QH // KEYVALUE_HEADS
    blocks = [(queries, token_positions)]
    prepared = [
        (head_major(block_q), jnp.tile(block_pos, group_size)) for block_q, block_pos in blocks
    ]
    initial = tuple(
        (
            (
                jnp.full((KEYVALUE_HEADS, head_q.shape[1]), mask_floor, jnp.float32),
                jnp.zeros((KEYVALUE_HEADS, head_q.shape[1]), jnp.float32),
                jnp.zeros((KEYVALUE_HEADS, head_q.shape[1], HEAD_SIZE), jnp.float32),
            )
            for head_q, block_pos in prepared
        )
    )
    finals = fold_keys(
        initial,
        (
            lax.all_gather(new_keys, "ctx", axis=0, tiled=True),
            lax.all_gather(new_values, "ctx", axis=0, tiled=True),
        ),
        prepared,
    )
    attended = finish_block(finals[0], tok_rows)
    out_delta = output_delta(attended, out_part)
    return (attended, out_delta)


PIECES = 8
GROUP = QH // KEYVALUE_HEADS
SECTIONS = ((0, 12288), (12288, 2048), (14336, 512), (14848, 2048), (16896, 4096))
DOWN_ROWS, QUERY_ROWS, KEYVAL_ROWS, DOWN_OUT_ROWS, UP_OUT_ROWS = 768, 128, 32, 128, 256
UP_ROWS = QUERY_ROWS + 2 * KEYVAL_ROWS
FIRST_ROWS = DOWN_ROWS + QUERY_ROWS + KEYVAL_ROWS


def pack_kernel(sections, pool, *refs):
    out, buffers, sems = refs[-3:]
    plane = lax.axis_index("groups")
    slabs, slab_rows = out.shape[:2]

    def copies(slab):
        listed = []
        offset = 0
        for first, rows in sections:
            share = rows // (2 * PIECES)
            begin = first + (slab * 2 + plane) * share
            listed.append(
                pltpu.make_async_copy(
                    pool.at[:, pl.ds(pl.multiple_of(begin * 128, 2048), share * 128)],
                    buffers.at[slab, :, pl.ds(offset, share * 128)],
                    sems.at[slab, len(listed)],
                )
            )
            offset += share * 128
        return listed

    for slab in range(slabs):
        for copy in copies(slab):
            copy.start()

    def step(slab, carried):
        for copy in copies(slab):
            copy.wait()

        def chunk(index, inner):
            line = buffers[slab, :, pl.ds(pl.multiple_of(index * 2048, 2048), 2048)]
            block = line.astype(jnp.float32).reshape(16, 128).astype(jnp.bfloat16)
            out[slab, pl.ds(pl.multiple_of(index * 16, 16), 16), :] = block
            return inner

        lax.fori_loop(0, slab_rows // 16, chunk, 0, unroll=8)
        return carried

    lax.fori_loop(0, slabs, step, 0)


def pack_row(pool, sections, *after):
    slab_rows = sum(rows for _, rows in sections) // (2 * PIECES)
    return pl.pallas_call(
        partial(pack_kernel, sections),
        out_shape=jax.ShapeDtypeStruct((PIECES, slab_rows, 128), jnp.bfloat16),
        in_specs=[pl.BlockSpec(memory_space=pl.ANY)] * (1 + len(after)),
        out_specs=pl.BlockSpec(memory_space=pltpu.VMEM),
        scratch_shapes=[
            pltpu.VMEM((PIECES, 1, slab_rows * 128), jnp.bfloat16),
            pltpu.SemaphoreType.DMA((PIECES, len(sections))),
        ],
        compiler_params=pltpu.CompilerParams(vmem_limit_bytes=60 << 20),
        cost_estimate=pl.CostEstimate(flops=0, bytes_accessed=8 << 20, transcendentals=0),
    )(pool, *after)


def pick_kernel(here, there, owner, spread, *refs):
    outs, lasts, sems = refs[:4], refs[4:6], refs[6]
    half = lax.axis_index("ctx") // PIECES
    last = spread.shape[1] - FIRST_ROWS
    copies = []
    for flip, out in enumerate(outs):
        wishes = there if flip >= 2 else here
        block = half ^ (flip & 1)
        row = lax.rem(owner[wishes[block]], PIECES)
        mirrored = lax.rem(owner[wishes[1 - block]], PIECES)
        pairs = (
            (spread.at[row, pl.ds(0, FIRST_ROWS)], out.at[pl.ds(0, FIRST_ROWS)]),
            (
                spread.at[mirrored, pl.ds(FIRST_ROWS - KEYVAL_ROWS, KEYVAL_ROWS)],
                out.at[pl.ds(FIRST_ROWS, KEYVAL_ROWS)],
            ),
            (spread.at[row, pl.ds(FIRST_ROWS, last)], lasts[flip % 2].at[flip // 2]),
        )
        for number, (source, target) in enumerate(pairs):
            copies.append(pltpu.make_async_copy(source, target, sems.at[flip, number]))
    for copy in copies:
        copy.start()
    for copy in copies:
        copy.wait()


def pick(spread, here, there, owner):
    last = spread.shape[1] - FIRST_ROWS
    first_shape = jax.ShapeDtypeStruct((FIRST_ROWS + KEYVAL_ROWS, 128), jnp.bfloat16)
    last_shape = jax.ShapeDtypeStruct((2, last, 128), jnp.bfloat16)
    outs = pl.pallas_call(
        pick_kernel,
        out_shape=(first_shape,) * 4 + (last_shape,) * 2,
        in_specs=[pl.BlockSpec(memory_space=pltpu.SMEM)] * 3 + [pl.BlockSpec(memory_space=pl.ANY)],
        out_specs=(pl.BlockSpec(memory_space=pltpu.VMEM),) * 6,
        scratch_shapes=[pltpu.SemaphoreType.DMA((4, 3))],
        compiler_params=pltpu.CompilerParams(vmem_limit_bytes=16 << 20),
        cost_estimate=pl.CostEstimate(flops=0, bytes_accessed=3 << 20, transcendentals=0),
    )(here, there, owner, spread)
    return outs[:4], outs[4], outs[5]


def deal_kernel(rows, even, odd, sems):
    seat = lax.rem(lax.axis_index("ctx"), PIECES)
    width = rows.shape[1] // PIECES
    copies = []
    for apart in range(PIECES):
        first = pl.multiple_of((seat ^ apart) * width, width)
        target = (odd if apart % 2 else even).at[apart // 2]
        copies.append(
            pltpu.make_async_copy(rows.at[:, pl.ds(first, width)], target, sems.at[apart])
        )
    for copy in copies:
        copy.start()
    for copy in copies:
        copy.wait()


def deal(rows, *after):
    slab = jax.ShapeDtypeStruct((PIECES // 2, rows.shape[0], rows.shape[1] // PIECES), rows.dtype)

    def kernel(rows, *refs):
        deal_kernel(rows, *refs[-3:])

    return pl.pallas_call(
        kernel,
        out_shape=(slab, slab),
        in_specs=[pl.BlockSpec(memory_space=pl.ANY)] * (1 + len(after)),
        out_specs=(pl.BlockSpec(memory_space=pltpu.VMEM),) * 2,
        scratch_shapes=[pltpu.SemaphoreType.DMA((PIECES,))],
        compiler_params=pltpu.CompilerParams(vmem_limit_bytes=16 << 20),
        cost_estimate=pl.CostEstimate(flops=0, bytes_accessed=2 << 20, transcendentals=0),
    )(rows, *after)


def nearest(here, owner, block):
    half = lax.axis_index("ctx") // PIECES
    return owner[here[block]] // PIECES == half


def choose(close, arrived, put):
    plane = lax.axis_index("groups")

    @pl.when(close)
    def _():
        put(arrived[0], plane)
        put(arrived[2], 1 - plane)

    @pl.when(jnp.logical_not(close))
    def _():
        put(arrived[1], plane)
        put(arrived[3], 1 - plane)


def join_kernel(here, owner, *refs):
    (across, own, mirror, both), (weight, ups), (flat, left, right) = refs[:4], refs[4:6], refs[6:]
    arrived = (own, mirror, across, both)
    half = lax.axis_index("ctx") // PIECES
    split = DOWN_ROWS + QUERY_ROWS + KEYVAL_ROWS

    def put_own(source, position):
        first = pl.multiple_of(position * DOWN_ROWS, DOWN_ROWS)
        flat[pl.ds(first, DOWN_ROWS), :] = source[:DOWN_ROWS, :].astype(jnp.float32)
        ups[position, : UP_ROWS - KEYVAL_ROWS, :] = source[DOWN_ROWS:split, :]

    def put_mirrored(source, position):
        ups[position, UP_ROWS - KEYVAL_ROWS :, :] = source[split:, :]

    choose(nearest(here, owner, half), arrived, put_own)
    choose(nearest(here, owner, 1 - half), arrived, put_mirrored)

    third = flat.shape[0] // 3
    one = flat[pl.ds(0, third, stride=3), :]
    two = pltpu.roll(flat[pl.ds(1, third, stride=3), :], 64, 1)
    three = pltpu.roll(flat[pl.ds(2, third, stride=3), :], 64, 1)
    lane = lax.broadcasted_iota(jnp.int32, one.shape, 1)
    left[pl.ds(0, third, stride=2), :] = one
    left[pl.ds(1, third, stride=2), :] = jnp.where(lane < 64, two, three)
    right[pl.ds(0, third, stride=2), :] = pltpu.roll(two, 64, 1)
    right[pl.ds(1, third, stride=2), :] = three
    weight[...] = jnp.concatenate([left[...], right[...]], 1).astype(jnp.bfloat16)


def join(here, owner, arrived):
    depth = D // PIECES
    return pl.pallas_call(
        join_kernel,
        out_shape=(
            jax.ShapeDtypeStruct((depth, 256), jnp.bfloat16),
            jax.ShapeDtypeStruct((2, UP_ROWS, 128), jnp.bfloat16),
        ),
        in_specs=[pl.BlockSpec(memory_space=pltpu.SMEM)] * 2
        + [pl.BlockSpec(memory_space=pltpu.VMEM)] * 4,
        out_specs=(pl.BlockSpec(memory_space=pltpu.VMEM),) * 2,
        scratch_shapes=[
            pltpu.VMEM((2 * DOWN_ROWS, 128), jnp.float32),
            pltpu.VMEM((depth, 128), jnp.float32),
            pltpu.VMEM((depth, 128), jnp.float32),
        ],
        compiler_params=pltpu.CompilerParams(vmem_limit_bytes=16 << 20),
        cost_estimate=pl.CostEstimate(flops=0, bytes_accessed=96 << 20, transcendentals=0),
    )(here, owner, arrived[2], arrived[0], arrived[1], arrived[3])


def settle_kernel(here, there, owner, near, far, own, across):
    half = lax.axis_index("ctx") // PIECES
    for number, (wishes, out) in enumerate(((here, own), (there, across))):
        close = nearest(wishes, owner, half)

        @pl.when(close)
        def _():
            out[...] = near[number]

        @pl.when(jnp.logical_not(close))
        def _():
            out[...] = far[number]


def settle(here, there, owner, near, far):
    slab = jax.ShapeDtypeStruct(near.shape[1:], jnp.bfloat16)
    return pl.pallas_call(
        settle_kernel,
        out_shape=(slab, slab),
        in_specs=[pl.BlockSpec(memory_space=pltpu.SMEM)] * 3
        + [pl.BlockSpec(memory_space=pltpu.VMEM)] * 2,
        out_specs=(pl.BlockSpec(memory_space=pltpu.VMEM),) * 2,
        compiler_params=pltpu.CompilerParams(vmem_limit_bytes=16 << 20),
        cost_estimate=pl.CostEstimate(flops=0, bytes_accessed=1 << 20, transcendentals=0),
    )(here, there, owner, near, far)


def narrow_kernel(weight, *refs):
    for block, out in zip(refs[:4], refs[4:]):
        sides, rows, depth = block.shape
        product = jnp.dot(
            block[...].reshape(sides * rows, depth),
            weight[...],
            preferred_element_type=jnp.float32,
        )
        out[...] = product[:, : 3 * ADAPTER_RANK].reshape(out.shape).astype(jnp.bfloat16)


def narrow(weight, dealt):
    sides, rows, depth = dealt[0].shape
    partial_sums = jax.ShapeDtypeStruct((sides, rows, 3 * ADAPTER_RANK), jnp.bfloat16)
    return pl.pallas_call(
        narrow_kernel,
        out_shape=(partial_sums,) * 4,
        in_specs=[pl.BlockSpec(memory_space=pltpu.VMEM)] * 5,
        out_specs=(pl.BlockSpec(memory_space=pltpu.VMEM),) * 4,
        compiler_params=pltpu.CompilerParams(vmem_limit_bytes=16 << 20),
        cost_estimate=pl.CostEstimate(
            flops=2 * 8 * rows * depth * 256, bytes_accessed=2 << 20, transcendentals=0
        ),
    )(weight, *dealt)


def attend_kernel(
    first_head,
    query_block,
    key_same,
    key_other,
    value_same,
    value_other,
    own_rank,
    rows_same,
    rows_other,
    cosines,
    sines,
    *refs,
):
    attended, flat_query, flat_keyval, keys, values = refs[-5:]
    step = pl.program_id(0) + first_head
    rows = query_block.shape[0]
    base = lax.axis_index("ctx") * rows
    half = lax.axis_index("ctx") // PIECES
    seat = lax.rem(lax.axis_index("ctx"), PIECES)
    dot = partial(jnp.dot, preferred_element_type=jnp.float32)

    @pl.when(pl.program_id(0) == 0)
    def _():
        for apart in range(PIECES):
            source = rows_other if apart % 2 else rows_same
            for position in range(2):
                begin = PIECES * rows + (apart // 2 * 2 + position) * UP_ROWS
                piece = source[begin : begin + UP_ROWS, :].astype(jnp.float32)
                place = (seat ^ apart) * 2 + position
                first = pl.multiple_of(place * QUERY_ROWS, QUERY_ROWS)
                flat_query[pl.ds(first, QUERY_ROWS), :] = piece[:QUERY_ROWS]
                first = pl.multiple_of(place * KEYVAL_ROWS, KEYVAL_ROWS)
                for side in range(2):
                    begin = QUERY_ROWS + side * KEYVAL_ROWS
                    flat_keyval[side, pl.ds(first, KEYVAL_ROWS), :] = piece[
                        begin : begin + KEYVAL_ROWS
                    ]

    def turned(delta, cosine, sine):
        return delta * cosine + pltpu.roll(delta, HEAD_SIZE // 2, 1) * sine

    def up(flat, first, stride):
        return flat[pl.ds(first, ADAPTER_RANK, stride=stride), :].astype(jnp.bfloat16)

    for side in range(2):
        heads = 2 * KEYVALUE_HEADS
        key_up = up(flat_keyval.at[side], step, heads)
        value_up = up(flat_keyval.at[side], step + KEYVALUE_HEADS, heads)
        for core in range(2):
            source = rows_other if core else rows_same
            rank = [
                source[(2 * chip + side) * rows : (2 * chip + side + 1) * rows, :]
                for chip in range(PIECES // 2)
            ]
            rank = jnp.concatenate(rank, 0)
            key_delta = adapter_scale * dot(rank[:, :ADAPTER_RANK], key_up)
            value_delta = adapter_scale * dot(rank[:, ADAPTER_RANK:], value_up)
            for chip in range(PIECES // 2):
                there = seat ^ (2 * chip + core)
                first = ((half ^ side) * PIECES + there) * rows
                span = pl.ds(pl.multiple_of(first, rows), rows)
                part = slice(chip * rows, (chip + 1) * rows)
                delta = turned(key_delta[part], cosines[span, :], sines[span, :])
                full = (key_other if core else key_same)[chip, side].astype(jnp.float32) + delta
                keys[span, :] = full.astype(jnp.bfloat16)
                full = (value_other if core else value_same)[chip, side].astype(jnp.float32)
                values[span, :] = (full + value_delta[part]).astype(jnp.bfloat16)
    here = pl.ds(pl.multiple_of(base, rows), rows)
    cosine = cosines[here, :]
    sine = sines[here, :]
    taken = GROUP
    limit = lax.broadcasted_iota(jnp.int32, (rows, 1), 0) + base
    limit = jnp.concatenate([limit] * taken, 0)
    for first in range(0, GROUP, taken):
        weight = [up(flat_query, step * GROUP + first + head, QH) for head in range(taken)]
        deltas = adapter_scale * dot(own_rank[:, :ADAPTER_RANK], jnp.concatenate(weight, 1))
        queries = []
        for place in range(taken):
            moved = turned(deltas[:, place * HEAD_SIZE : (place + 1) * HEAD_SIZE], cosine, sine)
            span = slice((first + place) * HEAD_SIZE, (first + place + 1) * HEAD_SIZE)
            queries.append(
                (query_block[:, span].astype(jnp.float32) + moved).astype(jnp.bfloat16)
            )
        queries = jnp.concatenate(queries, 0)
        scores = lax.dot_general(
            queries, keys[...], (((1,), (1,)), ((), ())), preferred_element_type=jnp.float32
        )
        column = lax.broadcasted_iota(jnp.int32, scores.shape, 1)
        scores = jnp.where(column <= limit, scores, mask_floor)
        scores = scores - jnp.max(scores, axis=-1, keepdims=True)
        weights = jnp.exp(scores * HEAD_SIZE ** (-0.5))
        divisor = jnp.sum(weights, axis=-1, keepdims=True)
        result = (dot(weights.astype(jnp.bfloat16), values[...]) / divisor).astype(jnp.bfloat16)
        for place in range(taken):
            span = slice((first + place) * HEAD_SIZE, (first + place + 1) * HEAD_SIZE)
            attended[:, span] = result[place * rows : (place + 1) * rows]


def attend(first_head, heads, before, query_base, base, own_rank, gathered, cosines, sines):
    rows = query_base.shape[0]
    seq = 4 * PIECES // 2 * rows
    width = GROUP * HEAD_SIZE

    def whole(shape):
        return pl.BlockSpec(shape, lambda h: (0,) * len(shape))

    key_spec = pl.BlockSpec((PIECES // 2, 2, rows, HEAD_SIZE), lambda h: (0, 0, 0, h + first_head))
    value_spec = pl.BlockSpec(
        (PIECES // 2, 2, rows, HEAD_SIZE), lambda h: (0, 0, 0, h + first_head + KEYVALUE_HEADS)
    )
    operands = (query_base, base[0], base[1], base[0], base[1], own_rank, *gathered)
    operands += (cosines, sines) + (() if before is None else (before,))
    query_spec = pl.BlockSpec((rows, width), lambda h: (0, h + first_head))
    return pl.pallas_call(
        partial(attend_kernel, first_head),
        grid=(heads,),
        out_shape=jax.ShapeDtypeStruct((rows, QH * HEAD_SIZE), jnp.bfloat16),
        in_specs=[
            query_spec,
            key_spec,
            key_spec,
            value_spec,
            value_spec,
            whole(own_rank.shape),
            whole(gathered[0].shape),
            whole(gathered[1].shape),
            whole(cosines.shape),
            whole(sines.shape),
        ]
        + [pl.BlockSpec(memory_space=pl.ANY)] * (len(operands) - 10),
        out_specs=query_spec,
        input_output_aliases={} if before is None else {len(operands) - 1: 0},
        scratch_shapes=[
            pltpu.VMEM((2 * PIECES * QUERY_ROWS, 128), jnp.float32),
            pltpu.VMEM((2, 2 * PIECES * KEYVAL_ROWS, 128), jnp.float32),
            pltpu.VMEM((seq, HEAD_SIZE), jnp.bfloat16),
            pltpu.VMEM((seq, HEAD_SIZE), jnp.bfloat16),
        ],
        compiler_params=pltpu.CompilerParams(vmem_limit_bytes=32 << 20),
        cost_estimate=pl.CostEstimate(
            flops=12 * heads * rows * QH * seq * HEAD_SIZE,
            bytes_accessed=10 << 20,
            transcendentals=heads * rows * GROUP * seq,
        ),
    )(*operands)


def widen_kernel(attended, same, other, out_delta, down_out, up_out):
    plane = lax.axis_index("groups")
    seat = lax.rem(lax.axis_index("ctx"), PIECES)
    for apart in range(PIECES):
        pieces = other if apart % 2 else same
        for position in range(2):
            piece = pieces[apart // 2, position].astype(jnp.float32)
            place = (seat ^ apart) * 2 + (position ^ plane)
            first = place * 2 * DOWN_OUT_ROWS
            block = piece[:DOWN_OUT_ROWS]
            down_out[pl.ds(first, DOWN_OUT_ROWS, stride=2), :] = block
            down_out[pl.ds(first + 1, DOWN_OUT_ROWS, stride=2), :] = pltpu.roll(block, 64, 1)
            first = pl.multiple_of(place * UP_OUT_ROWS, UP_OUT_ROWS)
            up_out[pl.ds(first, UP_OUT_ROWS), :] = piece[DOWN_OUT_ROWS:]
    dot = partial(jnp.dot, preferred_element_type=jnp.float32)
    rank = dot(attended[...], down_out[...].astype(jnp.bfloat16))[:, :ADAPTER_RANK]
    rank = rank.astype(jnp.bfloat16)
    blocks = D // 128
    for first in range(0, blocks, 4):
        weight = [
            up_out[pl.ds(first + block, ADAPTER_RANK, stride=blocks), :].astype(jnp.bfloat16)
            for block in range(4)
        ]
        delta = adapter_scale * dot(rank, jnp.concatenate(weight, 1))
        out_delta[:, first * 128 : (first + 4) * 128] = delta.astype(jnp.bfloat16)


def widen(attended, same, other):
    return pl.pallas_call(
        widen_kernel,
        out_shape=jax.ShapeDtypeStruct((attended.shape[0], D), jnp.bfloat16),
        in_specs=[pl.BlockSpec(memory_space=pltpu.VMEM)] * 3,
        out_specs=pl.BlockSpec(memory_space=pltpu.VMEM),
        scratch_shapes=[
            pltpu.VMEM((QH * HEAD_SIZE, 128), jnp.float32),
            pltpu.VMEM((ADAPTER_RANK * D // 128, 128), jnp.float32),
        ],
        compiler_params=pltpu.CompilerParams(vmem_limit_bytes=32 << 20),
        cost_estimate=pl.CostEstimate(flops=1 << 27, bytes_accessed=4 << 20, transcendentals=0),
    )(attended, same, other)


def swap(block, mask):
    return lax.ppermute(block, ("groups", "ctx"), [(i, i ^ mask) for i in range(4 * PIECES)])


def direct_shards(
    normed_input, query_base, key_base, value_base, adapter_pool, stretch_adapter, adapter_owner
):
    tok_rows = normed_input.shape[0]
    ctx = lax.axis_size("ctx")
    seq = ctx * tok_rows
    blocks = [list(range(PIECES)), list(range(PIECES, 2 * PIECES))]
    half_dim = HEAD_SIZE // 2
    frequency = rope_base ** (-(jnp.arange(half_dim, dtype=jnp.float32) * 2.0) / HEAD_SIZE)
    angle = jnp.arange(seq, dtype=jnp.int32).astype(jnp.float32)[:, None] * frequency[None, :]
    cosine = jnp.cos(angle)
    sine = jnp.sin(angle)
    cosines = jnp.concatenate([cosine, cosine], 1)
    sines = jnp.concatenate([-sine, sine], 1)

    def after(block, *others):
        return lax.optimization_barrier((block, others))[0]

    def exchange(sent):
        across = swap(sent[2], 2 * PIECES)
        return [sent[0], swap(sent[1], PIECES), across, swap(sent[3], 3 * PIECES)]

    def along_z(block):
        return jnp.stack([block, swap(block, 4)])

    def along_x(pair):
        quad = jnp.stack([pair, swap(pair, 2)], 1)
        return quad.reshape((PIECES // 2,) + pair.shape[1:])

    elsewhere = swap(stretch_adapter, 2 * PIECES)
    packed = pack_row(adapter_pool, SECTIONS)
    even, odd = deal(normed_input, packed)
    sibling = swap(odd, 1)
    base = jnp.concatenate([key_base, value_base], 1)
    base = jnp.stack([base, swap(base, PIECES)])

    spread = lax.all_to_all(packed, "ctx", 0, 0, axis_index_groups=blocks)
    spread = after(spread, sibling, base, cosines, sines)
    sent, near, far = pick(spread, stretch_adapter, elsewhere, adapter_owner)
    arrived = exchange(sent)
    dealt = [after(jnp.stack([even[j], sibling[j]]), sent) for j in range(PIECES // 2)]
    dealt = [swap(block, 2 * j) if j else block for j, block in enumerate(dealt)]

    weight, ups = join(stretch_adapter, adapter_owner, arrived)
    far = swap(after(far, weight), PIECES)
    partial_sums = narrow(weight, dealt)
    back = [swap(block, 2 * j) if j else block for j, block in enumerate(partial_sums)]
    back = after(back, far)
    back = sum(block.astype(jnp.float32) for block in back)
    own_rank = swap(back[1].astype(jnp.bfloat16), 1)
    own_rank = back[0] + own_rank.astype(jnp.float32)
    own_rank = own_rank.astype(jnp.bfloat16)
    ups = along_z(after(ups, *partial_sums))
    base = along_z(after(base, *partial_sums))
    all_rank = own_rank[:, ADAPTER_RANK:]
    base = along_x(after(base, own_rank))
    own, across = settle(
        stretch_adapter, elsewhere, adapter_owner, near, after(far, own_rank)
    )
    ends = jnp.stack([own, swap(across, 2 * PIECES)])
    all_rank = jnp.stack([all_rank, swap(all_rank, PIECES)])
    all_rank = after(all_rank, ups)
    ups = along_x(after(ups, all_rank))
    all_rank = jnp.stack([swap(all_rank, apart) if apart else all_rank for apart in (0, 2, 4, 6)])
    base = after(base, all_rank)
    base = (base, swap(base, 1))
    gathered = jnp.concatenate([all_rank.reshape(-1, 128), ups.reshape(-1, 128)])
    gathered = after(gathered, ends)
    gathered = (gathered, swap(gathered, 1))

    shared = (query_base, base, own_rank, gathered, cosines, sines)
    attended = attend(0, 1, None, *shared)
    ends = after(ends, attended)
    ends = jnp.stack([swap(ends, apart) if apart else ends for apart in (0, 2, 4, 6)])
    attended = attend(1, KEYVALUE_HEADS - 1, attended, *shared)
    ends = after(ends, attended)
    return attended, widen(attended, ends, swap(ends, 1))


def shards(normed_input, query_base, key_base, value_base, adapter_pool, stretch_adapter, owner):
    fits = (
        lax.axis_size("groups") == 2
        and lax.axis_size("ctx") == 2 * PIECES
        and normed_input.shape[0] * PIECES == BLOCK_TOKENS
        and adapter_pool.shape[0] == 1
    )
    plan = direct_shards if fits else spread_shards
    return plan(
        normed_input, query_base, key_base, value_base, adapter_pool, stretch_adapter, owner
    )


def solution(mesh):
    placed = (
        P(("groups", "ctx"), None),
        P(("groups", "ctx"), None),
        P(("groups", "ctx"), None),
        P(("groups", "ctx"), None),
        P("ctx", None),
        P("groups"),
        P(),
    )
    return jax.shard_map(
        shards,
        mesh=mesh,
        in_specs=placed,
        out_specs=(P(("groups", "ctx"), None), P(("groups", "ctx"), None)),
        check_vma=False,
    )
```

```python
from functools import partial
import math

import jax
import jax.numpy as jnp
from jax import lax
from jax.experimental import pallas as pl
from jax.experimental.pallas import tpu as pltpu
from jax.sharding import PartitionSpec as P

D = 8192
QH = 32
KEYVALUE_HEADS = 4
HEAD_SIZE = 128
ADAPTER_RANK = 64
BLOCK_TOKENS = 512
QKV_POOL = 1900544


adapter_scale = 2.0
rope_base = 500000.0
mask_floor = -1e30


def from_partner(block, axis, apart):
    count = lax.axis_size(axis)
    route = []
    for low in range(count):
        high = low | 1 << apart
        if high != low and high < count:
            route += [(low, high), (high, low)]
    return lax.ppermute(block, axis, route)


def rotate(delta, token_positions, heads):
    half_dim = HEAD_SIZE // 2
    frequency = rope_base ** (-(jnp.arange(half_dim, dtype=jnp.float32) * 2.0) / HEAD_SIZE)
    angle = token_positions.astype(jnp.float32)[:, None] * frequency[None, :]
    cosine = jnp.cos(angle)[:, None, :]
    sine_part = jnp.sin(angle)[:, None, :]
    shaped = delta.reshape(delta.shape[0], heads, HEAD_SIZE)
    first_half = shaped[..., :half_dim]
    second_half = shaped[..., half_dim:]
    joined = jnp.concatenate(
        [
            first_half * cosine - second_half * sine_part,
            second_half * cosine + first_half * sine_part,
        ],
        -1,
    )
    return joined.reshape(delta.shape[0], heads * HEAD_SIZE)


def project_heads(
    narrow_product, query_row_block, key_row_block, value_row_block, upper_part, token_positions
):
    query_up_weight = upper_part[: ADAPTER_RANK * QH * HEAD_SIZE].reshape(
        ADAPTER_RANK, QH * HEAD_SIZE
    )
    keyvalue_up_weight = upper_part[ADAPTER_RANK * QH * HEAD_SIZE :].reshape(
        ADAPTER_RANK, 2 * KEYVALUE_HEADS * HEAD_SIZE
    )
    query_correction = adapter_scale * jnp.dot(
        narrow_product[:, :ADAPTER_RANK], query_up_weight, preferred_element_type=jnp.float32
    )
    key_correction = adapter_scale * jnp.dot(
        narrow_product[:, ADAPTER_RANK : 2 * ADAPTER_RANK],
        keyvalue_up_weight[:, : KEYVALUE_HEADS * HEAD_SIZE],
        preferred_element_type=jnp.float32,
    )
    value_correction = adapter_scale * jnp.dot(
        narrow_product[:, 2 * ADAPTER_RANK :],
        keyvalue_up_weight[:, KEYVALUE_HEADS * HEAD_SIZE :],
        preferred_element_type=jnp.float32,
    )
    queries = (
        query_row_block.astype(jnp.float32) + rotate(query_correction, token_positions, QH)
    ).astype(jnp.bfloat16)
    new_keys = (
        key_row_block.astype(jnp.float32) + rotate(key_correction, token_positions, KEYVALUE_HEADS)
    ).astype(jnp.bfloat16)
    new_values = (value_row_block.astype(jnp.float32) + value_correction).astype(jnp.bfloat16)
    return (queries, new_keys, new_values)


def output_delta(attended_rows, out_part):
    down_out = out_part[: QH * HEAD_SIZE * ADAPTER_RANK].reshape(QH * HEAD_SIZE, ADAPTER_RANK)
    raised_output = out_part[QH * HEAD_SIZE * ADAPTER_RANK :].reshape(ADAPTER_RANK, D)
    narrow_product = jnp.dot(attended_rows, down_out, preferred_element_type=jnp.float32).astype(
        jnp.bfloat16
    )
    return (
        adapter_scale * jnp.dot(narrow_product, raised_output, preferred_element_type=jnp.float32)
    ).astype(jnp.bfloat16)


def head_major(query_row_block):
    count_rows = query_row_block.shape[0]
    group_size = QH // KEYVALUE_HEADS
    return (
        query_row_block.reshape(count_rows, KEYVALUE_HEADS, group_size, HEAD_SIZE)
        .transpose(1, 2, 0, 3)
        .reshape(KEYVALUE_HEADS, group_size * count_rows, HEAD_SIZE)
    )


def row_major(head_rows, count_rows):
    group_size = QH // KEYVALUE_HEADS
    return (
        head_rows.reshape(KEYVALUE_HEADS, group_size, count_rows, HEAD_SIZE)
        .transpose(2, 0, 1, 3)
        .reshape(count_rows, QH * HEAD_SIZE)
    )


def online_update(current, queries, query_pos, key_slice, value_slice, key_start):
    run_max, run_sum, run_acc = current
    scores = jnp.einsum(
        "hqd,khd->hqk", queries, key_slice, preferred_element_type=jnp.float32
    ) * HEAD_SIZE ** (-0.5)
    key_pos = key_start + jnp.arange(key_slice.shape[0], dtype=jnp.int32)
    allowed = (query_pos[:, None] >= key_pos[None, :])[None]
    new_max = jnp.maximum(run_max, jnp.max(jnp.where(allowed, scores, mask_floor), axis=-1))
    weights = jnp.where(allowed, jnp.exp(scores - new_max[..., None]), 0.0)
    rescale = jnp.exp(run_max - new_max)
    new_sum = run_sum * rescale + jnp.sum(weights, axis=-1)
    new_acc = run_acc * rescale[..., None] + jnp.einsum(
        "hqk,khd->hqd",
        weights.astype(jnp.bfloat16),
        value_slice,
        preferred_element_type=jnp.float32,
    )
    return (new_max, new_sum, new_acc)


def unchanged(current):
    return current


def fold_keys(carry_state, shard_part, prepared):
    key_row_block, value_row_block = shard_part
    key_count = key_row_block.shape[0]
    sub_width = math.gcd(key_count, 1024)
    key_heads = key_row_block.reshape(key_count // sub_width, sub_width, KEYVALUE_HEADS, HEAD_SIZE)
    value_heads = value_row_block.reshape(
        key_count // sub_width, sub_width, KEYVALUE_HEADS, HEAD_SIZE
    )

    def one_step(sub_index, carried):
        key_start = sub_index * sub_width
        key_slice = lax.dynamic_index_in_dim(key_heads, sub_index, 0, keepdims=False)
        value_slice = lax.dynamic_index_in_dim(value_heads, sub_index, 0, keepdims=False)
        updated = []
        for (queries, query_pos), running in zip(prepared, carried):
            advance = partial(
                online_update,
                queries=queries,
                query_pos=query_pos,
                key_slice=key_slice,
                value_slice=value_slice,
                key_start=key_start,
            )
            updated.append(lax.cond(key_start <= jnp.max(query_pos), advance, unchanged, running))
        return tuple(updated)

    return lax.fori_loop(0, key_count // sub_width, one_step, carry_state)


def finish_block(result, count_rows):
    run_max, run_sum, run_acc = result
    divisor = jnp.where(run_sum > 0.0, run_sum, 1.0)
    return row_major(run_acc / divisor[..., None], count_rows).astype(jnp.bfloat16)


def spread_shards(
    normed_input, query_base, key_base, value_base, adapter_pool, stretch_adapter, adapter_owner
):
    cycle_size = lax.axis_size("ctx")
    my_index = lax.axis_index("ctx")
    tok_rows = normed_input.shape[0]
    token_positions = my_index * tok_rows + jnp.arange(tok_rows, dtype=jnp.int32)
    device_ids = jnp.arange(cycle_size, dtype=jnp.int32)
    stretch_of = device_ids * tok_rows // BLOCK_TOKENS
    stretch_ids = jnp.arange(stretch_adapter.shape[0], dtype=jnp.int32)
    adapter_of = jnp.sum(
        jnp.where(stretch_of[:, None] == stretch_ids[None, :], stretch_adapter[None, :], 0), axis=1
    )
    adapter_ids = jnp.arange(adapter_owner.shape[0], dtype=jnp.int32)
    slot_of = jnp.sum(
        jnp.where(adapter_of[:, None] == adapter_ids[None, :], adapter_owner[None, :], 0), axis=1
    )
    down_size = 3 * ADAPTER_RANK * D
    group_count = BLOCK_TOKENS // tok_rows
    levels = group_count.bit_length() - 1
    local_index = my_index % group_count
    col_width = D // group_count
    piece_len = down_size // (group_count * cycle_size)
    pool_rows = adapter_pool.shape[0]
    down_shaped = adapter_pool[:, :down_size].reshape(pool_rows, group_count, cycle_size, piece_len)
    spread_down = lax.all_to_all(down_shaped, "ctx", split_axis=2, concat_axis=0, tiled=True)
    flat_down = spread_down.reshape(-1, piece_len)
    wanted = jnp.take(flat_down, slot_of * group_count + device_ids % group_count, axis=0)[
        :, None, :
    ]
    down_slice = lax.all_to_all(wanted, "ctx", split_axis=0, concat_axis=1, tiled=True).reshape(
        col_width, 3 * ADAPTER_RANK
    )
    spread_rest = lax.all_to_all(
        adapter_pool[:, down_size:], "ctx", split_axis=1, concat_axis=0, tiled=True
    )
    rest_row = lax.all_to_all(
        jnp.take(spread_rest, slot_of, axis=0), "ctx", split_axis=0, concat_axis=1, tiled=True
    )[0]
    upper_part = rest_row[: QKV_POOL - down_size]
    out_part = rest_row[QKV_POOL - down_size :]
    pieces = normed_input.reshape(tok_rows, group_count, col_width)
    slice_order = jnp.bitwise_xor(local_index, jnp.arange(group_count, dtype=jnp.int32))
    moving = jnp.take(pieces, slice_order, axis=1).transpose(1, 0, 2)
    for level in range(levels):
        shaped = moving.reshape(group_count >> level + 1, 2, 1 << level, tok_rows, col_width)
        arrived = from_partner(shaped[:, 1], "ctx", level)
        moving = jnp.stack([shaped[:, 0], arrived], 1).reshape(group_count, tok_rows, col_width)
    partial_rows = jnp.dot(
        moving.reshape(group_count * tok_rows, col_width),
        down_slice,
        preferred_element_type=jnp.float32,
    ).reshape(group_count, tok_rows, 3 * ADAPTER_RANK)
    for level in reversed(range(levels)):
        halves = partial_rows.reshape(2, partial_rows.shape[0] // 2, tok_rows, 3 * ADAPTER_RANK)
        partial_rows = halves[0] + from_partner(
            halves[1].astype(jnp.bfloat16), "ctx", level
        ).astype(jnp.float32)
    narrow_product = partial_rows[0].astype(jnp.bfloat16)
    queries, new_keys, new_values = project_heads(
        narrow_product, query_base, key_base, value_base, upper_part, token_positions
    )
    group_size = QH // KEYVALUE_HEADS
    blocks = [(queries, token_positions)]
    prepared = [
        (head_major(block_q), jnp.tile(block_pos, group_size)) for block_q, block_pos in blocks
    ]
    initial = tuple(
        (
            (
                jnp.full((KEYVALUE_HEADS, head_q.shape[1]), mask_floor, jnp.float32),
                jnp.zeros((KEYVALUE_HEADS, head_q.shape[1]), jnp.float32),
                jnp.zeros((KEYVALUE_HEADS, head_q.shape[1], HEAD_SIZE), jnp.float32),
            )
            for head_q, block_pos in prepared
        )
    )
    finals = fold_keys(
        initial,
        (
            lax.all_gather(new_keys, "ctx", axis=0, tiled=True),
            lax.all_gather(new_values, "ctx", axis=0, tiled=True),
        ),
        prepared,
    )
    attended = finish_block(finals[0], tok_rows)
    out_delta = output_delta(attended, out_part)
    return (attended, out_delta)


PIECES = 8
GROUP = QH // KEYVALUE_HEADS
SECTIONS = ((0, 12288), (12288, 2048), (14336, 512), (14848, 2048), (16896, 4096))
DOWN_ROWS, QUERY_ROWS, KEYVAL_ROWS, DOWN_OUT_ROWS, UP_OUT_ROWS = 768, 128, 32, 128, 256
UP_ROWS = QUERY_ROWS + 2 * KEYVAL_ROWS
FIRST_ROWS = DOWN_ROWS + QUERY_ROWS + KEYVAL_ROWS


def pack_kernel(sections, pool, *refs):
    out, buffers, sems = refs[-3:]
    plane = lax.axis_index("groups")
    slabs, slab_rows = out.shape[:2]

    def copies(slab):
        listed = []
        offset = 0
        for first, rows in sections:
            share = rows // (2 * PIECES)
            begin = first + (slab * 2 + plane) * share
            listed.append(
                pltpu.make_async_copy(
                    pool.at[:, pl.ds(pl.multiple_of(begin * 128, 2048), share * 128)],
                    buffers.at[slab, :, pl.ds(offset, share * 128)],
                    sems.at[slab, len(listed)],
                )
            )
            offset += share * 128
        return listed

    for slab in range(slabs):
        for copy in copies(slab):
            copy.start()

    def step(slab, carried):
        for copy in copies(slab):
            copy.wait()

        def chunk(index, inner):
            line = buffers[slab, :, pl.ds(pl.multiple_of(index * 2048, 2048), 2048)]
            block = line.astype(jnp.float32).reshape(16, 128).astype(jnp.bfloat16)
            out[slab, pl.ds(pl.multiple_of(index * 16, 16), 16), :] = block
            return inner

        lax.fori_loop(0, slab_rows // 16, chunk, 0, unroll=8)
        return carried

    lax.fori_loop(0, slabs, step, 0)


def pack_row(pool, sections, *after):
    slab_rows = sum(rows for _, rows in sections) // (2 * PIECES)
    return pl.pallas_call(
        partial(pack_kernel, sections),
        out_shape=jax.ShapeDtypeStruct((PIECES, slab_rows, 128), jnp.bfloat16),
        in_specs=[pl.BlockSpec(memory_space=pl.ANY)] * (1 + len(after)),
        out_specs=pl.BlockSpec(memory_space=pltpu.VMEM),
        scratch_shapes=[
            pltpu.VMEM((PIECES, 1, slab_rows * 128), jnp.bfloat16),
            pltpu.SemaphoreType.DMA((PIECES, len(sections))),
        ],
        compiler_params=pltpu.CompilerParams(vmem_limit_bytes=60 << 20),
        cost_estimate=pl.CostEstimate(flops=0, bytes_accessed=8 << 20, transcendentals=0),
    )(pool, *after)


def pick_kernel(here, there, owner, spread, *refs):
    outs, lasts, sems = refs[:4], refs[4:6], refs[6]
    half = lax.axis_index("ctx") // PIECES
    last = spread.shape[1] - FIRST_ROWS
    copies = []
    for flip, out in enumerate(outs):
        wishes = there if flip >= 2 else here
        block = half ^ (flip & 1)
        row = lax.rem(owner[wishes[block]], PIECES)
        mirrored = lax.rem(owner[wishes[1 - block]], PIECES)
        pairs = (
            (spread.at[row, pl.ds(0, FIRST_ROWS)], out.at[pl.ds(0, FIRST_ROWS)]),
            (
                spread.at[mirrored, pl.ds(FIRST_ROWS - KEYVAL_ROWS, KEYVAL_ROWS)],
                out.at[pl.ds(FIRST_ROWS, KEYVAL_ROWS)],
            ),
            (spread.at[row, pl.ds(FIRST_ROWS, last)], lasts[flip % 2].at[flip // 2]),
        )
        for number, (source, target) in enumerate(pairs):
            copies.append(pltpu.make_async_copy(source, target, sems.at[flip, number]))
    for copy in copies:
        copy.start()
    for copy in copies:
        copy.wait()


def pick(spread, here, there, owner):
    last = spread.shape[1] - FIRST_ROWS
    first_shape = jax.ShapeDtypeStruct((FIRST_ROWS + KEYVAL_ROWS, 128), jnp.bfloat16)
    last_shape = jax.ShapeDtypeStruct((2, last, 128), jnp.bfloat16)
    outs = pl.pallas_call(
        pick_kernel,
        out_shape=(first_shape,) * 4 + (last_shape,) * 2,
        in_specs=[pl.BlockSpec(memory_space=pltpu.SMEM)] * 3 + [pl.BlockSpec(memory_space=pl.ANY)],
        out_specs=(pl.BlockSpec(memory_space=pltpu.VMEM),) * 6,
        scratch_shapes=[pltpu.SemaphoreType.DMA((4, 3))],
        compiler_params=pltpu.CompilerParams(vmem_limit_bytes=16 << 20),
        cost_estimate=pl.CostEstimate(flops=0, bytes_accessed=3 << 20, transcendentals=0),
    )(here, there, owner, spread)
    return outs[:4], outs[4], outs[5]


def deal_kernel(rows, even, odd, sems):
    seat = lax.rem(lax.axis_index("ctx"), PIECES)
    width = rows.shape[1] // PIECES
    copies = []
    for apart in range(PIECES):
        first = pl.multiple_of((seat ^ apart) * width, width)
        target = (odd if apart % 2 else even).at[apart // 2]
        copies.append(
            pltpu.make_async_copy(rows.at[:, pl.ds(first, width)], target, sems.at[apart])
        )
    for copy in copies:
        copy.start()
    for copy in copies:
        copy.wait()


def deal(rows, *after):
    slab = jax.ShapeDtypeStruct((PIECES // 2, rows.shape[0], rows.shape[1] // PIECES), rows.dtype)

    def kernel(rows, *refs):
        deal_kernel(rows, *refs[-3:])

    return pl.pallas_call(
        kernel,
        out_shape=(slab, slab),
        in_specs=[pl.BlockSpec(memory_space=pl.ANY)] * (1 + len(after)),
        out_specs=(pl.BlockSpec(memory_space=pltpu.VMEM),) * 2,
        scratch_shapes=[pltpu.SemaphoreType.DMA((PIECES,))],
        compiler_params=pltpu.CompilerParams(vmem_limit_bytes=16 << 20),
        cost_estimate=pl.CostEstimate(flops=0, bytes_accessed=2 << 20, transcendentals=0),
    )(rows, *after)


def nearest(here, owner, block):
    half = lax.axis_index("ctx") // PIECES
    return owner[here[block]] // PIECES == half


def choose(close, arrived, put):
    plane = lax.axis_index("groups")

    @pl.when(close)
    def _():
        put(arrived[0], plane)
        put(arrived[2], 1 - plane)

    @pl.when(jnp.logical_not(close))
    def _():
        put(arrived[1], plane)
        put(arrived[3], 1 - plane)


def join_kernel(here, owner, *refs):
    (across, own, mirror, both), (weight, ups), (flat, left, right) = refs[:4], refs[4:6], refs[6:]
    arrived = (own, mirror, across, both)
    half = lax.axis_index("ctx") // PIECES
    split = DOWN_ROWS + QUERY_ROWS + KEYVAL_ROWS

    def put_own(source, position):
        first = pl.multiple_of(position * DOWN_ROWS, DOWN_ROWS)
        flat[pl.ds(first, DOWN_ROWS), :] = source[:DOWN_ROWS, :].astype(jnp.float32)
        ups[position, : UP_ROWS - KEYVAL_ROWS, :] = source[DOWN_ROWS:split, :]

    def put_mirrored(source, position):
        ups[position, UP_ROWS - KEYVAL_ROWS :, :] = source[split:, :]

    choose(nearest(here, owner, half), arrived, put_own)
    choose(nearest(here, owner, 1 - half), arrived, put_mirrored)

    third = flat.shape[0] // 3
    one = flat[pl.ds(0, third, stride=3), :]
    two = pltpu.roll(flat[pl.ds(1, third, stride=3), :], 64, 1)
    three = pltpu.roll(flat[pl.ds(2, third, stride=3), :], 64, 1)
    lane = lax.broadcasted_iota(jnp.int32, one.shape, 1)
    left[pl.ds(0, third, stride=2), :] = one
    left[pl.ds(1, third, stride=2), :] = jnp.where(lane < 64, two, three)
    right[pl.ds(0, third, stride=2), :] = pltpu.roll(two, 64, 1)
    right[pl.ds(1, third, stride=2), :] = three
    weight[...] = jnp.concatenate([left[...], right[...]], 1).astype(jnp.bfloat16)


def join(here, owner, arrived):
    depth = D // PIECES
    return pl.pallas_call(
        join_kernel,
        out_shape=(
            jax.ShapeDtypeStruct((depth, 256), jnp.bfloat16),
            jax.ShapeDtypeStruct((2, UP_ROWS, 128), jnp.bfloat16),
        ),
        in_specs=[pl.BlockSpec(memory_space=pltpu.SMEM)] * 2
        + [pl.BlockSpec(memory_space=pltpu.VMEM)] * 4,
        out_specs=(pl.BlockSpec(memory_space=pltpu.VMEM),) * 2,
        scratch_shapes=[
            pltpu.VMEM((2 * DOWN_ROWS, 128), jnp.float32),
            pltpu.VMEM((depth, 128), jnp.float32),
            pltpu.VMEM((depth, 128), jnp.float32),
        ],
        compiler_params=pltpu.CompilerParams(vmem_limit_bytes=16 << 20),
        cost_estimate=pl.CostEstimate(flops=0, bytes_accessed=96 << 20, transcendentals=0),
    )(here, owner, arrived[2], arrived[0], arrived[1], arrived[3])


def settle_kernel(here, there, owner, near, far, own, across):
    half = lax.axis_index("ctx") // PIECES
    for number, (wishes, out) in enumerate(((here, own), (there, across))):
        close = nearest(wishes, owner, half)

        @pl.when(close)
        def _():
            out[...] = near[number]

        @pl.when(jnp.logical_not(close))
        def _():
            out[...] = far[number]


def settle(here, there, owner, near, far):
    slab = jax.ShapeDtypeStruct(near.shape[1:], jnp.bfloat16)
    return pl.pallas_call(
        settle_kernel,
        out_shape=(slab, slab),
        in_specs=[pl.BlockSpec(memory_space=pltpu.SMEM)] * 3
        + [pl.BlockSpec(memory_space=pltpu.VMEM)] * 2,
        out_specs=(pl.BlockSpec(memory_space=pltpu.VMEM),) * 2,
        compiler_params=pltpu.CompilerParams(vmem_limit_bytes=16 << 20),
        cost_estimate=pl.CostEstimate(flops=0, bytes_accessed=1 << 20, transcendentals=0),
    )(here, there, owner, near, far)


def narrow_kernel(weight, *refs):
    for block, out in zip(refs[:4], refs[4:]):
        sides, rows, depth = block.shape
        product = jnp.dot(
            block[...].reshape(sides * rows, depth),
            weight[...],
            preferred_element_type=jnp.float32,
        )
        out[...] = product[:, : 3 * ADAPTER_RANK].reshape(out.shape).astype(jnp.bfloat16)


def narrow(weight, dealt):
    sides, rows, depth = dealt[0].shape
    partial_sums = jax.ShapeDtypeStruct((sides, rows, 3 * ADAPTER_RANK), jnp.bfloat16)
    return pl.pallas_call(
        narrow_kernel,
        out_shape=(partial_sums,) * 4,
        in_specs=[pl.BlockSpec(memory_space=pltpu.VMEM)] * 5,
        out_specs=(pl.BlockSpec(memory_space=pltpu.VMEM),) * 4,
        compiler_params=pltpu.CompilerParams(vmem_limit_bytes=16 << 20),
        cost_estimate=pl.CostEstimate(
            flops=2 * 8 * rows * depth * 256, bytes_accessed=2 << 20, transcendentals=0
        ),
    )(weight, *dealt)


def attend_kernel(
    first_head,
    query_block,
    key_same,
    key_other,
    value_same,
    value_other,
    own_rank,
    rows_same,
    rows_other,
    cosines,
    sines,
    *refs,
):
    attended, flat_query, flat_keyval, keys, values = refs[-5:]
    step = pl.program_id(0) + first_head
    rows = query_block.shape[0]
    base = lax.axis_index("ctx") * rows
    half = lax.axis_index("ctx") // PIECES
    seat = lax.rem(lax.axis_index("ctx"), PIECES)
    dot = partial(jnp.dot, preferred_element_type=jnp.float32)

    @pl.when(pl.program_id(0) == 0)
    def _():
        for apart in range(PIECES):
            source = rows_other if apart % 2 else rows_same
            for position in range(2):
                begin = PIECES * rows + (apart // 2 * 2 + position) * UP_ROWS
                piece = source[begin : begin + UP_ROWS, :].astype(jnp.float32)
                place = (seat ^ apart) * 2 + position
                first = pl.multiple_of(place * QUERY_ROWS, QUERY_ROWS)
                flat_query[pl.ds(first, QUERY_ROWS), :] = piece[:QUERY_ROWS]
                first = pl.multiple_of(place * KEYVAL_ROWS, KEYVAL_ROWS)
                for side in range(2):
                    begin = QUERY_ROWS + side * KEYVAL_ROWS
                    flat_keyval[side, pl.ds(first, KEYVAL_ROWS), :] = piece[
                        begin : begin + KEYVAL_ROWS
                    ]

    def turned(delta, cosine, sine):
        return delta * cosine + pltpu.roll(delta, HEAD_SIZE // 2, 1) * sine

    def up(flat, first, stride):
        return flat[pl.ds(first, ADAPTER_RANK, stride=stride), :].astype(jnp.bfloat16)

    for side in range(2):
        heads = 2 * KEYVALUE_HEADS
        key_up = up(flat_keyval.at[side], step, heads)
        value_up = up(flat_keyval.at[side], step + KEYVALUE_HEADS, heads)
        for core in range(2):
            source = rows_other if core else rows_same
            rank = [
                source[(2 * chip + side) * rows : (2 * chip + side + 1) * rows, :]
                for chip in range(PIECES // 2)
            ]
            rank = jnp.concatenate(rank, 0)
            key_delta = adapter_scale * dot(rank[:, :ADAPTER_RANK], key_up)
            value_delta = adapter_scale * dot(rank[:, ADAPTER_RANK:], value_up)
            for chip in range(PIECES // 2):
                there = seat ^ (2 * chip + core)
                first = ((half ^ side) * PIECES + there) * rows
                span = pl.ds(pl.multiple_of(first, rows), rows)
                part = slice(chip * rows, (chip + 1) * rows)
                delta = turned(key_delta[part], cosines[span, :], sines[span, :])
                full = (key_other if core else key_same)[chip, side].astype(jnp.float32) + delta
                keys[span, :] = full.astype(jnp.bfloat16)
                full = (value_other if core else value_same)[chip, side].astype(jnp.float32)
                values[span, :] = (full + value_delta[part]).astype(jnp.bfloat16)
    here = pl.ds(pl.multiple_of(base, rows), rows)
    cosine = cosines[here, :]
    sine = sines[here, :]
    taken = GROUP
    limit = lax.broadcasted_iota(jnp.int32, (rows, 1), 0) + base
    limit = jnp.concatenate([limit] * taken, 0)
    for first in range(0, GROUP, taken):
        weight = [up(flat_query, step * GROUP + first + head, QH) for head in range(taken)]
        deltas = adapter_scale * dot(own_rank[:, :ADAPTER_RANK], jnp.concatenate(weight, 1))
        queries = []
        for place in range(taken):
            moved = turned(deltas[:, place * HEAD_SIZE : (place + 1) * HEAD_SIZE], cosine, sine)
            span = slice((first + place) * HEAD_SIZE, (first + place + 1) * HEAD_SIZE)
            queries.append(
                (query_block[:, span].astype(jnp.float32) + moved).astype(jnp.bfloat16)
            )
        queries = jnp.concatenate(queries, 0)
        scores = lax.dot_general(
            queries, keys[...], (((1,), (1,)), ((), ())), preferred_element_type=jnp.float32
        )
        column = lax.broadcasted_iota(jnp.int32, scores.shape, 1)
        scores = jnp.where(column <= limit, scores, mask_floor)
        scores = scores - jnp.max(scores, axis=-1, keepdims=True)
        weights = jnp.exp(scores * HEAD_SIZE ** (-0.5))
        divisor = jnp.sum(weights, axis=-1, keepdims=True)
        result = (dot(weights.astype(jnp.bfloat16), values[...]) / divisor).astype(jnp.bfloat16)
        for place in range(taken):
            span = slice((first + place) * HEAD_SIZE, (first + place + 1) * HEAD_SIZE)
            attended[:, span] = result[place * rows : (place + 1) * rows]


def attend(first_head, heads, before, query_base, base, own_rank, gathered, cosines, sines):
    rows = query_base.shape[0]
    seq = 4 * PIECES // 2 * rows
    width = GROUP * HEAD_SIZE

    def whole(shape):
        return pl.BlockSpec(shape, lambda h: (0,) * len(shape))

    key_spec = pl.BlockSpec((PIECES // 2, 2, rows, HEAD_SIZE), lambda h: (0, 0, 0, h + first_head))
    value_spec = pl.BlockSpec(
        (PIECES // 2, 2, rows, HEAD_SIZE), lambda h: (0, 0, 0, h + first_head + KEYVALUE_HEADS)
    )
    operands = (query_base, base[0], base[1], base[0], base[1], own_rank, *gathered)
    operands += (cosines, sines) + (() if before is None else (before,))
    query_spec = pl.BlockSpec((rows, width), lambda h: (0, h + first_head))
    return pl.pallas_call(
        partial(attend_kernel, first_head),
        grid=(heads,),
        out_shape=jax.ShapeDtypeStruct((rows, QH * HEAD_SIZE), jnp.bfloat16),
        in_specs=[
            query_spec,
            key_spec,
            key_spec,
            value_spec,
            value_spec,
            whole(own_rank.shape),
            whole(gathered[0].shape),
            whole(gathered[1].shape),
            whole(cosines.shape),
            whole(sines.shape),
        ]
        + [pl.BlockSpec(memory_space=pl.ANY)] * (len(operands) - 10),
        out_specs=query_spec,
        input_output_aliases={} if before is None else {len(operands) - 1: 0},
        scratch_shapes=[
            pltpu.VMEM((2 * PIECES * QUERY_ROWS, 128), jnp.float32),
            pltpu.VMEM((2, 2 * PIECES * KEYVAL_ROWS, 128), jnp.float32),
            pltpu.VMEM((seq, HEAD_SIZE), jnp.bfloat16),
            pltpu.VMEM((seq, HEAD_SIZE), jnp.bfloat16),
        ],
        compiler_params=pltpu.CompilerParams(vmem_limit_bytes=32 << 20),
        cost_estimate=pl.CostEstimate(
            flops=12 * heads * rows * QH * seq * HEAD_SIZE,
            bytes_accessed=10 << 20,
            transcendentals=heads * rows * GROUP * seq,
        ),
    )(*operands)


def widen_kernel(attended, same, other, out_delta, down_out, up_out):
    plane = lax.axis_index("groups")
    seat = lax.rem(lax.axis_index("ctx"), PIECES)
    for apart in range(PIECES):
        pieces = other if apart % 2 else same
        for position in range(2):
            piece = pieces[apart // 2, position].astype(jnp.float32)
            place = (seat ^ apart) * 2 + (position ^ plane)
            first = place * 2 * DOWN_OUT_ROWS
            block = piece[:DOWN_OUT_ROWS]
            down_out[pl.ds(first, DOWN_OUT_ROWS, stride=2), :] = block
            down_out[pl.ds(first + 1, DOWN_OUT_ROWS, stride=2), :] = pltpu.roll(block, 64, 1)
            first = pl.multiple_of(place * UP_OUT_ROWS, UP_OUT_ROWS)
            up_out[pl.ds(first, UP_OUT_ROWS), :] = piece[DOWN_OUT_ROWS:]
    dot = partial(jnp.dot, preferred_element_type=jnp.float32)
    rank = dot(attended[...], down_out[...].astype(jnp.bfloat16))[:, :ADAPTER_RANK]
    rank = rank.astype(jnp.bfloat16)
    blocks = D // 128
    for first in range(0, blocks, 4):
        weight = [
            up_out[pl.ds(first + block, ADAPTER_RANK, stride=blocks), :].astype(jnp.bfloat16)
            for block in range(4)
        ]
        delta = adapter_scale * dot(rank, jnp.concatenate(weight, 1))
        out_delta[:, first * 128 : (first + 4) * 128] = delta.astype(jnp.bfloat16)


def widen(attended, same, other):
    return pl.pallas_call(
        widen_kernel,
        out_shape=jax.ShapeDtypeStruct((attended.shape[0], D), jnp.bfloat16),
        in_specs=[pl.BlockSpec(memory_space=pltpu.VMEM)] * 3,
        out_specs=pl.BlockSpec(memory_space=pltpu.VMEM),
        scratch_shapes=[
            pltpu.VMEM((QH * HEAD_SIZE, 128), jnp.float32),
            pltpu.VMEM((ADAPTER_RANK * D // 128, 128), jnp.float32),
        ],
        compiler_params=pltpu.CompilerParams(vmem_limit_bytes=32 << 20),
        cost_estimate=pl.CostEstimate(flops=1 << 27, bytes_accessed=4 << 20, transcendentals=0),
    )(attended, same, other)


def swap(block, mask):
    return lax.ppermute(block, ("groups", "ctx"), [(i, i ^ mask) for i in range(4 * PIECES)])


def direct_shards(
    normed_input, query_base, key_base, value_base, adapter_pool, stretch_adapter, adapter_owner
):
    tok_rows = normed_input.shape[0]
    ctx = lax.axis_size("ctx")
    seq = ctx * tok_rows
    blocks = [list(range(PIECES)), list(range(PIECES, 2 * PIECES))]
    half_dim = HEAD_SIZE // 2
    frequency = rope_base ** (-(jnp.arange(half_dim, dtype=jnp.float32) * 2.0) / HEAD_SIZE)
    angle = jnp.arange(seq, dtype=jnp.int32).astype(jnp.float32)[:, None] * frequency[None, :]
    cosine = jnp.cos(angle)
    sine = jnp.sin(angle)
    cosines = jnp.concatenate([cosine, cosine], 1)
    sines = jnp.concatenate([-sine, sine], 1)

    def after(block, *others):
        return lax.optimization_barrier((block, others))[0]

    def exchange(sent):
        across = swap(sent[2], 2 * PIECES)
        return [sent[0], swap(sent[1], PIECES), across, swap(sent[3], 3 * PIECES)]

    def along_z(block):
        return jnp.stack([block, swap(block, 4)])

    def along_x(pair):
        quad = jnp.stack([pair, swap(pair, 2)], 1)
        return quad.reshape((PIECES // 2,) + pair.shape[1:])

    elsewhere = swap(stretch_adapter, 2 * PIECES)
    packed = pack_row(adapter_pool, SECTIONS)
    even, odd = deal(normed_input, packed)
    sibling = swap(odd, 1)
    base = jnp.concatenate([key_base, value_base], 1)
    base = jnp.stack([base, swap(base, PIECES)])

    spread = lax.all_to_all(packed, "ctx", 0, 0, axis_index_groups=blocks)
    spread = after(spread, sibling, base, cosines, sines)
    sent, near, far = pick(spread, stretch_adapter, elsewhere, adapter_owner)
    arrived = exchange(sent)
    dealt = [after(jnp.stack([even[j], sibling[j]]), sent) for j in range(PIECES // 2)]
    dealt = [swap(block, 2 * j) if j else block for j, block in enumerate(dealt)]

    weight, ups = join(stretch_adapter, adapter_owner, arrived)
    far = swap(after(far, weight), PIECES)
    partial_sums = narrow(weight, dealt)
    back = [swap(block, 2 * j) if j else block for j, block in enumerate(partial_sums)]
    back = after(back, far)
    back = sum(block.astype(jnp.float32) for block in back)
    base = after(base, *partial_sums)
    base = [base, swap(base, 2), swap(base, 4)]
    own_rank = swap(after(back[1].astype(jnp.bfloat16), *base), 1)
    own_rank = back[0] + own_rank.astype(jnp.float32)
    own_rank = own_rank.astype(jnp.bfloat16)
    ups = along_z(after(ups, *partial_sums))
    all_rank = own_rank[:, ADAPTER_RANK:]
    base = jnp.stack(base + [swap(after(base[2], own_rank), 2)])
    own, across = settle(
        stretch_adapter, elsewhere, adapter_owner, near, after(far, own_rank)
    )
    ends = jnp.stack([own, swap(across, 2 * PIECES)])
    all_rank = jnp.stack([all_rank, swap(all_rank, PIECES)])
    all_rank = after(all_rank, ups)
    ups = along_x(after(ups, all_rank))
    all_rank = jnp.stack([swap(all_rank, apart) if apart else all_rank for apart in (0, 2, 4, 6)])
    base = after(base, all_rank)
    base = (base, swap(base, 1))
    gathered = jnp.concatenate([all_rank.reshape(-1, 128), ups.reshape(-1, 128)])
    gathered = after(gathered, ends)
    gathered = (gathered, swap(gathered, 1))

    shared = (query_base, base, own_rank, gathered, cosines, sines)
    attended = attend(0, 1, None, *shared)
    ends = after(ends, attended)
    ends = jnp.stack([swap(ends, apart) if apart else ends for apart in (0, 2, 4, 6)])
    attended = attend(1, KEYVALUE_HEADS - 1, attended, *shared)
    ends = after(ends, attended)
    return attended, widen(attended, ends, swap(ends, 1))


def shards(normed_input, query_base, key_base, value_base, adapter_pool, stretch_adapter, owner):
    fits = (
        lax.axis_size("groups") == 2
        and lax.axis_size("ctx") == 2 * PIECES
        and normed_input.shape[0] * PIECES == BLOCK_TOKENS
        and adapter_pool.shape[0] == 1
    )
    plan = direct_shards if fits else spread_shards
    return plan(
        normed_input, query_base, key_base, value_base, adapter_pool, stretch_adapter, owner
    )


def solution(mesh):
    placed = (
        P(("groups", "ctx"), None),
        P(("groups", "ctx"), None),
        P(("groups", "ctx"), None),
        P(("groups", "ctx"), None),
        P("ctx", None),
        P("groups"),
        P(),
    )
    return jax.shard_map(
        shards,
        mesh=mesh,
        in_specs=placed,
        out_specs=(P(("groups", "ctx"), None), P(("groups", "ctx"), None)),
        check_vma=False,
    )
```

```python
from functools import partial
import math

import jax
import jax.numpy as jnp
from jax import lax
from jax.experimental import pallas as pl
from jax.experimental.pallas import tpu as pltpu
from jax.sharding import PartitionSpec as P

D = 8192
QH = 32
KEYVALUE_HEADS = 4
HEAD_SIZE = 128
ADAPTER_RANK = 64
BLOCK_TOKENS = 512
QKV_POOL = 1900544


adapter_scale = 2.0
rope_base = 500000.0
mask_floor = -1e30


def from_partner(block, axis, apart):
    count = lax.axis_size(axis)
    route = []
    for low in range(count):
        high = low | 1 << apart
        if high != low and high < count:
            route += [(low, high), (high, low)]
    return lax.ppermute(block, axis, route)


def rotate(delta, token_positions, heads):
    half_dim = HEAD_SIZE // 2
    frequency = rope_base ** (-(jnp.arange(half_dim, dtype=jnp.float32) * 2.0) / HEAD_SIZE)
    angle = token_positions.astype(jnp.float32)[:, None] * frequency[None, :]
    cosine = jnp.cos(angle)[:, None, :]
    sine_part = jnp.sin(angle)[:, None, :]
    shaped = delta.reshape(delta.shape[0], heads, HEAD_SIZE)
    first_half = shaped[..., :half_dim]
    second_half = shaped[..., half_dim:]
    joined = jnp.concatenate(
        [
            first_half * cosine - second_half * sine_part,
            second_half * cosine + first_half * sine_part,
        ],
        -1,
    )
    return joined.reshape(delta.shape[0], heads * HEAD_SIZE)


def project_heads(
    narrow_product, query_row_block, key_row_block, value_row_block, upper_part, token_positions
):
    query_up_weight = upper_part[: ADAPTER_RANK * QH * HEAD_SIZE].reshape(
        ADAPTER_RANK, QH * HEAD_SIZE
    )
    keyvalue_up_weight = upper_part[ADAPTER_RANK * QH * HEAD_SIZE :].reshape(
        ADAPTER_RANK, 2 * KEYVALUE_HEADS * HEAD_SIZE
    )
    query_correction = adapter_scale * jnp.dot(
        narrow_product[:, :ADAPTER_RANK], query_up_weight, preferred_element_type=jnp.float32
    )
    key_correction = adapter_scale * jnp.dot(
        narrow_product[:, ADAPTER_RANK : 2 * ADAPTER_RANK],
        keyvalue_up_weight[:, : KEYVALUE_HEADS * HEAD_SIZE],
        preferred_element_type=jnp.float32,
    )
    value_correction = adapter_scale * jnp.dot(
        narrow_product[:, 2 * ADAPTER_RANK :],
        keyvalue_up_weight[:, KEYVALUE_HEADS * HEAD_SIZE :],
        preferred_element_type=jnp.float32,
    )
    queries = (
        query_row_block.astype(jnp.float32) + rotate(query_correction, token_positions, QH)
    ).astype(jnp.bfloat16)
    new_keys = (
        key_row_block.astype(jnp.float32) + rotate(key_correction, token_positions, KEYVALUE_HEADS)
    ).astype(jnp.bfloat16)
    new_values = (value_row_block.astype(jnp.float32) + value_correction).astype(jnp.bfloat16)
    return (queries, new_keys, new_values)


def output_delta(attended_rows, out_part):
    down_out = out_part[: QH * HEAD_SIZE * ADAPTER_RANK].reshape(QH * HEAD_SIZE, ADAPTER_RANK)
    raised_output = out_part[QH * HEAD_SIZE * ADAPTER_RANK :].reshape(ADAPTER_RANK, D)
    narrow_product = jnp.dot(attended_rows, down_out, preferred_element_type=jnp.float32).astype(
        jnp.bfloat16
    )
    return (
        adapter_scale * jnp.dot(narrow_product, raised_output, preferred_element_type=jnp.float32)
    ).astype(jnp.bfloat16)


def head_major(query_row_block):
    count_rows = query_row_block.shape[0]
    group_size = QH // KEYVALUE_HEADS
    return (
        query_row_block.reshape(count_rows, KEYVALUE_HEADS, group_size, HEAD_SIZE)
        .transpose(1, 2, 0, 3)
        .reshape(KEYVALUE_HEADS, group_size * count_rows, HEAD_SIZE)
    )


def row_major(head_rows, count_rows):
    group_size = QH // KEYVALUE_HEADS
    return (
        head_rows.reshape(KEYVALUE_HEADS, group_size, count_rows, HEAD_SIZE)
        .transpose(2, 0, 1, 3)
        .reshape(count_rows, QH * HEAD_SIZE)
    )


def online_update(current, queries, query_pos, key_slice, value_slice, key_start):
    run_max, run_sum, run_acc = current
    scores = jnp.einsum(
        "hqd,khd->hqk", queries, key_slice, preferred_element_type=jnp.float32
    ) * HEAD_SIZE ** (-0.5)
    key_pos = key_start + jnp.arange(key_slice.shape[0], dtype=jnp.int32)
    allowed = (query_pos[:, None] >= key_pos[None, :])[None]
    new_max = jnp.maximum(run_max, jnp.max(jnp.where(allowed, scores, mask_floor), axis=-1))
    weights = jnp.where(allowed, jnp.exp(scores - new_max[..., None]), 0.0)
    rescale = jnp.exp(run_max - new_max)
    new_sum = run_sum * rescale + jnp.sum(weights, axis=-1)
    new_acc = run_acc * rescale[..., None] + jnp.einsum(
        "hqk,khd->hqd",
        weights.astype(jnp.bfloat16),
        value_slice,
        preferred_element_type=jnp.float32,
    )
    return (new_max, new_sum, new_acc)


def unchanged(current):
    return current


def fold_keys(carry_state, shard_part, prepared):
    key_row_block, value_row_block = shard_part
    key_count = key_row_block.shape[0]
    sub_width = math.gcd(key_count, 1024)
    key_heads = key_row_block.reshape(key_count // sub_width, sub_width, KEYVALUE_HEADS, HEAD_SIZE)
    value_heads = value_row_block.reshape(
        key_count // sub_width, sub_width, KEYVALUE_HEADS, HEAD_SIZE
    )

    def one_step(sub_index, carried):
        key_start = sub_index * sub_width
        key_slice = lax.dynamic_index_in_dim(key_heads, sub_index, 0, keepdims=False)
        value_slice = lax.dynamic_index_in_dim(value_heads, sub_index, 0, keepdims=False)
        updated = []
        for (queries, query_pos), running in zip(prepared, carried):
            advance = partial(
                online_update,
                queries=queries,
                query_pos=query_pos,
                key_slice=key_slice,
                value_slice=value_slice,
                key_start=key_start,
            )
            updated.append(lax.cond(key_start <= jnp.max(query_pos), advance, unchanged, running))
        return tuple(updated)

    return lax.fori_loop(0, key_count // sub_width, one_step, carry_state)


def finish_block(result, count_rows):
    run_max, run_sum, run_acc = result
    divisor = jnp.where(run_sum > 0.0, run_sum, 1.0)
    return row_major(run_acc / divisor[..., None], count_rows).astype(jnp.bfloat16)


def spread_shards(
    normed_input, query_base, key_base, value_base, adapter_pool, stretch_adapter, adapter_owner
):
    cycle_size = lax.axis_size("ctx")
    my_index = lax.axis_index("ctx")
    tok_rows = normed_input.shape[0]
    token_positions = my_index * tok_rows + jnp.arange(tok_rows, dtype=jnp.int32)
    device_ids = jnp.arange(cycle_size, dtype=jnp.int32)
    stretch_of = device_ids * tok_rows // BLOCK_TOKENS
    stretch_ids = jnp.arange(stretch_adapter.shape[0], dtype=jnp.int32)
    adapter_of = jnp.sum(
        jnp.where(stretch_of[:, None] == stretch_ids[None, :], stretch_adapter[None, :], 0), axis=1
    )
    adapter_ids = jnp.arange(adapter_owner.shape[0], dtype=jnp.int32)
    slot_of = jnp.sum(
        jnp.where(adapter_of[:, None] == adapter_ids[None, :], adapter_owner[None, :], 0), axis=1
    )
    down_size = 3 * ADAPTER_RANK * D
    group_count = BLOCK_TOKENS // tok_rows
    levels = group_count.bit_length() - 1
    local_index = my_index % group_count
    col_width = D // group_count
    piece_len = down_size // (group_count * cycle_size)
    pool_rows = adapter_pool.shape[0]
    down_shaped = adapter_pool[:, :down_size].reshape(pool_rows, group_count, cycle_size, piece_len)
    spread_down = lax.all_to_all(down_shaped, "ctx", split_axis=2, concat_axis=0, tiled=True)
    flat_down = spread_down.reshape(-1, piece_len)
    wanted = jnp.take(flat_down, slot_of * group_count + device_ids % group_count, axis=0)[
        :, None, :
    ]
    down_slice = lax.all_to_all(wanted, "ctx", split_axis=0, concat_axis=1, tiled=True).reshape(
        col_width, 3 * ADAPTER_RANK
    )
    spread_rest = lax.all_to_all(
        adapter_pool[:, down_size:], "ctx", split_axis=1, concat_axis=0, tiled=True
    )
    rest_row = lax.all_to_all(
        jnp.take(spread_rest, slot_of, axis=0), "ctx", split_axis=0, concat_axis=1, tiled=True
    )[0]
    upper_part = rest_row[: QKV_POOL - down_size]
    out_part = rest_row[QKV_POOL - down_size :]
    pieces = normed_input.reshape(tok_rows, group_count, col_width)
    slice_order = jnp.bitwise_xor(local_index, jnp.arange(group_count, dtype=jnp.int32))
    moving = jnp.take(pieces, slice_order, axis=1).transpose(1, 0, 2)
    for level in range(levels):
        shaped = moving.reshape(group_count >> level + 1, 2, 1 << level, tok_rows, col_width)
        arrived = from_partner(shaped[:, 1], "ctx", level)
        moving = jnp.stack([shaped[:, 0], arrived], 1).reshape(group_count, tok_rows, col_width)
    partial_rows = jnp.dot(
        moving.reshape(group_count * tok_rows, col_width),
        down_slice,
        preferred_element_type=jnp.float32,
    ).reshape(group_count, tok_rows, 3 * ADAPTER_RANK)
    for level in reversed(range(levels)):
        halves = partial_rows.reshape(2, partial_rows.shape[0] // 2, tok_rows, 3 * ADAPTER_RANK)
        partial_rows = halves[0] + from_partner(
            halves[1].astype(jnp.bfloat16), "ctx", level
        ).astype(jnp.float32)
    narrow_product = partial_rows[0].astype(jnp.bfloat16)
    queries, new_keys, new_values = project_heads(
        narrow_product, query_base, key_base, value_base, upper_part, token_positions
    )
    group_size = QH // KEYVALUE_HEADS
    blocks = [(queries, token_positions)]
    prepared = [
        (head_major(block_q), jnp.tile(block_pos, group_size)) for block_q, block_pos in blocks
    ]
    initial = tuple(
        (
            (
                jnp.full((KEYVALUE_HEADS, head_q.shape[1]), mask_floor, jnp.float32),
                jnp.zeros((KEYVALUE_HEADS, head_q.shape[1]), jnp.float32),
                jnp.zeros((KEYVALUE_HEADS, head_q.shape[1], HEAD_SIZE), jnp.float32),
            )
            for head_q, block_pos in prepared
        )
    )
    finals = fold_keys(
        initial,
        (
            lax.all_gather(new_keys, "ctx", axis=0, tiled=True),
            lax.all_gather(new_values, "ctx", axis=0, tiled=True),
        ),
        prepared,
    )
    attended = finish_block(finals[0], tok_rows)
    out_delta = output_delta(attended, out_part)
    return (attended, out_delta)


PIECES = 8
GROUP = QH // KEYVALUE_HEADS
SECTIONS = ((0, 12288), (12288, 2048), (14336, 512), (14848, 2048), (16896, 4096))
DOWN_ROWS, QUERY_ROWS, KEYVAL_ROWS, DOWN_OUT_ROWS, UP_OUT_ROWS = 768, 128, 32, 128, 256
UP_ROWS = QUERY_ROWS + 2 * KEYVAL_ROWS
FIRST_ROWS = DOWN_ROWS + QUERY_ROWS + KEYVAL_ROWS


def pack_kernel(sections, pool, *refs):
    out, buffers, sems = refs[-3:]
    plane = lax.axis_index("groups")
    slabs, slab_rows = out.shape[:2]

    def copies(slab):
        listed = []
        offset = 0
        for first, rows in sections:
            share = rows // (2 * PIECES)
            begin = first + (slab * 2 + plane) * share
            listed.append(
                pltpu.make_async_copy(
                    pool.at[:, pl.ds(pl.multiple_of(begin * 128, 2048), share * 128)],
                    buffers.at[slab, :, pl.ds(offset, share * 128)],
                    sems.at[slab, len(listed)],
                )
            )
            offset += share * 128
        return listed

    for slab in range(slabs):
        for copy in copies(slab):
            copy.start()

    def step(slab, carried):
        for copy in copies(slab):
            copy.wait()

        def chunk(index, inner):
            line = buffers[slab, :, pl.ds(pl.multiple_of(index * 2048, 2048), 2048)]
            block = line.astype(jnp.float32).reshape(16, 128).astype(jnp.bfloat16)
            out[slab, pl.ds(pl.multiple_of(index * 16, 16), 16), :] = block
            return inner

        lax.fori_loop(0, slab_rows // 16, chunk, 0, unroll=8)
        return carried

    lax.fori_loop(0, slabs, step, 0)


def pack_row(pool, sections, *after):
    slab_rows = sum(rows for _, rows in sections) // (2 * PIECES)
    return pl.pallas_call(
        partial(pack_kernel, sections),
        out_shape=jax.ShapeDtypeStruct((PIECES, slab_rows, 128), jnp.bfloat16),
        in_specs=[pl.BlockSpec(memory_space=pl.ANY)] * (1 + len(after)),
        out_specs=pl.BlockSpec(memory_space=pltpu.VMEM),
        scratch_shapes=[
            pltpu.VMEM((PIECES, 1, slab_rows * 128), jnp.bfloat16),
            pltpu.SemaphoreType.DMA((PIECES, len(sections))),
        ],
        compiler_params=pltpu.CompilerParams(vmem_limit_bytes=60 << 20),
        cost_estimate=pl.CostEstimate(flops=0, bytes_accessed=8 << 20, transcendentals=0),
    )(pool, *after)


def pick_kernel(here, there, owner, spread, *refs):
    outs, lasts, sems = refs[:4], refs[4:6], refs[6]
    half = lax.axis_index("ctx") // PIECES
    last = spread.shape[1] - FIRST_ROWS
    copies = []
    for flip, out in enumerate(outs):
        wishes = there if flip >= 2 else here
        block = half ^ (flip & 1)
        row = lax.rem(owner[wishes[block]], PIECES)
        mirrored = lax.rem(owner[wishes[1 - block]], PIECES)
        pairs = (
            (spread.at[row, pl.ds(0, FIRST_ROWS)], out.at[pl.ds(0, FIRST_ROWS)]),
            (
                spread.at[mirrored, pl.ds(FIRST_ROWS - KEYVAL_ROWS, KEYVAL_ROWS)],
                out.at[pl.ds(FIRST_ROWS, KEYVAL_ROWS)],
            ),
            (spread.at[row, pl.ds(FIRST_ROWS, last)], lasts[flip % 2].at[flip // 2]),
        )
        for number, (source, target) in enumerate(pairs):
            copies.append(pltpu.make_async_copy(source, target, sems.at[flip, number]))
    for copy in copies:
        copy.start()
    for copy in copies:
        copy.wait()


def pick(spread, here, there, owner):
    last = spread.shape[1] - FIRST_ROWS
    first_shape = jax.ShapeDtypeStruct((FIRST_ROWS + KEYVAL_ROWS, 128), jnp.bfloat16)
    last_shape = jax.ShapeDtypeStruct((2, last, 128), jnp.bfloat16)
    outs = pl.pallas_call(
        pick_kernel,
        out_shape=(first_shape,) * 4 + (last_shape,) * 2,
        in_specs=[pl.BlockSpec(memory_space=pltpu.SMEM)] * 3 + [pl.BlockSpec(memory_space=pl.ANY)],
        out_specs=(pl.BlockSpec(memory_space=pltpu.VMEM),) * 6,
        scratch_shapes=[pltpu.SemaphoreType.DMA((4, 3))],
        compiler_params=pltpu.CompilerParams(vmem_limit_bytes=16 << 20),
        cost_estimate=pl.CostEstimate(flops=0, bytes_accessed=3 << 20, transcendentals=0),
    )(here, there, owner, spread)
    return outs[:4], outs[4], outs[5]


def deal_kernel(rows, even, odd, sems):
    seat = lax.rem(lax.axis_index("ctx"), PIECES)
    width = rows.shape[1] // PIECES
    copies = []
    for apart in range(PIECES):
        first = pl.multiple_of((seat ^ apart) * width, width)
        target = (odd if apart % 2 else even).at[apart // 2]
        copies.append(
            pltpu.make_async_copy(rows.at[:, pl.ds(first, width)], target, sems.at[apart])
        )
    for copy in copies:
        copy.start()
    for copy in copies:
        copy.wait()


def deal(rows, *after):
    slab = jax.ShapeDtypeStruct((PIECES // 2, rows.shape[0], rows.shape[1] // PIECES), rows.dtype)

    def kernel(rows, *refs):
        deal_kernel(rows, *refs[-3:])

    return pl.pallas_call(
        kernel,
        out_shape=(slab, slab),
        in_specs=[pl.BlockSpec(memory_space=pl.ANY)] * (1 + len(after)),
        out_specs=(pl.BlockSpec(memory_space=pltpu.VMEM),) * 2,
        scratch_shapes=[pltpu.SemaphoreType.DMA((PIECES,))],
        compiler_params=pltpu.CompilerParams(vmem_limit_bytes=16 << 20),
        cost_estimate=pl.CostEstimate(flops=0, bytes_accessed=2 << 20, transcendentals=0),
    )(rows, *after)


def nearest(here, owner, block):
    half = lax.axis_index("ctx") // PIECES
    return owner[here[block]] // PIECES == half


def choose(close, arrived, put):
    plane = lax.axis_index("groups")

    @pl.when(close)
    def _():
        put(arrived[0], plane)
        put(arrived[2], 1 - plane)

    @pl.when(jnp.logical_not(close))
    def _():
        put(arrived[1], plane)
        put(arrived[3], 1 - plane)


def join_kernel(here, owner, *refs):
    (across, own, mirror, both), (weight, ups), (flat, left, right) = refs[:4], refs[4:6], refs[6:]
    arrived = (own, mirror, across, both)
    half = lax.axis_index("ctx") // PIECES
    split = DOWN_ROWS + QUERY_ROWS + KEYVAL_ROWS

    def put_own(source, position):
        first = pl.multiple_of(position * DOWN_ROWS, DOWN_ROWS)
        flat[pl.ds(first, DOWN_ROWS), :] = source[:DOWN_ROWS, :].astype(jnp.float32)
        ups[position, : UP_ROWS - KEYVAL_ROWS, :] = source[DOWN_ROWS:split, :]

    def put_mirrored(source, position):
        ups[position, UP_ROWS - KEYVAL_ROWS :, :] = source[split:, :]

    choose(nearest(here, owner, half), arrived, put_own)
    choose(nearest(here, owner, 1 - half), arrived, put_mirrored)

    third = flat.shape[0] // 3
    one = flat[pl.ds(0, third, stride=3), :]
    two = pltpu.roll(flat[pl.ds(1, third, stride=3), :], 64, 1)
    three = pltpu.roll(flat[pl.ds(2, third, stride=3), :], 64, 1)
    lane = lax.broadcasted_iota(jnp.int32, one.shape, 1)
    left[pl.ds(0, third, stride=2), :] = one
    left[pl.ds(1, third, stride=2), :] = jnp.where(lane < 64, two, three)
    right[pl.ds(0, third, stride=2), :] = pltpu.roll(two, 64, 1)
    right[pl.ds(1, third, stride=2), :] = three
    weight[...] = jnp.concatenate([left[...], right[...]], 1).astype(jnp.bfloat16)


def join(here, owner, arrived):
    depth = D // PIECES
    return pl.pallas_call(
        join_kernel,
        out_shape=(
            jax.ShapeDtypeStruct((depth, 256), jnp.bfloat16),
            jax.ShapeDtypeStruct((2, UP_ROWS, 128), jnp.bfloat16),
        ),
        in_specs=[pl.BlockSpec(memory_space=pltpu.SMEM)] * 2
        + [pl.BlockSpec(memory_space=pltpu.VMEM)] * 4,
        out_specs=(pl.BlockSpec(memory_space=pltpu.VMEM),) * 2,
        scratch_shapes=[
            pltpu.VMEM((2 * DOWN_ROWS, 128), jnp.float32),
            pltpu.VMEM((depth, 128), jnp.float32),
            pltpu.VMEM((depth, 128), jnp.float32),
        ],
        compiler_params=pltpu.CompilerParams(vmem_limit_bytes=16 << 20),
        cost_estimate=pl.CostEstimate(flops=0, bytes_accessed=96 << 20, transcendentals=0),
    )(here, owner, arrived[2], arrived[0], arrived[1], arrived[3])


def settle_kernel(here, there, owner, near, far, own, across):
    half = lax.axis_index("ctx") // PIECES
    for number, (wishes, out) in enumerate(((here, own), (there, across))):
        close = nearest(wishes, owner, half)

        @pl.when(close)
        def _():
            out[...] = near[number]

        @pl.when(jnp.logical_not(close))
        def _():
            out[...] = far[number]


def settle(here, there, owner, near, far):
    slab = jax.ShapeDtypeStruct(near.shape[1:], jnp.bfloat16)
    return pl.pallas_call(
        settle_kernel,
        out_shape=(slab, slab),
        in_specs=[pl.BlockSpec(memory_space=pltpu.SMEM)] * 3
        + [pl.BlockSpec(memory_space=pltpu.VMEM)] * 2,
        out_specs=(pl.BlockSpec(memory_space=pltpu.VMEM),) * 2,
        compiler_params=pltpu.CompilerParams(vmem_limit_bytes=16 << 20),
        cost_estimate=pl.CostEstimate(flops=0, bytes_accessed=1 << 20, transcendentals=0),
    )(here, there, owner, near, far)


def narrow_kernel(weight, *refs):
    for block, out in zip(refs[:4], refs[4:]):
        sides, rows, depth = block.shape
        product = jnp.dot(
            block[...].reshape(sides * rows, depth),
            weight[...],
            preferred_element_type=jnp.float32,
        )
        out[...] = product[:, : 3 * ADAPTER_RANK].reshape(out.shape).astype(jnp.bfloat16)


def narrow(weight, dealt):
    sides, rows, depth = dealt[0].shape
    partial_sums = jax.ShapeDtypeStruct((sides, rows, 3 * ADAPTER_RANK), jnp.bfloat16)
    return pl.pallas_call(
        narrow_kernel,
        out_shape=(partial_sums,) * 4,
        in_specs=[pl.BlockSpec(memory_space=pltpu.VMEM)] * 5,
        out_specs=(pl.BlockSpec(memory_space=pltpu.VMEM),) * 4,
        compiler_params=pltpu.CompilerParams(vmem_limit_bytes=16 << 20),
        cost_estimate=pl.CostEstimate(
            flops=2 * 8 * rows * depth * 256, bytes_accessed=2 << 20, transcendentals=0
        ),
    )(weight, *dealt)


def attend_kernel(
    first_head,
    query_block,
    key_same,
    key_other,
    value_same,
    value_other,
    own_rank,
    rows_same,
    rows_other,
    cosines,
    sines,
    *refs,
):
    attended, flat_query, flat_keyval, keys, values = refs[-5:]
    step = pl.program_id(0) + first_head
    rows = query_block.shape[0]
    base = lax.axis_index("ctx") * rows
    half = lax.axis_index("ctx") // PIECES
    seat = lax.rem(lax.axis_index("ctx"), PIECES)
    dot = partial(jnp.dot, preferred_element_type=jnp.float32)

    @pl.when(pl.program_id(0) == 0)
    def _():
        for apart in range(PIECES):
            source = rows_other if apart % 2 else rows_same
            for position in range(2):
                begin = PIECES * rows + (apart // 2 * 2 + position) * UP_ROWS
                piece = source[begin : begin + UP_ROWS, :].astype(jnp.float32)
                place = (seat ^ apart) * 2 + position
                first = pl.multiple_of(place * QUERY_ROWS, QUERY_ROWS)
                flat_query[pl.ds(first, QUERY_ROWS), :] = piece[:QUERY_ROWS]
                first = pl.multiple_of(place * KEYVAL_ROWS, KEYVAL_ROWS)
                for side in range(2):
                    begin = QUERY_ROWS + side * KEYVAL_ROWS
                    flat_keyval[side, pl.ds(first, KEYVAL_ROWS), :] = piece[
                        begin : begin + KEYVAL_ROWS
                    ]

    def turned(delta, cosine, sine):
        return delta * cosine + pltpu.roll(delta, HEAD_SIZE // 2, 1) * sine

    def up(flat, first, stride):
        return flat[pl.ds(first, ADAPTER_RANK, stride=stride), :].astype(jnp.bfloat16)

    for side in range(2):
        heads = 2 * KEYVALUE_HEADS
        key_up = up(flat_keyval.at[side], step, heads)
        value_up = up(flat_keyval.at[side], step + KEYVALUE_HEADS, heads)
        for core in range(2):
            source = rows_other if core else rows_same
            rank = [
                source[(2 * chip + side) * rows : (2 * chip + side + 1) * rows, :]
                for chip in range(PIECES // 2)
            ]
            rank = jnp.concatenate(rank, 0)
            key_delta = adapter_scale * dot(rank[:, :ADAPTER_RANK], key_up)
            value_delta = adapter_scale * dot(rank[:, ADAPTER_RANK:], value_up)
            for chip in range(PIECES // 2):
                there = seat ^ (2 * chip + core)
                first = ((half ^ side) * PIECES + there) * rows
                span = pl.ds(pl.multiple_of(first, rows), rows)
                part = slice(chip * rows, (chip + 1) * rows)
                delta = turned(key_delta[part], cosines[span, :], sines[span, :])
                full = (key_other if core else key_same)[chip, side].astype(jnp.float32) + delta
                keys[span, :] = full.astype(jnp.bfloat16)
                full = (value_other if core else value_same)[chip, side].astype(jnp.float32)
                values[span, :] = (full + value_delta[part]).astype(jnp.bfloat16)
    here = pl.ds(pl.multiple_of(base, rows), rows)
    cosine = cosines[here, :]
    sine = sines[here, :]
    taken = GROUP
    limit = lax.broadcasted_iota(jnp.int32, (rows, 1), 0) + base
    limit = jnp.concatenate([limit] * taken, 0)
    for first in range(0, GROUP, taken):
        weight = [up(flat_query, step * GROUP + first + head, QH) for head in range(taken)]
        deltas = adapter_scale * dot(own_rank[:, :ADAPTER_RANK], jnp.concatenate(weight, 1))
        queries = []
        for place in range(taken):
            moved = turned(deltas[:, place * HEAD_SIZE : (place + 1) * HEAD_SIZE], cosine, sine)
            span = slice((first + place) * HEAD_SIZE, (first + place + 1) * HEAD_SIZE)
            queries.append(
                (query_block[:, span].astype(jnp.float32) + moved).astype(jnp.bfloat16)
            )
        queries = jnp.concatenate(queries, 0)
        scores = lax.dot_general(
            queries, keys[...], (((1,), (1,)), ((), ())), preferred_element_type=jnp.float32
        )
        column = lax.broadcasted_iota(jnp.int32, scores.shape, 1)
        scores = jnp.where(column <= limit, scores, mask_floor)
        scores = scores - jnp.max(scores, axis=-1, keepdims=True)
        weights = jnp.exp(scores * HEAD_SIZE ** (-0.5))
        divisor = jnp.sum(weights, axis=-1, keepdims=True)
        result = (dot(weights.astype(jnp.bfloat16), values[...]) / divisor).astype(jnp.bfloat16)
        for place in range(taken):
            span = slice((first + place) * HEAD_SIZE, (first + place + 1) * HEAD_SIZE)
            attended[:, span] = result[place * rows : (place + 1) * rows]


def attend(first_head, heads, before, query_base, base, own_rank, gathered, cosines, sines):
    rows = query_base.shape[0]
    seq = 4 * PIECES // 2 * rows
    width = GROUP * HEAD_SIZE

    def whole(shape):
        return pl.BlockSpec(shape, lambda h: (0,) * len(shape))

    key_spec = pl.BlockSpec((PIECES // 2, 2, rows, HEAD_SIZE), lambda h: (0, 0, 0, h + first_head))
    value_spec = pl.BlockSpec(
        (PIECES // 2, 2, rows, HEAD_SIZE), lambda h: (0, 0, 0, h + first_head + KEYVALUE_HEADS)
    )
    operands = (query_base, base[0], base[1], base[0], base[1], own_rank, *gathered)
    operands += (cosines, sines) + (() if before is None else (before,))
    query_spec = pl.BlockSpec((rows, width), lambda h: (0, h + first_head))
    return pl.pallas_call(
        partial(attend_kernel, first_head),
        grid=(heads,),
        out_shape=jax.ShapeDtypeStruct((rows, QH * HEAD_SIZE), jnp.bfloat16),
        in_specs=[
            query_spec,
            key_spec,
            key_spec,
            value_spec,
            value_spec,
            whole(own_rank.shape),
            whole(gathered[0].shape),
            whole(gathered[1].shape),
            whole(cosines.shape),
            whole(sines.shape),
        ]
        + [pl.BlockSpec(memory_space=pl.ANY)] * (len(operands) - 10),
        out_specs=query_spec,
        input_output_aliases={} if before is None else {len(operands) - 1: 0},
        scratch_shapes=[
            pltpu.VMEM((2 * PIECES * QUERY_ROWS, 128), jnp.float32),
            pltpu.VMEM((2, 2 * PIECES * KEYVAL_ROWS, 128), jnp.float32),
            pltpu.VMEM((seq, HEAD_SIZE), jnp.bfloat16),
            pltpu.VMEM((seq, HEAD_SIZE), jnp.bfloat16),
        ],
        compiler_params=pltpu.CompilerParams(vmem_limit_bytes=32 << 20),
        cost_estimate=pl.CostEstimate(
            flops=12 * heads * rows * QH * seq * HEAD_SIZE,
            bytes_accessed=10 << 20,
            transcendentals=heads * rows * GROUP * seq,
        ),
    )(*operands)


def widen_kernel(attended, same, other, out_delta, down_out, up_out):
    plane = lax.axis_index("groups")
    seat = lax.rem(lax.axis_index("ctx"), PIECES)
    for apart in range(PIECES):
        pieces = other if apart % 2 else same
        for position in range(2):
            piece = pieces[apart // 2, position].astype(jnp.float32)
            place = (seat ^ apart) * 2 + (position ^ plane)
            first = place * 2 * DOWN_OUT_ROWS
            block = piece[:DOWN_OUT_ROWS]
            down_out[pl.ds(first, DOWN_OUT_ROWS, stride=2), :] = block
            down_out[pl.ds(first + 1, DOWN_OUT_ROWS, stride=2), :] = pltpu.roll(block, 64, 1)
            first = pl.multiple_of(place * UP_OUT_ROWS, UP_OUT_ROWS)
            up_out[pl.ds(first, UP_OUT_ROWS), :] = piece[DOWN_OUT_ROWS:]
    dot = partial(jnp.dot, preferred_element_type=jnp.float32)
    rank = dot(attended[...], down_out[...].astype(jnp.bfloat16))[:, :ADAPTER_RANK]
    rank = rank.astype(jnp.bfloat16)
    blocks = D // 128
    for first in range(0, blocks, 4):
        weight = [
            up_out[pl.ds(first + block, ADAPTER_RANK, stride=blocks), :].astype(jnp.bfloat16)
            for block in range(4)
        ]
        delta = adapter_scale * dot(rank, jnp.concatenate(weight, 1))
        out_delta[:, first * 128 : (first + 4) * 128] = delta.astype(jnp.bfloat16)


def widen(attended, same, other):
    return pl.pallas_call(
        widen_kernel,
        out_shape=jax.ShapeDtypeStruct((attended.shape[0], D), jnp.bfloat16),
        in_specs=[pl.BlockSpec(memory_space=pltpu.VMEM)] * 3,
        out_specs=pl.BlockSpec(memory_space=pltpu.VMEM),
        scratch_shapes=[
            pltpu.VMEM((QH * HEAD_SIZE, 128), jnp.float32),
            pltpu.VMEM((ADAPTER_RANK * D // 128, 128), jnp.float32),
        ],
        compiler_params=pltpu.CompilerParams(vmem_limit_bytes=32 << 20),
        cost_estimate=pl.CostEstimate(flops=1 << 27, bytes_accessed=4 << 20, transcendentals=0),
    )(attended, same, other)


def swap(block, mask):
    return lax.ppermute(block, ("groups", "ctx"), [(i, i ^ mask) for i in range(4 * PIECES)])


def direct_shards(
    normed_input, query_base, key_base, value_base, adapter_pool, stretch_adapter, adapter_owner
):
    tok_rows = normed_input.shape[0]
    ctx = lax.axis_size("ctx")
    seq = ctx * tok_rows
    blocks = [list(range(PIECES)), list(range(PIECES, 2 * PIECES))]
    half_dim = HEAD_SIZE // 2
    frequency = rope_base ** (-(jnp.arange(half_dim, dtype=jnp.float32) * 2.0) / HEAD_SIZE)
    angle = jnp.arange(seq, dtype=jnp.int32).astype(jnp.float32)[:, None] * frequency[None, :]
    cosine = jnp.cos(angle)
    sine = jnp.sin(angle)
    cosines = jnp.concatenate([cosine, cosine], 1)
    sines = jnp.concatenate([-sine, sine], 1)

    def after(block, *others):
        return lax.optimization_barrier((block, others))[0]

    def exchange(sent):
        across = swap(sent[2], 2 * PIECES)
        return [sent[0], swap(sent[1], PIECES), across, swap(sent[3], 3 * PIECES)]

    def along_z(block):
        return jnp.stack([block, swap(block, 4)])

    def along_x(pair):
        quad = jnp.stack([pair, swap(pair, 2)], 1)
        return quad.reshape((PIECES // 2,) + pair.shape[1:])

    elsewhere = swap(stretch_adapter, 2 * PIECES)
    packed = pack_row(adapter_pool, SECTIONS)
    even, odd = deal(normed_input, packed)
    sibling = swap(odd, 1)
    base = jnp.concatenate([key_base, value_base], 1)
    base = jnp.stack([base, swap(base, PIECES)])

    spread = lax.all_to_all(packed, "ctx", 0, 0, axis_index_groups=blocks)
    spread = after(spread, sibling, base, cosines, sines)
    sent, near, far = pick(spread, stretch_adapter, elsewhere, adapter_owner)
    arrived = exchange(sent)
    dealt = [after(jnp.stack([even[j], sibling[j]]), sent) for j in range(PIECES // 2)]
    dealt = [swap(block, 2 * j) if j else block for j, block in enumerate(dealt)]

    weight, ups = join(stretch_adapter, adapter_owner, arrived)
    far = swap(after(far, weight), PIECES)
    partial_sums = narrow(weight, dealt)
    back = [swap(block, 2 * j) if j else block for j, block in enumerate(partial_sums)]
    back = after(back, far)
    back = sum(block.astype(jnp.float32) for block in back)
    base = after(base, *partial_sums)
    base = [base, swap(base, 2), swap(base, 4)]
    own_rank = swap(after(back[1].astype(jnp.bfloat16), base[1]), 1)
    own_rank = back[0] + own_rank.astype(jnp.float32)
    own_rank = own_rank.astype(jnp.bfloat16)
    ups = along_z(after(ups, *partial_sums))
    all_rank = own_rank[:, ADAPTER_RANK:]
    own, across = settle(
        stretch_adapter, elsewhere, adapter_owner, near, after(far, own_rank)
    )
    ends = jnp.stack([own, swap(across, 2 * PIECES)])
    all_rank = jnp.stack([all_rank, swap(all_rank, PIECES)])
    base = jnp.stack(base + [swap(after(base[2], all_rank), 2)])
    all_rank = after(all_rank, ups)
    ups = along_x(after(ups, all_rank))
    all_rank = jnp.stack([swap(all_rank, apart) if apart else all_rank for apart in (0, 2, 4, 6)])
    base = after(base, all_rank)
    base = (base, swap(base, 1))
    gathered = jnp.concatenate([all_rank.reshape(-1, 128), ups.reshape(-1, 128)])
    gathered = after(gathered, ends)
    gathered = (gathered, swap(gathered, 1))

    shared = (query_base, base, own_rank, gathered, cosines, sines)
    attended = attend(0, 1, None, *shared)
    ends = after(ends, attended)
    ends = jnp.stack([swap(ends, apart) if apart else ends for apart in (0, 2, 4, 6)])
    attended = attend(1, KEYVALUE_HEADS - 1, attended, *shared)
    ends = after(ends, attended)
    return attended, widen(attended, ends, swap(ends, 1))


def shards(normed_input, query_base, key_base, value_base, adapter_pool, stretch_adapter, owner):
    fits = (
        lax.axis_size("groups") == 2
        and lax.axis_size("ctx") == 2 * PIECES
        and normed_input.shape[0] * PIECES == BLOCK_TOKENS
        and adapter_pool.shape[0] == 1
    )
    plan = direct_shards if fits else spread_shards
    return plan(
        normed_input, query_base, key_base, value_base, adapter_pool, stretch_adapter, owner
    )


def solution(mesh):
    placed = (
        P(("groups", "ctx"), None),
        P(("groups", "ctx"), None),
        P(("groups", "ctx"), None),
        P(("groups", "ctx"), None),
        P("ctx", None),
        P("groups"),
        P(),
    )
    return jax.shard_map(
        shards,
        mesh=mesh,
        in_specs=placed,
        out_specs=(P(("groups", "ctx"), None), P(("groups", "ctx"), None)),
        check_vma=False,
    )
```

```python
from functools import partial
import math

import jax
import jax.numpy as jnp
from jax import lax
from jax.experimental import pallas as pl
from jax.experimental.pallas import tpu as pltpu
from jax.sharding import PartitionSpec as P

D = 8192
QH = 32
KEYVALUE_HEADS = 4
HEAD_SIZE = 128
ADAPTER_RANK = 64
BLOCK_TOKENS = 512
QKV_POOL = 1900544


adapter_scale = 2.0
rope_base = 500000.0
mask_floor = -1e30


def from_partner(block, axis, apart):
    count = lax.axis_size(axis)
    route = []
    for low in range(count):
        high = low | 1 << apart
        if high != low and high < count:
            route += [(low, high), (high, low)]
    return lax.ppermute(block, axis, route)


def rotate(delta, token_positions, heads):
    half_dim = HEAD_SIZE // 2
    frequency = rope_base ** (-(jnp.arange(half_dim, dtype=jnp.float32) * 2.0) / HEAD_SIZE)
    angle = token_positions.astype(jnp.float32)[:, None] * frequency[None, :]
    cosine = jnp.cos(angle)[:, None, :]
    sine_part = jnp.sin(angle)[:, None, :]
    shaped = delta.reshape(delta.shape[0], heads, HEAD_SIZE)
    first_half = shaped[..., :half_dim]
    second_half = shaped[..., half_dim:]
    joined = jnp.concatenate(
        [
            first_half * cosine - second_half * sine_part,
            second_half * cosine + first_half * sine_part,
        ],
        -1,
    )
    return joined.reshape(delta.shape[0], heads * HEAD_SIZE)


def project_heads(
    narrow_product, query_row_block, key_row_block, value_row_block, upper_part, token_positions
):
    query_up_weight = upper_part[: ADAPTER_RANK * QH * HEAD_SIZE].reshape(
        ADAPTER_RANK, QH * HEAD_SIZE
    )
    keyvalue_up_weight = upper_part[ADAPTER_RANK * QH * HEAD_SIZE :].reshape(
        ADAPTER_RANK, 2 * KEYVALUE_HEADS * HEAD_SIZE
    )
    query_correction = adapter_scale * jnp.dot(
        narrow_product[:, :ADAPTER_RANK], query_up_weight, preferred_element_type=jnp.float32
    )
    key_correction = adapter_scale * jnp.dot(
        narrow_product[:, ADAPTER_RANK : 2 * ADAPTER_RANK],
        keyvalue_up_weight[:, : KEYVALUE_HEADS * HEAD_SIZE],
        preferred_element_type=jnp.float32,
    )
    value_correction = adapter_scale * jnp.dot(
        narrow_product[:, 2 * ADAPTER_RANK :],
        keyvalue_up_weight[:, KEYVALUE_HEADS * HEAD_SIZE :],
        preferred_element_type=jnp.float32,
    )
    queries = (
        query_row_block.astype(jnp.float32) + rotate(query_correction, token_positions, QH)
    ).astype(jnp.bfloat16)
    new_keys = (
        key_row_block.astype(jnp.float32) + rotate(key_correction, token_positions, KEYVALUE_HEADS)
    ).astype(jnp.bfloat16)
    new_values = (value_row_block.astype(jnp.float32) + value_correction).astype(jnp.bfloat16)
    return (queries, new_keys, new_values)


def output_delta(attended_rows, out_part):
    down_out = out_part[: QH * HEAD_SIZE * ADAPTER_RANK].reshape(QH * HEAD_SIZE, ADAPTER_RANK)
    raised_output = out_part[QH * HEAD_SIZE * ADAPTER_RANK :].reshape(ADAPTER_RANK, D)
    narrow_product = jnp.dot(attended_rows, down_out, preferred_element_type=jnp.float32).astype(
        jnp.bfloat16
    )
    return (
        adapter_scale * jnp.dot(narrow_product, raised_output, preferred_element_type=jnp.float32)
    ).astype(jnp.bfloat16)


def head_major(query_row_block):
    count_rows = query_row_block.shape[0]
    group_size = QH // KEYVALUE_HEADS
    return (
        query_row_block.reshape(count_rows, KEYVALUE_HEADS, group_size, HEAD_SIZE)
        .transpose(1, 2, 0, 3)
        .reshape(KEYVALUE_HEADS, group_size * count_rows, HEAD_SIZE)
    )


def row_major(head_rows, count_rows):
    group_size = QH // KEYVALUE_HEADS
    return (
        head_rows.reshape(KEYVALUE_HEADS, group_size, count_rows, HEAD_SIZE)
        .transpose(2, 0, 1, 3)
        .reshape(count_rows, QH * HEAD_SIZE)
    )


def online_update(current, queries, query_pos, key_slice, value_slice, key_start):
    run_max, run_sum, run_acc = current
    scores = jnp.einsum(
        "hqd,khd->hqk", queries, key_slice, preferred_element_type=jnp.float32
    ) * HEAD_SIZE ** (-0.5)
    key_pos = key_start + jnp.arange(key_slice.shape[0], dtype=jnp.int32)
    allowed = (query_pos[:, None] >= key_pos[None, :])[None]
    new_max = jnp.maximum(run_max, jnp.max(jnp.where(allowed, scores, mask_floor), axis=-1))
    weights = jnp.where(allowed, jnp.exp(scores - new_max[..., None]), 0.0)
    rescale = jnp.exp(run_max - new_max)
    new_sum = run_sum * rescale + jnp.sum(weights, axis=-1)
    new_acc = run_acc * rescale[..., None] + jnp.einsum(
        "hqk,khd->hqd",
        weights.astype(jnp.bfloat16),
        value_slice,
        preferred_element_type=jnp.float32,
    )
    return (new_max, new_sum, new_acc)


def unchanged(current):
    return current


def fold_keys(carry_state, shard_part, prepared):
    key_row_block, value_row_block = shard_part
    key_count = key_row_block.shape[0]
    sub_width = math.gcd(key_count, 1024)
    key_heads = key_row_block.reshape(key_count // sub_width, sub_width, KEYVALUE_HEADS, HEAD_SIZE)
    value_heads = value_row_block.reshape(
        key_count // sub_width, sub_width, KEYVALUE_HEADS, HEAD_SIZE
    )

    def one_step(sub_index, carried):
        key_start = sub_index * sub_width
        key_slice = lax.dynamic_index_in_dim(key_heads, sub_index, 0, keepdims=False)
        value_slice = lax.dynamic_index_in_dim(value_heads, sub_index, 0, keepdims=False)
        updated = []
        for (queries, query_pos), running in zip(prepared, carried):
            advance = partial(
                online_update,
                queries=queries,
                query_pos=query_pos,
                key_slice=key_slice,
                value_slice=value_slice,
                key_start=key_start,
            )
            updated.append(lax.cond(key_start <= jnp.max(query_pos), advance, unchanged, running))
        return tuple(updated)

    return lax.fori_loop(0, key_count // sub_width, one_step, carry_state)


def finish_block(result, count_rows):
    run_max, run_sum, run_acc = result
    divisor = jnp.where(run_sum > 0.0, run_sum, 1.0)
    return row_major(run_acc / divisor[..., None], count_rows).astype(jnp.bfloat16)


def spread_shards(
    normed_input, query_base, key_base, value_base, adapter_pool, stretch_adapter, adapter_owner
):
    cycle_size = lax.axis_size("ctx")
    my_index = lax.axis_index("ctx")
    tok_rows = normed_input.shape[0]
    token_positions = my_index * tok_rows + jnp.arange(tok_rows, dtype=jnp.int32)
    device_ids = jnp.arange(cycle_size, dtype=jnp.int32)
    stretch_of = device_ids * tok_rows // BLOCK_TOKENS
    stretch_ids = jnp.arange(stretch_adapter.shape[0], dtype=jnp.int32)
    adapter_of = jnp.sum(
        jnp.where(stretch_of[:, None] == stretch_ids[None, :], stretch_adapter[None, :], 0), axis=1
    )
    adapter_ids = jnp.arange(adapter_owner.shape[0], dtype=jnp.int32)
    slot_of = jnp.sum(
        jnp.where(adapter_of[:, None] == adapter_ids[None, :], adapter_owner[None, :], 0), axis=1
    )
    down_size = 3 * ADAPTER_RANK * D
    group_count = BLOCK_TOKENS // tok_rows
    levels = group_count.bit_length() - 1
    local_index = my_index % group_count
    col_width = D // group_count
    piece_len = down_size // (group_count * cycle_size)
    pool_rows = adapter_pool.shape[0]
    down_shaped = adapter_pool[:, :down_size].reshape(pool_rows, group_count, cycle_size, piece_len)
    spread_down = lax.all_to_all(down_shaped, "ctx", split_axis=2, concat_axis=0, tiled=True)
    flat_down = spread_down.reshape(-1, piece_len)
    wanted = jnp.take(flat_down, slot_of * group_count + device_ids % group_count, axis=0)[
        :, None, :
    ]
    down_slice = lax.all_to_all(wanted, "ctx", split_axis=0, concat_axis=1, tiled=True).reshape(
        col_width, 3 * ADAPTER_RANK
    )
    spread_rest = lax.all_to_all(
        adapter_pool[:, down_size:], "ctx", split_axis=1, concat_axis=0, tiled=True
    )
    rest_row = lax.all_to_all(
        jnp.take(spread_rest, slot_of, axis=0), "ctx", split_axis=0, concat_axis=1, tiled=True
    )[0]
    upper_part = rest_row[: QKV_POOL - down_size]
    out_part = rest_row[QKV_POOL - down_size :]
    pieces = normed_input.reshape(tok_rows, group_count, col_width)
    slice_order = jnp.bitwise_xor(local_index, jnp.arange(group_count, dtype=jnp.int32))
    moving = jnp.take(pieces, slice_order, axis=1).transpose(1, 0, 2)
    for level in range(levels):
        shaped = moving.reshape(group_count >> level + 1, 2, 1 << level, tok_rows, col_width)
        arrived = from_partner(shaped[:, 1], "ctx", level)
        moving = jnp.stack([shaped[:, 0], arrived], 1).reshape(group_count, tok_rows, col_width)
    partial_rows = jnp.dot(
        moving.reshape(group_count * tok_rows, col_width),
        down_slice,
        preferred_element_type=jnp.float32,
    ).reshape(group_count, tok_rows, 3 * ADAPTER_RANK)
    for level in reversed(range(levels)):
        halves = partial_rows.reshape(2, partial_rows.shape[0] // 2, tok_rows, 3 * ADAPTER_RANK)
        partial_rows = halves[0] + from_partner(
            halves[1].astype(jnp.bfloat16), "ctx", level
        ).astype(jnp.float32)
    narrow_product = partial_rows[0].astype(jnp.bfloat16)
    queries, new_keys, new_values = project_heads(
        narrow_product, query_base, key_base, value_base, upper_part, token_positions
    )
    group_size = QH // KEYVALUE_HEADS
    blocks = [(queries, token_positions)]
    prepared = [
        (head_major(block_q), jnp.tile(block_pos, group_size)) for block_q, block_pos in blocks
    ]
    initial = tuple(
        (
            (
                jnp.full((KEYVALUE_HEADS, head_q.shape[1]), mask_floor, jnp.float32),
                jnp.zeros((KEYVALUE_HEADS, head_q.shape[1]), jnp.float32),
                jnp.zeros((KEYVALUE_HEADS, head_q.shape[1], HEAD_SIZE), jnp.float32),
            )
            for head_q, block_pos in prepared
        )
    )
    finals = fold_keys(
        initial,
        (
            lax.all_gather(new_keys, "ctx", axis=0, tiled=True),
            lax.all_gather(new_values, "ctx", axis=0, tiled=True),
        ),
        prepared,
    )
    attended = finish_block(finals[0], tok_rows)
    out_delta = output_delta(attended, out_part)
    return (attended, out_delta)


PIECES = 8
GROUP = QH // KEYVALUE_HEADS
SECTIONS = ((0, 12288), (12288, 2048), (14336, 512), (14848, 2048), (16896, 4096))
DOWN_ROWS, QUERY_ROWS, KEYVAL_ROWS, DOWN_OUT_ROWS, UP_OUT_ROWS = 768, 128, 32, 128, 256
UP_ROWS = QUERY_ROWS + 2 * KEYVAL_ROWS
FIRST_ROWS = DOWN_ROWS + QUERY_ROWS + KEYVAL_ROWS


def pack_kernel(sections, pool, *refs):
    out, buffers, sems = refs[-3:]
    plane = lax.axis_index("groups")
    slabs, slab_rows = out.shape[:2]

    def copies(slab):
        listed = []
        offset = 0
        for first, rows in sections:
            share = rows // (2 * PIECES)
            begin = first + (slab * 2 + plane) * share
            listed.append(
                pltpu.make_async_copy(
                    pool.at[:, pl.ds(pl.multiple_of(begin * 128, 2048), share * 128)],
                    buffers.at[slab, :, pl.ds(offset, share * 128)],
                    sems.at[slab, len(listed)],
                )
            )
            offset += share * 128
        return listed

    for slab in range(slabs):
        for copy in copies(slab):
            copy.start()

    def step(slab, carried):
        for copy in copies(slab):
            copy.wait()

        def chunk(index, inner):
            line = buffers[slab, :, pl.ds(pl.multiple_of(index * 2048, 2048), 2048)]
            block = line.astype(jnp.float32).reshape(16, 128).astype(jnp.bfloat16)
            out[slab, pl.ds(pl.multiple_of(index * 16, 16), 16), :] = block
            return inner

        lax.fori_loop(0, slab_rows // 16, chunk, 0, unroll=8)
        return carried

    lax.fori_loop(0, slabs, step, 0)


def pack_row(pool, sections, *after):
    slab_rows = sum(rows for _, rows in sections) // (2 * PIECES)
    return pl.pallas_call(
        partial(pack_kernel, sections),
        out_shape=jax.ShapeDtypeStruct((PIECES, slab_rows, 128), jnp.bfloat16),
        in_specs=[pl.BlockSpec(memory_space=pl.ANY)] * (1 + len(after)),
        out_specs=pl.BlockSpec(memory_space=pltpu.VMEM),
        scratch_shapes=[
            pltpu.VMEM((PIECES, 1, slab_rows * 128), jnp.bfloat16),
            pltpu.SemaphoreType.DMA((PIECES, len(sections))),
        ],
        compiler_params=pltpu.CompilerParams(vmem_limit_bytes=60 << 20),
        cost_estimate=pl.CostEstimate(flops=0, bytes_accessed=8 << 20, transcendentals=0),
    )(pool, *after)


def pick_kernel(here, there, owner, spread, *refs):
    outs, lasts, sems = refs[:4], refs[4:6], refs[6]
    half = lax.axis_index("ctx") // PIECES
    last = spread.shape[1] - FIRST_ROWS
    copies = []
    for flip, out in enumerate(outs):
        wishes = there if flip >= 2 else here
        block = half ^ (flip & 1)
        row = lax.rem(owner[wishes[block]], PIECES)
        mirrored = lax.rem(owner[wishes[1 - block]], PIECES)
        pairs = (
            (spread.at[row, pl.ds(0, FIRST_ROWS)], out.at[pl.ds(0, FIRST_ROWS)]),
            (
                spread.at[mirrored, pl.ds(FIRST_ROWS - KEYVAL_ROWS, KEYVAL_ROWS)],
                out.at[pl.ds(FIRST_ROWS, KEYVAL_ROWS)],
            ),
            (spread.at[row, pl.ds(FIRST_ROWS, last)], lasts[flip % 2].at[flip // 2]),
        )
        for number, (source, target) in enumerate(pairs):
            copies.append(pltpu.make_async_copy(source, target, sems.at[flip, number]))
    for copy in copies:
        copy.start()
    for copy in copies:
        copy.wait()


def pick(spread, here, there, owner):
    last = spread.shape[1] - FIRST_ROWS
    first_shape = jax.ShapeDtypeStruct((FIRST_ROWS + KEYVAL_ROWS, 128), jnp.bfloat16)
    last_shape = jax.ShapeDtypeStruct((2, last, 128), jnp.bfloat16)
    outs = pl.pallas_call(
        pick_kernel,
        out_shape=(first_shape,) * 4 + (last_shape,) * 2,
        in_specs=[pl.BlockSpec(memory_space=pltpu.SMEM)] * 3 + [pl.BlockSpec(memory_space=pl.ANY)],
        out_specs=(pl.BlockSpec(memory_space=pltpu.VMEM),) * 6,
        scratch_shapes=[pltpu.SemaphoreType.DMA((4, 3))],
        compiler_params=pltpu.CompilerParams(vmem_limit_bytes=16 << 20),
        cost_estimate=pl.CostEstimate(flops=0, bytes_accessed=3 << 20, transcendentals=0),
    )(here, there, owner, spread)
    return outs[:4], outs[4], outs[5]


def deal_kernel(rows, even, odd, sems):
    seat = lax.rem(lax.axis_index("ctx"), PIECES)
    width = rows.shape[1] // PIECES
    copies = []
    for apart in range(PIECES):
        first = pl.multiple_of((seat ^ apart) * width, width)
        target = (odd if apart % 2 else even).at[apart // 2]
        copies.append(
            pltpu.make_async_copy(rows.at[:, pl.ds(first, width)], target, sems.at[apart])
        )
    for copy in copies:
        copy.start()
    for copy in copies:
        copy.wait()


def deal(rows, *after):
    slab = jax.ShapeDtypeStruct((PIECES // 2, rows.shape[0], rows.shape[1] // PIECES), rows.dtype)

    def kernel(rows, *refs):
        deal_kernel(rows, *refs[-3:])

    return pl.pallas_call(
        kernel,
        out_shape=(slab, slab),
        in_specs=[pl.BlockSpec(memory_space=pl.ANY)] * (1 + len(after)),
        out_specs=(pl.BlockSpec(memory_space=pltpu.VMEM),) * 2,
        scratch_shapes=[pltpu.SemaphoreType.DMA((PIECES,))],
        compiler_params=pltpu.CompilerParams(vmem_limit_bytes=16 << 20),
        cost_estimate=pl.CostEstimate(flops=0, bytes_accessed=2 << 20, transcendentals=0),
    )(rows, *after)


def nearest(here, owner, block):
    half = lax.axis_index("ctx") // PIECES
    return owner[here[block]] // PIECES == half


def choose(close, arrived, put):
    plane = lax.axis_index("groups")

    @pl.when(close)
    def _():
        put(arrived[0], plane)
        put(arrived[2], 1 - plane)

    @pl.when(jnp.logical_not(close))
    def _():
        put(arrived[1], plane)
        put(arrived[3], 1 - plane)


def join_kernel(here, owner, *refs):
    (across, own, mirror, both), (weight, ups), (flat, left, right) = refs[:4], refs[4:6], refs[6:]
    arrived = (own, mirror, across, both)
    half = lax.axis_index("ctx") // PIECES
    split = DOWN_ROWS + QUERY_ROWS + KEYVAL_ROWS

    def put_own(source, position):
        first = pl.multiple_of(position * DOWN_ROWS, DOWN_ROWS)
        flat[pl.ds(first, DOWN_ROWS), :] = source[:DOWN_ROWS, :].astype(jnp.float32)
        ups[position, : UP_ROWS - KEYVAL_ROWS, :] = source[DOWN_ROWS:split, :]

    def put_mirrored(source, position):
        ups[position, UP_ROWS - KEYVAL_ROWS :, :] = source[split:, :]

    choose(nearest(here, owner, half), arrived, put_own)
    choose(nearest(here, owner, 1 - half), arrived, put_mirrored)

    third = flat.shape[0] // 3
    one = flat[pl.ds(0, third, stride=3), :]
    two = pltpu.roll(flat[pl.ds(1, third, stride=3), :], 64, 1)
    three = pltpu.roll(flat[pl.ds(2, third, stride=3), :], 64, 1)
    lane = lax.broadcasted_iota(jnp.int32, one.shape, 1)
    left[pl.ds(0, third, stride=2), :] = one
    left[pl.ds(1, third, stride=2), :] = jnp.where(lane < 64, two, three)
    right[pl.ds(0, third, stride=2), :] = pltpu.roll(two, 64, 1)
    right[pl.ds(1, third, stride=2), :] = three
    weight[...] = jnp.concatenate([left[...], right[...]], 1).astype(jnp.bfloat16)


def join(here, owner, arrived):
    depth = D // PIECES
    return pl.pallas_call(
        join_kernel,
        out_shape=(
            jax.ShapeDtypeStruct((depth, 256), jnp.bfloat16),
            jax.ShapeDtypeStruct((2, UP_ROWS, 128), jnp.bfloat16),
        ),
        in_specs=[pl.BlockSpec(memory_space=pltpu.SMEM)] * 2
        + [pl.BlockSpec(memory_space=pltpu.VMEM)] * 4,
        out_specs=(pl.BlockSpec(memory_space=pltpu.VMEM),) * 2,
        scratch_shapes=[
            pltpu.VMEM((2 * DOWN_ROWS, 128), jnp.float32),
            pltpu.VMEM((depth, 128), jnp.float32),
            pltpu.VMEM((depth, 128), jnp.float32),
        ],
        compiler_params=pltpu.CompilerParams(vmem_limit_bytes=16 << 20),
        cost_estimate=pl.CostEstimate(flops=0, bytes_accessed=96 << 20, transcendentals=0),
    )(here, owner, arrived[2], arrived[0], arrived[1], arrived[3])


def settle_kernel(here, there, owner, near, far, own, across):
    half = lax.axis_index("ctx") // PIECES
    for number, (wishes, out) in enumerate(((here, own), (there, across))):
        close = nearest(wishes, owner, half)

        @pl.when(close)
        def _():
            out[...] = near[number]

        @pl.when(jnp.logical_not(close))
        def _():
            out[...] = far[number]


def settle(here, there, owner, near, far):
    slab = jax.ShapeDtypeStruct(near.shape[1:], jnp.bfloat16)
    return pl.pallas_call(
        settle_kernel,
        out_shape=(slab, slab),
        in_specs=[pl.BlockSpec(memory_space=pltpu.SMEM)] * 3
        + [pl.BlockSpec(memory_space=pltpu.VMEM)] * 2,
        out_specs=(pl.BlockSpec(memory_space=pltpu.VMEM),) * 2,
        compiler_params=pltpu.CompilerParams(vmem_limit_bytes=16 << 20),
        cost_estimate=pl.CostEstimate(flops=0, bytes_accessed=1 << 20, transcendentals=0),
    )(here, there, owner, near, far)


def narrow_kernel(weight, *refs):
    for block, out in zip(refs[:4], refs[4:]):
        sides, rows, depth = block.shape
        product = jnp.dot(
            block[...].reshape(sides * rows, depth),
            weight[...],
            preferred_element_type=jnp.float32,
        )
        out[...] = product[:, : 3 * ADAPTER_RANK].reshape(out.shape).astype(jnp.bfloat16)


def narrow(weight, dealt):
    sides, rows, depth = dealt[0].shape
    partial_sums = jax.ShapeDtypeStruct((sides, rows, 3 * ADAPTER_RANK), jnp.bfloat16)
    return pl.pallas_call(
        narrow_kernel,
        out_shape=(partial_sums,) * 4,
        in_specs=[pl.BlockSpec(memory_space=pltpu.VMEM)] * 5,
        out_specs=(pl.BlockSpec(memory_space=pltpu.VMEM),) * 4,
        compiler_params=pltpu.CompilerParams(vmem_limit_bytes=16 << 20),
        cost_estimate=pl.CostEstimate(
            flops=2 * 8 * rows * depth * 256, bytes_accessed=2 << 20, transcendentals=0
        ),
    )(weight, *dealt)


def attend_kernel(
    first_head,
    query_block,
    key_same,
    key_other,
    value_same,
    value_other,
    own_rank,
    rows_same,
    rows_other,
    cosines,
    sines,
    *refs,
):
    attended, flat_query, flat_keyval, keys, values = refs[-5:]
    step = pl.program_id(0) + first_head
    rows = query_block.shape[0]
    base = lax.axis_index("ctx") * rows
    half = lax.axis_index("ctx") // PIECES
    seat = lax.rem(lax.axis_index("ctx"), PIECES)
    dot = partial(jnp.dot, preferred_element_type=jnp.float32)

    @pl.when(pl.program_id(0) == 0)
    def _():
        for apart in range(PIECES):
            source = rows_other if apart % 2 else rows_same
            for position in range(2):
                begin = PIECES * rows + (apart // 2 * 2 + position) * UP_ROWS
                piece = source[begin : begin + UP_ROWS, :].astype(jnp.float32)
                place = (seat ^ apart) * 2 + position
                first = pl.multiple_of(place * QUERY_ROWS, QUERY_ROWS)
                flat_query[pl.ds(first, QUERY_ROWS), :] = piece[:QUERY_ROWS]
                first = pl.multiple_of(place * KEYVAL_ROWS, KEYVAL_ROWS)
                for side in range(2):
                    begin = QUERY_ROWS + side * KEYVAL_ROWS
                    flat_keyval[side, pl.ds(first, KEYVAL_ROWS), :] = piece[
                        begin : begin + KEYVAL_ROWS
                    ]

    def turned(delta, cosine, sine):
        return delta * cosine + pltpu.roll(delta, HEAD_SIZE // 2, 1) * sine

    def up(flat, first, stride):
        return flat[pl.ds(first, ADAPTER_RANK, stride=stride), :].astype(jnp.bfloat16)

    for side in range(2):
        heads = 2 * KEYVALUE_HEADS
        key_up = up(flat_keyval.at[side], step, heads)
        value_up = up(flat_keyval.at[side], step + KEYVALUE_HEADS, heads)
        for core in range(2):
            source = rows_other if core else rows_same
            rank = [
                source[(2 * chip + side) * rows : (2 * chip + side + 1) * rows, :]
                for chip in range(PIECES // 2)
            ]
            rank = jnp.concatenate(rank, 0)
            key_delta = adapter_scale * dot(rank[:, :ADAPTER_RANK], key_up)
            value_delta = adapter_scale * dot(rank[:, ADAPTER_RANK:], value_up)
            for chip in range(PIECES // 2):
                there = seat ^ (2 * chip + core)
                first = ((half ^ side) * PIECES + there) * rows
                span = pl.ds(pl.multiple_of(first, rows), rows)
                part = slice(chip * rows, (chip + 1) * rows)
                delta = turned(key_delta[part], cosines[span, :], sines[span, :])
                full = (key_other if core else key_same)[chip, side].astype(jnp.float32) + delta
                keys[span, :] = full.astype(jnp.bfloat16)
                full = (value_other if core else value_same)[chip, side].astype(jnp.float32)
                values[span, :] = (full + value_delta[part]).astype(jnp.bfloat16)
    here = pl.ds(pl.multiple_of(base, rows), rows)
    cosine = cosines[here, :]
    sine = sines[here, :]
    taken = GROUP
    limit = lax.broadcasted_iota(jnp.int32, (rows, 1), 0) + base
    limit = jnp.concatenate([limit] * taken, 0)
    for first in range(0, GROUP, taken):
        weight = [up(flat_query, step * GROUP + first + head, QH) for head in range(taken)]
        deltas = adapter_scale * dot(own_rank[:, :ADAPTER_RANK], jnp.concatenate(weight, 1))
        queries = []
        for place in range(taken):
            moved = turned(deltas[:, place * HEAD_SIZE : (place + 1) * HEAD_SIZE], cosine, sine)
            span = slice((first + place) * HEAD_SIZE, (first + place + 1) * HEAD_SIZE)
            queries.append(
                (query_block[:, span].astype(jnp.float32) + moved).astype(jnp.bfloat16)
            )
        queries = jnp.concatenate(queries, 0)
        scores = lax.dot_general(
            queries, keys[...], (((1,), (1,)), ((), ())), preferred_element_type=jnp.float32
        )
        column = lax.broadcasted_iota(jnp.int32, scores.shape, 1)
        scores = jnp.where(column <= limit, scores, mask_floor)
        scores = scores - jnp.max(scores, axis=-1, keepdims=True)
        weights = jnp.exp(scores * HEAD_SIZE ** (-0.5))
        divisor = jnp.sum(weights, axis=-1, keepdims=True)
        result = (dot(weights.astype(jnp.bfloat16), values[...]) / divisor).astype(jnp.bfloat16)
        for place in range(taken):
            span = slice((first + place) * HEAD_SIZE, (first + place + 1) * HEAD_SIZE)
            attended[:, span] = result[place * rows : (place + 1) * rows]


def attend(first_head, heads, before, query_base, base, own_rank, gathered, cosines, sines):
    rows = query_base.shape[0]
    seq = 4 * PIECES // 2 * rows
    width = GROUP * HEAD_SIZE

    def whole(shape):
        return pl.BlockSpec(shape, lambda h: (0,) * len(shape))

    key_spec = pl.BlockSpec((PIECES // 2, 2, rows, HEAD_SIZE), lambda h: (0, 0, 0, h + first_head))
    value_spec = pl.BlockSpec(
        (PIECES // 2, 2, rows, HEAD_SIZE), lambda h: (0, 0, 0, h + first_head + KEYVALUE_HEADS)
    )
    operands = (query_base, base[0], base[1], base[0], base[1], own_rank, *gathered)
    operands += (cosines, sines) + (() if before is None else (before,))
    query_spec = pl.BlockSpec((rows, width), lambda h: (0, h + first_head))
    return pl.pallas_call(
        partial(attend_kernel, first_head),
        grid=(heads,),
        out_shape=jax.ShapeDtypeStruct((rows, QH * HEAD_SIZE), jnp.bfloat16),
        in_specs=[
            query_spec,
            key_spec,
            key_spec,
            value_spec,
            value_spec,
            whole(own_rank.shape),
            whole(gathered[0].shape),
            whole(gathered[1].shape),
            whole(cosines.shape),
            whole(sines.shape),
        ]
        + [pl.BlockSpec(memory_space=pl.ANY)] * (len(operands) - 10),
        out_specs=query_spec,
        input_output_aliases={} if before is None else {len(operands) - 1: 0},
        scratch_shapes=[
            pltpu.VMEM((2 * PIECES * QUERY_ROWS, 128), jnp.float32),
            pltpu.VMEM((2, 2 * PIECES * KEYVAL_ROWS, 128), jnp.float32),
            pltpu.VMEM((seq, HEAD_SIZE), jnp.bfloat16),
            pltpu.VMEM((seq, HEAD_SIZE), jnp.bfloat16),
        ],
        compiler_params=pltpu.CompilerParams(vmem_limit_bytes=32 << 20),
        cost_estimate=pl.CostEstimate(
            flops=12 * heads * rows * QH * seq * HEAD_SIZE,
            bytes_accessed=10 << 20,
            transcendentals=heads * rows * GROUP * seq,
        ),
    )(*operands)


def widen_kernel(attended, same, other, out_delta, down_out, up_out):
    plane = lax.axis_index("groups")
    seat = lax.rem(lax.axis_index("ctx"), PIECES)
    for apart in range(PIECES):
        pieces = other if apart % 2 else same
        for position in range(2):
            piece = pieces[apart // 2, position].astype(jnp.float32)
            place = (seat ^ apart) * 2 + (position ^ plane)
            first = place * 2 * DOWN_OUT_ROWS
            block = piece[:DOWN_OUT_ROWS]
            down_out[pl.ds(first, DOWN_OUT_ROWS, stride=2), :] = block
            down_out[pl.ds(first + 1, DOWN_OUT_ROWS, stride=2), :] = pltpu.roll(block, 64, 1)
            first = pl.multiple_of(place * UP_OUT_ROWS, UP_OUT_ROWS)
            up_out[pl.ds(first, UP_OUT_ROWS), :] = piece[DOWN_OUT_ROWS:]
    dot = partial(jnp.dot, preferred_element_type=jnp.float32)
    rank = dot(attended[...], down_out[...].astype(jnp.bfloat16))[:, :ADAPTER_RANK]
    rank = rank.astype(jnp.bfloat16)
    blocks = D // 128
    for first in range(0, blocks, 4):
        weight = [
            up_out[pl.ds(first + block, ADAPTER_RANK, stride=blocks), :].astype(jnp.bfloat16)
            for block in range(4)
        ]
        delta = adapter_scale * dot(rank, jnp.concatenate(weight, 1))
        out_delta[:, first * 128 : (first + 4) * 128] = delta.astype(jnp.bfloat16)


def widen(attended, same, other):
    return pl.pallas_call(
        widen_kernel,
        out_shape=jax.ShapeDtypeStruct((attended.shape[0], D), jnp.bfloat16),
        in_specs=[pl.BlockSpec(memory_space=pltpu.VMEM)] * 3,
        out_specs=pl.BlockSpec(memory_space=pltpu.VMEM),
        scratch_shapes=[
            pltpu.VMEM((QH * HEAD_SIZE, 128), jnp.float32),
            pltpu.VMEM((ADAPTER_RANK * D // 128, 128), jnp.float32),
        ],
        compiler_params=pltpu.CompilerParams(vmem_limit_bytes=32 << 20),
        cost_estimate=pl.CostEstimate(flops=1 << 27, bytes_accessed=4 << 20, transcendentals=0),
    )(attended, same, other)


def swap(block, mask):
    return lax.ppermute(block, ("groups", "ctx"), [(i, i ^ mask) for i in range(4 * PIECES)])


def direct_shards(
    normed_input, query_base, key_base, value_base, adapter_pool, stretch_adapter, adapter_owner
):
    tok_rows = normed_input.shape[0]
    ctx = lax.axis_size("ctx")
    seq = ctx * tok_rows
    blocks = [list(range(PIECES)), list(range(PIECES, 2 * PIECES))]
    half_dim = HEAD_SIZE // 2
    frequency = rope_base ** (-(jnp.arange(half_dim, dtype=jnp.float32) * 2.0) / HEAD_SIZE)
    angle = jnp.arange(seq, dtype=jnp.int32).astype(jnp.float32)[:, None] * frequency[None, :]
    cosine = jnp.cos(angle)
    sine = jnp.sin(angle)
    cosines = jnp.concatenate([cosine, cosine], 1)
    sines = jnp.concatenate([-sine, sine], 1)

    def after(block, *others):
        return lax.optimization_barrier((block, others))[0]

    def exchange(sent):
        across = swap(sent[2], 2 * PIECES)
        return [sent[0], swap(sent[1], PIECES), across, swap(sent[3], 3 * PIECES)]

    def along_z(block):
        return jnp.stack([block, swap(block, 4)])

    def along_x(pair):
        quad = jnp.stack([pair, swap(pair, 2)], 1)
        return quad.reshape((PIECES // 2,) + pair.shape[1:])

    elsewhere = swap(stretch_adapter, 2 * PIECES)
    packed = pack_row(adapter_pool, SECTIONS)
    even, odd = deal(normed_input, packed)
    sibling = swap(odd, 1)
    base = jnp.concatenate([key_base, value_base], 1)
    base = jnp.stack([base, swap(base, PIECES)])

    spread = lax.all_to_all(packed, "ctx", 0, 0, axis_index_groups=blocks)
    spread = after(spread, sibling, base, cosines, sines)
    sent, near, far = pick(spread, stretch_adapter, elsewhere, adapter_owner)
    arrived = exchange(sent)
    dealt = [after(jnp.stack([even[j], sibling[j]]), sent) for j in range(PIECES // 2)]
    dealt = [swap(block, 2 * j) if j else block for j, block in enumerate(dealt)]

    weight, ups = join(stretch_adapter, adapter_owner, arrived)
    far = swap(after(far, weight), PIECES)
    partial_sums = narrow(weight, dealt)
    back = [swap(block, 2 * j) if j else block for j, block in enumerate(partial_sums)]
    back = after(back, far)
    back = sum(block.astype(jnp.float32) for block in back)
    base = after(base, *partial_sums)
    base = [base, swap(base, 2), swap(base, 4)]
    own_rank = swap(after(back[1].astype(jnp.bfloat16), *base), 1)
    own_rank = back[0] + own_rank.astype(jnp.float32)
    own_rank = own_rank.astype(jnp.bfloat16)
    ups = along_z(after(ups, *partial_sums))
    all_rank = own_rank[:, ADAPTER_RANK:]
    base = jnp.stack(base + [swap(after(base[2], own_rank), 2)])
    own, across = settle(
        stretch_adapter, elsewhere, adapter_owner, near, after(far, own_rank)
    )
    ends = jnp.stack([own, swap(across, 2 * PIECES)])
    all_rank = jnp.stack([all_rank, swap(all_rank, PIECES)])
    all_rank = after(all_rank, ups)
    ups = along_x(after(ups, all_rank))
    all_rank = jnp.stack([swap(all_rank, apart) if apart else all_rank for apart in (0, 2, 4, 6)])
    base = after(base, all_rank)
    base = (base, swap(base, 1))
    gathered = jnp.concatenate([all_rank.reshape(-1, 128), ups.reshape(-1, 128)])
    gathered = after(gathered, ends)
    gathered = (gathered, swap(gathered, 1))

    shared = (query_base, base, own_rank, gathered, cosines, sines)
    attended = attend(0, 1, None, *shared)
    ends = along_x(after(along_z(ends), attended))
    attended = attend(1, KEYVALUE_HEADS - 1, attended, *shared)
    ends = after(ends, attended)
    return attended, widen(attended, ends, swap(ends, 1))


def shards(normed_input, query_base, key_base, value_base, adapter_pool, stretch_adapter, owner):
    fits = (
        lax.axis_size("groups") == 2
        and lax.axis_size("ctx") == 2 * PIECES
        and normed_input.shape[0] * PIECES == BLOCK_TOKENS
        and adapter_pool.shape[0] == 1
    )
    plan = direct_shards if fits else spread_shards
    return plan(
        normed_input, query_base, key_base, value_base, adapter_pool, stretch_adapter, owner
    )


def solution(mesh):
    placed = (
        P(("groups", "ctx"), None),
        P(("groups", "ctx"), None),
        P(("groups", "ctx"), None),
        P(("groups", "ctx"), None),
        P("ctx", None),
        P("groups"),
        P(),
    )
    return jax.shard_map(
        shards,
        mesh=mesh,
        in_specs=placed,
        out_specs=(P(("groups", "ctx"), None), P(("groups", "ctx"), None)),
        check_vma=False,
    )
```
